32 devices in a mesh: wide: 4 (over y, core), narrow: 8 (over z, x).
Axes of the slice: x: 2, y: 2, z: 4, core: 2. Of those that a mesh axis runs over, the one named last changes fastest.
Arguments:
- positions: float32 [3, 4, 8, 1, 128], P(None, 'wide', 'narrow'), may hold values from 0.08 to 0.92
- species: int32 [4, 8, 1, 128], P('wide', 'narrow'), may hold values 0 or 1
- neighbours: int32 [4, 8, 1, 128, 128], P('wide', 'narrow'), may hold values from 0 to 3455
- embed_one_w: float32 [2, 25], replicated, may hold values from -12 to 12
- embed_one_b: float32 [2, 25], replicated, may hold values from -6 to 6
- embed_two_w: float32 [25, 50], replicated, may hold values from -1.25 to 1.25
- embed_two_b: float32 [50], replicated, may hold values from -3 to 3
- embed_three_w: float32 [50, 100], replicated, may hold values from -0.875 to 0.875
- embed_three_b: float32 [100], replicated, may hold values from -3 to 3
- fit_one_w: float32 [1600, 240], replicated, may hold values from -0.15625 to 0.15625
- fit_one_b: float32 [240], replicated, may hold values from -6 to 6
- fit_two_w: float32 [240, 240], replicated, may hold values from -0.375 to 0.375
- fit_two_b: float32 [240], replicated, may hold values from -3 to 3
- fit_three_w: float32 [240, 240], replicated, may hold values from -0.375 to 0.375
- fit_three_b: float32 [240], replicated, may hold values from -3 to 3
- fit_out_w: float32 [240, 100], replicated, may hold values from -0.375 to 0.375
Outputs:
- dipole: float32 [3, 4, 8, 1, 128], P(None, 'wide', 'narrow')
- atom_field: float32 [4, 4, 8, 1, 128], P(None, 'wide', 'narrow')
- centroid_field: float32 [4, 4, 8, 1, 128], P(None, 'wide', 'narrow')
- energy: float32 [], replicated
The draws below stay inside these ranges and needn't reach their ends.
Inputs may be any that keep to these rules, and one draw needn't show every extreme that they name: `species`: 1 marks a hydrogen, 0 an oxygen. `neighbours`: entry c names slot c % 128 of the brick offset by (q // 9 - 1, q % 3 - 1, (q // 3) % 3 - 1) bricks along x, y, z from the atom's own, q = c // 128, periodically; an entry may name the atom itself.
All inputs are finite; a program needn't handle non-finite values. No bound on the sum of `species` on one device may be relied on, other than what follows from the above.
Results may differ from the reference program's by a relative error of at most 0.0003.
Values sent between devices are 32-bit elements; how exact they have to be, the bound alone decides.
No kernel may reach another device: no remote copies, remote signals or barrier semaphores. Data moves between devices by JAX's collectives and lax.ppermute only.
A program may use at most 128 MiB of HBM per device.

```python
import math
import jax
import jax.numpy as jnp
from jax import lax

GRID_X = 256
GRID_Y = 256
GRID_Z = 256
BRICKS_Y = 1
BRICK_ATOMS = 128
NEIGHBOURS = 128
EMBED_ONE = 25
EMBED_TWO = 50
EMBED_THREE = 100
AXIS_COLUMNS = 16
FITTING = 240
N_WIDE = 4
N_NARROW = 8


def touch_ends(values, own_key, smallest, largest):
    longest = values.shape.index(max(values.shape))
    spots = []
    for shift in (0, 1):
        where = [jax.random.randint(jax.random.fold_in(own_key, axis), (), 0, length) for axis, length in enumerate(values.shape)]
        where[longest] = (where[longest] + shift) % values.shape[longest]
        spots.append(tuple(where))
    return values.at[spots[0]].set(smallest).at[spots[1]].set(largest)


def block_scale(stream_key, shape, pieces, low, high):
    def one(axis_at, shards_of):
        heights = jax.random.uniform(jax.random.fold_in(jax.random.fold_in(stream_key, 6), axis_at), (shards_of,), jnp.float32, low / len(pieces), high / len(pieces))
        return jnp.repeat(jnp.exp(heights), shape[axis_at] // shards_of).reshape((-1,) + (1,) * (len(shape) - axis_at - 1))

    level = one(*pieces[0])
    for cut in pieces[1:]:
        level = level * one(*cut)
    return level


def centred(rng, dims, scale, bound, held_as=jnp.bfloat16):
    return jnp.clip(scale * jax.random.normal(rng, dims, jnp.float32), -bound, bound).astype(held_as)


def setup_inputs(seed: int = 0) -> dict:
    arg_keys = jax.random.split(jax.random.key(seed), 17)
    positions = jnp.clip(0.08 + 0.84000002 * jax.random.uniform(arg_keys[0], (3, N_WIDE, N_NARROW, BRICKS_Y, BRICK_ATOMS), jnp.float32) ** block_scale(arg_keys[0], (3, N_WIDE, N_NARROW, BRICKS_Y, BRICK_ATOMS), ((1, 4), (2, 8)), -0.2, 0.2), 0.08, 0.92)
    species = touch_ends((jax.random.randint(arg_keys[1], (N_WIDE, N_NARROW, BRICKS_Y, BRICK_ATOMS), 0, 3) < 2).astype(jnp.int32), jax.random.fold_in(arg_keys[1], 1), 0, 1)
    neighbours = touch_ends(jax.random.randint(arg_keys[2], (N_WIDE, N_NARROW, BRICKS_Y, BRICK_ATOMS, NEIGHBOURS), 0, 27 * BRICK_ATOMS), jax.random.fold_in(arg_keys[2], 1), 0, (27 * BRICK_ATOMS) - 1).astype(jnp.int32)
    embed_one_w = centred(arg_keys[3], (2, EMBED_ONE), 2.0, 12.0, jnp.float32)
    embed_one_b = centred(arg_keys[4], (2, EMBED_ONE), 1.0, 6.0, jnp.float32)
    embed_two_w = centred(arg_keys[5], (EMBED_ONE, EMBED_TWO), EMBED_ONE ** -0.5, 1.25, jnp.float32)
    embed_two_b = centred(arg_keys[6], (EMBED_TWO,), 0.5, 3.0, jnp.float32)
    embed_three_w = centred(arg_keys[7], (EMBED_TWO, EMBED_THREE), EMBED_TWO ** -0.5, 0.875, jnp.float32)
    embed_three_b = centred(arg_keys[8], (EMBED_THREE,), 0.5, 3.0, jnp.float32)
    fit_one_w = centred(arg_keys[9], (AXIS_COLUMNS * EMBED_THREE, FITTING), (AXIS_COLUMNS * EMBED_THREE) ** -0.5, 0.15625, jnp.float32)
    fit_one_b = centred(arg_keys[10], (FITTING,), 1.0, 6.0, jnp.float32)
    fit_two_w = centred(arg_keys[11], (FITTING, FITTING), FITTING ** -0.5, 0.375, jnp.float32)
    fit_two_b = centred(arg_keys[12], (FITTING,), 0.5, 3.0, jnp.float32)
    fit_three_w = centred(arg_keys[13], (FITTING, FITTING), FITTING ** -0.5, 0.375, jnp.float32)
    fit_three_b = centred(arg_keys[14], (FITTING,), 0.5, 3.0, jnp.float32)
    fit_out_w = centred(arg_keys[15], (FITTING, EMBED_THREE), FITTING ** -0.5, 0.375, jnp.float32)
    return {"positions": positions, "species": species, "neighbours": neighbours, "embed_one_w": embed_one_w, "embed_one_b": embed_one_b, "embed_two_w": embed_two_w, "embed_two_b": embed_two_b, "embed_three_w": embed_three_w, "embed_three_b": embed_three_b, "fit_one_w": fit_one_w, "fit_one_b": fit_one_b, "fit_two_w": fit_two_w, "fit_two_b": fit_two_b, "fit_three_w": fit_three_w, "fit_three_b": fit_three_b, "fit_out_w": fit_out_w}


radius_scale = 24.0
wannier_reach = 0.5
ewald_beta = 0.9
coulomb = 0.25
atom_block = 64
largest_value = lax.Precision.HIGHEST


def spline(offset):
    square = offset * offset
    offset_cube = square * offset
    remain = 4.0 - offset
    piece_one = offset_cube / 6.0
    piece_two = (-3.0 * offset_cube + 12.0 * square - 12.0 * offset + 4.0) / 6.0
    piece_three = (3.0 * offset_cube - 24.0 * square + 60.0 * offset - 44.0) / 6.0
    piece_four = remain * remain * remain / 6.0
    result_value = jnp.where(offset < 1.0, piece_one, jnp.where(offset < 2.0, piece_two, jnp.where(offset < 3.0, piece_three, piece_four)))
    inside = (offset >= 0.0) & (offset < 4.0)
    return jnp.where(inside, result_value, jnp.zeros_like(offset))


def slope(offset):
    square = offset * offset
    remain = 4.0 - offset
    piece_one = square / 2.0
    piece_two = (-9.0 * square + 24.0 * offset - 12.0) / 6.0
    piece_three = (9.0 * square - 48.0 * offset + 60.0) / 6.0
    piece_four = -remain * remain / 2.0
    result_value = jnp.where(offset < 1.0, piece_one, jnp.where(offset < 2.0, piece_two, jnp.where(offset < 3.0, piece_three, piece_four)))
    inside = (offset >= 0.0) & (offset < 4.0)
    return jnp.where(inside, result_value, jnp.zeros_like(offset))


def environment(relative, hydrogen, one_w, one_b, second_weight, second_bias, third_weight, third_bias):
    scaled = relative / radius_scale
    square = jnp.sum(scaled * scaled, axis=0)
    smooth = 1.0 / (1.0 + square)
    radial = jnp.concatenate([smooth[None], smooth[None] * scaled], axis=0)
    is_hydrogen = hydrogen[None] > 0.5
    weight = jnp.where(is_hydrogen, one_w[1][:, None, None], one_w[0][:, None, None])
    offset_b = jnp.where(is_hydrogen, one_b[1][:, None, None], one_b[0][:, None, None])
    first_layer = jnp.tanh(weight * smooth[None] + offset_b)
    second_layer = jnp.tanh(jnp.einsum('tky,ti->iky', first_layer, second_weight, precision=largest_value) + second_bias[:, None, None]) + jnp.concatenate([first_layer, first_layer], axis=0)
    third_layer = jnp.tanh(jnp.einsum('tky,ti->iky', second_layer, third_weight, precision=largest_value) + third_bias[:, None, None]) + jnp.concatenate([second_layer, second_layer], axis=0)
    return jnp.einsum('pbn,dbn->pdb', radial, third_layer, precision=largest_value) / relative.shape[2]


def fitting(matrix, one_w, one_b, second_weight, second_bias, third_weight, third_bias, out_w):
    descriptor = jnp.einsum('pda,pea->dea', matrix, matrix[:, :AXIS_COLUMNS], precision=largest_value)
    descriptor = descriptor.reshape(-1, matrix.shape[2])
    hidden = jnp.tanh(jnp.einsum('fh,fa->ha', one_w, descriptor, precision=largest_value) + one_b[:, None])
    hidden = hidden + jnp.tanh(jnp.einsum('gh,ga->ha', second_weight, hidden, precision=largest_value) + second_bias[:, None])
    hidden = hidden + jnp.tanh(jnp.einsum('gh,ga->ha', third_weight, hidden, precision=largest_value) + third_bias[:, None])
    coeffs = jnp.einsum('hk,ha->ka', out_w, hidden, precision=largest_value)
    return jnp.einsum('ka,cka->ca', coeffs, matrix[1:], precision=largest_value)


def folded(mode_index, length):
    wrapped = mode_index % length
    return jnp.where(2 * wrapped >= length, wrapped - length, wrapped)


def modulus(mode_index, length):
    phase_angle = (mode_index % length).astype(jnp.float32) * (2.0 * math.pi / length)
    divisor = (4.0 + 2.0 * jnp.cos(phase_angle)) / 6.0
    return 1.0 / (divisor * divisor)


def influence(index_x, index_y, index_z):
    fold_x = folded(index_x, GRID_X)
    fold_y = folded(index_y, GRID_Y)
    fold_z = folded(index_z, GRID_Z)
    freq_x = fold_x.astype(jnp.float32) / GRID_X
    freq_y = fold_y.astype(jnp.float32) / GRID_Y
    freq_z = fold_z.astype(jnp.float32) / GRID_Z
    square = freq_x * freq_x + freq_y * freq_y + freq_z * freq_z
    is_zero = (fold_x == 0) & (fold_y == 0) & (fold_z == 0)
    safe_square = jnp.where(is_zero, 1.0, square)
    result_value = jnp.exp(-(math.pi * math.pi) * square / (ewald_beta * ewald_beta)) / safe_square
    result_value = result_value * modulus(index_x, GRID_X) * modulus(index_y, GRID_Y) * modulus(index_z, GRID_Z)
    return jnp.where(is_zero, 0.0, result_value) * (coulomb / (math.pi * GRID_X * GRID_Y * GRID_Z))


def stencil(local, anchor, length):
    lower_cell = jnp.floor(local)
    counter = jnp.arange(4, dtype=jnp.int32)
    offsets = (local - lower_cell)[:, None] + counter.astype(local.dtype)[None, :]
    cell_index = (anchor[:, None] + lower_cell.astype(jnp.int32)[:, None] - counter[None, :]) % length
    return cell_index, spline(offsets), slope(offsets)


def reference(positions, species, neighbours, embed_one_w, embed_one_b, embed_two_w, embed_two_b, embed_three_w, embed_three_b, fit_one_w, fit_one_b, fit_two_w, fit_two_b, fit_three_w, fit_three_b, fit_out_w):
    cells_x = GRID_X // N_WIDE
    cells_z = GRID_Z // N_NARROW
    brick_y = GRID_Y // BRICKS_Y
    device_atoms = BRICKS_Y * BRICK_ATOMS
    atom_total = N_WIDE * N_NARROW * device_atoms
    pair_shape = (N_WIDE, N_NARROW, BRICKS_Y, BRICK_ATOMS, NEIGHBOURS)
    wide_at = lax.broadcasted_iota(jnp.int32, pair_shape, 0)
    narrow_at = lax.broadcasted_iota(jnp.int32, pair_shape, 1)
    brick_at = lax.broadcasted_iota(jnp.int32, pair_shape, 2)
    slot_index = neighbours % BRICK_ATOMS
    offset = neighbours // BRICK_ATOMS
    step_x = offset // 9
    step_z = (offset // 3) % 3
    step_y = offset % 3
    source = (((wide_at + step_x - 1) % N_WIDE * N_NARROW + (narrow_at + step_z - 1) % N_NARROW) * BRICKS_Y + (brick_at + step_y - 1) % BRICKS_Y) * BRICK_ATOMS + slot_index
    source = source.reshape(atom_total, NEIGHBOURS)
    flat_positions = positions.reshape(3, atom_total)
    hydrogen = species.reshape(atom_total).astype(jnp.float32)
    nearby = jnp.take(flat_positions, source, axis=1)
    near_kind = jnp.take(hydrogen, source)
    extent = jnp.array([cells_x, brick_y, cells_z], jnp.float32)[:, None, None]
    steps_all = (jnp.stack([step_x, step_y, step_z]) - 1).reshape(3, atom_total, NEIGHBOURS)
    relative = steps_all.astype(jnp.float32) * extent + (nearby - flat_positions[:, :, None]) * extent

    block_size = min(atom_block, device_atoms)
    block_count = atom_total // block_size
    rel_blocks = relative.reshape(3, block_count, block_size, NEIGHBOURS).transpose(1, 0, 2, 3)
    kind_blocks = near_kind.reshape(block_count, block_size, NEIGHBOURS)

    def one_block(operands):
        matrix = environment(operands[0], operands[1], embed_one_w, embed_one_b, embed_two_w, embed_two_b, embed_three_w, embed_three_b)
        return fitting(matrix, fit_one_w, fit_one_b, fit_two_w, fit_two_b, fit_three_w, fit_three_b, fit_out_w)

    dipole = lax.map(one_block, (rel_blocks, kind_blocks))
    dipole = dipole.transpose(1, 0, 2).reshape(3, atom_total)
    oxygen = 1.0 - hydrogen

    atom_shape = (N_WIDE, N_NARROW, BRICKS_Y, BRICK_ATOMS)
    wide_index = lax.broadcasted_iota(jnp.int32, atom_shape, 0).reshape(atom_total)
    narrow_index = lax.broadcasted_iota(jnp.int32, atom_shape, 1).reshape(atom_total)
    home_y = lax.broadcasted_iota(jnp.int32, atom_shape, 2).reshape(atom_total).astype(jnp.float32)
    atom_x = flat_positions[0] * cells_x
    atom_y = home_y * brick_y + flat_positions[1] * brick_y
    atom_z = flat_positions[2] * cells_z
    displace = wannier_reach * jnp.tanh(dipole)
    site_x = jnp.concatenate([atom_x, atom_x + displace[0]])
    site_y = jnp.concatenate([atom_y, atom_y + displace[1]])
    site_z = jnp.concatenate([atom_z, atom_z + displace[2]])
    charge = jnp.concatenate([6.0 * oxygen + hydrogen, -8.0 * oxygen])
    anchor_x = jnp.concatenate([wide_index, wide_index]) * cells_x
    anchor_z = jnp.concatenate([narrow_index, narrow_index]) * cells_z
    anchor_y = jnp.zeros_like(anchor_x)
    cell_x, weight_x, slope_x = stencil(site_x, anchor_x, GRID_X)
    cell_y, weight_y, slope_y = stencil(site_y, anchor_y, GRID_Y)
    cell_z, weight_z, slope_z = stencil(site_z, anchor_z, GRID_Z)
    place_x = cell_x[:, :, None, None]
    place_y = cell_y[:, None, :, None]
    place_z = cell_z[:, None, None, :]
    spread_values = charge[:, None, None, None] * weight_x[:, :, None, None] * weight_y[:, None, :, None] * weight_z[:, None, None, :]
    charge_grid = jnp.zeros((GRID_X, GRID_Y, GRID_Z), jnp.float32).at[place_x, place_y, place_z].add(spread_values)

    spectrum = jnp.fft.fftn(charge_grid)
    index_x = jnp.arange(GRID_X, dtype=jnp.int32)[:, None, None]
    index_y = jnp.arange(GRID_Y, dtype=jnp.int32)[None, :, None]
    index_z = jnp.arange(GRID_Z, dtype=jnp.int32)[None, None, :]
    green_table = influence(index_x, index_y, index_z)
    real_part = jnp.real(spectrum)
    imag_part = jnp.imag(spectrum)
    energy = 0.5 * jnp.sum(green_table * (real_part * real_part + imag_part * imag_part)) / atom_total
    potential_grid = jnp.real(jnp.fft.ifftn(green_table * spectrum)) * (GRID_X * GRID_Y * GRID_Z)

    local_values = potential_grid[place_x, place_y, place_z]
    potential = jnp.sum(local_values * weight_x[:, :, None, None] * weight_y[:, None, :, None] * weight_z[:, None, None, :], axis=(1, 2, 3))
    field_x = -jnp.sum(local_values * slope_x[:, :, None, None] * weight_y[:, None, :, None] * weight_z[:, None, None, :], axis=(1, 2, 3))
    field_y = -jnp.sum(local_values * weight_x[:, :, None, None] * slope_y[:, None, :, None] * weight_z[:, None, None, :], axis=(1, 2, 3))
    field_z = -jnp.sum(local_values * weight_x[:, :, None, None] * weight_y[:, None, :, None] * slope_z[:, None, None, :], axis=(1, 2, 3))
    fields = jnp.stack([potential, field_x, field_y, field_z])
    atom_field = fields[:, :atom_total].reshape(4, N_WIDE, N_NARROW, BRICKS_Y, BRICK_ATOMS)
    centroid_field = (fields[:, atom_total:] * oxygen[None]).reshape(4, N_WIDE, N_NARROW, BRICKS_Y, BRICK_ATOMS)
    dipole_out = (dipole * oxygen[None]).reshape(3, N_WIDE, N_NARROW, BRICKS_Y, BRICK_ATOMS)
    return (dipole_out, atom_field, centroid_field, energy)
```

```python
import math

import jax
import jax.numpy as jnp
import numpy as np
from jax import lax
from jax.experimental import pallas as pl
from jax.experimental.pallas import tpu as pltpu
from jax.sharding import PartitionSpec as P

GRID_X = 256
GRID_Y = 256
GRID_Z = 256
AXIS_COLUMNS = 16

radius_scale = 24.0
wannier_reach = 0.5
ewald_beta = 0.9
coulomb = 0.25

ROW_PAD = 32
SLOT_CHUNK = 16
HALO_X = 16
HALO_Z = 8

NN = (((1,), (0,)), ((), ()))
NT = (((1,), (1,)), ((), ()))


def split(value):
    high = value.astype(jnp.bfloat16)
    low = (value - high.astype(jnp.float32)).astype(jnp.bfloat16)
    return high, low


def multiply(left, right, dims=NN):
    def one(a, b):
        return lax.dot_general(a, b, dims, preferred_element_type=jnp.float32)

    return one(left[0], right[0]) + (one(left[1], right[0]) + one(left[0], right[1]))


def spline_pair(offset):
    centred = offset - 2.0
    away = jnp.abs(centred)
    outer = jnp.maximum(2.0 - away, 0.0)
    inner = jnp.maximum(1.0 - away, 0.0)
    outer_square = outer * outer
    inner_square = inner * inner
    value = (outer_square * outer - 4.0 * (inner_square * inner)) * (1.0 / 6.0)
    slope = jnp.where(centred < 0.0, 0.5, -0.5) * (outer_square - 4.0 * inner_square)
    return value, slope


def centroid_kernel(
    place,
    table,
    codes,
    columns,
    second,
    third,
    fit_one_w,
    fit_one_b,
    fit_two_w,
    fit_two_b,
    fit_three_w,
    fit_three_b,
    fit_out_w,
    dipole_ref,
    shift_ref,
    matrix,
    descriptor,
):
    wide_count, narrow_count, _, atoms = table.shape
    listed = codes.shape[0]
    width_one = fit_out_w.shape[1] // 4
    width_three = fit_out_w.shape[1]
    cells = (GRID_X // wide_count, GRID_Y, GRID_Z // narrow_count)
    at_wide = place[0]
    at_narrow = place[1]
    own = table[at_wide, at_narrow]
    nearby = []
    for step in range(9):
        wide_at = lax.rem(at_wide + (step // 3 - 1) + wide_count, wide_count)
        narrow_at = lax.rem(at_narrow + (step % 3 - 1) + narrow_count, narrow_count)
        nearby.append(table[wide_at, narrow_at])

    second_high, second_low = split(second[...])
    second_all = jnp.concatenate([second_high, second_high, second_low], axis=1)
    third_high, third_low = split(third[...])
    third_all = jnp.concatenate([third_high, third_high, third_low], axis=1)
    weight_oxygen = columns[0:ROW_PAD, 0:1]
    weight_hydrogen = columns[0:ROW_PAD, 1:2]
    bias_oxygen = columns[0:ROW_PAD, 2:3]
    bias_hydrogen = columns[0:ROW_PAD, 3:4]
    second_bias = columns[0 : 2 * ROW_PAD, 4:5]
    third_bias = columns[0 : 4 * ROW_PAD, 5:6]
    matrix[...] = jnp.zeros_like(matrix)

    def chunk(index, carry):
        first = pl.multiple_of(index * SLOT_CHUNK, SLOT_CHUNK)
        code = codes[pl.ds(first, SLOT_CHUNK), :]
        offset = code // atoms
        slot = code - offset * atoms
        step_x = jnp.where(offset >= 9, 1, 0) + jnp.where(offset >= 18, 1, 0)
        rest = offset - 9 * step_x
        step_z = jnp.where(rest >= 3, 1, 0) + jnp.where(rest >= 6, 1, 0)
        step_y = rest - 3 * step_z
        brick = step_x * 3 + step_z
        found = []
        for component in range(4):
            picked = jnp.zeros((SLOT_CHUNK, atoms), jnp.float32)
            for step in range(9):
                row = jnp.broadcast_to(
                    nearby[step][component : component + 1], (SLOT_CHUNK, atoms)
                )
                here = jnp.take_along_axis(row, slot, axis=1, mode="promise_in_bounds")
                picked = jnp.where(brick == step, here, picked)
            found.append(picked)
        scaled = []
        for component, step in enumerate((step_x, step_y, step_z)):
            extent = float(cells[component])
            relative = (step - 1).astype(jnp.float32) * extent + (
                found[component] - own[component : component + 1]
            ) * extent
            scaled.append(relative * (1.0 / radius_scale))
        smooth = 1.0 / (
            1.0 + (scaled[0] * scaled[0] + scaled[1] * scaled[1] + scaled[2] * scaled[2])
        )
        radial = [smooth] + [smooth * part for part in scaled]
        hydrogen = found[3] > 0.5
        first_layers = []
        for k in range(SLOT_CHUNK):
            row = smooth[k : k + 1]
            kind = hydrogen[k : k + 1]
            weight = jnp.where(kind, weight_hydrogen, weight_oxygen)
            bias = jnp.where(kind, bias_hydrogen, bias_oxygen)
            first_layers.append(jnp.tanh(weight * row + bias))
        layer_one = jnp.concatenate(first_layers, axis=1)
        high, low = split(layer_one)
        layer_two = lax.dot_general(
            second_all,
            jnp.concatenate([high, low, high], axis=0),
            NN,
            preferred_element_type=jnp.float32,
        )
        layer_two = jnp.tanh(layer_two + second_bias) + jnp.concatenate(
            [layer_one, layer_one], axis=0
        )
        high, low = split(layer_two)
        layer_three = lax.dot_general(
            third_all,
            jnp.concatenate([high, low, high], axis=0),
            NN,
            preferred_element_type=jnp.float32,
        )
        layer_three = jnp.tanh(layer_three + third_bias) + jnp.concatenate(
            [layer_two, layer_two], axis=0
        )
        for part in range(4):
            total = matrix[part]
            for k in range(SLOT_CHUNK):
                total = total + layer_three[:, k * atoms : (k + 1) * atoms] * radial[part][k : k + 1]
            matrix[part] = total
        return carry

    lax.fori_loop(0, listed // SLOT_CHUNK, chunk, 0)

    parts = []
    for part in range(4):
        padded = matrix[part] * (1.0 / listed)
        parts.append(
            jnp.concatenate(
                [padded[k * ROW_PAD : k * ROW_PAD + width_one] for k in range(4)], axis=0
            )
        )
    leading = [part[0:AXIS_COLUMNS] for part in parts]
    for row in range(width_three):
        total = parts[0][row : row + 1] * leading[0]
        for part in range(1, 4):
            total = total + parts[part][row : row + 1] * leading[part]
        descriptor[row * AXIS_COLUMNS : (row + 1) * AXIS_COLUMNS, :] = total
    entries = width_three * AXIS_COLUMNS
    descriptor[entries:, :] = jnp.zeros((descriptor.shape[0] - entries, atoms), jnp.float32)
    turned = jnp.transpose(descriptor[...])
    hidden = jnp.tanh(
        multiply(split(turned[:, :entries]), split(fit_one_w[...])) + fit_one_b[...]
    )
    hidden = hidden + jnp.tanh(multiply(split(hidden), split(fit_two_w[...])) + fit_two_b[...])
    hidden = hidden + jnp.tanh(multiply(split(hidden), split(fit_three_w[...])) + fit_three_b[...])
    coeffs = multiply(split(hidden), split(fit_out_w[...]))
    coeffs = jnp.concatenate(
        [coeffs, jnp.zeros((atoms, 128 - width_three), jnp.float32)], axis=1
    )
    coeffs = jnp.transpose(coeffs)[:width_three]
    vector = jnp.concatenate(
        [jnp.sum(coeffs * parts[1 + c], axis=0, keepdims=True) for c in range(3)], axis=0
    )
    dipole_ref[...] = vector * (1.0 - own[3:4])
    moved = wannier_reach * jnp.tanh(vector)
    moved = jnp.concatenate([moved, jnp.zeros((1, atoms), jnp.float32)], axis=0)
    for target in range(shift_ref.shape[0]):
        shift_ref[target] = moved


def mesh_kernel(
    place,
    factors,
    table,
    shifts,
    phase,
    factor_row,
    factor_column,
    ahead_high,
    ahead_low,
    back_high,
    back_low,
    out_ref,
    grid,
    modes,
    weight_high,
    weight_low,
    slope_high,
    slope_low,
    waves,
    wave_slopes,
):
    wide_count, narrow_count, _, atoms = table.shape
    cells_x = GRID_X // wide_count
    cells_z = GRID_Z // narrow_count
    window = cells_z + HALO_Z
    pair = 2 * atoms
    length = wide_count * pair
    channels = 2 * (grid.shape[0] - 1)
    fine = channels // 2
    piece = place[0] * narrow_count + place[1]
    ahead = (ahead_high, ahead_low)
    back = (back_high, back_low)

    def read(pair_of_refs):
        return (pair_of_refs[0][...], pair_of_refs[1][...])

    def sites(at_wide, at_narrow):
        atom = table[at_wide, at_narrow]
        moved = shifts[at_wide, at_narrow]
        rows = []
        for component, extent in enumerate((cells_x, GRID_Y, cells_z)):
            start = atom[component : component + 1] * float(extent)
            rows.append(jnp.concatenate([start, start + moved[component : component + 1]], axis=1))
        oxygen = 1.0 - atom[3:4]
        rows.append(jnp.concatenate([6.0 * oxygen + atom[3:4], -8.0 * oxygen], axis=1))
        return rows

    def line(at_narrow):
        groups = [sites(at_wide, at_narrow) for at_wide in range(wide_count)]
        return [jnp.concatenate([g[k] for g in groups], axis=1) for k in range(4)]

    def weights_z(row):
        counter = lax.broadcasted_iota(jnp.int32, (window, 1), 0).astype(jnp.float32)
        return spline_pair(row - (counter - float(HALO_Z)))

    def fill_x(row, targets):
        counter = lax.broadcasted_iota(jnp.int32, (cells_x + HALO_X, 1), 0).astype(jnp.float32)
        for at_wide in range(wide_count):
            lanes = slice(at_wide * pair, (at_wide + 1) * pair)
            both = spline_pair(row[:, lanes] - (counter - float(HALO_X)))
            for values, (high_ref, low_ref) in zip(both, targets):
                high, low = split(values)
                below = (at_wide * cells_x - HALO_X) % GRID_X
                start = at_wide * cells_x
                for ref, half in ((high_ref, high), (low_ref, low)):
                    ref[below : below + HALO_X, lanes] = half[:HALO_X]
                    ref[start : start + cells_x, lanes] = half[HALO_X:]

    for ref in (weight_high, weight_low, slope_high, slope_low):
        ref[...] = jnp.zeros_like(ref)
    grid[...] = jnp.zeros_like(grid)
    weights = (weight_high, weight_low)
    slopes = (slope_high, slope_low)

    def spread(at_narrow, carry):
        row_x, row_y, row_z, charge = line(at_narrow)
        lower = jnp.floor(row_y)
        share = row_y - lower
        cell = lower.astype(jnp.int32)
        rows = phase.shape[0]
        wave_blocks = []
        slope_blocks = []
        for block in range(length // 128):
            lanes = slice(block * 128, (block + 1) * 128)
            wave = jnp.zeros((rows, 128), jnp.float32)
            wave_slope = jnp.zeros((rows, 128), jnp.float32)
            for back_by in range(4):
                where = lax.rem(cell[:, lanes] + (GRID_Y - back_by), GRID_Y)
                value, slope = spline_pair(share[:, lanes] + float(back_by))
                found = jnp.zeros((rows, 128), jnp.float32)
                for part in range(GRID_Y // 128):
                    spot = jnp.broadcast_to(where - part * 128, (rows, 128))
                    inside = (spot >= 0) & (spot < 128)
                    here = jnp.take_along_axis(
                        phase[:, part * 128 : (part + 1) * 128],
                        jnp.where(inside, spot, 0),
                        axis=1,
                        mode="promise_in_bounds",
                    )
                    found = jnp.where(inside, here, found)
                wave = wave + value * found
                wave_slope = wave_slope + slope * found
            wave_blocks.append(wave)
            slope_blocks.append(wave_slope)
        wave = jnp.concatenate(wave_blocks, axis=1)
        waves[at_narrow] = wave
        wave_slopes[at_narrow] = jnp.concatenate(slope_blocks, axis=1)
        fill_x(row_x, (weights,))
        value_z, _ = weights_z(row_z)
        charged = wave * charge
        left = jnp.concatenate([value_z * charged[c : c + 1] for c in range(channels)], axis=0)
        total = multiply(split(left), read(weights), NT)
        first = pl.multiple_of(at_narrow * cells_z, HALO_Z)
        for c in range(channels):
            lanes = slice((c % 2) * GRID_X, (c % 2 + 1) * GRID_X)
            grid[c // 2, pl.ds(first, window), lanes] += total[c * window : (c + 1) * window]
        return carry

    lax.fori_loop(0, narrow_count, spread, 0)
    for j in range(fine):
        grid[j, GRID_Z : GRID_Z + HALO_Z, :] += grid[j, 0:HALO_Z, :]
    is_first = piece == 0
    second_plane = grid[0, :, GRID_X:]
    empty = jnp.zeros_like(second_plane)
    grid[fine, :, 0:GRID_X] = jnp.where(is_first, second_plane, empty)
    grid[0, :, GRID_X:] = jnp.where(is_first, empty, second_plane)

    def to_modes(j, energy):
        plane = multiply(split(grid[j, HALO_Z:, :]), read(ahead))
        plane = jnp.concatenate([plane[:, :GRID_X], plane[:, GRID_X:]], axis=0)
        spectrum = multiply(read(back), split(plane))
        real = spectrum[:GRID_Z]
        imag = spectrum[GRID_Z:]
        mode = jnp.where(j == fine, GRID_Y // 2, piece * fine + j)
        square = factors[1, mode] + factor_row[1:2, :] + factor_column[:, 1:2]
        top = factors[0, mode] * (factor_row[0:1, :] * factor_column[:, 0:1])
        green = jnp.where(square == 0.0, 0.0, top / jnp.where(square == 0.0, 1.0, square))
        share = jnp.where((mode == 0) | (mode == GRID_Y // 2), 0.5, 1.0)
        energy = energy + share * jnp.sum(green * (real * real + imag * imag))
        modes[j, 0:GRID_Z, :] = green * real
        modes[j, GRID_Z:, :] = green * imag
        return energy

    energy = lax.fori_loop(0, fine + 1, to_modes, jnp.float32(0.0))
    modes[0, 0:GRID_Z, :] -= modes[fine, GRID_Z:, :]
    modes[0, GRID_Z:, :] += modes[fine, 0:GRID_Z, :]

    def to_grid(j, carry):
        plane = multiply(read(ahead), split(modes[j]))
        plane = jnp.concatenate([plane[:GRID_Z], plane[GRID_Z:]], axis=1)
        plane = multiply(split(plane), read(back))
        mode = piece * fine + j
        plane = plane * jnp.where(mode == 0, 1.0, 2.0)
        grid[j, HALO_Z:, :] = plane
        grid[j, 0:HALO_Z, :] = plane[GRID_Z - HALO_Z :]
        return carry

    lax.fori_loop(0, fine, to_grid, 0)

    def collect(at_narrow, carry):
        row_x, _, row_z, _ = line(at_narrow)
        fill_x(row_x, (weights, slopes))
        value_z, slope_z = weights_z(row_z)
        first = pl.multiple_of(at_narrow * cells_z, HALO_Z)
        left = jnp.concatenate(
            [
                grid[c // 2, pl.ds(first, window), (c % 2) * GRID_X : (c % 2 + 1) * GRID_X]
                for c in range(channels)
            ],
            axis=0,
        )
        left = split(left)
        wave = waves[at_narrow]
        wave_slope = wave_slopes[at_narrow]
        for at_wide in range(wide_count):
            lanes = slice(at_wide * pair, (at_wide + 1) * pair)
            value = multiply(left, (weight_high[:, lanes], weight_low[:, lanes]))
            slope = multiply(left, (slope_high[:, lanes], slope_low[:, lanes]))
            plain = jnp.zeros((window, pair), jnp.float32)
            along_x = plain
            along_y = plain
            for c in range(channels):
                rows = slice(c * window, (c + 1) * window)
                plain = plain + value[rows] * wave[c : c + 1, lanes]
                along_x = along_x + slope[rows] * wave[c : c + 1, lanes]
                along_y = along_y + value[rows] * wave_slope[c : c + 1, lanes]
            near = value_z[:, lanes]
            near_slope = slope_z[:, lanes]
            results = [
                jnp.sum(near * plain, axis=0, keepdims=True),
                -jnp.sum(near * along_x, axis=0, keepdims=True),
                -jnp.sum(near * along_y, axis=0, keepdims=True),
                -jnp.sum(near_slope * plain, axis=0, keepdims=True),
            ]
            for k, row in enumerate(results):
                out_ref[at_wide, at_narrow, :, k * pair : (k + 1) * pair] = row
            out_ref[at_wide, at_narrow, :, 4 * pair :] = jnp.full((1, 128), energy, jnp.float32)
        return carry

    lax.fori_loop(0, narrow_count, collect, 0)


def mode_factors(length):
    counter = np.arange(length)
    wrapped = np.where(2 * counter >= length, counter - length, counter)
    square = (wrapped / length) ** 2
    ratio = (4.0 + 2.0 * np.cos(2.0 * math.pi * counter / length)) / 6.0
    return np.stack([np.exp(-(math.pi**2) * square / ewald_beta**2) / ratio**2, square])


def halves(table):
    high = table.astype(jnp.bfloat16)
    low = (table - high.astype(np.float64)).astype(jnp.bfloat16)
    return high, low


def grouped(array, width):
    parts = array.reshape((-1, width) + array.shape[1:])
    pads = ((0, 0), (0, ROW_PAD - width)) + ((0, 0),) * (array.ndim - 1)
    parts = jnp.pad(parts, pads)
    return parts.reshape((-1,) + array.shape[1:])


def vmem(count):
    return [pl.BlockSpec(memory_space=pltpu.VMEM)] * count


def smem(count):
    return [pl.BlockSpec(memory_space=pltpu.SMEM)] * count


def local(
    positions,
    species,
    neighbours,
    embed_one_w,
    embed_one_b,
    embed_two_w,
    embed_two_b,
    embed_three_w,
    embed_three_b,
    fit_one_w,
    fit_one_b,
    fit_two_w,
    fit_two_b,
    fit_three_w,
    fit_three_b,
    fit_out_w,
):
    axes = ("wide", "narrow")
    wide_count = lax.axis_size("wide")
    narrow_count = lax.axis_size("narrow")
    pieces = wide_count * narrow_count
    atoms = positions.shape[4]
    listed = neighbours.shape[4]
    place = jnp.stack([lax.axis_index("wide"), lax.axis_index("narrow")]).astype(jnp.int32)
    piece = place[0] * narrow_count + place[1]

    kinds = species.reshape(1, atoms).astype(jnp.float32)
    packed = jnp.concatenate([positions.reshape(3, atoms), kinds], axis=0)
    table = lax.all_to_all(
        jnp.broadcast_to(packed[None], (pieces, 4, atoms)), axes, 0, 0, tiled=True
    )
    table = table.reshape(wide_count, narrow_count, 4, atoms)

    width_one = embed_one_w.shape[1]
    tall = 4 * ROW_PAD
    column_list = [
        embed_one_w[0],
        embed_one_w[1],
        embed_one_b[0],
        embed_one_b[1],
        embed_two_b,
        embed_three_b,
    ]
    columns = []
    for column in column_list:
        rows = grouped(column, width_one)
        columns.append(jnp.pad(rows, (0, tall - rows.shape[0])))
    columns = jnp.stack(columns, axis=1)
    second = grouped(jnp.pad(embed_two_w.T, ((0, 0), (0, ROW_PAD - width_one))), width_one)
    third = grouped(grouped(embed_three_w, width_one).T, width_one)
    codes = neighbours.reshape(atoms, listed).T
    entries = fit_one_w.shape[0]
    dipole, shifts = pl.pallas_call(
        centroid_kernel,
        out_shape=(
            jax.ShapeDtypeStruct((3, atoms), jnp.float32),
            jax.ShapeDtypeStruct((pieces, 4, atoms), jnp.float32),
        ),
        in_specs=smem(1) + vmem(12),
        out_specs=tuple(vmem(2)),
        scratch_shapes=[
            pltpu.VMEM((4, tall, atoms), jnp.float32),
            pltpu.VMEM((-(-entries // 128) * 128, atoms), jnp.float32),
        ],
        compiler_params=pltpu.CompilerParams(vmem_limit_bytes=32 * 1024 * 1024),
        name="centroids",
    )(
        place,
        table,
        codes,
        columns,
        second,
        third,
        fit_one_w,
        fit_one_b[None],
        fit_two_w,
        fit_two_b[None],
        fit_three_w,
        fit_three_b[None],
        fit_out_w,
    )
    shifts = lax.all_to_all(shifts, axes, 0, 0, tiled=True)
    shifts = shifts.reshape(wide_count, narrow_count, 4, atoms)

    fine = GRID_Y // 2 // pieces
    mode = piece * fine + jnp.arange(fine, dtype=jnp.int32)
    counter = jnp.arange(GRID_Y, dtype=jnp.int32)
    angle = (mode[:, None] * counter[None, :] % GRID_Y).astype(jnp.float32) * (
        2.0 * math.pi / GRID_Y
    )
    alternate = (1 - 2 * (counter % 2)).astype(jnp.float32)
    sine = jnp.where(mode[:, None] == 0, alternate[None, :], -jnp.sin(angle))
    phase = jnp.stack([jnp.cos(angle), sine], axis=1).reshape(2 * fine, GRID_Y)
    phase = jnp.pad(phase, ((0, -2 * fine % 8), (0, 0)))

    turns = np.outer(np.arange(GRID_X), np.arange(GRID_X)) % GRID_X * (2.0 * math.pi / GRID_X)
    cosine = np.cos(turns)
    sines = np.sin(turns)
    ahead = np.block([[cosine, -sines], [sines, cosine]])
    scale = coulomb / (math.pi * GRID_X * GRID_Y * GRID_Z)
    factors = mode_factors(GRID_Y)
    factors[0] *= scale
    window = GRID_Z // narrow_count + HALO_Z
    length = wide_count * 2 * atoms
    out_width = 8 * atoms + 128
    partial = pl.pallas_call(
        mesh_kernel,
        out_shape=jax.ShapeDtypeStruct((wide_count, narrow_count, 1, out_width), jnp.float32),
        in_specs=smem(2) + vmem(9),
        out_specs=vmem(1)[0],
        scratch_shapes=[
            pltpu.VMEM((fine + 1, HALO_Z + GRID_Z, 2 * GRID_X), jnp.float32),
            pltpu.VMEM((fine + 1, 2 * GRID_Z, GRID_X), jnp.float32),
        ]
        + [pltpu.VMEM((GRID_X, length), jnp.bfloat16)] * 4
        + [pltpu.VMEM((narrow_count, phase.shape[0], length), jnp.float32)] * 2,
        compiler_params=pltpu.CompilerParams(vmem_limit_bytes=48 * 1024 * 1024),
        name="mesh",
    )(
        place,
        jnp.asarray(factors, jnp.float32),
        table,
        shifts,
        phase,
        jnp.asarray(mode_factors(GRID_X), jnp.float32),
        jnp.asarray(mode_factors(GRID_Z).T, jnp.float32),
        *[jnp.asarray(half) for half in halves(ahead)],
        *[jnp.asarray(half) for half in halves(ahead.T)],
    )
    arrived = lax.all_to_all(
        partial.reshape(pieces, 1, out_width), axes, 0, 0, tiled=True
    )
    total = jnp.sum(arrived, axis=(0, 1))
    fields = total[: 8 * atoms].reshape(4, 2, atoms)
    energy = total[8 * atoms] / (atoms * pieces)
    atom_field = fields[:, 0].reshape(4, 1, 1, 1, atoms)
    centroid_field = (fields[:, 1] * (1.0 - kinds)).reshape(4, 1, 1, 1, atoms)
    return (dipole.reshape(3, 1, 1, 1, atoms), atom_field, centroid_field, energy)


def solution(mesh):
    column = P(None, "wide", "narrow", None, None)
    in_specs = (column, P("wide", "narrow", None, None), P("wide", "narrow", None, None, None))
    in_specs = in_specs + (P(),) * 13
    out_specs = (column, column, column, P())
    return jax.shard_map(local, mesh=mesh, in_specs=in_specs, out_specs=out_specs, check_vma=False)
```

```python
import math

import jax
import jax.numpy as jnp
import numpy as np
from jax import lax
from jax.experimental import pallas as pl
from jax.experimental.pallas import tpu as pltpu
from jax.sharding import PartitionSpec as P

GRID_X = 256
GRID_Y = 256
GRID_Z = 256
AXIS_COLUMNS = 16

radius_scale = 24.0
wannier_reach = 0.5
ewald_beta = 0.9
coulomb = 0.25

ROW_PAD = 32
SLOT_CHUNK = 16
HALO_X = 16
HALO_Z = 8

NN = (((1,), (0,)), ((), ()))
NT = (((1,), (1,)), ((), ()))


def split(value):
    high = value.astype(jnp.bfloat16)
    low = (value - high.astype(jnp.float32)).astype(jnp.bfloat16)
    return high, low


def multiply(left, right, dims=NN):
    def one(a, b):
        return lax.dot_general(a, b, dims, preferred_element_type=jnp.float32)

    return one(left[0], right[0]) + (one(left[1], right[0]) + one(left[0], right[1]))


def spline_pair(offset):
    centred = offset - 2.0
    away = jnp.abs(centred)
    outer = jnp.maximum(2.0 - away, 0.0)
    inner = jnp.maximum(1.0 - away, 0.0)
    outer_square = outer * outer
    inner_square = inner * inner
    value = (outer_square * outer - 4.0 * (inner_square * inner)) * (1.0 / 6.0)
    slope = jnp.where(centred < 0.0, 0.5, -0.5) * (outer_square - 4.0 * inner_square)
    return value, slope


def lookup(row_table, spot):
    found = None
    for part in range(row_table.shape[1] // 128):
        inside = spot // 128 == part
        here = jnp.take_along_axis(
            jnp.broadcast_to(row_table[:, part * 128 : (part + 1) * 128], spot.shape),
            lax.rem(spot, 128),
            axis=1,
            mode="promise_in_bounds",
        )
        found = here if found is None else jnp.where(inside, here, found)
    return found


def pack_kernel(positions, species, out_ref):
    rows = [positions[component] for component in range(3)]
    rows.append(species[...].astype(jnp.float32))
    rows = jnp.concatenate(rows, axis=0)
    for target in range(out_ref.shape[0]):
        out_ref[target] = rows


def prepare_kernel(
    neighbours,
    embed_one_w,
    embed_one_b,
    embed_two_w,
    embed_two_b,
    embed_three_w,
    embed_three_b,
    fit_one_w,
    fit_one_b,
    fit_two_w,
    fit_two_b,
    fit_three_w,
    fit_three_b,
    circle,
    codes_ref,
    columns_ref,
    second_ref,
    third_ref,
    one_high_ref,
    one_low_ref,
    two_high_ref,
    two_low_ref,
    three_high_ref,
    three_low_ref,
    phase_ref,
    rows,
    square,
):
    pieces = lax.axis_size("wide") * lax.axis_size("narrow")
    piece = lax.axis_index("wide") * lax.axis_size("narrow") + lax.axis_index("narrow")
    width_one = embed_one_w.shape[1]
    hidden = fit_two_w.shape[0]
    codes_ref[...] = jnp.transpose(neighbours[...].astype(jnp.float32)).astype(jnp.int32)
    rows[...] = jnp.zeros_like(rows)
    for kind in range(2):
        rows[kind : kind + 1, 0:width_one] = embed_one_w[kind : kind + 1, :]
        rows[2 + kind : 3 + kind, 0:width_one] = embed_one_b[kind : kind + 1, :]
    for row, source, groups in ((4, embed_two_b, 2), (5, embed_three_b, 4)):
        for k in range(groups):
            rows[row : row + 1, k * ROW_PAD : k * ROW_PAD + width_one] = source[
                :, k * width_one : (k + 1) * width_one
            ]
    for row, source in ((6, fit_one_b), (7, fit_two_b), (8, fit_three_b)):
        rows[row : row + 1, 0:hidden] = source[...]
    columns_ref[...] = jnp.transpose(rows[...])

    square[...] = jnp.zeros_like(square)
    for k in range(2):
        square[0:width_one, k * ROW_PAD : k * ROW_PAD + width_one] = embed_two_w[
            :, k * width_one : (k + 1) * width_one
        ]
    high, low = split(jnp.transpose(square[0:128, 0:128])[0 : 2 * ROW_PAD, 0:ROW_PAD])
    second_ref[...] = jnp.concatenate([high, high, low], axis=1)
    square[0:128, 0:128] = jnp.zeros((128, 128), jnp.float32)
    for g in range(2):
        for k in range(4):
            square[
                g * ROW_PAD : g * ROW_PAD + width_one, k * ROW_PAD : k * ROW_PAD + width_one
            ] = embed_three_w[
                g * width_one : (g + 1) * width_one, k * width_one : (k + 1) * width_one
            ]
    high, low = split(jnp.transpose(square[0:128, 0:128])[:, 0 : 2 * ROW_PAD])
    third_ref[...] = jnp.concatenate([high, high, low], axis=1)
    one_high_ref[...], one_low_ref[...] = split(fit_one_w[...])
    for source, high_ref, low_ref in (
        (fit_two_w, two_high_ref, two_low_ref),
        (fit_three_w, three_high_ref, three_low_ref),
    ):
        square[0:hidden, 0:hidden] = source[...]
        high_ref[...], low_ref[...] = split(jnp.transpose(square[...])[0:hidden, 0:hidden])

    fine = GRID_Y // 2 // pieces
    shape = (phase_ref.shape[0], 128)
    row = lax.broadcasted_iota(jnp.int32, shape, 0)
    mode = piece * fine + row // 2
    for part in range(GRID_Y // 128):
        cell = lax.broadcasted_iota(jnp.int32, shape, 1) + part * 128
        spot = lax.rem(mode * cell, GRID_Y)
        cosine = lookup(circle[0:1, :], spot)
        sine = lookup(circle[1:2, :], spot)
        alternate = (1 - 2 * lax.rem(cell, 2)).astype(jnp.float32)
        odd = jnp.where(mode == 0, alternate, -sine)
        value = jnp.where(lax.rem(row, 2) == 0, cosine, odd)
        phase_ref[:, part * 128 : (part + 1) * 128] = jnp.where(row < 2 * fine, value, 0.0)


def centroid_kernel(
    table,
    codes,
    columns,
    second,
    third,
    one_high,
    one_low,
    two_high,
    two_low,
    three_high,
    three_low,
    fit_out_w,
    dipole_ref,
    shift_ref,
    matrix,
    descriptor,
):
    wide_count, narrow_count, _, atoms = table.shape
    listed = codes.shape[0]
    width_three = fit_out_w.shape[0]
    width_one = width_three // 4
    hidden_width = two_high.shape[0]
    cells = (GRID_X // wide_count, GRID_Y, GRID_Z // narrow_count)
    at_wide = lax.axis_index("wide")
    at_narrow = lax.axis_index("narrow")
    own = table[at_wide, at_narrow]
    nearby = []
    for step in range(9):
        wide_at = lax.rem(at_wide + (step // 3 - 1) + wide_count, wide_count)
        narrow_at = lax.rem(at_narrow + (step % 3 - 1) + narrow_count, narrow_count)
        nearby.append(table[wide_at, narrow_at])

    second_all = second[...]
    third_all = third[...]
    weight_oxygen = jnp.broadcast_to(columns[0:ROW_PAD, 0:1], (ROW_PAD, atoms))
    weight_hydrogen = jnp.broadcast_to(columns[0:ROW_PAD, 1:2], (ROW_PAD, atoms))
    bias_oxygen = jnp.broadcast_to(columns[0:ROW_PAD, 2:3], (ROW_PAD, atoms))
    bias_hydrogen = jnp.broadcast_to(columns[0:ROW_PAD, 3:4], (ROW_PAD, atoms))
    second_bias = columns[0 : 2 * ROW_PAD, 4:5]
    third_bias = columns[0 : 4 * ROW_PAD, 5:6]
    matrix[...] = jnp.zeros_like(matrix)

    def chunk(index, carry):
        first = pl.multiple_of(index * SLOT_CHUNK, SLOT_CHUNK)
        code = codes[pl.ds(first, SLOT_CHUNK), :]
        offset = code // atoms
        slot = code - offset * atoms
        step_x = jnp.where(offset >= 9, 1, 0) + jnp.where(offset >= 18, 1, 0)
        rest = offset - 9 * step_x
        step_z = jnp.where(rest >= 3, 1, 0) + jnp.where(rest >= 6, 1, 0)
        step_y = rest - 3 * step_z
        brick = step_x * 3 + step_z
        found = []
        for component in range(4):
            picked = jnp.zeros((SLOT_CHUNK, atoms), jnp.float32)
            for step in range(9):
                row = jnp.broadcast_to(
                    nearby[step][component : component + 1], (SLOT_CHUNK, atoms)
                )
                here = jnp.take_along_axis(row, slot, axis=1, mode="promise_in_bounds")
                picked = jnp.where(brick == step, here, picked)
            found.append(picked)
        scaled = []
        for component, step in enumerate((step_x, step_y, step_z)):
            extent = float(cells[component])
            relative = (step - 1).astype(jnp.float32) * extent + (
                found[component] - own[component : component + 1]
            ) * extent
            scaled.append(relative * (1.0 / radius_scale))
        smooth = 1.0 / (
            1.0 + (scaled[0] * scaled[0] + scaled[1] * scaled[1] + scaled[2] * scaled[2])
        )
        radial = [smooth] + [smooth * part for part in scaled]
        hydrogen = found[3] > 0.5
        first_layers = []
        for k in range(SLOT_CHUNK):
            row = smooth[k : k + 1]
            kind = hydrogen[k : k + 1]
            weight = jnp.where(kind, weight_hydrogen, weight_oxygen)
            bias = jnp.where(kind, bias_hydrogen, bias_oxygen)
            first_layers.append(jnp.tanh(weight * row + bias))
        layer_one = jnp.concatenate(first_layers, axis=1)
        high, low = split(layer_one)
        layer_two = lax.dot_general(
            second_all,
            jnp.concatenate([high, low, high], axis=0),
            NN,
            preferred_element_type=jnp.float32,
        )
        layer_two = jnp.tanh(layer_two + second_bias) + jnp.concatenate(
            [layer_one, layer_one], axis=0
        )
        high, low = split(layer_two)
        layer_three = lax.dot_general(
            third_all,
            jnp.concatenate([high, low, high], axis=0),
            NN,
            preferred_element_type=jnp.float32,
        )
        layer_three = jnp.tanh(layer_three + third_bias) + jnp.concatenate(
            [layer_two, layer_two], axis=0
        )
        for part in range(4):
            total = matrix[part]
            for k in range(SLOT_CHUNK):
                total = total + layer_three[:, k * atoms : (k + 1) * atoms] * radial[part][k : k + 1]
            matrix[part] = total
        return carry

    lax.fori_loop(0, listed // SLOT_CHUNK, chunk, 0)

    parts = []
    for part in range(4):
        padded = matrix[part] * (1.0 / listed)
        parts.append(
            jnp.concatenate(
                [padded[k * ROW_PAD : k * ROW_PAD + width_one] for k in range(4)], axis=0
            )
        )
    leading = [part[0:AXIS_COLUMNS] for part in parts]
    for row in range(width_three):
        total = parts[0][row : row + 1] * leading[0]
        for part in range(1, 4):
            total = total + parts[part][row : row + 1] * leading[part]
        descriptor[row * AXIS_COLUMNS : (row + 1) * AXIS_COLUMNS, :] = total
    def layer(high_ref, low_ref, given, column):
        weights = (high_ref[...], low_ref[...])
        return jnp.tanh(multiply(weights, split(given)) + columns[0:hidden_width, column : column + 1])

    hidden = layer(one_high, one_low, descriptor[...], 6)
    hidden = hidden + layer(two_high, two_low, hidden, 7)
    hidden = hidden + layer(three_high, three_low, hidden, 8)
    coeffs = multiply(split(fit_out_w[...]), split(hidden))
    vector = jnp.concatenate(
        [jnp.sum(coeffs * parts[1 + c], axis=0, keepdims=True) for c in range(3)], axis=0
    )
    oxygen = 1.0 - own[3:4]
    for c in range(3):
        dipole_ref[c] = vector[c : c + 1] * oxygen
    moved = wannier_reach * jnp.tanh(vector)
    moved = jnp.concatenate([moved, jnp.zeros((1, atoms), jnp.float32)], axis=0)
    for target in range(shift_ref.shape[0]):
        shift_ref[target] = moved


def mesh_kernel(
    factors,
    table,
    shifts,
    phase,
    factor_row,
    factor_column,
    fold_high,
    fold_low,
    unfold_high,
    unfold_low,
    out_ref,
    grid,
    planes,
    weights,
    slopes,
    waves,
    wave_slopes,
):
    wide_count, narrow_count, _, atoms = table.shape
    cells_x = GRID_X // wide_count
    cells_z = GRID_Z // narrow_count
    window = cells_z + HALO_Z
    reach = cells_x + HALO_X
    pair = 2 * atoms
    length = wide_count * pair
    copies = grid.shape[0]
    fine = grid.shape[1]
    channels = 2 * fine
    rows = phase.shape[0]
    half_x = GRID_X // 2
    half_z = GRID_Z // 2
    piece = lax.axis_index("wide") * narrow_count + lax.axis_index("narrow")
    lane_zero = lax.broadcasted_iota(jnp.int32, (1, half_x), 1) == 0
    row_zero = lax.broadcasted_iota(jnp.int32, (half_z, 1), 0) == 0

    def fold():
        return (fold_high[...], fold_low[...])

    def unfold():
        return (unfold_high[...], unfold_low[...])

    def sites(at_wide, at_narrow):
        atom = table[at_wide, at_narrow]
        moved = shifts[at_wide, at_narrow]
        found = []
        for component, extent in enumerate((cells_x, GRID_Y, cells_z)):
            start = atom[component : component + 1] * float(extent)
            found.append(jnp.concatenate([start, start + moved[component : component + 1]], axis=1))
        oxygen = 1.0 - atom[3:4]
        found.append(jnp.concatenate([6.0 * oxygen + atom[3:4], -8.0 * oxygen], axis=1))
        return found

    def line(at_narrow):
        groups = [sites(at_wide, at_narrow) for at_wide in range(wide_count)]
        return [jnp.concatenate([g[k] for g in groups], axis=1) for k in range(4)]

    def weights_z(row):
        counter = lax.broadcasted_iota(jnp.int32, (window, 1), 0).astype(jnp.float32)
        return spline_pair(row - (counter - float(HALO_Z)))

    def fill_x(row, targets):
        counter = lax.broadcasted_iota(jnp.int32, (reach, 1), 0).astype(jnp.float32)
        both = spline_pair(row - (counter - float(HALO_X)))
        for values, ref in zip(both, targets):
            high, low = split(values)
            ref[0:reach, :] = high
            ref[128 : 128 + reach, :] = low

    weights[...] = jnp.zeros_like(weights)
    slopes[...] = jnp.zeros_like(slopes)
    grid[...] = jnp.zeros_like(grid)

    def spread(at_narrow, carry):
        row_x, row_y, row_z, charge = line(at_narrow)
        lower = jnp.floor(row_y)
        back = lax.broadcasted_iota(jnp.int32, (8, 1), 0)
        value_y, slope_y = spline_pair((row_y - lower) + back.astype(jnp.float32))
        cell = lax.rem(lower.astype(jnp.int32) - back + GRID_Y, GRID_Y)
        wave_blocks = []
        slope_blocks = []
        for block in range(length // 128):
            lanes = slice(block * 128, (block + 1) * 128)
            wave = jnp.zeros((rows, 128), jnp.float32)
            wave_slope = jnp.zeros((rows, 128), jnp.float32)
            for k in range(4):
                spot = jnp.broadcast_to(cell[k : k + 1, lanes], (rows, 128))
                found = lookup(phase[...], spot)
                wave = wave + value_y[k : k + 1, lanes] * found
                wave_slope = wave_slope + slope_y[k : k + 1, lanes] * found
            wave_blocks.append(wave)
            slope_blocks.append(wave_slope)
        wave = jnp.concatenate(wave_blocks, axis=1)
        waves[at_narrow] = wave
        wave_slopes[at_narrow] = jnp.concatenate(slope_blocks, axis=1)
        fill_x(row_x, (weights,))
        value_z, _ = weights_z(row_z)
        charged = wave * charge
        first = pl.multiple_of(at_narrow * cells_z, HALO_Z)
        for at_wide in range(wide_count):
            lanes = slice(at_wide * pair, (at_wide + 1) * pair)
            near = value_z[:, lanes]
            left = jnp.concatenate(
                [near * charged[c : c + 1, lanes] for c in range(channels)], axis=0
            )
            high, low = split(left)
            total = lax.dot_general(high, weights[:, lanes], NT, preferred_element_type=jnp.float32)
            total = total[:, 0:128] + (
                total[:, 128:256]
                + lax.dot_general(low, weights[0:128, lanes], NT, preferred_element_type=jnp.float32)
            )
            start = at_wide // copies * 128
            for c in range(channels):
                spot = c % 2 * GRID_X + start
                grid[
                    at_wide % copies, c // 2, pl.ds(first, window), spot : spot + 128
                ] += total[c * window : (c + 1) * window]
        return carry

    lax.fori_loop(0, narrow_count, spread, 0)

    def gather(j, carry):
        for lanes in (slice(0, GRID_X), slice(GRID_X, 2 * GRID_X)):
            total = None
            for k in range(copies):
                moved = pltpu.roll(grid[k, j, :, lanes], (k * cells_x - HALO_X) % GRID_X, 1)
                total = moved if total is None else total + moved
            planes[j, :, lanes] = total[HALO_Z:]
            planes[j, GRID_Z - HALO_Z :, lanes] += total[:HALO_Z]
        return carry

    lax.fori_loop(0, fine, gather, 0)
    is_first = piece == 0
    second_plane = planes[0, :, GRID_X:]
    empty = jnp.zeros_like(second_plane)
    planes[fine, :, 0:GRID_X] = jnp.where(is_first, second_plane, empty)
    planes[fine, :, GRID_X:] = empty
    planes[0, :, GRID_X:] = jnp.where(is_first, empty, second_plane)

    def to_modes(j, energy):
        real = multiply(split(planes[j, :, 0:GRID_X]), fold())
        imag = multiply(split(planes[j, :, GRID_X:]), fold())
        real_c, real_s = real[:, :half_x], real[:, half_x:]
        imag_c, imag_s = imag[:, :half_x], imag[:, half_x:]
        plane = jnp.concatenate(
            [
                real_c + jnp.where(lane_zero, 0.0, imag_s),
                jnp.where(lane_zero, real_s, real_c - imag_s),
                imag_c - jnp.where(lane_zero, 0.0, real_s),
                jnp.where(lane_zero, imag_s, imag_c + real_s),
            ],
            axis=1,
        )
        plane = multiply(unfold(), split(plane))
        real_c, real_s = plane[:half_z, :GRID_X], plane[half_z:, :GRID_X]
        imag_c, imag_s = plane[:half_z, GRID_X:], plane[half_z:, GRID_X:]
        real = jnp.concatenate(
            [
                real_c + jnp.where(row_zero, 0.0, imag_s),
                jnp.where(row_zero, real_s, real_c - imag_s),
            ],
            axis=0,
        )
        imag = jnp.concatenate(
            [
                imag_c - jnp.where(row_zero, 0.0, real_s),
                jnp.where(row_zero, imag_s, imag_c + real_s),
            ],
            axis=0,
        )
        mode = jnp.where(j == fine, GRID_Y // 2, piece * fine + j)
        square = (factors[1, mode] + factor_row[1:2, :]) + factor_column[:, 1:2]
        top = (factors[0, mode] * factor_row[0:1, :]) * factor_column[:, 0:1]
        green = jnp.where(square == 0.0, 0.0, top / jnp.where(square == 0.0, 1.0, square))
        share = jnp.where((mode == 0) | (mode == GRID_Y // 2), 0.5, 1.0)
        energy = energy + share * jnp.sum(green * (real * real + imag * imag))
        planes[j, :, 0:GRID_X] = green * real
        planes[j, :, GRID_X:] = green * imag
        return energy

    energy = lax.fori_loop(0, fine + 1, to_modes, jnp.float32(0.0))
    planes[0, :, 0:GRID_X] -= planes[fine, :, GRID_X:]
    planes[0, :, GRID_X:] += planes[fine, :, 0:GRID_X]

    def to_grid(j, carry):
        real_a, real_b = planes[j, :half_z, :GRID_X], planes[j, half_z:, :GRID_X]
        imag_a, imag_b = planes[j, :half_z, GRID_X:], planes[j, half_z:, GRID_X:]
        real = jnp.concatenate(
            [
                real_a + jnp.where(row_zero, 0.0, real_b),
                jnp.where(row_zero, real_b, imag_b - imag_a),
            ],
            axis=0,
        )
        imag = jnp.concatenate(
            [
                imag_a + jnp.where(row_zero, 0.0, imag_b),
                jnp.where(row_zero, imag_b, real_a - real_b),
            ],
            axis=0,
        )
        real = multiply(fold(), split(real))
        imag = multiply(fold(), split(imag))
        real_a, real_b = real[:, :half_x], real[:, half_x:]
        imag_a, imag_b = imag[:, :half_x], imag[:, half_x:]
        scale = jnp.where(piece * fine + j == 0, 1.0, 2.0)
        real = jnp.concatenate(
            [
                real_a + jnp.where(lane_zero, 0.0, real_b),
                jnp.where(lane_zero, real_b, imag_b - imag_a),
            ],
            axis=1,
        )
        imag = jnp.concatenate(
            [
                imag_a + jnp.where(lane_zero, 0.0, imag_b),
                jnp.where(lane_zero, imag_b, real_a - real_b),
            ],
            axis=1,
        )
        for part, lanes in ((real, slice(0, GRID_X)), (imag, slice(GRID_X, 2 * GRID_X))):
            part = multiply(split(part * scale), unfold())
            for k in range(copies):
                moved = pltpu.roll(part, (HALO_X - k * cells_x) % GRID_X, 1)
                grid[k, j, HALO_Z:, lanes] = moved
                grid[k, j, 0:HALO_Z, lanes] = moved[GRID_Z - HALO_Z :]
        return carry

    lax.fori_loop(0, fine, to_grid, 0)

    def collect(at_narrow, carry):
        row_x, _, row_z, _ = line(at_narrow)
        fill_x(row_x, (weights, slopes))
        value_z, slope_z = weights_z(row_z)
        first = pl.multiple_of(at_narrow * cells_z, HALO_Z)
        lefts = []
        for k in range(copies):
            left = jnp.concatenate(
                [
                    grid[k, c // 2, pl.ds(first, window), c % 2 * GRID_X : (c % 2 + 1) * GRID_X]
                    for c in range(channels)
                ],
                axis=0,
            )
            lefts.append(split(left))
        wave = waves[at_narrow]
        wave_slope = wave_slopes[at_narrow]
        for at_wide in range(wide_count):
            lanes = slice(at_wide * pair, (at_wide + 1) * pair)
            start = at_wide // copies * 128
            high = lefts[at_wide % copies][0][:, start : start + 128]
            low = lefts[at_wide % copies][1][:, start : start + 128]
            twice = jnp.concatenate([high, high], axis=1)

            def across(ref):
                return lax.dot_general(
                    twice, ref[:, lanes], NN, preferred_element_type=jnp.float32
                ) + lax.dot_general(
                    low, ref[0:128, lanes], NN, preferred_element_type=jnp.float32
                )

            value = across(weights)
            slope = across(slopes)
            plain = jnp.zeros((window, pair), jnp.float32)
            along_x = plain
            along_y = plain
            for c in range(channels):
                block = slice(c * window, (c + 1) * window)
                plain = plain + value[block] * wave[c : c + 1, lanes]
                along_x = along_x + slope[block] * wave[c : c + 1, lanes]
                along_y = along_y + value[block] * wave_slope[c : c + 1, lanes]
            near = value_z[:, lanes]
            near_slope = slope_z[:, lanes]
            results = [
                jnp.sum(near * plain, axis=0, keepdims=True),
                -jnp.sum(near * along_x, axis=0, keepdims=True),
                -jnp.sum(near * along_y, axis=0, keepdims=True),
                -jnp.sum(near_slope * plain, axis=0, keepdims=True),
            ]
            for k, row in enumerate(results):
                out_ref[at_wide, at_narrow, :, k * pair : (k + 1) * pair] = row
            out_ref[at_wide, at_narrow, :, 4 * pair :] = jnp.full((1, 128), energy, jnp.float32)
        return carry

    lax.fori_loop(0, narrow_count, collect, 0)


def finish_kernel(arrived, species, atom_ref, centroid_ref, energy_ref):
    atoms = species.shape[1]
    total = arrived[0]
    for k in range(1, arrived.shape[0]):
        total = total + arrived[k]
    oxygen = 1.0 - species[...].astype(jnp.float32)
    for k in range(4):
        atom_ref[k] = total[:, 2 * k * atoms : (2 * k + 1) * atoms]
        centroid_ref[k] = total[:, (2 * k + 1) * atoms : (2 * k + 2) * atoms] * oxygen
    energy_ref[...] = total[:, 8 * atoms :] * (1.0 / (atoms * arrived.shape[0]))


def mode_factors(length, order):
    wrapped = np.where(2 * order >= length, order - length, order)
    square = (wrapped / length) ** 2
    ratio = (4.0 + 2.0 * np.cos(2.0 * math.pi * order / length)) / 6.0
    return np.stack([np.exp(-(math.pi**2) * square / ewald_beta**2) / ratio**2, square])


def folded_order(length):
    half = length // 2
    counter = np.arange(half)
    return np.concatenate([counter, np.where(counter == 0, half, length - counter)])


def fold_table(length):
    half = length // 2
    turns = np.outer(np.arange(length), np.arange(half)) % length * (2.0 * math.pi / length)
    sines = np.sin(turns)
    sines[:, 0] = 1.0 - 2.0 * (np.arange(length) % 2)
    return np.concatenate([np.cos(turns), sines], axis=1)


def halves(table):
    high = table.astype(jnp.bfloat16)
    low = (table - high.astype(np.float64)).astype(jnp.bfloat16)
    return high, low


def vmem(count):
    return [pl.BlockSpec(memory_space=pltpu.VMEM)] * count


def smem(count):
    return [pl.BlockSpec(memory_space=pltpu.SMEM)] * count


def shaped(shape, dtype=jnp.float32):
    return jax.ShapeDtypeStruct(shape, dtype)


def limits(mebibytes):
    return pltpu.CompilerParams(vmem_limit_bytes=mebibytes * 1024 * 1024)


def local(
    positions,
    species,
    neighbours,
    embed_one_w,
    embed_one_b,
    embed_two_w,
    embed_two_b,
    embed_three_w,
    embed_three_b,
    fit_one_w,
    fit_one_b,
    fit_two_w,
    fit_two_b,
    fit_three_w,
    fit_three_b,
    fit_out_w,
):
    axes = ("wide", "narrow")
    wide_count = lax.axis_size("wide")
    narrow_count = lax.axis_size("narrow")
    pieces = wide_count * narrow_count
    atoms = positions.shape[4]
    listed = neighbours.shape[4]
    fine = GRID_Y // 2 // pieces
    width_three = embed_three_w.shape[1]
    entries, hidden = fit_one_w.shape
    kinds = species.reshape(1, atoms)

    packed = pl.pallas_call(
        pack_kernel,
        out_shape=shaped((pieces, 4, atoms)),
        in_specs=vmem(2),
        out_specs=vmem(1)[0],
        name="pack",
    )(positions.reshape(3, 1, atoms), kinds)
    table = lax.all_to_all(packed, axes, 0, 0, tiled=True)
    table = table.reshape(wide_count, narrow_count, 4, atoms)

    tall = 4 * ROW_PAD
    bf16 = jnp.bfloat16
    wave_rows = -(-2 * fine // 8) * 8
    angle = np.arange(GRID_Y) * (2.0 * math.pi / GRID_Y)
    circle = jnp.asarray(np.stack([np.cos(angle), np.sin(angle)]), jnp.float32)
    prepared = pl.pallas_call(
        prepare_kernel,
        out_shape=(
            shaped((listed, atoms), jnp.int32),
            shaped((256, 16)),
            shaped((2 * ROW_PAD, 3 * ROW_PAD), bf16),
            shaped((tall, 6 * ROW_PAD), bf16),
            shaped((hidden, entries), bf16),
            shaped((hidden, entries), bf16),
        )
        + (shaped((hidden, hidden), bf16),) * 4
        + (shaped((wave_rows, GRID_Y)),),
        in_specs=vmem(14),
        out_specs=tuple(vmem(11)),
        scratch_shapes=[pltpu.VMEM((16, 256), jnp.float32), pltpu.VMEM((256, 256), jnp.float32)],
        compiler_params=limits(32),
        cost_estimate=pl.CostEstimate(
            flops=1000000, bytes_accessed=8 * entries * hidden, transcendentals=0
        ),
        name="prepare",
    )(
        neighbours.reshape(atoms, listed),
        embed_one_w,
        embed_one_b,
        embed_two_w,
        embed_two_b[None],
        embed_three_w,
        embed_three_b[None],
        fit_one_w.T,
        fit_one_b[None],
        fit_two_w,
        fit_two_b[None],
        fit_three_w,
        fit_three_b[None],
        circle,
    )
    phase = prepared[10]
    dipole, shifts = pl.pallas_call(
        centroid_kernel,
        out_shape=(shaped((3, 1, atoms)), shaped((pieces, 4, atoms))),
        in_specs=vmem(12),
        out_specs=tuple(vmem(2)),
        scratch_shapes=[
            pltpu.VMEM((4, tall, atoms), jnp.float32),
            pltpu.VMEM((width_three * AXIS_COLUMNS, atoms), jnp.float32),
        ],
        compiler_params=limits(32),
        name="centroids",
    )(table, *prepared[:10], fit_out_w.T)
    shifts = lax.all_to_all(shifts, axes, 0, 0, tiled=True)
    shifts = shifts.reshape(wide_count, narrow_count, 4, atoms)

    factors = mode_factors(GRID_Y, np.arange(GRID_Y))
    factors[0] *= coulomb / (math.pi * GRID_X * GRID_Y * GRID_Z)
    cells_x = GRID_X // wide_count
    copies = 128 // cells_x
    length = wide_count * 2 * atoms
    out_width = 8 * atoms + 128
    partial = pl.pallas_call(
        mesh_kernel,
        out_shape=shaped((wide_count, narrow_count, 1, out_width)),
        in_specs=smem(1) + vmem(9),
        out_specs=vmem(1)[0],
        scratch_shapes=[
            pltpu.VMEM((copies, fine, HALO_Z + GRID_Z, 2 * GRID_X), jnp.float32),
            pltpu.VMEM((fine + 1, GRID_Z, 2 * GRID_X), jnp.float32),
        ]
        + [pltpu.VMEM((256, length), bf16)] * 2
        + [pltpu.VMEM((narrow_count, wave_rows, length), jnp.float32)] * 2,
        compiler_params=limits(48),
        name="mesh",
    )(
        jnp.asarray(factors, jnp.float32),
        table,
        shifts,
        phase,
        jnp.asarray(mode_factors(GRID_X, folded_order(GRID_X)), jnp.float32),
        jnp.asarray(mode_factors(GRID_Z, folded_order(GRID_Z)).T, jnp.float32),
        *[jnp.asarray(half) for half in halves(fold_table(GRID_X))],
        *[jnp.asarray(half) for half in halves(fold_table(GRID_X).T)],
    )
    arrived = lax.all_to_all(partial.reshape(pieces, 1, out_width), axes, 0, 0, tiled=True)
    atom_field, centroid_field, energy = pl.pallas_call(
        finish_kernel,
        out_shape=(shaped((4, 1, atoms)), shaped((4, 1, atoms)), shaped((1, 128))),
        in_specs=vmem(2),
        out_specs=tuple(vmem(3)),
        name="finish",
    )(arrived, kinds)
    atom_field = atom_field.reshape(4, 1, 1, 1, atoms)
    centroid_field = centroid_field.reshape(4, 1, 1, 1, atoms)
    return (dipole.reshape(3, 1, 1, 1, atoms), atom_field, centroid_field, energy[0, 0])


def solution(mesh):
    column = P(None, "wide", "narrow", None, None)
    in_specs = (column, P("wide", "narrow", None, None), P("wide", "narrow", None, None, None))
    in_specs = in_specs + (P(),) * 13
    out_specs = (column, column, column, P())
    return jax.shard_map(local, mesh=mesh, in_specs=in_specs, out_specs=out_specs, check_vma=False)
```

```python
import math

import jax
import jax.numpy as jnp
import numpy as np
from jax import lax
from jax.experimental import pallas as pl
from jax.experimental.pallas import tpu as pltpu
from jax.sharding import PartitionSpec as P

GRID_X = 256
GRID_Y = 256
GRID_Z = 256
AXIS_COLUMNS = 16

radius_scale = 24.0
wannier_reach = 0.5
ewald_beta = 0.9
coulomb = 0.25

ROW_PAD = 32
SLOT_CHUNK = 16
HALO_X = 16
HALO_Z = 8

NN = (((1,), (0,)), ((), ()))
NT = (((1,), (1,)), ((), ()))


def split(value):
    high = value.astype(jnp.bfloat16)
    low = (value - high.astype(jnp.float32)).astype(jnp.bfloat16)
    return high, low


def multiply(left, right, dims=NN):
    def one(a, b):
        return lax.dot_general(a, b, dims, preferred_element_type=jnp.float32)

    return one(left[0], right[0]) + (one(left[1], right[0]) + one(left[0], right[1]))


def spline_pair(offset):
    centred = offset - 2.0
    away = jnp.abs(centred)
    outer = jnp.maximum(2.0 - away, 0.0)
    inner = jnp.maximum(1.0 - away, 0.0)
    outer_square = outer * outer
    inner_square = inner * inner
    value = (outer_square * outer - 4.0 * (inner_square * inner)) * (1.0 / 6.0)
    slope = jnp.where(centred < 0.0, 0.5, -0.5) * (outer_square - 4.0 * inner_square)
    return value, slope


def lookup(row_table, spot):
    found = None
    for part in range(row_table.shape[1] // 128):
        inside = spot // 128 == part
        here = jnp.take_along_axis(
            jnp.broadcast_to(row_table[:, part * 128 : (part + 1) * 128], spot.shape),
            lax.rem(spot, 128),
            axis=1,
            mode="promise_in_bounds",
        )
        found = here if found is None else jnp.where(inside, here, found)
    return found


def pack_kernel(positions, species, out_ref):
    rows = [positions[component] for component in range(3)]
    rows.append(species[...].astype(jnp.float32))
    rows = jnp.concatenate(rows, axis=0)
    for target in range(out_ref.shape[0]):
        out_ref[target] = rows


def prepare_kernel(
    neighbours,
    embed_one_w,
    embed_one_b,
    embed_two_w,
    embed_two_b,
    embed_three_w,
    embed_three_b,
    fit_one_w,
    fit_one_b,
    fit_two_w,
    fit_two_b,
    fit_three_w,
    fit_three_b,
    constants,
    codes_ref,
    columns_ref,
    second_ref,
    third_ref,
    one_high_ref,
    one_low_ref,
    two_high_ref,
    two_low_ref,
    three_high_ref,
    three_low_ref,
    phase_ref,
    green_ref,
    rows,
    square,
    arrivals,
    *held,
):
    sources = (
        neighbours,
        embed_one_w,
        embed_one_b,
        embed_two_w,
        embed_two_b,
        embed_three_w,
        embed_three_b,
        fit_one_b,
        fit_two_b,
        fit_three_b,
        constants,
        fit_two_w,
        fit_three_w,
        fit_one_w,
    )
    copies = [
        pltpu.make_async_copy(source, target, arrivals.at[k])
        for k, (source, target) in enumerate(zip(sources, held))
    ]
    for copy in copies:
        copy.start()
    (
        neighbours,
        embed_one_w,
        embed_one_b,
        embed_two_w,
        embed_two_b,
        embed_three_w,
        embed_three_b,
        fit_one_b,
        fit_two_b,
        fit_three_b,
        constants,
        fit_two_w,
        fit_three_w,
        fit_one_w,
    ) = held
    for copy in copies[:11]:
        copy.wait()
    pieces = lax.axis_size("wide") * lax.axis_size("narrow")
    piece = lax.axis_index("wide") * lax.axis_size("narrow") + lax.axis_index("narrow")
    width_one = embed_one_w.shape[1]
    hidden = fit_two_w.shape[0]
    codes_ref[...] = jnp.transpose(neighbours[...].astype(jnp.float32)).astype(jnp.int32)
    rows[...] = jnp.zeros_like(rows)
    for kind in range(2):
        rows[kind : kind + 1, 0:width_one] = embed_one_w[kind : kind + 1, :]
        rows[2 + kind : 3 + kind, 0:width_one] = embed_one_b[kind : kind + 1, :]
    for row, source, groups in ((4, embed_two_b, 2), (5, embed_three_b, 4)):
        for k in range(groups):
            rows[row : row + 1, k * ROW_PAD : k * ROW_PAD + width_one] = source[
                :, k * width_one : (k + 1) * width_one
            ]
    for row, source in ((6, fit_one_b), (7, fit_two_b), (8, fit_three_b)):
        rows[row : row + 1, 0:hidden] = source[...]
    columns_ref[...] = jnp.transpose(rows[...])

    square[...] = jnp.zeros_like(square)
    for k in range(2):
        square[0:width_one, k * ROW_PAD : k * ROW_PAD + width_one] = embed_two_w[
            :, k * width_one : (k + 1) * width_one
        ]
    high, low = split(jnp.transpose(square[0:128, 0:128])[0 : 2 * ROW_PAD, 0:ROW_PAD])
    second_ref[...] = jnp.concatenate([high, high, low], axis=1)
    square[0:128, 0:128] = jnp.zeros((128, 128), jnp.float32)
    for g in range(2):
        for k in range(4):
            square[
                g * ROW_PAD : g * ROW_PAD + width_one, k * ROW_PAD : k * ROW_PAD + width_one
            ] = embed_three_w[
                g * width_one : (g + 1) * width_one, k * width_one : (k + 1) * width_one
            ]
    high, low = split(jnp.transpose(square[0:128, 0:128])[:, 0 : 2 * ROW_PAD])
    third_ref[...] = jnp.concatenate([high, high, low], axis=1)
    for copy in copies[11:13]:
        copy.wait()
    for source, high_ref, low_ref in (
        (fit_two_w, two_high_ref, two_low_ref),
        (fit_three_w, three_high_ref, three_low_ref),
    ):
        square[0:hidden, 0:hidden] = source[...]
        high_ref[...], low_ref[...] = split(jnp.transpose(square[...])[0:hidden, 0:hidden])

    fine = GRID_Y // 2 // pieces
    shape = (phase_ref.shape[0], 128)
    row = lax.broadcasted_iota(jnp.int32, shape, 0)
    mode = piece * fine + row // 2
    for part in range(GRID_Y // 128):
        cell = lax.broadcasted_iota(jnp.int32, shape, 1) + part * 128
        spot = lax.rem(mode * cell, GRID_Y)
        cosine = lookup(constants[0:1, :], spot)
        sine = lookup(constants[1:2, :], spot)
        alternate = (1 - 2 * lax.rem(cell, 2)).astype(jnp.float32)
        odd = jnp.where(mode == 0, alternate, -sine)
        value = jnp.where(lax.rem(row, 2) == 0, cosine, odd)
        phase_ref[:, part * 128 : (part + 1) * 128] = jnp.where(row < 2 * fine, value, 0.0)

    column = jnp.transpose(constants[...])
    lane = lax.broadcasted_iota(jnp.int32, (1, GRID_Y), 1)
    for j in range(fine + 1):
        here = lane == (GRID_Y // 2 if j == fine else piece * fine + j)
        factor = jnp.sum(jnp.where(here, constants[2:3, :], 0.0), axis=1, keepdims=True)
        part = jnp.sum(jnp.where(here, constants[3:4, :], 0.0), axis=1, keepdims=True)
        wave = (part + constants[5:6, :]) + column[:, 7:8]
        top = (factor * constants[4:5, :]) * column[:, 6:7]
        green_ref[j] = jnp.where(wave == 0.0, 0.0, top / jnp.where(wave == 0.0, 1.0, wave))

    copies[13].wait()
    one_high_ref[...], one_low_ref[...] = split(fit_one_w[...])


def centroid_kernel(
    table,
    codes,
    columns,
    second,
    third,
    one_high,
    one_low,
    two_high,
    two_low,
    three_high,
    three_low,
    fit_out_w,
    dipole_ref,
    shift_ref,
    matrix,
    descriptor,
):
    wide_count, narrow_count, _, atoms = table.shape
    listed = codes.shape[0]
    width_three = fit_out_w.shape[0]
    width_one = width_three // 4
    hidden_width = two_high.shape[0]
    cells = (GRID_X // wide_count, GRID_Y, GRID_Z // narrow_count)
    at_wide = lax.axis_index("wide")
    at_narrow = lax.axis_index("narrow")
    own = table[at_wide, at_narrow]
    nearby = []
    for step in range(9):
        wide_at = lax.rem(at_wide + (step // 3 - 1) + wide_count, wide_count)
        narrow_at = lax.rem(at_narrow + (step % 3 - 1) + narrow_count, narrow_count)
        nearby.append(table[wide_at, narrow_at])

    second_all = second[...]
    third_all = third[...]
    weight_oxygen = jnp.broadcast_to(columns[0:ROW_PAD, 0:1], (ROW_PAD, atoms))
    weight_hydrogen = jnp.broadcast_to(columns[0:ROW_PAD, 1:2], (ROW_PAD, atoms))
    bias_oxygen = jnp.broadcast_to(columns[0:ROW_PAD, 2:3], (ROW_PAD, atoms))
    bias_hydrogen = jnp.broadcast_to(columns[0:ROW_PAD, 3:4], (ROW_PAD, atoms))
    second_bias = columns[0 : 2 * ROW_PAD, 4:5]
    third_bias = columns[0 : 4 * ROW_PAD, 5:6]
    matrix[...] = jnp.zeros_like(matrix)

    def chunk(index, carry):
        first = pl.multiple_of(index * SLOT_CHUNK, SLOT_CHUNK)
        code = codes[pl.ds(first, SLOT_CHUNK), :]
        offset = code // atoms
        slot = code - offset * atoms
        step_x = jnp.where(offset >= 9, 1, 0) + jnp.where(offset >= 18, 1, 0)
        rest = offset - 9 * step_x
        step_z = jnp.where(rest >= 3, 1, 0) + jnp.where(rest >= 6, 1, 0)
        step_y = rest - 3 * step_z
        brick = step_x * 3 + step_z
        found = []
        for component in range(4):
            picked = jnp.zeros((SLOT_CHUNK, atoms), jnp.float32)
            for step in range(9):
                row = jnp.broadcast_to(
                    nearby[step][component : component + 1], (SLOT_CHUNK, atoms)
                )
                here = jnp.take_along_axis(row, slot, axis=1, mode="promise_in_bounds")
                picked = jnp.where(brick == step, here, picked)
            found.append(picked)
        scaled = []
        for component, step in enumerate((step_x, step_y, step_z)):
            extent = float(cells[component])
            relative = (step - 1).astype(jnp.float32) * extent + (
                found[component] - own[component : component + 1]
            ) * extent
            scaled.append(relative * (1.0 / radius_scale))
        smooth = 1.0 / (
            1.0 + (scaled[0] * scaled[0] + scaled[1] * scaled[1] + scaled[2] * scaled[2])
        )
        radial = [smooth] + [smooth * part for part in scaled]
        hydrogen = found[3] > 0.5
        first_layers = []
        for k in range(SLOT_CHUNK):
            row = smooth[k : k + 1]
            kind = hydrogen[k : k + 1]
            weight = jnp.where(kind, weight_hydrogen, weight_oxygen)
            bias = jnp.where(kind, bias_hydrogen, bias_oxygen)
            first_layers.append(jnp.tanh(weight * row + bias))
        layer_one = jnp.concatenate(first_layers, axis=1)
        high, low = split(layer_one)
        layer_two = lax.dot_general(
            second_all,
            jnp.concatenate([high, low, high], axis=0),
            NN,
            preferred_element_type=jnp.float32,
        )
        layer_two = jnp.tanh(layer_two + second_bias) + jnp.concatenate(
            [layer_one, layer_one], axis=0
        )
        high, low = split(layer_two)
        layer_three = lax.dot_general(
            third_all,
            jnp.concatenate([high, low, high], axis=0),
            NN,
            preferred_element_type=jnp.float32,
        )
        layer_three = jnp.tanh(layer_three + third_bias) + jnp.concatenate(
            [layer_two, layer_two], axis=0
        )
        for part in range(4):
            total = matrix[part]
            for k in range(SLOT_CHUNK):
                total = total + layer_three[:, k * atoms : (k + 1) * atoms] * radial[part][k : k + 1]
            matrix[part] = total
        return carry

    lax.fori_loop(0, listed // SLOT_CHUNK, chunk, 0)

    parts = []
    for part in range(4):
        padded = matrix[part] * (1.0 / listed)
        parts.append(
            jnp.concatenate(
                [padded[k * ROW_PAD : k * ROW_PAD + width_one] for k in range(4)], axis=0
            )
        )
    leading = [part[0:AXIS_COLUMNS] for part in parts]
    for row in range(width_three):
        total = parts[0][row : row + 1] * leading[0]
        for part in range(1, 4):
            total = total + parts[part][row : row + 1] * leading[part]
        descriptor[row * AXIS_COLUMNS : (row + 1) * AXIS_COLUMNS, :] = total
    def layer(high_ref, low_ref, given, column):
        weights = (high_ref[...], low_ref[...])
        return jnp.tanh(multiply(weights, split(given)) + columns[0:hidden_width, column : column + 1])

    hidden = layer(one_high, one_low, descriptor[...], 6)
    hidden = hidden + layer(two_high, two_low, hidden, 7)
    hidden = hidden + layer(three_high, three_low, hidden, 8)
    coeffs = multiply(split(fit_out_w[...]), split(hidden))
    vector = jnp.concatenate(
        [jnp.sum(coeffs * parts[1 + c], axis=0, keepdims=True) for c in range(3)], axis=0
    )
    oxygen = 1.0 - own[3:4]
    for c in range(3):
        dipole_ref[c] = vector[c : c + 1] * oxygen
    moved = wannier_reach * jnp.tanh(vector)
    moved = jnp.concatenate([moved, jnp.zeros((1, atoms), jnp.float32)], axis=0)
    for target in range(shift_ref.shape[0]):
        shift_ref[target] = moved


def mesh_kernel(
    table,
    shifts,
    phase,
    green_ref,
    fold_high,
    fold_low,
    unfold_high,
    unfold_low,
    out_ref,
    grid,
    planes,
    weights,
    slopes,
    weights_z,
    waves,
    wave_slopes,
):
    wide_count, narrow_count, _, atoms = table.shape
    cells_x = GRID_X // wide_count
    cells_z = GRID_Z // narrow_count
    window = cells_z + HALO_Z
    reach = cells_x + HALO_X
    pair = 2 * atoms
    length = wide_count * pair
    copies = grid.shape[0]
    fine = grid.shape[1]
    channels = 2 * fine
    rows = phase.shape[0]
    half_x = GRID_X // 2
    half_z = GRID_Z // 2
    piece = lax.axis_index("wide") * narrow_count + lax.axis_index("narrow")
    lane_zero = lax.broadcasted_iota(jnp.int32, (1, half_x), 1) == 0
    row_zero = lax.broadcasted_iota(jnp.int32, (half_z, 1), 0) == 0

    def fold():
        return (fold_high[...], fold_low[...])

    def unfold():
        return (unfold_high[...], unfold_low[...])

    def sites(at_wide, at_narrow):
        atom = table[at_wide, at_narrow]
        moved = shifts[at_wide, at_narrow]
        found = []
        for component, extent in enumerate((cells_x, GRID_Y, cells_z)):
            start = atom[component : component + 1] * float(extent)
            found.append(jnp.concatenate([start, start + moved[component : component + 1]], axis=1))
        oxygen = 1.0 - atom[3:4]
        found.append(jnp.concatenate([6.0 * oxygen + atom[3:4], -8.0 * oxygen], axis=1))
        return found

    def line(at_narrow):
        groups = [sites(at_wide, at_narrow) for at_wide in range(wide_count)]
        return [jnp.concatenate([g[k] for g in groups], axis=1) for k in range(4)]

    def splines_z(row):
        counter = lax.broadcasted_iota(jnp.int32, (window, 1), 0).astype(jnp.float32)
        return spline_pair(row - (counter - float(HALO_Z)))

    def fill_x(row, targets):
        counter = lax.broadcasted_iota(jnp.int32, (reach, 1), 0).astype(jnp.float32)
        both = spline_pair(row - (counter - float(HALO_X)))
        rest = jnp.zeros((128 - reach, length), jnp.bfloat16)
        for values, ref in zip(both, targets):
            if ref is not None:
                high, low = split(values)
                ref[0:reach, :] = high
                ref[reach:128, :] = rest
                ref[128 : 128 + reach, :] = low
                ref[128 + reach : 256, :] = rest

    grid[:, :, 0:HALO_Z, :] = jnp.zeros((copies, fine, HALO_Z, 2 * GRID_X), jnp.float32)

    def spread(at_narrow):
        row_x, row_y, row_z, charge = line(at_narrow)
        lower = jnp.floor(row_y)
        back = lax.broadcasted_iota(jnp.int32, (8, 1), 0)
        value_y, slope_y = spline_pair((row_y - lower) + back.astype(jnp.float32))
        cell = lax.rem(lower.astype(jnp.int32) - back + GRID_Y, GRID_Y)
        wave_blocks = []
        slope_blocks = []
        for block in range(length // 128):
            lanes = slice(block * 128, (block + 1) * 128)
            wave = jnp.zeros((rows, 128), jnp.float32)
            wave_slope = jnp.zeros((rows, 128), jnp.float32)
            for k in range(4):
                spot = jnp.broadcast_to(cell[k : k + 1, lanes], (rows, 128))
                found = lookup(phase[...], spot)
                wave = wave + value_y[k : k + 1, lanes] * found
                wave_slope = wave_slope + slope_y[k : k + 1, lanes] * found
            wave_blocks.append(wave)
            slope_blocks.append(wave_slope)
        wave = jnp.concatenate(wave_blocks, axis=1)
        waves[at_narrow] = wave
        wave_slopes[at_narrow] = jnp.concatenate(slope_blocks, axis=1)
        fill_x(row_x, (weights.at[at_narrow], None))
        value_z, _ = splines_z(row_z)
        weights_z[at_narrow] = value_z
        charged = wave * charge
        first = pl.multiple_of(at_narrow * cells_z, HALO_Z)
        for at_wide in range(wide_count):
            lanes = slice(at_wide * pair, (at_wide + 1) * pair)
            near = value_z[:, lanes]
            left = jnp.concatenate(
                [near * charged[c : c + 1, lanes] for c in range(channels)], axis=0
            )
            high, low = split(left)
            across = weights[at_narrow, :, lanes]
            total = lax.dot_general(high, across, NT, preferred_element_type=jnp.float32)
            total = total[:, 0:128] + (
                total[:, 128:256]
                + lax.dot_general(low, across[0:128], NT, preferred_element_type=jnp.float32)
            )
            start = at_wide // copies * 128
            for c in range(channels):
                spot = slice(c % 2 * GRID_X + start, c % 2 * GRID_X + start + 128)
                k = at_wide % copies
                part = total[c * window : (c + 1) * window]
                grid[k, c // 2, pl.ds(first, HALO_Z), spot] += part[:HALO_Z]
                grid[k, c // 2, pl.ds(first + HALO_Z, cells_z), spot] = part[HALO_Z:]

    def in_pairs(step):
        def both(index, carry):
            step(2 * index, 0)
            step(2 * index + 1, 1)
            return carry

        lax.fori_loop(0, narrow_count // 2, both, 0)

    in_pairs(lambda at_narrow, _: spread(at_narrow))

    def gather(j, carry):
        for lanes in (slice(0, GRID_X), slice(GRID_X, 2 * GRID_X)):
            total = None
            for k in range(copies):
                moved = pltpu.roll(grid[k, j, :, lanes], (k * cells_x - HALO_X) % GRID_X, 1)
                total = moved if total is None else total + moved
            planes[j, :, lanes] = total[HALO_Z:]
            planes[j, GRID_Z - HALO_Z :, lanes] += total[:HALO_Z]
        return carry

    lax.fori_loop(0, fine, gather, 0)
    is_first = piece == 0

    def paired(real, imag, zero, axis):
        half = real.shape[axis] // 2
        first = (slice(None),) * axis + (slice(0, half),)
        second = (slice(None),) * axis + (slice(half, 2 * half),)
        real_c, real_s = real[first], real[second]
        if imag is None:
            none = jnp.zeros_like(real_s)
            real_all = [real_c, jnp.where(zero, real_s, real_c)]
            imag_all = [jnp.where(zero, none, -real_s), jnp.where(zero, none, real_s)]
        else:
            imag_c, imag_s = imag[first], imag[second]
            real_all = [
                real_c + jnp.where(zero, 0.0, imag_s),
                jnp.where(zero, real_s, real_c - imag_s),
            ]
            imag_all = [
                imag_c - jnp.where(zero, 0.0, real_s),
                jnp.where(zero, imag_s, imag_c + real_s),
            ]
        return jnp.concatenate(real_all, axis=axis), jnp.concatenate(imag_all, axis=axis)

    def merged(real, imag, zero, axis):
        half = real.shape[axis] // 2
        first = (slice(None),) * axis + (slice(0, half),)
        second = (slice(None),) * axis + (slice(half, 2 * half),)
        real_a, real_b = real[first], real[second]
        imag_a, imag_b = imag[first], imag[second]
        real = [
            real_a + jnp.where(zero, 0.0, real_b),
            jnp.where(zero, real_b, imag_b - imag_a),
        ]
        imag = [
            imag_a + jnp.where(zero, 0.0, imag_b),
            jnp.where(zero, imag_b, real_a - real_b),
        ]
        return jnp.concatenate(real, axis=axis), jnp.concatenate(imag, axis=axis)

    def to_modes(real, imag, j):
        real = multiply(split(real), fold())
        if imag is not None:
            imag = multiply(split(imag), fold())
        real, imag = paired(real, imag, lane_zero, 1)
        real = multiply(unfold(), split(real))
        imag = multiply(unfold(), split(imag))
        real, imag = paired(real, imag, row_zero, 0)
        green = green_ref[j]
        mode = GRID_Y // 2 if j == fine else piece * fine + j
        share = jnp.where((mode == 0) | (mode == GRID_Y // 2), 0.5, 1.0)
        part = jnp.sum(green * (real * real + imag * imag), axis=0, keepdims=True)
        return green * real, green * imag, share * part

    second_plane = jnp.where(is_first, planes[0, :, GRID_X:], 0.0)
    last_real, last_imag, energy = to_modes(second_plane, None, fine)
    for j in range(fine):
        imag = planes[j, :, GRID_X:]
        if j == 0:
            imag = jnp.where(is_first, 0.0, imag)
        real, imag, part = to_modes(planes[j, :, 0:GRID_X], imag, j)
        energy = energy + part
        if j == 0:
            real, imag = real - last_imag, imag + last_real
        real, imag = merged(real, imag, row_zero, 0)
        real = multiply(fold(), split(real))
        imag = multiply(fold(), split(imag))
        real, imag = merged(real, imag, lane_zero, 1)
        scale = jnp.where(piece * fine + j == 0, 1.0, 2.0)
        for part, lanes in ((real, slice(0, GRID_X)), (imag, slice(GRID_X, 2 * GRID_X))):
            part = multiply(split(part * scale), unfold())
            for k in range(copies):
                moved = pltpu.roll(part, (HALO_X - k * cells_x) % GRID_X, 1)
                grid[k, j, HALO_Z:, lanes] = moved
                grid[k, j, 0:HALO_Z, lanes] = moved[GRID_Z - HALO_Z :]
    energy = jnp.broadcast_to(jnp.sum(energy, axis=1, keepdims=True), (1, 128))

    def collect(at_narrow, buffer):
        row_x, _, row_z, _ = line(at_narrow)
        fill_x(row_x, (None, slopes.at[buffer]))
        value_z = weights_z[at_narrow]
        _, slope_z = splines_z(row_z)
        first = pl.multiple_of(at_narrow * cells_z, HALO_Z)
        lefts = []
        for k in range(copies):
            left = jnp.concatenate(
                [
                    grid[k, c // 2, pl.ds(first, window), c % 2 * GRID_X : (c % 2 + 1) * GRID_X]
                    for c in range(channels)
                ],
                axis=0,
            )
            lefts.append(split(left))
        wave = waves[at_narrow]
        wave_slope = wave_slopes[at_narrow]
        for at_wide in range(wide_count):
            lanes = slice(at_wide * pair, (at_wide + 1) * pair)
            start = at_wide // copies * 128
            high = lefts[at_wide % copies][0][:, start : start + 128]
            low = lefts[at_wide % copies][1][:, start : start + 128]
            twice = jnp.concatenate([high, high], axis=1)

            def across(right):
                return lax.dot_general(
                    twice, right, NN, preferred_element_type=jnp.float32
                ) + lax.dot_general(low, right[0:128], NN, preferred_element_type=jnp.float32)

            value = across(weights[at_narrow, :, lanes])
            slope = across(slopes[buffer, :, lanes])
            plain = jnp.zeros((window, pair), jnp.float32)
            along_x = plain
            along_y = plain
            for c in range(channels):
                block = slice(c * window, (c + 1) * window)
                plain = plain + value[block] * wave[c : c + 1, lanes]
                along_x = along_x + slope[block] * wave[c : c + 1, lanes]
                along_y = along_y + value[block] * wave_slope[c : c + 1, lanes]
            near = value_z[:, lanes]
            near_slope = slope_z[:, lanes]
            results = [
                jnp.sum(near * plain, axis=0, keepdims=True),
                -jnp.sum(near * along_x, axis=0, keepdims=True),
                -jnp.sum(near * along_y, axis=0, keepdims=True),
                -jnp.sum(near_slope * plain, axis=0, keepdims=True),
            ]
            for k, row in enumerate(results):
                out_ref[at_wide, at_narrow, :, k * pair : (k + 1) * pair] = row
            out_ref[at_wide, at_narrow, :, 4 * pair :] = energy

    in_pairs(collect)


def finish_kernel(arrived, species, atom_ref, centroid_ref, energy_ref):
    atoms = species.shape[1]
    total = arrived[0]
    for k in range(1, arrived.shape[0]):
        total = total + arrived[k]
    oxygen = 1.0 - species[...].astype(jnp.float32)
    for k in range(4):
        atom_ref[k] = total[:, 2 * k * atoms : (2 * k + 1) * atoms]
        centroid_ref[k] = total[:, (2 * k + 1) * atoms : (2 * k + 2) * atoms] * oxygen
    energy_ref[...] = total[:, 8 * atoms :] * (1.0 / (atoms * arrived.shape[0]))


def mode_factors(length, order):
    wrapped = np.where(2 * order >= length, order - length, order)
    square = (wrapped / length) ** 2
    ratio = (4.0 + 2.0 * np.cos(2.0 * math.pi * order / length)) / 6.0
    return np.stack([np.exp(-(math.pi**2) * square / ewald_beta**2) / ratio**2, square])


def folded_order(length):
    half = length // 2
    counter = np.arange(half)
    return np.concatenate([counter, np.where(counter == 0, half, length - counter)])


def fold_table(length):
    half = length // 2
    turns = np.outer(np.arange(length), np.arange(half)) % length * (2.0 * math.pi / length)
    sines = np.sin(turns)
    sines[:, 0] = 1.0 - 2.0 * (np.arange(length) % 2)
    return np.concatenate([np.cos(turns), sines], axis=1)


def halves(table):
    high = table.astype(jnp.bfloat16)
    low = (table - high.astype(np.float64)).astype(jnp.bfloat16)
    return high, low


def vmem(count):
    return [pl.BlockSpec(memory_space=pltpu.VMEM)] * count


def shaped(shape, dtype=jnp.float32):
    return jax.ShapeDtypeStruct(shape, dtype)


def limits(mebibytes):
    return pltpu.CompilerParams(vmem_limit_bytes=mebibytes * 1024 * 1024)


def local(
    positions,
    species,
    neighbours,
    embed_one_w,
    embed_one_b,
    embed_two_w,
    embed_two_b,
    embed_three_w,
    embed_three_b,
    fit_one_w,
    fit_one_b,
    fit_two_w,
    fit_two_b,
    fit_three_w,
    fit_three_b,
    fit_out_w,
):
    axes = ("wide", "narrow")
    wide_count = lax.axis_size("wide")
    narrow_count = lax.axis_size("narrow")
    pieces = wide_count * narrow_count
    atoms = positions.shape[4]
    listed = neighbours.shape[4]
    fine = GRID_Y // 2 // pieces
    width_three = embed_three_w.shape[1]
    entries, hidden = fit_one_w.shape
    kinds = species.reshape(1, atoms)

    packed = pl.pallas_call(
        pack_kernel,
        out_shape=shaped((pieces, 4, atoms)),
        in_specs=vmem(2),
        out_specs=vmem(1)[0],
        name="pack",
    )(positions.reshape(3, 1, atoms), kinds)
    table = lax.all_to_all(packed, axes, 0, 0, tiled=True)
    table = table.reshape(wide_count, narrow_count, 4, atoms)

    tall = 4 * ROW_PAD
    bf16 = jnp.bfloat16
    wave_rows = -(-2 * fine // 8) * 8
    angle = np.arange(GRID_Y) * (2.0 * math.pi / GRID_Y)
    constants = np.concatenate(
        [
            np.stack([np.cos(angle), np.sin(angle)]),
            mode_factors(GRID_Y, np.arange(GRID_Y)),
            mode_factors(GRID_X, folded_order(GRID_X)),
            mode_factors(GRID_Z, folded_order(GRID_Z)),
        ]
    )
    constants[2] *= coulomb / (math.pi * GRID_X * GRID_Y * GRID_Z)
    arguments = (
        neighbours.reshape(atoms, listed),
        embed_one_w,
        embed_one_b,
        embed_two_w,
        embed_two_b[None],
        embed_three_w,
        embed_three_b[None],
        fit_one_w.T,
        fit_one_b[None],
        fit_two_w,
        fit_two_b[None],
        fit_three_w,
        fit_three_b[None],
        jnp.asarray(constants, jnp.float32),
    )
    held = [arguments[k] for k in (0, 1, 2, 3, 4, 5, 6, 8, 10, 12, 13, 9, 11, 7)]
    prepared = pl.pallas_call(
        prepare_kernel,
        out_shape=(
            shaped((listed, atoms), jnp.int32),
            shaped((256, 16)),
            shaped((2 * ROW_PAD, 3 * ROW_PAD), bf16),
            shaped((tall, 6 * ROW_PAD), bf16),
            shaped((hidden, entries), bf16),
            shaped((hidden, entries), bf16),
        )
        + (shaped((hidden, hidden), bf16),) * 4
        + (shaped((wave_rows, GRID_Y)), shaped((fine + 1, GRID_Z, GRID_X))),
        in_specs=[pl.BlockSpec(memory_space=pltpu.HBM)] * len(arguments),
        out_specs=tuple(vmem(12)),
        scratch_shapes=[
            pltpu.VMEM((16, 256), jnp.float32),
            pltpu.VMEM((256, 256), jnp.float32),
            pltpu.SemaphoreType.DMA((len(held),)),
        ]
        + [pltpu.VMEM(array.shape, array.dtype) for array in held],
        compiler_params=limits(32),
        cost_estimate=pl.CostEstimate(
            flops=1000000, bytes_accessed=8 * entries * hidden, transcendentals=0
        ),
        name="prepare",
    )(*arguments)
    phase, green = prepared[10:]
    dipole, shifts = pl.pallas_call(
        centroid_kernel,
        out_shape=(shaped((3, 1, atoms)), shaped((pieces, 4, atoms))),
        in_specs=vmem(12),
        out_specs=tuple(vmem(2)),
        scratch_shapes=[
            pltpu.VMEM((4, tall, atoms), jnp.float32),
            pltpu.VMEM((width_three * AXIS_COLUMNS, atoms), jnp.float32),
        ],
        compiler_params=limits(32),
        name="centroids",
    )(table, *prepared[:10], fit_out_w.T)
    shifts = lax.all_to_all(shifts, axes, 0, 0, tiled=True)
    shifts = shifts.reshape(wide_count, narrow_count, 4, atoms)

    cells_x = GRID_X // wide_count
    copies = 128 // cells_x
    length = wide_count * 2 * atoms
    out_width = 8 * atoms + 128
    partial = pl.pallas_call(
        mesh_kernel,
        out_shape=shaped((wide_count, narrow_count, 1, out_width)),
        in_specs=vmem(8),
        out_specs=vmem(1)[0],
        scratch_shapes=[
            pltpu.VMEM((copies, fine, HALO_Z + GRID_Z, 2 * GRID_X), jnp.float32),
            pltpu.VMEM((fine + 1, GRID_Z, 2 * GRID_X), jnp.float32),
        ]
        + [pltpu.VMEM((narrow_count, 256, length), bf16), pltpu.VMEM((2, 256, length), bf16)]
        + [pltpu.VMEM((narrow_count, GRID_Z // narrow_count + HALO_Z, length), jnp.float32)]
        + [pltpu.VMEM((narrow_count, wave_rows, length), jnp.float32)] * 2,
        compiler_params=limits(48),
        name="mesh",
    )(
        table,
        shifts,
        phase,
        green,
        *[jnp.asarray(half) for half in halves(fold_table(GRID_X))],
        *[jnp.asarray(half) for half in halves(fold_table(GRID_X).T)],
    )
    arrived = lax.all_to_all(partial.reshape(pieces, 1, out_width), axes, 0, 0, tiled=True)
    atom_field, centroid_field, energy = pl.pallas_call(
        finish_kernel,
        out_shape=(shaped((4, 1, atoms)), shaped((4, 1, atoms)), shaped((1, 128))),
        in_specs=vmem(2),
        out_specs=tuple(vmem(3)),
        name="finish",
    )(arrived, kinds)
    atom_field = atom_field.reshape(4, 1, 1, 1, atoms)
    centroid_field = centroid_field.reshape(4, 1, 1, 1, atoms)
    return (dipole.reshape(3, 1, 1, 1, atoms), atom_field, centroid_field, energy[0, 0])


def solution(mesh):
    column = P(None, "wide", "narrow", None, None)
    in_specs = (column, P("wide", "narrow", None, None), P("wide", "narrow", None, None, None))
    in_specs = in_specs + (P(),) * 13
    out_specs = (column, column, column, P())
    return jax.shard_map(local, mesh=mesh, in_specs=in_specs, out_specs=out_specs, check_vma=False)
```

```python
import math

import jax
import jax.numpy as jnp
import numpy as np
from jax import lax
from jax.experimental import pallas as pl
from jax.experimental.pallas import tpu as pltpu
from jax.sharding import PartitionSpec as P

GRID_X = 256
GRID_Y = 256
GRID_Z = 256
AXIS_COLUMNS = 16

radius_scale = 24.0
wannier_reach = 0.5
ewald_beta = 0.9
coulomb = 0.25

ROW_PAD = 32
SLOT_CHUNK = 16
HALO_X = 16
HALO_Z = 8

NN = (((1,), (0,)), ((), ()))
NT = (((1,), (1,)), ((), ()))


def split(value):
    high = value.astype(jnp.bfloat16)
    low = (value - high.astype(jnp.float32)).astype(jnp.bfloat16)
    return high, low


def multiply(left, right, dims=NN):
    def one(a, b):
        return lax.dot_general(a, b, dims, preferred_element_type=jnp.float32)

    return one(left[0], right[0]) + (one(left[1], right[0]) + one(left[0], right[1]))


def spline_pair(offset):
    centred = offset - 2.0
    away = jnp.abs(centred)
    outer = jnp.maximum(2.0 - away, 0.0)
    inner = jnp.maximum(1.0 - away, 0.0)
    outer_square = outer * outer
    inner_square = inner * inner
    value = (outer_square * outer - 4.0 * (inner_square * inner)) * (1.0 / 6.0)
    slope = jnp.where(centred < 0.0, 0.5, -0.5) * (outer_square - 4.0 * inner_square)
    return value, slope


def lookup(row_table, spot):
    found = None
    for part in range(row_table.shape[1] // 128):
        inside = spot // 128 == part
        here = jnp.take_along_axis(
            jnp.broadcast_to(row_table[:, part * 128 : (part + 1) * 128], spot.shape),
            lax.rem(spot, 128),
            axis=1,
            mode="promise_in_bounds",
        )
        found = here if found is None else jnp.where(inside, here, found)
    return found


def pack_kernel(positions, species, out_ref):
    rows = [positions[component] for component in range(3)]
    rows.append(species[...].astype(jnp.float32))
    rows = jnp.concatenate(rows, axis=0)
    for target in range(out_ref.shape[0]):
        out_ref[target] = rows


def prepare_kernel(
    neighbours,
    embed_one_w,
    embed_one_b,
    embed_two_w,
    embed_two_b,
    embed_three_w,
    embed_three_b,
    fit_one_w,
    fit_one_b,
    fit_two_w,
    fit_two_b,
    fit_three_w,
    fit_three_b,
    constants,
    codes_ref,
    columns_ref,
    second_ref,
    third_ref,
    one_high_ref,
    one_low_ref,
    two_high_ref,
    two_low_ref,
    three_high_ref,
    three_low_ref,
    phase_ref,
    green_ref,
    rows,
    square,
    arrivals,
    *held,
):
    sources = (
        neighbours,
        embed_one_w,
        embed_one_b,
        embed_two_w,
        embed_two_b,
        embed_three_w,
        embed_three_b,
        fit_one_b,
        fit_two_b,
        fit_three_b,
        constants,
        fit_two_w,
        fit_three_w,
        fit_one_w,
    )
    copies = [
        pltpu.make_async_copy(source, target, arrivals.at[k])
        for k, (source, target) in enumerate(zip(sources, held))
    ]
    for copy in copies:
        copy.start()
    (
        neighbours,
        embed_one_w,
        embed_one_b,
        embed_two_w,
        embed_two_b,
        embed_three_w,
        embed_three_b,
        fit_one_b,
        fit_two_b,
        fit_three_b,
        constants,
        fit_two_w,
        fit_three_w,
        fit_one_w,
    ) = held
    for copy in copies[:11]:
        copy.wait()
    pieces = lax.axis_size("wide") * lax.axis_size("narrow")
    piece = lax.axis_index("wide") * lax.axis_size("narrow") + lax.axis_index("narrow")
    width_one = embed_one_w.shape[1]
    hidden = fit_two_w.shape[0]
    codes_ref[...] = jnp.transpose(neighbours[...].astype(jnp.float32)).astype(jnp.int32)
    rows[...] = jnp.zeros_like(rows)
    for kind in range(2):
        rows[kind : kind + 1, 0:width_one] = embed_one_w[kind : kind + 1, :]
        rows[2 + kind : 3 + kind, 0:width_one] = embed_one_b[kind : kind + 1, :]
    for row, source, groups in ((4, embed_two_b, 2), (5, embed_three_b, 4)):
        for k in range(groups):
            rows[row : row + 1, k * ROW_PAD : k * ROW_PAD + width_one] = source[
                :, k * width_one : (k + 1) * width_one
            ]
    for row, source in ((6, fit_one_b), (7, fit_two_b), (8, fit_three_b)):
        rows[row : row + 1, 0:hidden] = source[...]
    columns_ref[...] = jnp.transpose(rows[...])

    square[...] = jnp.zeros_like(square)
    for k in range(2):
        square[0:width_one, k * ROW_PAD : k * ROW_PAD + width_one] = embed_two_w[
            :, k * width_one : (k + 1) * width_one
        ]
    high, low = split(jnp.transpose(square[0:128, 0:128])[0 : 2 * ROW_PAD, 0:ROW_PAD])
    second_ref[...] = jnp.concatenate([high, high, low], axis=1)
    square[0:128, 0:128] = jnp.zeros((128, 128), jnp.float32)
    for g in range(2):
        for k in range(4):
            square[
                g * ROW_PAD : g * ROW_PAD + width_one, k * ROW_PAD : k * ROW_PAD + width_one
            ] = embed_three_w[
                g * width_one : (g + 1) * width_one, k * width_one : (k + 1) * width_one
            ]
    high, low = split(jnp.transpose(square[0:128, 0:128])[:, 0 : 2 * ROW_PAD])
    third_ref[...] = jnp.concatenate([high, high, low], axis=1)
    for copy in copies[11:13]:
        copy.wait()
    for source, high_ref, low_ref in (
        (fit_two_w, two_high_ref, two_low_ref),
        (fit_three_w, three_high_ref, three_low_ref),
    ):
        square[0:hidden, 0:hidden] = source[...]
        high_ref[...], low_ref[...] = split(jnp.transpose(square[...])[0:hidden, 0:hidden])

    fine = GRID_Y // 2 // pieces
    shape = (phase_ref.shape[0], 128)
    row = lax.broadcasted_iota(jnp.int32, shape, 0)
    mode = piece * fine + row // 2
    for part in range(GRID_Y // 128):
        cell = lax.broadcasted_iota(jnp.int32, shape, 1) + part * 128
        spot = lax.rem(mode * cell, GRID_Y)
        cosine = lookup(constants[0:1, :], spot)
        sine = lookup(constants[1:2, :], spot)
        alternate = (1 - 2 * lax.rem(cell, 2)).astype(jnp.float32)
        odd = jnp.where(mode == 0, alternate, -sine)
        value = jnp.where(lax.rem(row, 2) == 0, cosine, odd)
        phase_ref[:, part * 128 : (part + 1) * 128] = jnp.where(row < 2 * fine, value, 0.0)

    column = jnp.transpose(constants[...])
    lane = lax.broadcasted_iota(jnp.int32, (1, GRID_Y), 1)
    for j in range(fine + 1):
        here = lane == (GRID_Y // 2 if j == fine else piece * fine + j)
        factor = jnp.sum(jnp.where(here, constants[2:3, :], 0.0), axis=1, keepdims=True)
        part = jnp.sum(jnp.where(here, constants[3:4, :], 0.0), axis=1, keepdims=True)
        wave = (part + constants[5:6, :]) + column[:, 7:8]
        top = (factor * constants[4:5, :]) * column[:, 6:7]
        green_ref[j] = jnp.where(wave == 0.0, 0.0, top / jnp.where(wave == 0.0, 1.0, wave))

    copies[13].wait()
    one_high_ref[...], one_low_ref[...] = split(fit_one_w[...])


def centroid_kernel(
    table,
    codes,
    columns,
    second,
    third,
    one_high,
    one_low,
    two_high,
    two_low,
    three_high,
    three_low,
    fit_out_w,
    dipole_ref,
    shift_ref,
    matrix,
    descriptor,
    arrivals,
    *held,
):
    sources = (one_high, one_low, two_high, two_low, three_high, three_low, fit_out_w)
    copies = [
        pltpu.make_async_copy(source, target, arrivals.at[k])
        for k, (source, target) in enumerate(zip(sources, held))
    ]
    for copy in copies:
        copy.start()
    one_high, one_low, two_high, two_low, three_high, three_low, fit_out_w = held
    wide_count, narrow_count, _, atoms = table.shape
    listed = codes.shape[0]
    width_three = fit_out_w.shape[0]
    width_one = width_three // 4
    hidden_width = two_high.shape[0]
    cells = (GRID_X // wide_count, GRID_Y, GRID_Z // narrow_count)
    at_wide = lax.axis_index("wide")
    at_narrow = lax.axis_index("narrow")
    own = table[at_wide, at_narrow]
    nearby = []
    for step in range(9):
        wide_at = lax.rem(at_wide + (step // 3 - 1) + wide_count, wide_count)
        narrow_at = lax.rem(at_narrow + (step % 3 - 1) + narrow_count, narrow_count)
        nearby.append(table[wide_at, narrow_at])

    second_all = second[...]
    third_all = third[...]
    weight_oxygen = jnp.broadcast_to(columns[0:ROW_PAD, 0:1], (ROW_PAD, atoms))
    weight_hydrogen = jnp.broadcast_to(columns[0:ROW_PAD, 1:2], (ROW_PAD, atoms))
    bias_oxygen = jnp.broadcast_to(columns[0:ROW_PAD, 2:3], (ROW_PAD, atoms))
    bias_hydrogen = jnp.broadcast_to(columns[0:ROW_PAD, 3:4], (ROW_PAD, atoms))
    second_bias = columns[0 : 2 * ROW_PAD, 4:5]
    third_bias = columns[0 : 4 * ROW_PAD, 5:6]
    matrix[...] = jnp.zeros_like(matrix)

    def chunk(index, carry):
        first = pl.multiple_of(index * SLOT_CHUNK, SLOT_CHUNK)
        code = codes[pl.ds(first, SLOT_CHUNK), :]
        offset = code // atoms
        slot = code - offset * atoms
        step_x = jnp.where(offset >= 9, 1, 0) + jnp.where(offset >= 18, 1, 0)
        rest = offset - 9 * step_x
        step_z = jnp.where(rest >= 3, 1, 0) + jnp.where(rest >= 6, 1, 0)
        step_y = rest - 3 * step_z
        brick = step_x * 3 + step_z
        found = []
        for component in range(4):
            picked = jnp.zeros((SLOT_CHUNK, atoms), jnp.float32)
            for step in range(9):
                row = jnp.broadcast_to(
                    nearby[step][component : component + 1], (SLOT_CHUNK, atoms)
                )
                here = jnp.take_along_axis(row, slot, axis=1, mode="promise_in_bounds")
                picked = jnp.where(brick == step, here, picked)
            found.append(picked)
        scaled = []
        for component, step in enumerate((step_x, step_y, step_z)):
            extent = float(cells[component])
            relative = (step - 1).astype(jnp.float32) * extent + (
                found[component] - own[component : component + 1]
            ) * extent
            scaled.append(relative * (1.0 / radius_scale))
        smooth = 1.0 / (
            1.0 + (scaled[0] * scaled[0] + scaled[1] * scaled[1] + scaled[2] * scaled[2])
        )
        radial = [smooth] + [smooth * part for part in scaled]
        hydrogen = found[3] > 0.5
        first_layers = []
        for k in range(SLOT_CHUNK):
            row = smooth[k : k + 1]
            kind = hydrogen[k : k + 1]
            weight = jnp.where(kind, weight_hydrogen, weight_oxygen)
            bias = jnp.where(kind, bias_hydrogen, bias_oxygen)
            first_layers.append(jnp.tanh(weight * row + bias))
        layer_one = jnp.concatenate(first_layers, axis=1)
        high, low = split(layer_one)
        layer_two = lax.dot_general(
            second_all,
            jnp.concatenate([high, low, high], axis=0),
            NN,
            preferred_element_type=jnp.float32,
        )
        layer_two = jnp.tanh(layer_two + second_bias) + jnp.concatenate(
            [layer_one, layer_one], axis=0
        )
        high, low = split(layer_two)
        layer_three = lax.dot_general(
            third_all,
            jnp.concatenate([high, low, high], axis=0),
            NN,
            preferred_element_type=jnp.float32,
        )
        layer_three = jnp.tanh(layer_three + third_bias) + jnp.concatenate(
            [layer_two, layer_two], axis=0
        )
        for part in range(4):
            total = matrix[part]
            for k in range(SLOT_CHUNK):
                total = total + layer_three[:, k * atoms : (k + 1) * atoms] * radial[part][k : k + 1]
            matrix[part] = total
        return carry

    lax.fori_loop(0, listed // SLOT_CHUNK, chunk, 0)

    parts = []
    for part in range(4):
        padded = matrix[part] * (1.0 / listed)
        parts.append(
            jnp.concatenate(
                [padded[k * ROW_PAD : k * ROW_PAD + width_one] for k in range(4)], axis=0
            )
        )
    leading = [part[0:AXIS_COLUMNS] for part in parts]
    for row in range(width_three):
        total = parts[0][row : row + 1] * leading[0]
        for part in range(1, 4):
            total = total + parts[part][row : row + 1] * leading[part]
        descriptor[row * AXIS_COLUMNS : (row + 1) * AXIS_COLUMNS, :] = total
    for copy in copies:
        copy.wait()

    def layer(high_ref, low_ref, given, column):
        weights = (high_ref[...], low_ref[...])
        return jnp.tanh(multiply(weights, split(given)) + columns[0:hidden_width, column : column + 1])

    hidden = layer(one_high, one_low, descriptor[...], 6)
    hidden = hidden + layer(two_high, two_low, hidden, 7)
    hidden = hidden + layer(three_high, three_low, hidden, 8)
    coeffs = multiply(split(fit_out_w[...]), split(hidden))
    vector = jnp.concatenate(
        [jnp.sum(coeffs * parts[1 + c], axis=0, keepdims=True) for c in range(3)], axis=0
    )
    oxygen = 1.0 - own[3:4]
    for c in range(3):
        dipole_ref[c] = vector[c : c + 1] * oxygen
    moved = wannier_reach * jnp.tanh(vector)
    moved = jnp.concatenate([moved, jnp.zeros((1, atoms), jnp.float32)], axis=0)
    for target in range(shift_ref.shape[0]):
        shift_ref[target] = moved


def mesh_kernel(
    table,
    shifts,
    phase,
    green_ref,
    fold_high,
    fold_low,
    unfold_high,
    unfold_low,
    out_ref,
    grid,
    planes,
    weights,
    slopes,
    weights_z,
    waves,
    wave_slopes,
):
    wide_count, narrow_count, _, atoms = table.shape
    cells_x = GRID_X // wide_count
    cells_z = GRID_Z // narrow_count
    window = cells_z + HALO_Z
    reach = cells_x + HALO_X
    pair = 2 * atoms
    length = wide_count * pair
    copies = grid.shape[0]
    fine = grid.shape[1]
    channels = 2 * fine
    rows = phase.shape[0]
    half_x = GRID_X // 2
    half_z = GRID_Z // 2
    piece = lax.axis_index("wide") * narrow_count + lax.axis_index("narrow")
    lane_zero = lax.broadcasted_iota(jnp.int32, (1, half_x), 1) == 0
    row_zero = lax.broadcasted_iota(jnp.int32, (half_z, 1), 0) == 0

    def fold():
        return (fold_high[...], fold_low[...])

    def unfold():
        return (unfold_high[...], unfold_low[...])

    def sites(at_wide, at_narrow):
        atom = table[at_wide, at_narrow]
        moved = shifts[at_wide, at_narrow]
        found = []
        for component, extent in enumerate((cells_x, GRID_Y, cells_z)):
            start = atom[component : component + 1] * float(extent)
            found.append(jnp.concatenate([start, start + moved[component : component + 1]], axis=1))
        oxygen = 1.0 - atom[3:4]
        found.append(jnp.concatenate([6.0 * oxygen + atom[3:4], -8.0 * oxygen], axis=1))
        return found

    def line(at_narrow):
        groups = [sites(at_wide, at_narrow) for at_wide in range(wide_count)]
        return [jnp.concatenate([g[k] for g in groups], axis=1) for k in range(4)]

    def splines_z(row):
        counter = lax.broadcasted_iota(jnp.int32, (window, 1), 0).astype(jnp.float32)
        return spline_pair(row - (counter - float(HALO_Z)))

    def fill_x(row, targets):
        counter = lax.broadcasted_iota(jnp.int32, (reach, 1), 0).astype(jnp.float32)
        both = spline_pair(row - (counter - float(HALO_X)))
        rest = jnp.zeros((128 - reach, length), jnp.bfloat16)
        for values, ref in zip(both, targets):
            if ref is not None:
                high, low = split(values)
                ref[0:reach, :] = high
                ref[reach:128, :] = rest
                ref[128 : 128 + reach, :] = low
                ref[128 + reach : 256, :] = rest

    grid[:, :, 0:HALO_Z, :] = jnp.zeros((copies, fine, HALO_Z, 2 * GRID_X), jnp.float32)

    def spread(at_narrow):
        row_x, row_y, row_z, charge = line(at_narrow)
        lower = jnp.floor(row_y)
        back = lax.broadcasted_iota(jnp.int32, (8, 1), 0)
        value_y, slope_y = spline_pair((row_y - lower) + back.astype(jnp.float32))
        cell = lax.rem(lower.astype(jnp.int32) - back + GRID_Y, GRID_Y)
        wave_blocks = []
        slope_blocks = []
        for block in range(length // 128):
            lanes = slice(block * 128, (block + 1) * 128)
            wave = jnp.zeros((rows, 128), jnp.float32)
            wave_slope = jnp.zeros((rows, 128), jnp.float32)
            for k in range(4):
                spot = jnp.broadcast_to(cell[k : k + 1, lanes], (rows, 128))
                found = lookup(phase[...], spot)
                wave = wave + value_y[k : k + 1, lanes] * found
                wave_slope = wave_slope + slope_y[k : k + 1, lanes] * found
            wave_blocks.append(wave)
            slope_blocks.append(wave_slope)
        wave = jnp.concatenate(wave_blocks, axis=1)
        waves[at_narrow] = wave
        wave_slopes[at_narrow] = jnp.concatenate(slope_blocks, axis=1)
        fill_x(row_x, (weights.at[at_narrow], None))
        value_z, _ = splines_z(row_z)
        weights_z[at_narrow] = value_z
        charged = wave * charge
        first = pl.multiple_of(at_narrow * cells_z, HALO_Z)
        for at_wide in range(wide_count):
            lanes = slice(at_wide * pair, (at_wide + 1) * pair)
            near = value_z[:, lanes]
            left = jnp.concatenate(
                [near * charged[c : c + 1, lanes] for c in range(channels)], axis=0
            )
            high, low = split(left)
            across = weights[at_narrow, :, lanes]
            total = lax.dot_general(high, across, NT, preferred_element_type=jnp.float32)
            total = total[:, 0:128] + (
                total[:, 128:256]
                + lax.dot_general(low, across[0:128], NT, preferred_element_type=jnp.float32)
            )
            start = at_wide // copies * 128
            for c in range(channels):
                spot = slice(c % 2 * GRID_X + start, c % 2 * GRID_X + start + 128)
                k = at_wide % copies
                part = total[c * window : (c + 1) * window]
                grid[k, c // 2, pl.ds(first, HALO_Z), spot] += part[:HALO_Z]
                grid[k, c // 2, pl.ds(first + HALO_Z, cells_z), spot] = part[HALO_Z:]

    def in_pairs(step):
        def both(index, carry):
            step(2 * index, 0)
            step(2 * index + 1, 1)
            return carry

        lax.fori_loop(0, narrow_count // 2, both, 0)

    in_pairs(lambda at_narrow, _: spread(at_narrow))

    def gather(j, carry):
        for lanes in (slice(0, GRID_X), slice(GRID_X, 2 * GRID_X)):
            total = None
            for k in range(copies):
                moved = pltpu.roll(grid[k, j, :, lanes], (k * cells_x - HALO_X) % GRID_X, 1)
                total = moved if total is None else total + moved
            planes[j, :, lanes] = total[HALO_Z:]
            planes[j, GRID_Z - HALO_Z :, lanes] += total[:HALO_Z]
        return carry

    lax.fori_loop(0, fine, gather, 0)
    is_first = piece == 0

    def paired(real, imag, zero, axis):
        half = real.shape[axis] // 2
        first = (slice(None),) * axis + (slice(0, half),)
        second = (slice(None),) * axis + (slice(half, 2 * half),)
        real_c, real_s = real[first], real[second]
        if imag is None:
            none = jnp.zeros_like(real_s)
            real_all = [real_c, jnp.where(zero, real_s, real_c)]
            imag_all = [jnp.where(zero, none, -real_s), jnp.where(zero, none, real_s)]
        else:
            imag_c, imag_s = imag[first], imag[second]
            real_all = [
                real_c + jnp.where(zero, 0.0, imag_s),
                jnp.where(zero, real_s, real_c - imag_s),
            ]
            imag_all = [
                imag_c - jnp.where(zero, 0.0, real_s),
                jnp.where(zero, imag_s, imag_c + real_s),
            ]
        return jnp.concatenate(real_all, axis=axis), jnp.concatenate(imag_all, axis=axis)

    def merged(real, imag, zero, axis):
        half = real.shape[axis] // 2
        first = (slice(None),) * axis + (slice(0, half),)
        second = (slice(None),) * axis + (slice(half, 2 * half),)
        real_a, real_b = real[first], real[second]
        imag_a, imag_b = imag[first], imag[second]
        real = [
            real_a + jnp.where(zero, 0.0, real_b),
            jnp.where(zero, real_b, imag_b - imag_a),
        ]
        imag = [
            imag_a + jnp.where(zero, 0.0, imag_b),
            jnp.where(zero, imag_b, real_a - real_b),
        ]
        return jnp.concatenate(real, axis=axis), jnp.concatenate(imag, axis=axis)

    def to_modes(real, imag, j):
        real = multiply(split(real), fold())
        if imag is not None:
            imag = multiply(split(imag), fold())
        real, imag = paired(real, imag, lane_zero, 1)
        real = multiply(unfold(), split(real))
        imag = multiply(unfold(), split(imag))
        real, imag = paired(real, imag, row_zero, 0)
        green = green_ref[j]
        mode = GRID_Y // 2 if j == fine else piece * fine + j
        share = jnp.where((mode == 0) | (mode == GRID_Y // 2), 0.5, 1.0)
        part = jnp.sum(green * (real * real + imag * imag), axis=0, keepdims=True)
        return green * real, green * imag, share * part

    second_plane = jnp.where(is_first, planes[0, :, GRID_X:], 0.0)
    last_real, last_imag, energy = to_modes(second_plane, None, fine)
    for j in range(fine):
        imag = planes[j, :, GRID_X:]
        if j == 0:
            imag = jnp.where(is_first, 0.0, imag)
        real, imag, part = to_modes(planes[j, :, 0:GRID_X], imag, j)
        energy = energy + part
        if j == 0:
            real, imag = real - last_imag, imag + last_real
        real, imag = merged(real, imag, row_zero, 0)
        real = multiply(fold(), split(real))
        imag = multiply(fold(), split(imag))
        real, imag = merged(real, imag, lane_zero, 1)
        scale = jnp.where(piece * fine + j == 0, 1.0, 2.0)
        for part, lanes in ((real, slice(0, GRID_X)), (imag, slice(GRID_X, 2 * GRID_X))):
            part = multiply(split(part * scale), unfold())
            for k in range(copies):
                moved = pltpu.roll(part, (HALO_X - k * cells_x) % GRID_X, 1)
                grid[k, j, HALO_Z:, lanes] = moved
                grid[k, j, 0:HALO_Z, lanes] = moved[GRID_Z - HALO_Z :]
    energy = jnp.broadcast_to(jnp.sum(energy, axis=1, keepdims=True), (1, 128))

    def collect(at_narrow, buffer):
        row_x, _, row_z, _ = line(at_narrow)
        fill_x(row_x, (None, slopes.at[buffer]))
        value_z = weights_z[at_narrow]
        _, slope_z = splines_z(row_z)
        first = pl.multiple_of(at_narrow * cells_z, HALO_Z)
        lefts = []
        for k in range(copies):
            left = jnp.concatenate(
                [
                    grid[k, c // 2, pl.ds(first, window), c % 2 * GRID_X : (c % 2 + 1) * GRID_X]
                    for c in range(channels)
                ],
                axis=0,
            )
            lefts.append(split(left))
        wave = waves[at_narrow]
        wave_slope = wave_slopes[at_narrow]
        for at_wide in range(wide_count):
            lanes = slice(at_wide * pair, (at_wide + 1) * pair)
            start = at_wide // copies * 128
            high = lefts[at_wide % copies][0][:, start : start + 128]
            low = lefts[at_wide % copies][1][:, start : start + 128]
            twice = jnp.concatenate([high, high], axis=1)

            def across(right):
                return lax.dot_general(
                    twice, right, NN, preferred_element_type=jnp.float32
                ) + lax.dot_general(low, right[0:128], NN, preferred_element_type=jnp.float32)

            value = across(weights[at_narrow, :, lanes])
            slope = across(slopes[buffer, :, lanes])
            plain = jnp.zeros((window, pair), jnp.float32)
            along_x = plain
            along_y = plain
            for c in range(channels):
                block = slice(c * window, (c + 1) * window)
                plain = plain + value[block] * wave[c : c + 1, lanes]
                along_x = along_x + slope[block] * wave[c : c + 1, lanes]
                along_y = along_y + value[block] * wave_slope[c : c + 1, lanes]
            near = value_z[:, lanes]
            near_slope = slope_z[:, lanes]
            results = [
                jnp.sum(near * plain, axis=0, keepdims=True),
                -jnp.sum(near * along_x, axis=0, keepdims=True),
                -jnp.sum(near * along_y, axis=0, keepdims=True),
                -jnp.sum(near_slope * plain, axis=0, keepdims=True),
            ]
            for k, row in enumerate(results):
                out_ref[at_wide, at_narrow, :, k * pair : (k + 1) * pair] = row
            out_ref[at_wide, at_narrow, :, 4 * pair :] = energy

    in_pairs(collect)


def finish_kernel(arrived, species, atom_ref, centroid_ref, energy_ref):
    atoms = species.shape[1]
    total = arrived[0]
    for k in range(1, arrived.shape[0]):
        total = total + arrived[k]
    oxygen = 1.0 - species[...].astype(jnp.float32)
    for k in range(4):
        atom_ref[k] = total[:, 2 * k * atoms : (2 * k + 1) * atoms]
        centroid_ref[k] = total[:, (2 * k + 1) * atoms : (2 * k + 2) * atoms] * oxygen
    energy_ref[...] = total[:, 8 * atoms :] * (1.0 / (atoms * arrived.shape[0]))


def mode_factors(length, order):
    wrapped = np.where(2 * order >= length, order - length, order)
    square = (wrapped / length) ** 2
    ratio = (4.0 + 2.0 * np.cos(2.0 * math.pi * order / length)) / 6.0
    return np.stack([np.exp(-(math.pi**2) * square / ewald_beta**2) / ratio**2, square])


def folded_order(length):
    half = length // 2
    counter = np.arange(half)
    return np.concatenate([counter, np.where(counter == 0, half, length - counter)])


def fold_table(length):
    half = length // 2
    turns = np.outer(np.arange(length), np.arange(half)) % length * (2.0 * math.pi / length)
    sines = np.sin(turns)
    sines[:, 0] = 1.0 - 2.0 * (np.arange(length) % 2)
    return np.concatenate([np.cos(turns), sines], axis=1)


def halves(table):
    high = table.astype(jnp.bfloat16)
    low = (table - high.astype(np.float64)).astype(jnp.bfloat16)
    return high, low


def vmem(count):
    return [pl.BlockSpec(memory_space=pltpu.VMEM)] * count


def hbm(count):
    return [pl.BlockSpec(memory_space=pltpu.HBM)] * count


def shaped(shape, dtype=jnp.float32):
    return jax.ShapeDtypeStruct(shape, dtype)


def limits(mebibytes):
    return pltpu.CompilerParams(vmem_limit_bytes=mebibytes * 1024 * 1024)


def local(
    positions,
    species,
    neighbours,
    embed_one_w,
    embed_one_b,
    embed_two_w,
    embed_two_b,
    embed_three_w,
    embed_three_b,
    fit_one_w,
    fit_one_b,
    fit_two_w,
    fit_two_b,
    fit_three_w,
    fit_three_b,
    fit_out_w,
):
    axes = ("wide", "narrow")
    wide_count = lax.axis_size("wide")
    narrow_count = lax.axis_size("narrow")
    pieces = wide_count * narrow_count
    atoms = positions.shape[4]
    listed = neighbours.shape[4]
    fine = GRID_Y // 2 // pieces
    width_three = embed_three_w.shape[1]
    entries, hidden = fit_one_w.shape
    kinds = species.reshape(1, atoms)

    packed = pl.pallas_call(
        pack_kernel,
        out_shape=shaped((pieces, 4, atoms)),
        in_specs=vmem(2),
        out_specs=vmem(1)[0],
        name="pack",
    )(positions.reshape(3, 1, atoms), kinds)
    table = lax.all_to_all(packed, axes, 0, 0, tiled=True)
    table = table.reshape(wide_count, narrow_count, 4, atoms)

    tall = 4 * ROW_PAD
    bf16 = jnp.bfloat16
    wave_rows = -(-2 * fine // 8) * 8
    angle = np.arange(GRID_Y) * (2.0 * math.pi / GRID_Y)
    constants = np.concatenate(
        [
            np.stack([np.cos(angle), np.sin(angle)]),
            mode_factors(GRID_Y, np.arange(GRID_Y)),
            mode_factors(GRID_X, folded_order(GRID_X)),
            mode_factors(GRID_Z, folded_order(GRID_Z)),
        ]
    )
    constants[2] *= coulomb / (math.pi * GRID_X * GRID_Y * GRID_Z)
    arguments = (
        neighbours.reshape(atoms, listed),
        embed_one_w,
        embed_one_b,
        embed_two_w,
        embed_two_b[None],
        embed_three_w,
        embed_three_b[None],
        fit_one_w.T,
        fit_one_b[None],
        fit_two_w,
        fit_two_b[None],
        fit_three_w,
        fit_three_b[None],
        jnp.asarray(constants, jnp.float32),
    )
    held = [arguments[k] for k in (0, 1, 2, 3, 4, 5, 6, 8, 10, 12, 13, 9, 11, 7)]
    prepared = pl.pallas_call(
        prepare_kernel,
        out_shape=(
            shaped((listed, atoms), jnp.int32),
            shaped((256, 16)),
            shaped((2 * ROW_PAD, 3 * ROW_PAD), bf16),
            shaped((tall, 6 * ROW_PAD), bf16),
            shaped((hidden, entries), bf16),
            shaped((hidden, entries), bf16),
        )
        + (shaped((hidden, hidden), bf16),) * 4
        + (shaped((wave_rows, GRID_Y)), shaped((fine + 1, GRID_Z, GRID_X))),
        in_specs=hbm(len(arguments)),
        out_specs=tuple(vmem(12)),
        scratch_shapes=[
            pltpu.VMEM((16, 256), jnp.float32),
            pltpu.VMEM((256, 256), jnp.float32),
            pltpu.SemaphoreType.DMA((len(held),)),
        ]
        + [pltpu.VMEM(array.shape, array.dtype) for array in held],
        compiler_params=limits(62),
        cost_estimate=pl.CostEstimate(
            flops=1000000, bytes_accessed=8 * entries * hidden, transcendentals=0
        ),
        name="prepare",
    )(*arguments)
    phase, green = prepared[10:]
    fitted = (*prepared[4:10], fit_out_w.T)
    dipole, shifts = pl.pallas_call(
        centroid_kernel,
        out_shape=(shaped((3, 1, atoms)), shaped((pieces, 4, atoms))),
        in_specs=vmem(5) + hbm(7),
        out_specs=tuple(vmem(2)),
        scratch_shapes=[
            pltpu.VMEM((4, tall, atoms), jnp.float32),
            pltpu.VMEM((width_three * AXIS_COLUMNS, atoms), jnp.float32),
            pltpu.SemaphoreType.DMA((len(fitted),)),
        ]
        + [pltpu.VMEM(array.shape, array.dtype) for array in fitted],
        compiler_params=limits(62),
        name="centroids",
    )(table, *prepared[:4], *fitted)
    shifts = lax.all_to_all(shifts, axes, 0, 0, tiled=True)
    shifts = shifts.reshape(wide_count, narrow_count, 4, atoms)

    cells_x = GRID_X // wide_count
    copies = 128 // cells_x
    length = wide_count * 2 * atoms
    out_width = 8 * atoms + 128
    partial = pl.pallas_call(
        mesh_kernel,
        out_shape=shaped((wide_count, narrow_count, 1, out_width)),
        in_specs=vmem(8),
        out_specs=vmem(1)[0],
        scratch_shapes=[
            pltpu.VMEM((copies, fine, HALO_Z + GRID_Z, 2 * GRID_X), jnp.float32),
            pltpu.VMEM((fine + 1, GRID_Z, 2 * GRID_X), jnp.float32),
        ]
        + [pltpu.VMEM((narrow_count, 256, length), bf16), pltpu.VMEM((2, 256, length), bf16)]
        + [pltpu.VMEM((narrow_count, GRID_Z // narrow_count + HALO_Z, length), jnp.float32)]
        + [pltpu.VMEM((narrow_count, wave_rows, length), jnp.float32)] * 2,
        compiler_params=limits(48),
        name="mesh",
    )(
        table,
        shifts,
        phase,
        green,
        *[jnp.asarray(half) for half in halves(fold_table(GRID_X))],
        *[jnp.asarray(half) for half in halves(fold_table(GRID_X).T)],
    )
    arrived = lax.all_to_all(partial.reshape(pieces, 1, out_width), axes, 0, 0, tiled=True)
    atom_field, centroid_field, energy = pl.pallas_call(
        finish_kernel,
        out_shape=(shaped((4, 1, atoms)), shaped((4, 1, atoms)), shaped((1, 128))),
        in_specs=vmem(2),
        out_specs=tuple(vmem(3)),
        name="finish",
    )(arrived, kinds)
    atom_field = atom_field.reshape(4, 1, 1, 1, atoms)
    centroid_field = centroid_field.reshape(4, 1, 1, 1, atoms)
    return (dipole.reshape(3, 1, 1, 1, atoms), atom_field, centroid_field, energy[0, 0])


def solution(mesh):
    column = P(None, "wide", "narrow", None, None)
    in_specs = (column, P("wide", "narrow", None, None), P("wide", "narrow", None, None, None))
    in_specs = in_specs + (P(),) * 13
    out_specs = (column, column, column, P())
    return jax.shard_map(local, mesh=mesh, in_specs=in_specs, out_specs=out_specs, check_vma=False)
```

```python
import math

import jax
import jax.numpy as jnp
import numpy as np
from jax import lax
from jax.experimental import pallas as pl
from jax.experimental.pallas import tpu as pltpu
from jax.sharding import PartitionSpec as P

GRID_X = 256
GRID_Y = 256
GRID_Z = 256
AXIS_COLUMNS = 16

radius_scale = 24.0
wannier_reach = 0.5
ewald_beta = 0.9
coulomb = 0.25

ROW_PAD = 32
SLOT_CHUNK = 16
HALO_X = 16
HALO_Z = 8

NN = (((1,), (0,)), ((), ()))
NT = (((1,), (1,)), ((), ()))


def split(value):
    high = value.astype(jnp.bfloat16)
    low = (value - high.astype(jnp.float32)).astype(jnp.bfloat16)
    return high, low


def multiply(left, right, dims=NN):
    def one(a, b):
        return lax.dot_general(a, b, dims, preferred_element_type=jnp.float32)

    return one(left[0], right[0]) + (one(left[1], right[0]) + one(left[0], right[1]))


def spline_pair(offset):
    centred = offset - 2.0
    away = jnp.abs(centred)
    outer = jnp.maximum(2.0 - away, 0.0)
    inner = jnp.maximum(1.0 - away, 0.0)
    outer_square = outer * outer
    inner_square = inner * inner
    value = (outer_square * outer - 4.0 * (inner_square * inner)) * (1.0 / 6.0)
    slope = jnp.where(centred < 0.0, 0.5, -0.5) * (outer_square - 4.0 * inner_square)
    return value, slope


def lookup(row_table, spot):
    found = None
    for part in range(row_table.shape[1] // 128):
        inside = spot // 128 == part
        here = jnp.take_along_axis(
            jnp.broadcast_to(row_table[:, part * 128 : (part + 1) * 128], spot.shape),
            lax.rem(spot, 128),
            axis=1,
            mode="promise_in_bounds",
        )
        found = here if found is None else jnp.where(inside, here, found)
    return found


def pack_kernel(positions, species, out_ref):
    rows = [positions[component] for component in range(3)]
    rows.append(species[...].astype(jnp.float32))
    rows = jnp.concatenate(rows, axis=0)
    for target in range(out_ref.shape[0]):
        out_ref[target] = rows


def prepare_kernel(
    neighbours,
    embed_one_w,
    embed_one_b,
    embed_two_w,
    embed_two_b,
    embed_three_w,
    embed_three_b,
    fit_one_w,
    fit_one_b,
    fit_two_w,
    fit_two_b,
    fit_three_w,
    fit_three_b,
    constants,
    codes_ref,
    columns_ref,
    second_ref,
    third_ref,
    one_high_ref,
    one_low_ref,
    two_high_ref,
    two_low_ref,
    three_high_ref,
    three_low_ref,
    phase_ref,
    green_ref,
    rows,
    square,
    arrivals,
    *held,
):
    sources = (
        neighbours,
        embed_one_w,
        embed_one_b,
        embed_two_w,
        embed_two_b,
        embed_three_w,
        embed_three_b,
        fit_one_b,
        fit_two_b,
        fit_three_b,
        constants,
        fit_two_w,
        fit_three_w,
        fit_one_w,
    )
    copies = [
        pltpu.make_async_copy(source, target, arrivals.at[k])
        for k, (source, target) in enumerate(zip(sources, held))
    ]
    for copy in copies:
        copy.start()
    (
        neighbours,
        embed_one_w,
        embed_one_b,
        embed_two_w,
        embed_two_b,
        embed_three_w,
        embed_three_b,
        fit_one_b,
        fit_two_b,
        fit_three_b,
        constants,
        fit_two_w,
        fit_three_w,
        fit_one_w,
    ) = held
    for copy in copies[:11]:
        copy.wait()
    pieces = lax.axis_size("wide") * lax.axis_size("narrow")
    piece = lax.axis_index("wide") * lax.axis_size("narrow") + lax.axis_index("narrow")
    width_one = embed_one_w.shape[1]
    hidden = fit_two_w.shape[0]
    codes_ref[...] = jnp.transpose(neighbours[...].astype(jnp.float32)).astype(jnp.int32)
    rows[...] = jnp.zeros_like(rows)
    for kind in range(2):
        rows[kind : kind + 1, 0:width_one] = embed_one_w[kind : kind + 1, :]
        rows[2 + kind : 3 + kind, 0:width_one] = embed_one_b[kind : kind + 1, :]
        rows[2 + kind : 3 + kind, width_one : width_one + 1] = jnp.full((1, 1), 40.0, jnp.float32)
    for row, source in ((4, fit_one_b), (5, fit_two_b), (6, fit_three_b)):
        rows[row : row + 1, 0:hidden] = source[...]
    columns_ref[...] = jnp.transpose(rows[...])

    square[...] = jnp.zeros_like(square)
    for k in range(2):
        square[0:width_one, k * ROW_PAD : k * ROW_PAD + width_one] = embed_two_w[
            :, k * width_one : (k + 1) * width_one
        ]
        square[
            width_one : width_one + 1, k * ROW_PAD : k * ROW_PAD + width_one
        ] = embed_two_b[:, k * width_one : (k + 1) * width_one]
    high, low = split(jnp.transpose(square[0:128, 0:128])[0 : 2 * ROW_PAD, 0:ROW_PAD])
    second_ref[...] = jnp.concatenate([high, high, low], axis=1)
    square[0:128, 0:128] = jnp.zeros((128, 128), jnp.float32)
    for g in range(2):
        for k in range(4):
            square[
                g * ROW_PAD : g * ROW_PAD + width_one, k * ROW_PAD : k * ROW_PAD + width_one
            ] = embed_three_w[
                g * width_one : (g + 1) * width_one, k * width_one : (k + 1) * width_one
            ]
    for k in range(4):
        square[
            width_one : width_one + 1, k * ROW_PAD : k * ROW_PAD + width_one
        ] = embed_three_b[:, k * width_one : (k + 1) * width_one]
    high, low = split(jnp.transpose(square[0:128, 0:128])[:, 0 : 2 * ROW_PAD])
    third_ref[...] = jnp.concatenate([high, high, low], axis=1)
    for copy in copies[11:13]:
        copy.wait()
    for source, high_ref, low_ref in (
        (fit_two_w, two_high_ref, two_low_ref),
        (fit_three_w, three_high_ref, three_low_ref),
    ):
        square[0:hidden, 0:hidden] = source[...]
        high_ref[...], low_ref[...] = split(jnp.transpose(square[...])[0:hidden, 0:hidden])

    fine = GRID_Y // 2 // pieces
    shape = (phase_ref.shape[0], 128)
    row = lax.broadcasted_iota(jnp.int32, shape, 0)
    mode = piece * fine + row // 2
    for part in range(GRID_Y // 128):
        cell = lax.broadcasted_iota(jnp.int32, shape, 1) + part * 128
        spot = lax.rem(mode * cell, GRID_Y)
        cosine = lookup(constants[0:1, :], spot)
        sine = lookup(constants[1:2, :], spot)
        alternate = (1 - 2 * lax.rem(cell, 2)).astype(jnp.float32)
        odd = jnp.where(mode == 0, alternate, -sine)
        value = jnp.where(lax.rem(row, 2) == 0, cosine, odd)
        phase_ref[:, part * 128 : (part + 1) * 128] = jnp.where(row < 2 * fine, value, 0.0)

    column = jnp.transpose(constants[...])
    lane = lax.broadcasted_iota(jnp.int32, (1, GRID_Y), 1)
    for j in range(fine + 1):
        here = lane == (GRID_Y // 2 if j == fine else piece * fine + j)
        factor = jnp.sum(jnp.where(here, constants[2:3, :], 0.0), axis=1, keepdims=True)
        part = jnp.sum(jnp.where(here, constants[3:4, :], 0.0), axis=1, keepdims=True)
        wave = (part + constants[5:6, :]) + column[:, 7:8]
        top = (factor * constants[4:5, :]) * column[:, 6:7]
        green_ref[j] = jnp.where(wave == 0.0, 0.0, top / jnp.where(wave == 0.0, 1.0, wave))

    copies[13].wait()
    one_high_ref[...], one_low_ref[...] = split(fit_one_w[...])


def centroid_kernel(
    table,
    codes,
    columns,
    second,
    third,
    one_high,
    one_low,
    two_high,
    two_low,
    three_high,
    three_low,
    fit_out_w,
    dipole_ref,
    shift_ref,
    matrix,
    descriptor,
    arrivals,
    *held,
):
    sources = (one_high, one_low, two_high, two_low, three_high, three_low, fit_out_w)
    copies = [
        pltpu.make_async_copy(source, target, arrivals.at[k])
        for k, (source, target) in enumerate(zip(sources, held))
    ]
    for copy in copies:
        copy.start()
    one_high, one_low, two_high, two_low, three_high, three_low, fit_out_w = held
    wide_count, narrow_count, _, atoms = table.shape
    listed = codes.shape[0]
    width_three = fit_out_w.shape[0]
    width_one = width_three // 4
    hidden_width = two_high.shape[0]
    cells = (GRID_X // wide_count, GRID_Y, GRID_Z // narrow_count)
    at_wide = lax.axis_index("wide")
    at_narrow = lax.axis_index("narrow")
    own = table[at_wide, at_narrow]
    nearby = []
    for step in range(9):
        wide_at = lax.rem(at_wide + (step // 3 - 1) + wide_count, wide_count)
        narrow_at = lax.rem(at_narrow + (step % 3 - 1) + narrow_count, narrow_count)
        nearby.append(table[wide_at, narrow_at])

    second_all = second[...]
    third_all = third[...]
    weight_oxygen = jnp.broadcast_to(columns[0:ROW_PAD, 0:1], (ROW_PAD, atoms))
    weight_hydrogen = jnp.broadcast_to(columns[0:ROW_PAD, 1:2], (ROW_PAD, atoms))
    bias_oxygen = jnp.broadcast_to(columns[0:ROW_PAD, 2:3], (ROW_PAD, atoms))
    bias_hydrogen = jnp.broadcast_to(columns[0:ROW_PAD, 3:4], (ROW_PAD, atoms))
    matrix[...] = jnp.zeros_like(matrix)

    def chunk(first):
        code = codes[pl.ds(first, SLOT_CHUNK), :]
        offset = code // atoms
        slot = code - offset * atoms
        step_x = jnp.where(offset >= 9, 1, 0) + jnp.where(offset >= 18, 1, 0)
        rest = offset - 9 * step_x
        step_z = jnp.where(rest >= 3, 1, 0) + jnp.where(rest >= 6, 1, 0)
        step_y = rest - 3 * step_z
        brick = step_x * 3 + step_z
        found = []
        for component in range(4):
            picked = jnp.zeros((SLOT_CHUNK, atoms), jnp.float32)
            for step in range(9):
                row = jnp.broadcast_to(
                    nearby[step][component : component + 1], (SLOT_CHUNK, atoms)
                )
                here = jnp.take_along_axis(row, slot, axis=1, mode="promise_in_bounds")
                picked = jnp.where(brick == step, here, picked)
            found.append(picked)
        scaled = []
        for component, step in enumerate((step_x, step_y, step_z)):
            extent = float(cells[component])
            relative = (step - 1).astype(jnp.float32) * extent + (
                found[component] - own[component : component + 1]
            ) * extent
            scaled.append(relative * (1.0 / radius_scale))
        smooth = 1.0 / (
            1.0 + (scaled[0] * scaled[0] + scaled[1] * scaled[1] + scaled[2] * scaled[2])
        )
        radial = [smooth] + [smooth * part for part in scaled]
        hydrogen = found[3] > 0.5
        first_layers = []
        for k in range(SLOT_CHUNK):
            row = smooth[k : k + 1]
            kind = hydrogen[k : k + 1]
            weight = jnp.where(kind, weight_hydrogen, weight_oxygen)
            bias = jnp.where(kind, bias_hydrogen, bias_oxygen)
            first_layers.append(jnp.tanh(weight * row + bias))
        layer_one = jnp.concatenate(first_layers, axis=1)
        high, low = split(layer_one)
        layer_two = lax.dot_general(
            second_all,
            jnp.concatenate([high, low, high], axis=0),
            NN,
            preferred_element_type=jnp.float32,
        )
        layer_two = jnp.tanh(layer_two) + jnp.concatenate(
            [layer_one, layer_one], axis=0
        )
        high, low = split(layer_two)
        layer_three = lax.dot_general(
            third_all,
            jnp.concatenate([high, low, high], axis=0),
            NN,
            preferred_element_type=jnp.float32,
        )
        layer_three = jnp.tanh(layer_three) + jnp.concatenate(
            [layer_two, layer_two], axis=0
        )
        for part in range(4):
            total = matrix[part]
            for k in range(SLOT_CHUNK):
                total = total + layer_three[:, k * atoms : (k + 1) * atoms] * radial[part][k : k + 1]
            matrix[part] = total

    def two_chunks(index, carry):
        first = pl.multiple_of(index * (2 * SLOT_CHUNK), 2 * SLOT_CHUNK)
        chunk(first)
        chunk(pl.multiple_of(first + SLOT_CHUNK, SLOT_CHUNK))
        return carry

    lax.fori_loop(0, listed // (2 * SLOT_CHUNK), two_chunks, 0)

    parts = []
    for part in range(4):
        padded = matrix[part] * (1.0 / listed)
        parts.append(
            jnp.concatenate(
                [padded[k * ROW_PAD : k * ROW_PAD + width_one] for k in range(4)], axis=0
            )
        )
    leading = [part[0:AXIS_COLUMNS] for part in parts]
    for row in range(width_three):
        total = parts[0][row : row + 1] * leading[0]
        for part in range(1, 4):
            total = total + parts[part][row : row + 1] * leading[part]
        descriptor[row * AXIS_COLUMNS : (row + 1) * AXIS_COLUMNS, :] = total
    for copy in copies:
        copy.wait()

    def layer(high_ref, low_ref, given, column):
        weights = (high_ref[...], low_ref[...])
        return jnp.tanh(multiply(weights, split(given)) + columns[0:hidden_width, column : column + 1])

    hidden = layer(one_high, one_low, descriptor[...], 4)
    hidden = hidden + layer(two_high, two_low, hidden, 5)
    hidden = hidden + layer(three_high, three_low, hidden, 6)
    coeffs = multiply(split(fit_out_w[...]), split(hidden))
    vector = jnp.concatenate(
        [jnp.sum(coeffs * parts[1 + c], axis=0, keepdims=True) for c in range(3)], axis=0
    )
    oxygen = 1.0 - own[3:4]
    for c in range(3):
        dipole_ref[c] = vector[c : c + 1] * oxygen
    moved = wannier_reach * jnp.tanh(vector)
    moved = jnp.concatenate([moved, jnp.zeros((1, atoms), jnp.float32)], axis=0)
    for target in range(shift_ref.shape[0]):
        shift_ref[target] = moved


def splines_z(row, window):
    counter = lax.broadcasted_iota(jnp.int32, (window, 1), 0).astype(jnp.float32)
    return spline_pair(row - (counter - float(HALO_Z)))


def splines_x(row, reach, value_ref, slope_ref):
    counter = lax.broadcasted_iota(jnp.int32, (reach, 1), 0).astype(jnp.float32)
    both = spline_pair(row - (counter - float(HALO_X)))
    rest = jnp.zeros((128 - reach, row.shape[1]), jnp.bfloat16)
    for values, ref in zip(both, (value_ref, slope_ref)):
        if ref is not None:
            high, low = split(values)
            ref[0:reach, :] = high
            ref[reach:128, :] = rest
            ref[128 : 128 + reach, :] = low
            ref[128 + reach : 256, :] = rest


def in_pairs(count, step):
    def both(index, carry):
        step(2 * index, 0)
        step(2 * index + 1, 1)
        return carry

    lax.fori_loop(0, count // 2, both, 0)


def site_rows(table, shifts, at_narrow):
    wide_count, narrow_count, _, _ = table.shape
    extents = (GRID_X // wide_count, GRID_Y, GRID_Z // narrow_count)
    rows = [[], [], [], []]
    for at_wide in range(wide_count):
        atom = table[at_wide, at_narrow]
        for component, extent in enumerate(extents):
            row = atom[component : component + 1] * float(extent)
            if shifts is not None:
                row = row + shifts[at_wide, at_narrow, component : component + 1, :]
            rows[component].append(row)
        hydrogen = atom[3:4]
        oxygen = 1.0 - hydrogen
        rows[3].append(6.0 * oxygen + hydrogen if shifts is None else -8.0 * oxygen)
    return [jnp.concatenate(row, axis=1) for row in rows]


def spread_sites(table, shifts, phase, grid, weights, weights_z, waves, wave_slopes):
    wide_count, narrow_count, _, atoms = table.shape
    cells_x = GRID_X // wide_count
    cells_z = GRID_Z // narrow_count
    window = cells_z + HALO_Z
    copies, fine = grid.shape[:2]
    rows = phase.shape[0]
    grid[:, :, 0:HALO_Z, :] = jnp.zeros((copies, fine, HALO_Z, 2 * GRID_X), jnp.float32)

    def spread(at_narrow, _):
        row_x, row_y, row_z, charge = site_rows(table, shifts, at_narrow)
        lower = jnp.floor(row_y)
        back = lax.broadcasted_iota(jnp.int32, (8, 1), 0)
        value_y, slope_y = spline_pair((row_y - lower) + back.astype(jnp.float32))
        cell = lax.rem(lower.astype(jnp.int32) - back + GRID_Y, GRID_Y)
        wave_blocks = []
        slope_blocks = []
        for at_wide in range(wide_count):
            lanes = slice(at_wide * atoms, (at_wide + 1) * atoms)
            wave = jnp.zeros((rows, atoms), jnp.float32)
            wave_slope = jnp.zeros((rows, atoms), jnp.float32)
            for k in range(4):
                spot = jnp.broadcast_to(cell[k : k + 1, lanes], (rows, atoms))
                found = lookup(phase[...], spot)
                wave = wave + value_y[k : k + 1, lanes] * found
                wave_slope = wave_slope + slope_y[k : k + 1, lanes] * found
            wave_blocks.append(wave)
            slope_blocks.append(wave_slope)
        wave = jnp.concatenate(wave_blocks, axis=1)
        waves[at_narrow] = wave
        wave_slopes[at_narrow] = jnp.concatenate(slope_blocks, axis=1)
        splines_x(row_x, cells_x + HALO_X, weights.at[at_narrow], None)
        value_z, _ = splines_z(row_z, window)
        weights_z[at_narrow] = value_z
        charged = wave * charge
        first = pl.multiple_of(at_narrow * cells_z, HALO_Z)
        for at_wide in range(wide_count):
            lanes = slice(at_wide * atoms, (at_wide + 1) * atoms)
            near = value_z[:, lanes]
            left = jnp.concatenate(
                [near * charged[c : c + 1, lanes] for c in range(2 * fine)], axis=0
            )
            across = weights[at_narrow, :, lanes]
            total = lax.dot_general(
                jnp.concatenate(split(left), axis=1),
                jnp.concatenate([across, across], axis=1),
                NT,
                preferred_element_type=jnp.float32,
            )
            total = total[:, 0:128] + total[:, 128:256]
            start = at_wide // copies * 128
            for c in range(2 * fine):
                spot = slice(c % 2 * GRID_X + start, c % 2 * GRID_X + start + 128)
                k = at_wide % copies
                part = total[c * window : (c + 1) * window]
                grid[k, c // 2, pl.ds(first, HALO_Z), spot] += part[:HALO_Z]
                grid[k, c // 2, pl.ds(first + HALO_Z, cells_z), spot] = part[HALO_Z:]

    in_pairs(narrow_count, spread)


def joined(grid, j, lanes, cells_x):
    total = None
    for k in range(grid.shape[0]):
        moved = pltpu.roll(grid[k, j, :, lanes], (k * cells_x - HALO_X) % GRID_X, 1)
        total = moved if total is None else total + moved
    plane = total[HALO_Z:]
    rest = plane[: GRID_Z - HALO_Z]
    return jnp.concatenate([rest, plane[GRID_Z - HALO_Z :] + total[:HALO_Z]], axis=0)


HALVES = (slice(0, GRID_X), slice(GRID_X, 2 * GRID_X))


def atoms_kernel(table, phase, planes, weights, weights_z, waves, wave_slopes, grid):
    cells_x = GRID_X // table.shape[0]
    spread_sites(table, None, phase, grid, weights, weights_z, waves, wave_slopes)
    for j in range(grid.shape[1]):
        for lanes in HALVES:
            planes[j, :, lanes] = joined(grid, j, lanes, cells_x)


def mesh_kernel(
    table,
    shifts,
    phase,
    green_ref,
    fold_high,
    fold_low,
    unfold_high,
    unfold_low,
    planes,
    atom_weights,
    atom_weights_z,
    atom_waves,
    atom_wave_slopes,
    out_ref,
    grid,
    weights,
    weights_z,
    waves,
    wave_slopes,
    slopes,
):
    wide_count, narrow_count, _, atoms = table.shape
    cells_x = GRID_X // wide_count
    cells_z = GRID_Z // narrow_count
    window = cells_z + HALO_Z
    copies, fine = grid.shape[:2]
    channels = 2 * fine
    piece = lax.axis_index("wide") * narrow_count + lax.axis_index("narrow")
    lane_zero = lax.broadcasted_iota(jnp.int32, (1, GRID_X // 2), 1) == 0
    row_zero = lax.broadcasted_iota(jnp.int32, (GRID_Z // 2, 1), 0) == 0

    def fold():
        return (fold_high[...], fold_low[...])

    def unfold():
        return (unfold_high[...], unfold_low[...])

    spread_sites(table, shifts, phase, grid, weights, weights_z, waves, wave_slopes)

    def whole(j):
        return [planes[j, :, lanes] + joined(grid, j, lanes, cells_x) for lanes in HALVES]

    is_first = piece == 0

    def paired(real, imag, zero, axis):
        half = real.shape[axis] // 2
        first = (slice(None),) * axis + (slice(0, half),)
        second = (slice(None),) * axis + (slice(half, 2 * half),)
        real_c, real_s = real[first], real[second]
        if imag is None:
            none = jnp.zeros_like(real_s)
            real_all = [real_c, jnp.where(zero, real_s, real_c)]
            imag_all = [jnp.where(zero, none, -real_s), jnp.where(zero, none, real_s)]
        else:
            imag_c, imag_s = imag[first], imag[second]
            real_all = [
                real_c + jnp.where(zero, 0.0, imag_s),
                jnp.where(zero, real_s, real_c - imag_s),
            ]
            imag_all = [
                imag_c - jnp.where(zero, 0.0, real_s),
                jnp.where(zero, imag_s, imag_c + real_s),
            ]
        return jnp.concatenate(real_all, axis=axis), jnp.concatenate(imag_all, axis=axis)

    def merged(real, imag, zero, axis):
        half = real.shape[axis] // 2
        first = (slice(None),) * axis + (slice(0, half),)
        second = (slice(None),) * axis + (slice(half, 2 * half),)
        real_a, real_b = real[first], real[second]
        imag_a, imag_b = imag[first], imag[second]
        real = [
            real_a + jnp.where(zero, 0.0, real_b),
            jnp.where(zero, real_b, imag_b - imag_a),
        ]
        imag = [
            imag_a + jnp.where(zero, 0.0, imag_b),
            jnp.where(zero, imag_b, real_a - real_b),
        ]
        return jnp.concatenate(real, axis=axis), jnp.concatenate(imag, axis=axis)

    def to_modes(real, imag, j):
        real = multiply(split(real), fold())
        if imag is not None:
            imag = multiply(split(imag), fold())
        real, imag = paired(real, imag, lane_zero, 1)
        real = multiply(unfold(), split(real))
        imag = multiply(unfold(), split(imag))
        real, imag = paired(real, imag, row_zero, 0)
        green = green_ref[j]
        mode = GRID_Y // 2 if j == fine else piece * fine + j
        share = jnp.where((mode == 0) | (mode == GRID_Y // 2), 0.5, 1.0)
        part = jnp.sum(green * (real * real + imag * imag), axis=0, keepdims=True)
        return green * real, green * imag, share * part

    first_real, first_imag = whole(0)
    last_real, last_imag, energy = to_modes(jnp.where(is_first, first_imag, 0.0), None, fine)
    for j in range(fine):
        if j == 0:
            real, imag = first_real, jnp.where(is_first, 0.0, first_imag)
        else:
            real, imag = whole(j)
        real, imag, part = to_modes(real, imag, j)
        energy = energy + part
        if j == 0:
            real, imag = real - last_imag, imag + last_real
        real, imag = merged(real, imag, row_zero, 0)
        real = multiply(fold(), split(real))
        imag = multiply(fold(), split(imag))
        real, imag = merged(real, imag, lane_zero, 1)
        scale = jnp.where(piece * fine + j == 0, 1.0, 2.0)
        for part, lanes in zip((real, imag), HALVES):
            part = multiply(split(part * scale), unfold())
            for k in range(copies):
                moved = pltpu.roll(part, (HALO_X - k * cells_x) % GRID_X, 1)
                grid[k, j, HALO_Z:, lanes] = moved
                grid[k, j, 0:HALO_Z, lanes] = moved[GRID_Z - HALO_Z :]
    energy = jnp.broadcast_to(jnp.sum(energy, axis=1, keepdims=True), (1, 128))

    def collect(at_narrow, buffer):
        kinds = (
            (None, atom_weights, atom_weights_z, atom_waves, atom_wave_slopes),
            (shifts, weights, weights_z, waves, wave_slopes),
        )
        slopes_z = []
        for kind, given in enumerate(kinds):
            row_x, _, row_z, _ = site_rows(table, given[0], at_narrow)
            splines_x(row_x, cells_x + HALO_X, None, slopes.at[buffer, kind])
            slopes_z.append(splines_z(row_z, window)[1])
        first = pl.multiple_of(at_narrow * cells_z, HALO_Z)
        lefts = []
        for k in range(copies):
            left = jnp.concatenate(
                [
                    grid[k, c // 2, pl.ds(first, window), HALVES[c % 2]]
                    for c in range(channels)
                ],
                axis=0,
            )
            lefts.append(split(left))
        for at_wide in range(wide_count):
            lanes = slice(at_wide * atoms, (at_wide + 1) * atoms)
            start = at_wide // copies * 128
            high = lefts[at_wide % copies][0][:, start : start + 128]
            low = lefts[at_wide % copies][1][:, start : start + 128]
            twice = jnp.concatenate([high, high], axis=1)

            def across(right):
                return lax.dot_general(
                    twice, right, NN, preferred_element_type=jnp.float32
                ) + lax.dot_general(low, right[0:128], NN, preferred_element_type=jnp.float32)

            def both(index):
                return jnp.concatenate([given[index][at_narrow, :, lanes] for given in kinds], axis=1)

            value = across(both(1))
            slope = across(
                jnp.concatenate([slopes[buffer, kind, :, lanes] for kind in range(2)], axis=1)
            )
            near = both(2)
            near_slope = jnp.concatenate([row[:, lanes] for row in slopes_z], axis=1)
            wave = both(3)
            wave_slope = both(4)
            plain = jnp.zeros((window, 2 * atoms), jnp.float32)
            along_x = plain
            along_y = plain
            for c in range(channels):
                block = slice(c * window, (c + 1) * window)
                plain = plain + value[block] * wave[c : c + 1]
                along_x = along_x + slope[block] * wave[c : c + 1]
                along_y = along_y + value[block] * wave_slope[c : c + 1]
            results = [
                jnp.sum(near * plain, axis=0, keepdims=True),
                -jnp.sum(near * along_x, axis=0, keepdims=True),
                -jnp.sum(near * along_y, axis=0, keepdims=True),
                -jnp.sum(near_slope * plain, axis=0, keepdims=True),
            ]
            for k, row in enumerate(results):
                out_ref[at_wide, at_narrow, :, 2 * k * atoms : 2 * (k + 1) * atoms] = row
            out_ref[at_wide, at_narrow, :, 8 * atoms :] = energy

    in_pairs(narrow_count, collect)


def finish_kernel(arrived, species, atom_ref, centroid_ref, energy_ref):
    atoms = species.shape[1]
    total = arrived[0]
    for k in range(1, arrived.shape[0]):
        total = total + arrived[k]
    oxygen = 1.0 - species[...].astype(jnp.float32)
    for k in range(4):
        atom_ref[k] = total[:, 2 * k * atoms : (2 * k + 1) * atoms]
        centroid_ref[k] = total[:, (2 * k + 1) * atoms : (2 * k + 2) * atoms] * oxygen
    energy_ref[...] = total[:, 8 * atoms :] * (1.0 / (atoms * arrived.shape[0]))


def mode_factors(length, order):
    wrapped = np.where(2 * order >= length, order - length, order)
    square = (wrapped / length) ** 2
    ratio = (4.0 + 2.0 * np.cos(2.0 * math.pi * order / length)) / 6.0
    return np.stack([np.exp(-(math.pi**2) * square / ewald_beta**2) / ratio**2, square])


def folded_order(length):
    half = length // 2
    counter = np.arange(half)
    return np.concatenate([counter, np.where(counter == 0, half, length - counter)])


def fold_table(length):
    half = length // 2
    turns = np.outer(np.arange(length), np.arange(half)) % length * (2.0 * math.pi / length)
    sines = np.sin(turns)
    sines[:, 0] = 1.0 - 2.0 * (np.arange(length) % 2)
    return np.concatenate([np.cos(turns), sines], axis=1)


def halves(table):
    high = table.astype(jnp.bfloat16)
    low = (table - high.astype(np.float64)).astype(jnp.bfloat16)
    return high, low


def vmem(count):
    return [pl.BlockSpec(memory_space=pltpu.VMEM)] * count


def hbm(count):
    return [pl.BlockSpec(memory_space=pltpu.HBM)] * count


def shaped(shape, dtype=jnp.float32):
    return jax.ShapeDtypeStruct(shape, dtype)


def limits(mebibytes):
    return pltpu.CompilerParams(vmem_limit_bytes=mebibytes * 1024 * 1024)


def local(
    positions,
    species,
    neighbours,
    embed_one_w,
    embed_one_b,
    embed_two_w,
    embed_two_b,
    embed_three_w,
    embed_three_b,
    fit_one_w,
    fit_one_b,
    fit_two_w,
    fit_two_b,
    fit_three_w,
    fit_three_b,
    fit_out_w,
):
    axes = ("wide", "narrow")
    wide_count = lax.axis_size("wide")
    narrow_count = lax.axis_size("narrow")
    pieces = wide_count * narrow_count
    atoms = positions.shape[4]
    listed = neighbours.shape[4]
    fine = GRID_Y // 2 // pieces
    width_three = embed_three_w.shape[1]
    entries, hidden = fit_one_w.shape
    kinds = species.reshape(1, atoms)

    packed = pl.pallas_call(
        pack_kernel,
        out_shape=shaped((pieces, 4, atoms)),
        in_specs=vmem(2),
        out_specs=vmem(1)[0],
        name="pack",
    )(positions.reshape(3, 1, atoms), kinds)
    table = lax.all_to_all(packed, axes, 0, 0, tiled=True)
    table = table.reshape(wide_count, narrow_count, 4, atoms)

    tall = 4 * ROW_PAD
    bf16 = jnp.bfloat16
    wave_rows = -(-2 * fine // 8) * 8
    angle = np.arange(GRID_Y) * (2.0 * math.pi / GRID_Y)
    constants = np.concatenate(
        [
            np.stack([np.cos(angle), np.sin(angle)]),
            mode_factors(GRID_Y, np.arange(GRID_Y)),
            mode_factors(GRID_X, folded_order(GRID_X)),
            mode_factors(GRID_Z, folded_order(GRID_Z)),
        ]
    )
    constants[2] *= coulomb / (math.pi * GRID_X * GRID_Y * GRID_Z)
    arguments = (
        neighbours.reshape(atoms, listed),
        embed_one_w,
        embed_one_b,
        embed_two_w,
        embed_two_b[None],
        embed_three_w,
        embed_three_b[None],
        fit_one_w.T,
        fit_one_b[None],
        fit_two_w,
        fit_two_b[None],
        fit_three_w,
        fit_three_b[None],
        jnp.asarray(constants, jnp.float32),
    )
    held = [arguments[k] for k in (0, 1, 2, 3, 4, 5, 6, 8, 10, 12, 13, 9, 11, 7)]
    prepared = pl.pallas_call(
        prepare_kernel,
        out_shape=(
            shaped((listed, atoms), jnp.int32),
            shaped((256, 16)),
            shaped((2 * ROW_PAD, 3 * ROW_PAD), bf16),
            shaped((tall, 6 * ROW_PAD), bf16),
            shaped((hidden, entries), bf16),
            shaped((hidden, entries), bf16),
        )
        + (shaped((hidden, hidden), bf16),) * 4
        + (shaped((wave_rows, GRID_Y)), shaped((fine + 1, GRID_Z, GRID_X))),
        in_specs=hbm(len(arguments)),
        out_specs=tuple(vmem(12)),
        scratch_shapes=[
            pltpu.VMEM((16, 256), jnp.float32),
            pltpu.VMEM((256, 256), jnp.float32),
            pltpu.SemaphoreType.DMA((len(held),)),
        ]
        + [pltpu.VMEM(array.shape, array.dtype) for array in held],
        compiler_params=limits(62),
        cost_estimate=pl.CostEstimate(
            flops=1000000, bytes_accessed=8 * entries * hidden, transcendentals=0
        ),
        name="prepare",
    )(*arguments)
    phase, green = prepared[10:]
    fitted = (*prepared[4:10], fit_out_w.T)
    dipole, shifts = pl.pallas_call(
        centroid_kernel,
        out_shape=(shaped((3, 1, atoms)), shaped((pieces, 4, atoms))),
        in_specs=vmem(5) + hbm(7),
        out_specs=tuple(vmem(2)),
        scratch_shapes=[
            pltpu.VMEM((4, tall, atoms), jnp.float32),
            pltpu.VMEM((width_three * AXIS_COLUMNS, atoms), jnp.float32),
            pltpu.SemaphoreType.DMA((len(fitted),)),
        ]
        + [pltpu.VMEM(array.shape, array.dtype) for array in fitted],
        compiler_params=limits(62),
        name="centroids",
    )(table, *prepared[:4], *fitted)
    shifts = lax.all_to_all(shifts, axes, 0, 0, tiled=True)
    shifts = shifts.reshape(wide_count, narrow_count, 4, atoms)

    copies = 128 // (GRID_X // wide_count)
    window = GRID_Z // narrow_count + HALO_Z
    length = wide_count * atoms
    grid = pltpu.VMEM((copies, fine, HALO_Z + GRID_Z, 2 * GRID_X), jnp.float32)
    kept = (
        shaped((narrow_count, 256, length), bf16),
        shaped((narrow_count, window, length)),
        shaped((narrow_count, wave_rows, length)),
        shaped((narrow_count, wave_rows, length)),
    )
    spread_atoms = pl.pallas_call(
        atoms_kernel,
        out_shape=(shaped((fine, GRID_Z, 2 * GRID_X)),) + kept,
        in_specs=vmem(2),
        out_specs=tuple(vmem(5)),
        scratch_shapes=[grid],
        compiler_params=limits(24),
        cost_estimate=pl.CostEstimate(
            flops=2 * 3 * pieces * atoms * 2 * fine * window * 128,
            bytes_accessed=8 * 1024 * 1024,
            transcendentals=0,
        ),
        name="atoms",
    )(table, phase)
    out_width = 8 * atoms + 128
    tables = halves(fold_table(GRID_X)) + halves(fold_table(GRID_X).T)
    partial = pl.pallas_call(
        mesh_kernel,
        out_shape=shaped((wide_count, narrow_count, 1, out_width)),
        in_specs=vmem(13),
        out_specs=vmem(1)[0],
        scratch_shapes=[grid]
        + [pltpu.VMEM(array.shape, array.dtype) for array in kept]
        + [pltpu.VMEM((2, 2, 256, length), bf16)],
        compiler_params=limits(36),
        name="mesh",
    )(table, shifts, phase, green, *[jnp.asarray(half) for half in tables], *spread_atoms)
    arrived = lax.all_to_all(partial.reshape(pieces, 1, out_width), axes, 0, 0, tiled=True)
    atom_field, centroid_field, energy = pl.pallas_call(
        finish_kernel,
        out_shape=(shaped((4, 1, atoms)), shaped((4, 1, atoms)), shaped((1, 128))),
        in_specs=vmem(2),
        out_specs=tuple(vmem(3)),
        name="finish",
    )(arrived, kinds)
    atom_field = atom_field.reshape(4, 1, 1, 1, atoms)
    centroid_field = centroid_field.reshape(4, 1, 1, 1, atoms)
    return (dipole.reshape(3, 1, 1, 1, atoms), atom_field, centroid_field, energy[0, 0])


def solution(mesh):
    column = P(None, "wide", "narrow", None, None)
    in_specs = (column, P("wide", "narrow", None, None), P("wide", "narrow", None, None, None))
    in_specs = in_specs + (P(),) * 13
    out_specs = (column, column, column, P())
    return jax.shard_map(local, mesh=mesh, in_specs=in_specs, out_specs=out_specs, check_vma=False)
```

```python
import math

import jax
import jax.numpy as jnp
import numpy as np
from jax import lax
from jax.experimental import pallas as pl
from jax.experimental.pallas import tpu as pltpu
from jax.sharding import PartitionSpec as P

GRID_X = 256
GRID_Y = 256
GRID_Z = 256
AXIS_COLUMNS = 16

radius_scale = 24.0
wannier_reach = 0.5
ewald_beta = 0.9
coulomb = 0.25

ROW_PAD = 32
SLOT_CHUNK = 16
HALO_X = 16
HALO_Z = 8

NN = (((1,), (0,)), ((), ()))
NT = (((1,), (1,)), ((), ()))


def split(value):
    high = value.astype(jnp.bfloat16)
    low = (value - high.astype(jnp.float32)).astype(jnp.bfloat16)
    return high, low


def multiply(left, right, dims=NN):
    def one(a, b):
        return lax.dot_general(a, b, dims, preferred_element_type=jnp.float32)

    return one(left[0], right[0]) + (one(left[1], right[0]) + one(left[0], right[1]))


def product(left, right, dims=NN):
    return lax.dot_general(left, right, dims, preferred_element_type=jnp.float32)


def as_left(value):
    high, low = split(value)
    return jnp.concatenate([high, low, high], axis=1)


def as_right(value):
    high, low = split(value)
    return jnp.concatenate([high, high, low], axis=0)


def spline_pair(offset):
    centred = offset - 2.0
    away = jnp.abs(centred)
    outer = jnp.maximum(2.0 - away, 0.0)
    inner = jnp.maximum(1.0 - away, 0.0)
    outer_square = outer * outer
    inner_square = inner * inner
    value = (outer_square * outer - 4.0 * (inner_square * inner)) * (1.0 / 6.0)
    slope = jnp.where(centred < 0.0, 0.5, -0.5) * (outer_square - 4.0 * inner_square)
    return value, slope


def lookup(row_table, spot):
    found = None
    for part in range(row_table.shape[1] // 128):
        inside = spot // 128 == part
        here = jnp.take_along_axis(
            jnp.broadcast_to(row_table[:, part * 128 : (part + 1) * 128], spot.shape),
            lax.rem(spot, 128),
            axis=1,
            mode="promise_in_bounds",
        )
        found = here if found is None else jnp.where(inside, here, found)
    return found


def pack_kernel(positions, species, out_ref):
    rows = [positions[component] for component in range(3)]
    rows.append(species[...].astype(jnp.float32))
    rows = jnp.concatenate(rows, axis=0)
    for target in range(out_ref.shape[0]):
        out_ref[target] = rows


def prepare_kernel(
    neighbours,
    embed_one_w,
    embed_one_b,
    embed_two_w,
    embed_two_b,
    embed_three_w,
    embed_three_b,
    fit_one_w,
    fit_one_b,
    fit_two_w,
    fit_two_b,
    fit_three_w,
    fit_three_b,
    constants,
    codes_ref,
    columns_ref,
    second_ref,
    third_ref,
    one_high_ref,
    one_low_ref,
    two_high_ref,
    two_low_ref,
    three_high_ref,
    three_low_ref,
    phase_ref,
    green_ref,
    rows,
    square,
    arrivals,
    *held,
):
    sources = (
        neighbours,
        embed_one_w,
        embed_one_b,
        embed_two_w,
        embed_two_b,
        embed_three_w,
        embed_three_b,
        fit_one_b,
        fit_two_b,
        fit_three_b,
        constants,
        fit_two_w,
        fit_three_w,
        fit_one_w,
    )
    copies = [
        pltpu.make_async_copy(source, target, arrivals.at[k])
        for k, (source, target) in enumerate(zip(sources, held))
    ]
    for copy in copies:
        copy.start()
    (
        neighbours,
        embed_one_w,
        embed_one_b,
        embed_two_w,
        embed_two_b,
        embed_three_w,
        embed_three_b,
        fit_one_b,
        fit_two_b,
        fit_three_b,
        constants,
        fit_two_w,
        fit_three_w,
        fit_one_w,
    ) = held
    for copy in copies[:11]:
        copy.wait()
    pieces = lax.axis_size("wide") * lax.axis_size("narrow")
    piece = lax.axis_index("wide") * lax.axis_size("narrow") + lax.axis_index("narrow")
    width_one = embed_one_w.shape[1]
    hidden = fit_two_w.shape[0]
    codes_ref[...] = jnp.transpose(neighbours[...].astype(jnp.float32)).astype(jnp.int32)
    rows[...] = jnp.zeros_like(rows)
    for kind in range(2):
        rows[kind : kind + 1, 0:width_one] = embed_one_w[kind : kind + 1, :]
        rows[2 + kind : 3 + kind, 0:width_one] = embed_one_b[kind : kind + 1, :]
        rows[2 + kind : 3 + kind, width_one : width_one + 1] = jnp.full((1, 1), 40.0, jnp.float32)
    for row, source in ((4, fit_one_b), (5, fit_two_b), (6, fit_three_b)):
        rows[row : row + 1, 0:hidden] = source[...]
    columns_ref[...] = jnp.transpose(rows[...])

    square[...] = jnp.zeros_like(square)
    for k in range(2):
        square[0:width_one, k * ROW_PAD : k * ROW_PAD + width_one] = embed_two_w[
            :, k * width_one : (k + 1) * width_one
        ]
        square[
            width_one : width_one + 1, k * ROW_PAD : k * ROW_PAD + width_one
        ] = embed_two_b[:, k * width_one : (k + 1) * width_one]
    high, low = split(jnp.transpose(square[0:128, 0:128])[0 : 2 * ROW_PAD, 0:ROW_PAD])
    second_ref[...] = jnp.concatenate([high, high, low], axis=1)
    square[0:128, 0:128] = jnp.zeros((128, 128), jnp.float32)
    for g in range(2):
        for k in range(4):
            square[
                g * ROW_PAD : g * ROW_PAD + width_one, k * ROW_PAD : k * ROW_PAD + width_one
            ] = embed_three_w[
                g * width_one : (g + 1) * width_one, k * width_one : (k + 1) * width_one
            ]
    for k in range(4):
        square[
            width_one : width_one + 1, k * ROW_PAD : k * ROW_PAD + width_one
        ] = embed_three_b[:, k * width_one : (k + 1) * width_one]
    high, low = split(jnp.transpose(square[0:128, 0:128])[:, 0 : 2 * ROW_PAD])
    third_ref[...] = jnp.concatenate([high, high, low], axis=1)
    for copy in copies[11:13]:
        copy.wait()
    for source, high_ref, low_ref in (
        (fit_two_w, two_high_ref, two_low_ref),
        (fit_three_w, three_high_ref, three_low_ref),
    ):
        square[0:hidden, 0:hidden] = source[...]
        high_ref[...], low_ref[...] = split(jnp.transpose(square[...])[0:hidden, 0:hidden])

    fine = GRID_Y // 2 // pieces
    shape = (phase_ref.shape[0], 128)
    row = lax.broadcasted_iota(jnp.int32, shape, 0)
    mode = piece * fine + row // 2
    for part in range(GRID_Y // 128):
        cell = lax.broadcasted_iota(jnp.int32, shape, 1) + part * 128
        spot = lax.rem(mode * cell, GRID_Y)
        cosine = lookup(constants[0:1, :], spot)
        sine = lookup(constants[1:2, :], spot)
        alternate = (1 - 2 * lax.rem(cell, 2)).astype(jnp.float32)
        odd = jnp.where(mode == 0, alternate, -sine)
        value = jnp.where(lax.rem(row, 2) == 0, cosine, odd)
        phase_ref[:, part * 128 : (part + 1) * 128] = jnp.where(row < 2 * fine, value, 0.0)

    column = jnp.transpose(constants[...])
    lane = lax.broadcasted_iota(jnp.int32, (1, GRID_Y), 1)
    for j in range(fine + 1):
        here = lane == (GRID_Y // 2 if j == fine else piece * fine + j)
        factor = jnp.sum(jnp.where(here, constants[2:3, :], 0.0), axis=1, keepdims=True)
        part = jnp.sum(jnp.where(here, constants[3:4, :], 0.0), axis=1, keepdims=True)
        wave = (part + constants[5:6, :]) + column[:, 7:8]
        top = (factor * constants[4:5, :]) * column[:, 6:7]
        green_ref[j] = jnp.where(wave == 0.0, 0.0, top / jnp.where(wave == 0.0, 1.0, wave))

    copies[13].wait()
    one_high_ref[...], one_low_ref[...] = split(fit_one_w[...])


def centroid_kernel(
    table,
    codes,
    columns,
    second,
    third,
    one_high,
    one_low,
    two_high,
    two_low,
    three_high,
    three_low,
    fit_out_w,
    dipole_ref,
    shift_ref,
    matrix,
    descriptor,
    arrivals,
    *held,
):
    sources = (table, codes, columns, second, third)
    sources += (one_high, one_low, two_high, two_low, three_high, three_low, fit_out_w)
    copies = [
        pltpu.make_async_copy(source, target, arrivals.at[k])
        for k, (source, target) in enumerate(zip(sources, held))
    ]
    for copy in copies:
        copy.start()
    table, codes, columns, second, third = held[:5]
    one_high, one_low, two_high, two_low, three_high, three_low, fit_out_w = held[5:]
    for copy in copies[:5]:
        copy.wait()
    wide_count, narrow_count, _, atoms = table.shape
    listed = codes.shape[0]
    width_three = fit_out_w.shape[0]
    width_one = width_three // 4
    hidden_width = two_high.shape[0]
    cells = (GRID_X // wide_count, GRID_Y, GRID_Z // narrow_count)
    at_wide = lax.axis_index("wide")
    at_narrow = lax.axis_index("narrow")
    own = table[at_wide, at_narrow]
    nearby = []
    for step in range(9):
        wide_at = lax.rem(at_wide + (step // 3 - 1) + wide_count, wide_count)
        narrow_at = lax.rem(at_narrow + (step % 3 - 1) + narrow_count, narrow_count)
        nearby.append(table[wide_at, narrow_at])

    second_all = second[...]
    third_all = third[...]
    weight_oxygen = jnp.broadcast_to(columns[0:ROW_PAD, 0:1], (ROW_PAD, atoms))
    weight_hydrogen = jnp.broadcast_to(columns[0:ROW_PAD, 1:2], (ROW_PAD, atoms))
    bias_oxygen = jnp.broadcast_to(columns[0:ROW_PAD, 2:3], (ROW_PAD, atoms))
    bias_hydrogen = jnp.broadcast_to(columns[0:ROW_PAD, 3:4], (ROW_PAD, atoms))
    matrix[...] = jnp.zeros_like(matrix)

    def chunk(first):
        code = codes[pl.ds(first, SLOT_CHUNK), :]
        offset = code // atoms
        slot = code - offset * atoms
        step_x = jnp.where(offset >= 9, 1, 0) + jnp.where(offset >= 18, 1, 0)
        rest = offset - 9 * step_x
        step_z = jnp.where(rest >= 3, 1, 0) + jnp.where(rest >= 6, 1, 0)
        step_y = rest - 3 * step_z
        brick = step_x * 3 + step_z
        found = []
        for component in range(4):
            picked = jnp.zeros((SLOT_CHUNK, atoms), jnp.float32)
            for step in range(9):
                row = jnp.broadcast_to(
                    nearby[step][component : component + 1], (SLOT_CHUNK, atoms)
                )
                here = jnp.take_along_axis(row, slot, axis=1, mode="promise_in_bounds")
                picked = jnp.where(brick == step, here, picked)
            found.append(picked)
        scaled = []
        for component, step in enumerate((step_x, step_y, step_z)):
            extent = float(cells[component])
            relative = (step - 1).astype(jnp.float32) * extent + (
                found[component] - own[component : component + 1]
            ) * extent
            scaled.append(relative * (1.0 / radius_scale))
        smooth = 1.0 / (
            1.0 + (scaled[0] * scaled[0] + scaled[1] * scaled[1] + scaled[2] * scaled[2])
        )
        radial = [smooth] + [smooth * part for part in scaled]
        hydrogen = found[3] > 0.5
        first_layers = []
        for k in range(SLOT_CHUNK):
            row = smooth[k : k + 1]
            kind = hydrogen[k : k + 1]
            weight = jnp.where(kind, weight_hydrogen, weight_oxygen)
            bias = jnp.where(kind, bias_hydrogen, bias_oxygen)
            first_layers.append(jnp.tanh(weight * row + bias))
        layer_one = jnp.concatenate(first_layers, axis=1)
        high, low = split(layer_one)
        layer_two = lax.dot_general(
            second_all,
            jnp.concatenate([high, low, high], axis=0),
            NN,
            preferred_element_type=jnp.float32,
        )
        layer_two = jnp.tanh(layer_two) + jnp.concatenate(
            [layer_one, layer_one], axis=0
        )
        high, low = split(layer_two)
        layer_three = lax.dot_general(
            third_all,
            jnp.concatenate([high, low, high], axis=0),
            NN,
            preferred_element_type=jnp.float32,
        )
        layer_three = jnp.tanh(layer_three) + jnp.concatenate(
            [layer_two, layer_two], axis=0
        )
        for part in range(4):
            total = matrix[part]
            for k in range(SLOT_CHUNK):
                total = total + layer_three[:, k * atoms : (k + 1) * atoms] * radial[part][k : k + 1]
            matrix[part] = total

    def two_chunks(index, carry):
        first = pl.multiple_of(index * (2 * SLOT_CHUNK), 2 * SLOT_CHUNK)
        chunk(first)
        chunk(pl.multiple_of(first + SLOT_CHUNK, SLOT_CHUNK))
        return carry

    lax.fori_loop(0, listed // (2 * SLOT_CHUNK), two_chunks, 0)

    parts = []
    for part in range(4):
        padded = matrix[part] * (1.0 / listed)
        parts.append(
            jnp.concatenate(
                [padded[k * ROW_PAD : k * ROW_PAD + width_one] for k in range(4)], axis=0
            )
        )
    leading = [part[0:AXIS_COLUMNS] for part in parts]
    for row in range(width_three):
        total = parts[0][row : row + 1] * leading[0]
        for part in range(1, 4):
            total = total + parts[part][row : row + 1] * leading[part]
        descriptor[row * AXIS_COLUMNS : (row + 1) * AXIS_COLUMNS, :] = total
    for copy in copies[5:]:
        copy.wait()

    def layer(high_ref, low_ref, given, column):
        weights = (high_ref[...], low_ref[...])
        return jnp.tanh(multiply(weights, split(given)) + columns[0:hidden_width, column : column + 1])

    hidden = layer(one_high, one_low, descriptor[...], 4)
    hidden = hidden + layer(two_high, two_low, hidden, 5)
    hidden = hidden + layer(three_high, three_low, hidden, 6)
    coeffs = multiply(split(fit_out_w[...]), split(hidden))
    vector = jnp.concatenate(
        [jnp.sum(coeffs * parts[1 + c], axis=0, keepdims=True) for c in range(3)], axis=0
    )
    oxygen = 1.0 - own[3:4]
    for c in range(3):
        dipole_ref[c] = vector[c : c + 1] * oxygen
    moved = wannier_reach * jnp.tanh(vector)
    moved = jnp.concatenate([moved, jnp.zeros((1, atoms), jnp.float32)], axis=0)
    for target in range(shift_ref.shape[0]):
        shift_ref[target] = moved


def mesh_kernel(
    table,
    shifts,
    phase,
    green_ref,
    fold_left,
    fold_right,
    unfold_left,
    unfold_right,
    out_ref,
    grid,
    planes,
    weights,
    slopes,
    weights_z,
    waves,
    wave_slopes,
):
    wide_count, narrow_count, _, atoms = table.shape
    cells_x = GRID_X // wide_count
    cells_z = GRID_Z // narrow_count
    window = cells_z + HALO_Z
    reach = cells_x + HALO_X
    pair = 2 * atoms
    length = wide_count * pair
    copies = grid.shape[0]
    fine = grid.shape[1]
    channels = 2 * fine
    rows = phase.shape[0]
    half_x = GRID_X // 2
    half_z = GRID_Z // 2
    piece = lax.axis_index("wide") * narrow_count + lax.axis_index("narrow")
    lane_zero = lax.broadcasted_iota(jnp.int32, (1, half_x), 1) == 0
    row_zero = lax.broadcasted_iota(jnp.int32, (half_z, 1), 0) == 0

    def sites(at_wide, at_narrow):
        atom = table[at_wide, at_narrow]
        moved = shifts[at_wide, at_narrow]
        found = []
        for component, extent in enumerate((cells_x, GRID_Y, cells_z)):
            start = atom[component : component + 1] * float(extent)
            found.append(jnp.concatenate([start, start + moved[component : component + 1]], axis=1))
        oxygen = 1.0 - atom[3:4]
        found.append(jnp.concatenate([6.0 * oxygen + atom[3:4], -8.0 * oxygen], axis=1))
        return found

    def line(at_narrow):
        groups = [sites(at_wide, at_narrow) for at_wide in range(wide_count)]
        return [jnp.concatenate([g[k] for g in groups], axis=1) for k in range(4)]

    def splines_z(row):
        counter = lax.broadcasted_iota(jnp.int32, (window, 1), 0).astype(jnp.float32)
        return spline_pair(row - (counter - float(HALO_Z)))

    def fill_x(row, targets):
        counter = lax.broadcasted_iota(jnp.int32, (reach, 1), 0).astype(jnp.float32)
        both = spline_pair(row - (counter - float(HALO_X)))
        rest = jnp.zeros((128 - reach, length), jnp.bfloat16)
        for values, ref in zip(both, targets):
            if ref is not None:
                high, low = split(values)
                ref[0:reach, :] = high
                ref[reach:128, :] = rest
                ref[128 : 128 + reach, :] = low
                ref[128 + reach : 256, :] = rest

    grid[:, :, 0:HALO_Z, :] = jnp.zeros((copies, fine, HALO_Z, 2 * GRID_X), jnp.float32)

    def spread(at_narrow):
        row_x, row_y, row_z, charge = line(at_narrow)
        lower = jnp.floor(row_y)
        back = lax.broadcasted_iota(jnp.int32, (8, 1), 0)
        value_y, slope_y = spline_pair((row_y - lower) + back.astype(jnp.float32))
        cell = lax.rem(lower.astype(jnp.int32) - back + GRID_Y, GRID_Y)
        wave_blocks = []
        slope_blocks = []
        for block in range(length // 128):
            lanes = slice(block * 128, (block + 1) * 128)
            wave = jnp.zeros((rows, 128), jnp.float32)
            wave_slope = jnp.zeros((rows, 128), jnp.float32)
            for k in range(4):
                spot = jnp.broadcast_to(cell[k : k + 1, lanes], (rows, 128))
                found = lookup(phase[...], spot)
                wave = wave + value_y[k : k + 1, lanes] * found
                wave_slope = wave_slope + slope_y[k : k + 1, lanes] * found
            wave_blocks.append(wave)
            slope_blocks.append(wave_slope)
        wave = jnp.concatenate(wave_blocks, axis=1)
        waves[at_narrow] = wave
        wave_slopes[at_narrow] = jnp.concatenate(slope_blocks, axis=1)
        fill_x(row_x, (weights.at[at_narrow], None))
        value_z, _ = splines_z(row_z)
        weights_z[at_narrow] = value_z
        charged = wave * charge
        first = pl.multiple_of(at_narrow * cells_z, HALO_Z)
        for at_wide in range(wide_count):
            lanes = slice(at_wide * pair, (at_wide + 1) * pair)
            near = value_z[:, lanes]
            left = jnp.concatenate(
                [near * charged[c : c + 1, lanes] for c in range(channels)], axis=0
            )
            high, low = split(left)
            across = weights[at_narrow, :, lanes]
            total = product(
                jnp.concatenate([high, low], axis=1), jnp.concatenate([across, across], axis=1), NT
            )
            total = total[:, 0:128] + total[:, 128:256]
            start = at_wide // copies * 128
            for c in range(channels):
                spot = slice(c % 2 * GRID_X + start, c % 2 * GRID_X + start + 128)
                k = at_wide % copies
                part = total[c * window : (c + 1) * window]
                grid[k, c // 2, pl.ds(first, HALO_Z), spot] += part[:HALO_Z]
                grid[k, c // 2, pl.ds(first + HALO_Z, cells_z), spot] = part[HALO_Z:]

    def in_pairs(step):
        def both(index, carry):
            step(2 * index, 0)
            step(2 * index + 1, 1)
            return carry

        lax.fori_loop(0, narrow_count // 2, both, 0)

    in_pairs(lambda at_narrow, _: spread(at_narrow))

    def gather(j, carry):
        for lanes in (slice(0, GRID_X), slice(GRID_X, 2 * GRID_X)):
            total = None
            for k in range(copies):
                moved = pltpu.roll(grid[k, j, :, lanes], (k * cells_x - HALO_X) % GRID_X, 1)
                total = moved if total is None else total + moved
            planes[j, :, lanes] = total[HALO_Z:]
            planes[j, GRID_Z - HALO_Z :, lanes] += total[:HALO_Z]
        return carry

    lax.fori_loop(0, fine, gather, 0)
    is_first = piece == 0

    def paired(real, imag, zero, axis):
        half = real.shape[axis] // 2
        first = (slice(None),) * axis + (slice(0, half),)
        second = (slice(None),) * axis + (slice(half, 2 * half),)
        real_c, real_s = real[first], real[second]
        if imag is None:
            none = jnp.zeros_like(real_s)
            real_all = [real_c, jnp.where(zero, real_s, real_c)]
            imag_all = [jnp.where(zero, none, -real_s), jnp.where(zero, none, real_s)]
        else:
            imag_c, imag_s = imag[first], imag[second]
            real_all = [
                real_c + jnp.where(zero, 0.0, imag_s),
                jnp.where(zero, real_s, real_c - imag_s),
            ]
            imag_all = [
                imag_c - jnp.where(zero, 0.0, real_s),
                jnp.where(zero, imag_s, imag_c + real_s),
            ]
        return jnp.concatenate(real_all, axis=axis), jnp.concatenate(imag_all, axis=axis)

    def merged(real, imag, zero, axis):
        half = real.shape[axis] // 2
        first = (slice(None),) * axis + (slice(0, half),)
        second = (slice(None),) * axis + (slice(half, 2 * half),)
        real_a, real_b = real[first], real[second]
        imag_a, imag_b = imag[first], imag[second]
        real = [
            real_a + jnp.where(zero, 0.0, real_b),
            jnp.where(zero, real_b, imag_b - imag_a),
        ]
        imag = [
            imag_a + jnp.where(zero, 0.0, imag_b),
            jnp.where(zero, imag_b, real_a - real_b),
        ]
        return jnp.concatenate(real, axis=axis), jnp.concatenate(imag, axis=axis)

    def to_modes(real, imag, j):
        real = product(as_left(real), fold_right[...])
        if imag is not None:
            imag = product(as_left(imag), fold_right[...])
        real, imag = paired(real, imag, lane_zero, 1)
        real = product(unfold_left[...], as_right(real))
        imag = product(unfold_left[...], as_right(imag))
        real, imag = paired(real, imag, row_zero, 0)
        green = green_ref[j]
        mode = GRID_Y // 2 if j == fine else piece * fine + j
        share = jnp.where((mode == 0) | (mode == GRID_Y // 2), 0.5, 1.0)
        part = jnp.sum(green * (real * real + imag * imag), axis=0, keepdims=True)
        return green * real, green * imag, share * part

    second_plane = jnp.where(is_first, planes[0, :, GRID_X:], 0.0)
    last_real, last_imag, energy = to_modes(second_plane, None, fine)
    for j in range(fine):
        imag = planes[j, :, GRID_X:]
        if j == 0:
            imag = jnp.where(is_first, 0.0, imag)
        real, imag, part = to_modes(planes[j, :, 0:GRID_X], imag, j)
        energy = energy + part
        if j == 0:
            real, imag = real - last_imag, imag + last_real
        real, imag = merged(real, imag, row_zero, 0)
        real = product(fold_left[...], as_right(real))
        imag = product(fold_left[...], as_right(imag))
        real, imag = merged(real, imag, lane_zero, 1)
        scale = jnp.where(piece * fine + j == 0, 1.0, 2.0)
        for part, lanes in ((real, slice(0, GRID_X)), (imag, slice(GRID_X, 2 * GRID_X))):
            part = product(as_left(part * scale), unfold_right[...])
            for k in range(copies):
                moved = pltpu.roll(part, (HALO_X - k * cells_x) % GRID_X, 1)
                grid[k, j, HALO_Z:, lanes] = moved
                grid[k, j, 0:HALO_Z, lanes] = moved[GRID_Z - HALO_Z :]
    energy = jnp.broadcast_to(jnp.sum(energy, axis=1, keepdims=True), (1, 128))

    def collect(at_narrow, buffer):
        row_x, _, row_z, _ = line(at_narrow)
        fill_x(row_x, (None, slopes.at[buffer]))
        value_z = weights_z[at_narrow]
        _, slope_z = splines_z(row_z)
        first = pl.multiple_of(at_narrow * cells_z, HALO_Z)
        lefts = []
        for k in range(copies):
            left = jnp.concatenate(
                [
                    grid[k, c // 2, pl.ds(first, window), c % 2 * GRID_X : (c % 2 + 1) * GRID_X]
                    for c in range(channels)
                ],
                axis=0,
            )
            lefts.append(split(left))
        wave = waves[at_narrow]
        wave_slope = wave_slopes[at_narrow]
        for at_wide in range(wide_count):
            lanes = slice(at_wide * pair, (at_wide + 1) * pair)
            start = at_wide // copies * 128
            high = lefts[at_wide % copies][0][:, start : start + 128]
            low = lefts[at_wide % copies][1][:, start : start + 128]
            thrice = jnp.concatenate([high, high, low], axis=1)

            def across(right):
                return product(thrice, jnp.concatenate([right, right[0:128]], axis=0))

            value = across(weights[at_narrow, :, lanes])
            slope = across(slopes[buffer, :, lanes])
            plain = jnp.zeros((window, pair), jnp.float32)
            along_x = plain
            along_y = plain
            for c in range(channels):
                block = slice(c * window, (c + 1) * window)
                plain = plain + value[block] * wave[c : c + 1, lanes]
                along_x = along_x + slope[block] * wave[c : c + 1, lanes]
                along_y = along_y + value[block] * wave_slope[c : c + 1, lanes]
            near = value_z[:, lanes]
            near_slope = slope_z[:, lanes]
            results = [
                jnp.sum(near * plain, axis=0, keepdims=True),
                -jnp.sum(near * along_x, axis=0, keepdims=True),
                -jnp.sum(near * along_y, axis=0, keepdims=True),
                -jnp.sum(near_slope * plain, axis=0, keepdims=True),
            ]
            for k, row in enumerate(results):
                out_ref[at_wide, at_narrow, :, k * pair : (k + 1) * pair] = row
            out_ref[at_wide, at_narrow, :, 4 * pair :] = energy

    in_pairs(collect)


def finish_kernel(arrived, species, atom_ref, centroid_ref, energy_ref):
    atoms = species.shape[1]
    total = arrived[0]
    for k in range(1, arrived.shape[0]):
        total = total + arrived[k]
    oxygen = 1.0 - species[...].astype(jnp.float32)
    for k in range(4):
        atom_ref[k] = total[:, 2 * k * atoms : (2 * k + 1) * atoms]
        centroid_ref[k] = total[:, (2 * k + 1) * atoms : (2 * k + 2) * atoms] * oxygen
    energy_ref[...] = total[:, 8 * atoms :] * (1.0 / (atoms * arrived.shape[0]))


def mode_factors(length, order):
    wrapped = np.where(2 * order >= length, order - length, order)
    square = (wrapped / length) ** 2
    ratio = (4.0 + 2.0 * np.cos(2.0 * math.pi * order / length)) / 6.0
    return np.stack([np.exp(-(math.pi**2) * square / ewald_beta**2) / ratio**2, square])


def folded_order(length):
    half = length // 2
    counter = np.arange(half)
    return np.concatenate([counter, np.where(counter == 0, half, length - counter)])


def fold_table(length):
    half = length // 2
    turns = np.outer(np.arange(length), np.arange(half)) % length * (2.0 * math.pi / length)
    sines = np.sin(turns)
    sines[:, 0] = 1.0 - 2.0 * (np.arange(length) % 2)
    return np.concatenate([np.cos(turns), sines], axis=1)


def sides(table):
    high = table.astype(jnp.bfloat16)
    low = (table - high.astype(np.float64)).astype(jnp.bfloat16)
    return np.concatenate([high, low, high], axis=1), np.concatenate([high, high, low], axis=0)


def vmem(count):
    return [pl.BlockSpec(memory_space=pltpu.VMEM)] * count


def hbm(count):
    return [pl.BlockSpec(memory_space=pltpu.HBM)] * count


def shaped(shape, dtype=jnp.float32):
    return jax.ShapeDtypeStruct(shape, dtype)


def limits(mebibytes):
    return pltpu.CompilerParams(vmem_limit_bytes=mebibytes * 1024 * 1024)


def local(
    positions,
    species,
    neighbours,
    embed_one_w,
    embed_one_b,
    embed_two_w,
    embed_two_b,
    embed_three_w,
    embed_three_b,
    fit_one_w,
    fit_one_b,
    fit_two_w,
    fit_two_b,
    fit_three_w,
    fit_three_b,
    fit_out_w,
):
    axes = ("wide", "narrow")
    wide_count = lax.axis_size("wide")
    narrow_count = lax.axis_size("narrow")
    pieces = wide_count * narrow_count
    atoms = positions.shape[4]
    listed = neighbours.shape[4]
    fine = GRID_Y // 2 // pieces
    width_three = embed_three_w.shape[1]
    entries, hidden = fit_one_w.shape
    kinds = species.reshape(1, atoms)

    packed = pl.pallas_call(
        pack_kernel,
        out_shape=shaped((pieces, 4, atoms)),
        in_specs=vmem(2),
        out_specs=vmem(1)[0],
        name="pack",
    )(positions.reshape(3, 1, atoms), kinds)
    table = lax.all_to_all(packed, axes, 0, 0, tiled=True)
    table = table.reshape(wide_count, narrow_count, 4, atoms)

    tall = 4 * ROW_PAD
    bf16 = jnp.bfloat16
    wave_rows = -(-2 * fine // 8) * 8
    angle = np.arange(GRID_Y) * (2.0 * math.pi / GRID_Y)
    constants = np.concatenate(
        [
            np.stack([np.cos(angle), np.sin(angle)]),
            mode_factors(GRID_Y, np.arange(GRID_Y)),
            mode_factors(GRID_X, folded_order(GRID_X)),
            mode_factors(GRID_Z, folded_order(GRID_Z)),
        ]
    )
    constants[2] *= coulomb / (math.pi * GRID_X * GRID_Y * GRID_Z)
    arguments = (
        neighbours.reshape(atoms, listed),
        embed_one_w,
        embed_one_b,
        embed_two_w,
        embed_two_b[None],
        embed_three_w,
        embed_three_b[None],
        fit_one_w.T,
        fit_one_b[None],
        fit_two_w,
        fit_two_b[None],
        fit_three_w,
        fit_three_b[None],
        jnp.asarray(constants, jnp.float32),
    )
    held = [arguments[k] for k in (0, 1, 2, 3, 4, 5, 6, 8, 10, 12, 13, 9, 11, 7)]
    prepared = pl.pallas_call(
        prepare_kernel,
        out_shape=(
            shaped((listed, atoms), jnp.int32),
            shaped((256, 16)),
            shaped((2 * ROW_PAD, 3 * ROW_PAD), bf16),
            shaped((tall, 6 * ROW_PAD), bf16),
            shaped((hidden, entries), bf16),
            shaped((hidden, entries), bf16),
        )
        + (shaped((hidden, hidden), bf16),) * 4
        + (shaped((wave_rows, GRID_Y)), shaped((fine + 1, GRID_Z, GRID_X))),
        in_specs=hbm(len(arguments)),
        out_specs=tuple(vmem(12)),
        scratch_shapes=[
            pltpu.VMEM((16, 256), jnp.float32),
            pltpu.VMEM((256, 256), jnp.float32),
            pltpu.SemaphoreType.DMA((len(held),)),
        ]
        + [pltpu.VMEM(array.shape, array.dtype) for array in held],
        compiler_params=limits(62),
        cost_estimate=pl.CostEstimate(
            flops=1000000, bytes_accessed=8 * entries * hidden, transcendentals=0
        ),
        name="prepare",
    )(*arguments)
    phase, green = prepared[10:]
    fitted = (table, *prepared[:10], fit_out_w.T)
    dipole, shifts = pl.pallas_call(
        centroid_kernel,
        out_shape=(shaped((3, 1, atoms)), shaped((pieces, 4, atoms))),
        in_specs=hbm(12),
        out_specs=tuple(vmem(2)),
        scratch_shapes=[
            pltpu.VMEM((4, tall, atoms), jnp.float32),
            pltpu.VMEM((width_three * AXIS_COLUMNS, atoms), jnp.float32),
            pltpu.SemaphoreType.DMA((len(fitted),)),
        ]
        + [pltpu.VMEM(array.shape, array.dtype) for array in fitted],
        compiler_params=limits(62),
        name="centroids",
    )(*fitted)
    shifts = lax.all_to_all(shifts, axes, 0, 0, tiled=True)
    shifts = shifts.reshape(wide_count, narrow_count, 4, atoms)

    cells_x = GRID_X // wide_count
    copies = 128 // cells_x
    length = wide_count * 2 * atoms
    out_width = 8 * atoms + 128
    partial = pl.pallas_call(
        mesh_kernel,
        out_shape=shaped((wide_count, narrow_count, 1, out_width)),
        in_specs=vmem(8),
        out_specs=vmem(1)[0],
        scratch_shapes=[
            pltpu.VMEM((copies, fine, HALO_Z + GRID_Z, 2 * GRID_X), jnp.float32),
            pltpu.VMEM((fine + 1, GRID_Z, 2 * GRID_X), jnp.float32),
        ]
        + [pltpu.VMEM((narrow_count, 256, length), bf16), pltpu.VMEM((2, 256, length), bf16)]
        + [pltpu.VMEM((narrow_count, GRID_Z // narrow_count + HALO_Z, length), jnp.float32)]
        + [pltpu.VMEM((narrow_count, wave_rows, length), jnp.float32)] * 2,
        compiler_params=limits(48),
        name="mesh",
    )(
        table,
        shifts,
        phase,
        green,
        *[jnp.asarray(side) for side in sides(fold_table(GRID_X))],
        *[jnp.asarray(side) for side in sides(fold_table(GRID_X).T)],
    )
    arrived = lax.all_to_all(partial.reshape(pieces, 1, out_width), axes, 0, 0, tiled=True)
    atom_field, centroid_field, energy = pl.pallas_call(
        finish_kernel,
        out_shape=(shaped((4, 1, atoms)), shaped((4, 1, atoms)), shaped((1, 128))),
        in_specs=vmem(2),
        out_specs=tuple(vmem(3)),
        name="finish",
    )(arrived, kinds)
    atom_field = atom_field.reshape(4, 1, 1, 1, atoms)
    centroid_field = centroid_field.reshape(4, 1, 1, 1, atoms)
    return (dipole.reshape(3, 1, 1, 1, atoms), atom_field, centroid_field, energy[0, 0])


def solution(mesh):
    column = P(None, "wide", "narrow", None, None)
    in_specs = (column, P("wide", "narrow", None, None), P("wide", "narrow", None, None, None))
    in_specs = in_specs + (P(),) * 13
    out_specs = (column, column, column, P())
    return jax.shard_map(local, mesh=mesh, in_specs=in_specs, out_specs=out_specs, check_vma=False)
```

```python
import math

import jax
import jax.numpy as jnp
import numpy as np
from jax import lax
from jax.experimental import pallas as pl
from jax.experimental.pallas import tpu as pltpu
from jax.sharding import PartitionSpec as P

GRID_X = 256
GRID_Y = 256
GRID_Z = 256
AXIS_COLUMNS = 16

radius_scale = 24.0
wannier_reach = 0.5
ewald_beta = 0.9
coulomb = 0.25

ROW_PAD = 32
SLOT_CHUNK = 16
HALO_X = 16
HALO_Z = 8
HALO_BITS = 16

NN = (((1,), (0,)), ((), ()))
NT = (((1,), (1,)), ((), ()))


def split(value):
    high = value.astype(jnp.bfloat16)
    low = (value - high.astype(jnp.float32)).astype(jnp.bfloat16)
    return high, low


def multiply(left, right, dims=NN):
    def one(a, b):
        return lax.dot_general(a, b, dims, preferred_element_type=jnp.float32)

    return one(left[0], right[0]) + (one(left[1], right[0]) + one(left[0], right[1]))


def spline_pair(offset):
    centred = offset - 2.0
    away = jnp.abs(centred)
    outer = jnp.maximum(2.0 - away, 0.0)
    inner = jnp.maximum(1.0 - away, 0.0)
    outer_square = outer * outer
    inner_square = inner * inner
    value = (outer_square * outer - 4.0 * (inner_square * inner)) * (1.0 / 6.0)
    slope = jnp.where(centred < 0.0, 0.5, -0.5) * (outer_square - 4.0 * inner_square)
    return value, slope


def lookup(row_table, spot):
    found = None
    for part in range(row_table.shape[1] // 128):
        inside = spot // 128 == part
        here = jnp.take_along_axis(
            jnp.broadcast_to(row_table[:, part * 128 : (part + 1) * 128], spot.shape),
            lax.rem(spot, 128),
            axis=1,
            mode="promise_in_bounds",
        )
        found = here if found is None else jnp.where(inside, here, found)
    return found


def pack_kernel(positions, species, out_ref):
    kinds = species[...]
    rows = [positions[component] for component in range(3)]
    rows[0] = jnp.where(kinds > 0, -rows[0], rows[0])
    rows.append(kinds.astype(jnp.float32))
    rows = jnp.concatenate(rows, axis=0)
    for target in range(out_ref.shape[0]):
        out_ref[target] = rows


def prepare_kernel(
    neighbours,
    embed_one_w,
    embed_one_b,
    embed_two_w,
    embed_two_b,
    embed_three_w,
    embed_three_b,
    fit_one_w,
    fit_one_b,
    fit_two_w,
    fit_two_b,
    fit_three_w,
    fit_three_b,
    constants,
    codes_ref,
    columns_ref,
    second_ref,
    third_ref,
    one_high_ref,
    one_low_ref,
    two_high_ref,
    two_low_ref,
    three_high_ref,
    three_low_ref,
    phase_ref,
    green_ref,
    rows,
    square,
    arrivals,
    *held,
):
    sources = (
        neighbours,
        embed_one_w,
        embed_one_b,
        embed_two_w,
        embed_two_b,
        embed_three_w,
        embed_three_b,
        fit_one_b,
        fit_two_b,
        fit_three_b,
        constants,
        fit_two_w,
        fit_three_w,
        fit_one_w,
    )
    copies = [
        pltpu.make_async_copy(source, target, arrivals.at[k])
        for k, (source, target) in enumerate(zip(sources, held))
    ]
    for copy in copies:
        copy.start()
    (
        neighbours,
        embed_one_w,
        embed_one_b,
        embed_two_w,
        embed_two_b,
        embed_three_w,
        embed_three_b,
        fit_one_b,
        fit_two_b,
        fit_three_b,
        constants,
        fit_two_w,
        fit_three_w,
        fit_one_w,
    ) = held
    for copy in copies[:11]:
        copy.wait()
    pieces = lax.axis_size("wide") * lax.axis_size("narrow")
    piece = lax.axis_index("wide") * lax.axis_size("narrow") + lax.axis_index("narrow")
    width_one = embed_one_w.shape[1]
    hidden = fit_two_w.shape[0]
    codes_ref[...] = jnp.transpose(neighbours[...].astype(jnp.float32)).astype(jnp.int32)
    rows[...] = jnp.zeros_like(rows)
    for kind in range(2):
        rows[kind : kind + 1, 0:width_one] = embed_one_w[kind : kind + 1, :]
        rows[2 + kind : 3 + kind, 0:width_one] = embed_one_b[kind : kind + 1, :]
        rows[2 + kind : 3 + kind, width_one : width_one + 1] = jnp.full((1, 1), 40.0, jnp.float32)
    for row, source in ((4, fit_one_b), (5, fit_two_b), (6, fit_three_b)):
        rows[row : row + 1, 0:hidden] = source[...]
    columns_ref[...] = jnp.transpose(rows[...])

    square[...] = jnp.zeros_like(square)
    for k in range(2):
        square[0:width_one, k * ROW_PAD : k * ROW_PAD + width_one] = embed_two_w[
            :, k * width_one : (k + 1) * width_one
        ]
        square[
            width_one : width_one + 1, k * ROW_PAD : k * ROW_PAD + width_one
        ] = embed_two_b[:, k * width_one : (k + 1) * width_one]
    high, low = split(jnp.transpose(square[0:128, 0:128])[0 : 2 * ROW_PAD, 0:ROW_PAD])
    second_ref[...] = jnp.concatenate([high, high, low], axis=1)
    square[0:128, 0:128] = jnp.zeros((128, 128), jnp.float32)
    for g in range(2):
        for k in range(4):
            square[
                g * ROW_PAD : g * ROW_PAD + width_one, k * ROW_PAD : k * ROW_PAD + width_one
            ] = embed_three_w[
                g * width_one : (g + 1) * width_one, k * width_one : (k + 1) * width_one
            ]
    for k in range(4):
        square[
            width_one : width_one + 1, k * ROW_PAD : k * ROW_PAD + width_one
        ] = embed_three_b[:, k * width_one : (k + 1) * width_one]
    high, low = split(jnp.transpose(square[0:128, 0:128])[:, 0 : 2 * ROW_PAD])
    third_ref[...] = jnp.concatenate([high, high, low], axis=1)
    for copy in copies[11:13]:
        copy.wait()
    for source, high_ref, low_ref in (
        (fit_two_w, two_high_ref, two_low_ref),
        (fit_three_w, three_high_ref, three_low_ref),
    ):
        square[0:hidden, 0:hidden] = source[...]
        high_ref[...], low_ref[...] = split(jnp.transpose(square[...])[0:hidden, 0:hidden])

    fine = GRID_Y // 2 // pieces
    shape = (phase_ref.shape[0], 128)
    row = lax.broadcasted_iota(jnp.int32, shape, 0)
    mode = piece * fine + row // 2
    for part in range(GRID_Y // 128):
        cell = lax.broadcasted_iota(jnp.int32, shape, 1) + part * 128
        spot = lax.rem(mode * cell, GRID_Y)
        cosine = lookup(constants[0:1, :], spot)
        sine = lookup(constants[1:2, :], spot)
        alternate = (1 - 2 * lax.rem(cell, 2)).astype(jnp.float32)
        odd = jnp.where(mode == 0, alternate, -sine)
        value = jnp.where(lax.rem(row, 2) == 0, cosine, odd)
        phase_ref[:, part * 128 : (part + 1) * 128] = jnp.where(row < 2 * fine, value, 0.0)

    column = jnp.transpose(constants[...])
    lane = lax.broadcasted_iota(jnp.int32, (1, GRID_Y), 1)
    for j in range(fine + 1):
        here = lane == (GRID_Y // 2 if j == fine else piece * fine + j)
        factor = jnp.sum(jnp.where(here, constants[2:3, :], 0.0), axis=1, keepdims=True)
        part = jnp.sum(jnp.where(here, constants[3:4, :], 0.0), axis=1, keepdims=True)
        wave = (part + constants[5:6, :]) + column[:, 7:8]
        top = (factor * constants[4:5, :]) * column[:, 6:7]
        green_ref[j] = jnp.where(wave == 0.0, 0.0, top / jnp.where(wave == 0.0, 1.0, wave))

    copies[13].wait()
    one_high_ref[...], one_low_ref[...] = split(fit_one_w[...])


def centroid_kernel(
    table,
    codes,
    columns,
    second,
    third,
    one_high,
    one_low,
    two_high,
    two_low,
    three_high,
    three_low,
    fit_out_w,
    dipole_ref,
    shift_ref,
    matrix,
    descriptor,
    arrivals,
    *held,
):
    sources = (table, codes, columns, second, third)
    sources += (one_high, one_low, two_high, two_low, three_high, three_low, fit_out_w)
    copies = [
        pltpu.make_async_copy(source, target, arrivals.at[k])
        for k, (source, target) in enumerate(zip(sources, held))
    ]
    for copy in copies:
        copy.start()
    table, codes, columns, second, third = held[:5]
    one_high, one_low, two_high, two_low, three_high, three_low, fit_out_w = held[5:]
    for copy in copies[:5]:
        copy.wait()
    wide_count, narrow_count, _, atoms = table.shape
    listed = codes.shape[0]
    width_three = fit_out_w.shape[0]
    width_one = width_three // 4
    hidden_width = two_high.shape[0]
    cells = (GRID_X // wide_count, GRID_Y, GRID_Z // narrow_count)
    at_wide = lax.axis_index("wide")
    at_narrow = lax.axis_index("narrow")
    own = jnp.abs(table[at_wide, at_narrow])
    nearby = []
    for step in range(9):
        wide_at = lax.rem(at_wide + (step // 3 - 1) + wide_count, wide_count)
        narrow_at = lax.rem(at_narrow + (step % 3 - 1) + narrow_count, narrow_count)
        nearby.append(table[wide_at, narrow_at])

    second_all = second[...]
    third_all = third[...]
    weight_oxygen = jnp.broadcast_to(columns[0:ROW_PAD, 0:1], (ROW_PAD, atoms))
    weight_hydrogen = jnp.broadcast_to(columns[0:ROW_PAD, 1:2], (ROW_PAD, atoms))
    bias_oxygen = jnp.broadcast_to(columns[0:ROW_PAD, 2:3], (ROW_PAD, atoms))
    bias_hydrogen = jnp.broadcast_to(columns[0:ROW_PAD, 3:4], (ROW_PAD, atoms))
    matrix[...] = jnp.zeros_like(matrix)

    def chunk(first):
        code = codes[pl.ds(first, SLOT_CHUNK), :]
        offset = code // atoms
        slot = code - offset * atoms
        step_x = jnp.where(offset >= 9, 1, 0) + jnp.where(offset >= 18, 1, 0)
        rest = offset - 9 * step_x
        step_z = jnp.where(rest >= 3, 1, 0) + jnp.where(rest >= 6, 1, 0)
        step_y = rest - 3 * step_z
        brick = step_x * 3 + step_z
        found = []
        for component in range(3):
            picked = jnp.zeros((SLOT_CHUNK, atoms), jnp.float32)
            for step in range(9):
                row = jnp.broadcast_to(
                    nearby[step][component : component + 1], (SLOT_CHUNK, atoms)
                )
                here = jnp.take_along_axis(row, slot, axis=1, mode="promise_in_bounds")
                picked = jnp.where(brick == step, here, picked)
            found.append(picked)
        hydrogen = found[0] < 0.0
        found[0] = jnp.abs(found[0])
        scaled = []
        for component, step in enumerate((step_x, step_y, step_z)):
            extent = float(cells[component])
            relative = (step - 1).astype(jnp.float32) * extent + (
                found[component] - own[component : component + 1]
            ) * extent
            scaled.append(relative * (1.0 / radius_scale))
        smooth = 1.0 / (
            1.0 + (scaled[0] * scaled[0] + scaled[1] * scaled[1] + scaled[2] * scaled[2])
        )
        radial = [smooth] + [smooth * part for part in scaled]
        first_layers = []
        for k in range(SLOT_CHUNK):
            row = smooth[k : k + 1]
            kind = hydrogen[k : k + 1]
            weight = jnp.where(kind, weight_hydrogen, weight_oxygen)
            bias = jnp.where(kind, bias_hydrogen, bias_oxygen)
            first_layers.append(jnp.tanh(weight * row + bias))
        layer_one = jnp.concatenate(first_layers, axis=1)
        high, low = split(layer_one)
        layer_two = lax.dot_general(
            second_all,
            jnp.concatenate([high, low, high], axis=0),
            NN,
            preferred_element_type=jnp.float32,
        )
        layer_two = jnp.tanh(layer_two) + jnp.concatenate(
            [layer_one, layer_one], axis=0
        )
        high, low = split(layer_two)
        layer_three = lax.dot_general(
            third_all,
            jnp.concatenate([high, low, high], axis=0),
            NN,
            preferred_element_type=jnp.float32,
        )
        layer_three = jnp.tanh(layer_three) + jnp.concatenate(
            [layer_two, layer_two], axis=0
        )
        for part in range(4):
            total = matrix[part]
            for k in range(SLOT_CHUNK):
                total = total + layer_three[:, k * atoms : (k + 1) * atoms] * radial[part][k : k + 1]
            matrix[part] = total

    def two_chunks(index, carry):
        first = pl.multiple_of(index * (2 * SLOT_CHUNK), 2 * SLOT_CHUNK)
        chunk(first)
        chunk(pl.multiple_of(first + SLOT_CHUNK, SLOT_CHUNK))
        return carry

    lax.fori_loop(0, listed // (2 * SLOT_CHUNK), two_chunks, 0)

    parts = []
    for part in range(4):
        padded = matrix[part] * (1.0 / listed)
        parts.append(
            jnp.concatenate(
                [padded[k * ROW_PAD : k * ROW_PAD + width_one] for k in range(4)], axis=0
            )
        )
    leading = [part[0:AXIS_COLUMNS] for part in parts]
    for row in range(width_three):
        total = parts[0][row : row + 1] * leading[0]
        for part in range(1, 4):
            total = total + parts[part][row : row + 1] * leading[part]
        descriptor[row * AXIS_COLUMNS : (row + 1) * AXIS_COLUMNS, :] = total
    for copy in copies[5:]:
        copy.wait()

    def layer(high_ref, low_ref, given, column):
        weights = (high_ref[...], low_ref[...])
        return jnp.tanh(multiply(weights, split(given)) + columns[0:hidden_width, column : column + 1])

    hidden = layer(one_high, one_low, descriptor[...], 4)
    hidden = hidden + layer(two_high, two_low, hidden, 5)
    hidden = hidden + layer(three_high, three_low, hidden, 6)
    coeffs = multiply(split(fit_out_w[...]), split(hidden))
    vector = jnp.concatenate(
        [jnp.sum(coeffs * parts[1 + c], axis=0, keepdims=True) for c in range(3)], axis=0
    )
    oxygen = 1.0 - own[3:4]
    for c in range(3):
        dipole_ref[c] = vector[c : c + 1] * oxygen
    moved = wannier_reach * jnp.tanh(vector)
    moved = jnp.concatenate([moved, jnp.zeros((1, atoms), jnp.float32)], axis=0)
    for target in range(shift_ref.shape[0]):
        shift_ref[target] = moved


def mesh_kernel(
    table,
    shifts,
    phase,
    green_ref,
    fold_high,
    fold_low,
    unfold_high,
    unfold_low,
    out_ref,
    grid,
    planes,
    packed,
    weights,
    slopes,
    weights_z,
    waves,
    wave_slopes,
):
    wide_count, narrow_count, _, atoms = table.shape
    cells_x = GRID_X // wide_count
    cells_z = GRID_Z // narrow_count
    window = cells_z + HALO_Z
    reach = cells_x + HALO_X
    pair = 2 * atoms
    length = wide_count * pair
    copies = grid.shape[0]
    fine = grid.shape[1]
    channels = 2 * fine
    rows = phase.shape[0]
    half_x = GRID_X // 2
    half_z = GRID_Z // 2
    piece = lax.axis_index("wide") * narrow_count + lax.axis_index("narrow")
    lane_zero = lax.broadcasted_iota(jnp.int32, (1, half_x), 1) == 0
    row_zero = lax.broadcasted_iota(jnp.int32, (half_z, 1), 0) == 0

    def fold():
        return (fold_high[...], fold_low[...])

    def unfold():
        return (unfold_high[...], unfold_low[...])

    def sites(at_wide, at_narrow):
        atom = jnp.abs(table[at_wide, at_narrow])
        moved = shifts[at_wide, at_narrow]
        found = []
        for component, extent in enumerate((cells_x, GRID_Y, cells_z)):
            start = atom[component : component + 1] * float(extent)
            found.append(jnp.concatenate([start, start + moved[component : component + 1]], axis=1))
        oxygen = 1.0 - atom[3:4]
        found.append(jnp.concatenate([6.0 * oxygen + atom[3:4], -8.0 * oxygen], axis=1))
        return found

    def line(at_narrow):
        groups = [sites(at_wide, at_narrow) for at_wide in range(wide_count)]
        return [jnp.concatenate([g[k] for g in groups], axis=1) for k in range(4)]

    def splines_z(row):
        counter = lax.broadcasted_iota(jnp.int32, (window, 1), 0).astype(jnp.float32)
        return spline_pair(row - (counter - float(HALO_Z)))

    def fill_x(row, targets):
        counter = lax.broadcasted_iota(jnp.int32, (reach, 1), 0).astype(jnp.float32)
        both = spline_pair(row - (counter - float(HALO_X)))
        rest = jnp.zeros((128 - reach, length), jnp.bfloat16)
        for values, ref in zip(both, targets):
            if ref is not None:
                high, low = split(values)
                ref[0:reach, :] = high
                ref[reach:128, :] = rest
                ref[128 : 128 + reach, :] = low
                ref[128 + reach : 256, :] = rest

    grid[:, :, 0:HALO_Z, :] = jnp.zeros((copies, fine, HALO_Z, 2 * GRID_X), jnp.float32)

    def spread(at_narrow):
        row_x, row_y, row_z, charge = line(at_narrow)
        lower = jnp.floor(row_y)
        back = lax.broadcasted_iota(jnp.int32, (8, 1), 0)
        value_y, slope_y = spline_pair((row_y - lower) + back.astype(jnp.float32))
        cell = lax.rem(lower.astype(jnp.int32) - back + GRID_Y, GRID_Y)
        wave_blocks = []
        slope_blocks = []
        for block in range(length // 128):
            lanes = slice(block * 128, (block + 1) * 128)
            wave = jnp.zeros((rows, 128), jnp.float32)
            wave_slope = jnp.zeros((rows, 128), jnp.float32)
            for k in range(4):
                spot = jnp.broadcast_to(cell[k : k + 1, lanes], (rows, 128))
                found = lookup(phase[...], spot)
                wave = wave + value_y[k : k + 1, lanes] * found
                wave_slope = wave_slope + slope_y[k : k + 1, lanes] * found
            wave_blocks.append(wave)
            slope_blocks.append(wave_slope)
        wave = jnp.concatenate(wave_blocks, axis=1)
        waves[at_narrow] = wave
        wave_slopes[at_narrow] = jnp.concatenate(slope_blocks, axis=1)
        fill_x(row_x, (weights.at[at_narrow], None))
        value_z, _ = splines_z(row_z)
        weights_z[at_narrow] = value_z
        charged = wave * charge
        first = pl.multiple_of(at_narrow * cells_z, HALO_Z)
        for at_wide in range(wide_count):
            lanes = slice(at_wide * pair, (at_wide + 1) * pair)
            near = value_z[:, lanes]
            left = jnp.concatenate(
                [near * charged[c : c + 1, lanes] for c in range(channels)], axis=0
            )
            high, low = split(left)
            across = weights[at_narrow, :, lanes]
            total = lax.dot_general(high, across, NT, preferred_element_type=jnp.float32)
            total = total[:, 0:128] + (
                total[:, 128:256]
                + lax.dot_general(low, across[0:128], NT, preferred_element_type=jnp.float32)
            )
            start = at_wide // copies * 128
            for c in range(channels):
                spot = slice(c % 2 * GRID_X + start, c % 2 * GRID_X + start + 128)
                k = at_wide % copies
                part = total[c * window : (c + 1) * window]
                grid[k, c // 2, pl.ds(first, HALO_Z), spot] += part[:HALO_Z]
                grid[k, c // 2, pl.ds(first + HALO_Z, cells_z), spot] = part[HALO_Z:]

    def in_pairs(step):
        def both(index, carry):
            step(2 * index, 0)
            step(2 * index + 1, 1)
            return carry

        lax.fori_loop(0, narrow_count // 2, both, 0)

    in_pairs(lambda at_narrow, _: spread(at_narrow))

    def gather(j, carry):
        for lanes in (slice(0, GRID_X), slice(GRID_X, 2 * GRID_X)):
            total = None
            for k in range(copies):
                moved = pltpu.roll(grid[k, j, :, lanes], (k * cells_x - HALO_X) % GRID_X, 1)
                total = moved if total is None else total + moved
            planes[j, :, lanes] = total[HALO_Z:]
            planes[j, GRID_Z - HALO_Z :, lanes] += total[:HALO_Z]
        return carry

    lax.fori_loop(0, fine, gather, 0)
    is_first = piece == 0

    def paired(real, imag, zero, axis):
        half = real.shape[axis] // 2
        first = (slice(None),) * axis + (slice(0, half),)
        second = (slice(None),) * axis + (slice(half, 2 * half),)
        real_c, real_s = real[first], real[second]
        if imag is None:
            none = jnp.zeros_like(real_s)
            real_all = [real_c, jnp.where(zero, real_s, real_c)]
            imag_all = [jnp.where(zero, none, -real_s), jnp.where(zero, none, real_s)]
        else:
            imag_c, imag_s = imag[first], imag[second]
            real_all = [
                real_c + jnp.where(zero, 0.0, imag_s),
                jnp.where(zero, real_s, real_c - imag_s),
            ]
            imag_all = [
                imag_c - jnp.where(zero, 0.0, real_s),
                jnp.where(zero, imag_s, imag_c + real_s),
            ]
        return jnp.concatenate(real_all, axis=axis), jnp.concatenate(imag_all, axis=axis)

    def merged(real, imag, zero, axis):
        half = real.shape[axis] // 2
        first = (slice(None),) * axis + (slice(0, half),)
        second = (slice(None),) * axis + (slice(half, 2 * half),)
        real_a, real_b = real[first], real[second]
        imag_a, imag_b = imag[first], imag[second]
        real = [
            real_a + jnp.where(zero, 0.0, real_b),
            jnp.where(zero, real_b, imag_b - imag_a),
        ]
        imag = [
            imag_a + jnp.where(zero, 0.0, imag_b),
            jnp.where(zero, imag_b, real_a - real_b),
        ]
        return jnp.concatenate(real, axis=axis), jnp.concatenate(imag, axis=axis)

    def to_modes(real, imag, j):
        real = multiply(split(real), fold())
        if imag is not None:
            imag = multiply(split(imag), fold())
        real, imag = paired(real, imag, lane_zero, 1)
        real = multiply(unfold(), split(real))
        imag = multiply(unfold(), split(imag))
        real, imag = paired(real, imag, row_zero, 0)
        green = green_ref[j]
        mode = GRID_Y // 2 if j == fine else piece * fine + j
        share = jnp.where((mode == 0) | (mode == GRID_Y // 2), 0.5, 1.0)
        part = jnp.sum(green * (real * real + imag * imag), axis=0, keepdims=True)
        return green * real, green * imag, share * part

    second_plane = jnp.where(is_first, planes[0, :, GRID_X:], 0.0)
    last_real, last_imag, energy = to_modes(second_plane, None, fine)
    for j in range(fine):
        imag = planes[j, :, GRID_X:]
        if j == 0:
            imag = jnp.where(is_first, 0.0, imag)
        real, imag, part = to_modes(planes[j, :, 0:GRID_X], imag, j)
        energy = energy + part
        if j == 0:
            real, imag = real - last_imag, imag + last_real
        real, imag = merged(real, imag, row_zero, 0)
        real = multiply(fold(), split(real))
        imag = multiply(fold(), split(imag))
        real, imag = merged(real, imag, lane_zero, 1)
        scale = jnp.where(piece * fine + j == 0, 1.0, 2.0)
        for part, lanes in ((real, slice(0, GRID_X)), (imag, slice(GRID_X, 2 * GRID_X))):
            part = multiply(split(part * scale), unfold())
            channel = 2 * j + (0 if lanes.start == 0 else 1)
            for at_wide in range(wide_count):
                moved = pltpu.roll(part, (HALO_X - at_wide * cells_x) % GRID_X, 1)[:, 0:128]
                high = moved.astype(jnp.bfloat16).astype(jnp.float32)
                again = pltpu.roll(high, reach % 128, 1)
                low = pltpu.roll(moved - high, 2 * reach % 128, 1)
                sides = []
                for side in range(2):
                    lane = lax.broadcasted_iota(jnp.int32, (1, 128), 1) + side * 128
                    value = jnp.where(lane < 2 * reach, again, low)
                    if side == 0:
                        value = jnp.where(lane < reach, high, value)
                    sides.append(value.astype(jnp.bfloat16))
                block = jnp.concatenate(sides, axis=1)
                packed[at_wide, channel, HALO_BITS:, :] = block
                packed[at_wide, channel, 0:HALO_BITS, :] = block[GRID_Z - HALO_BITS :]
    energy = jnp.broadcast_to(jnp.sum(energy, axis=1, keepdims=True), (1, 128))

    def collect(at_narrow, buffer):
        row_x, _, row_z, _ = line(at_narrow)
        fill_x(row_x, (None, slopes.at[buffer]))
        value_z = weights_z[at_narrow]
        _, slope_z = splines_z(row_z)
        first = pl.multiple_of(at_narrow * cells_z, HALO_BITS)
        wave = waves[at_narrow]
        wave_slope = wave_slopes[at_narrow]
        for at_wide in range(wide_count):
            lanes = slice(at_wide * pair, (at_wide + 1) * pair)
            tall = cells_z + HALO_BITS
            left = jnp.concatenate(
                [packed[at_wide, c, pl.ds(first, tall), :] for c in range(channels)], axis=0
            )

            def across(right):
                high = right[0:reach]
                rest = jnp.zeros((256 - 3 * reach, pair), jnp.bfloat16)
                right = jnp.concatenate([high, right[128 : 128 + reach], high, rest], axis=0)
                return lax.dot_general(left, right, NN, preferred_element_type=jnp.float32)

            value = across(weights[at_narrow, :, lanes])
            slope = across(slopes[buffer, :, lanes])
            plain = jnp.zeros((window, pair), jnp.float32)
            along_x = plain
            along_y = plain
            for c in range(channels):
                block = slice((c + 1) * tall - window, (c + 1) * tall)
                plain = plain + value[block] * wave[c : c + 1, lanes]
                along_x = along_x + slope[block] * wave[c : c + 1, lanes]
                along_y = along_y + value[block] * wave_slope[c : c + 1, lanes]
            near = value_z[:, lanes]
            near_slope = slope_z[:, lanes]
            results = [
                jnp.sum(near * plain, axis=0, keepdims=True),
                -jnp.sum(near * along_x, axis=0, keepdims=True),
                -jnp.sum(near * along_y, axis=0, keepdims=True),
                -jnp.sum(near_slope * plain, axis=0, keepdims=True),
            ]
            for k, row in enumerate(results):
                out_ref[at_wide, at_narrow, :, k * pair : (k + 1) * pair] = row
            out_ref[at_wide, at_narrow, :, 4 * pair :] = energy

    in_pairs(collect)


def finish_kernel(arrived, species, atom_ref, centroid_ref, energy_ref):
    atoms = species.shape[1]
    total = arrived[0]
    for k in range(1, arrived.shape[0]):
        total = total + arrived[k]
    oxygen = 1.0 - species[...].astype(jnp.float32)
    for k in range(4):
        atom_ref[k] = total[:, 2 * k * atoms : (2 * k + 1) * atoms]
        centroid_ref[k] = total[:, (2 * k + 1) * atoms : (2 * k + 2) * atoms] * oxygen
    energy_ref[...] = total[:, 8 * atoms :] * (1.0 / (atoms * arrived.shape[0]))


def mode_factors(length, order):
    wrapped = np.where(2 * order >= length, order - length, order)
    square = (wrapped / length) ** 2
    ratio = (4.0 + 2.0 * np.cos(2.0 * math.pi * order / length)) / 6.0
    return np.stack([np.exp(-(math.pi**2) * square / ewald_beta**2) / ratio**2, square])


def folded_order(length):
    half = length // 2
    counter = np.arange(half)
    return np.concatenate([counter, np.where(counter == 0, half, length - counter)])


def fold_table(length):
    half = length // 2
    turns = np.outer(np.arange(length), np.arange(half)) % length * (2.0 * math.pi / length)
    sines = np.sin(turns)
    sines[:, 0] = 1.0 - 2.0 * (np.arange(length) % 2)
    return np.concatenate([np.cos(turns), sines], axis=1)


def halves(table):
    high = table.astype(jnp.bfloat16)
    low = (table - high.astype(np.float64)).astype(jnp.bfloat16)
    return high, low


def vmem(count):
    return [pl.BlockSpec(memory_space=pltpu.VMEM)] * count


def hbm(count):
    return [pl.BlockSpec(memory_space=pltpu.HBM)] * count


def shaped(shape, dtype=jnp.float32):
    return jax.ShapeDtypeStruct(shape, dtype)


def limits(mebibytes):
    return pltpu.CompilerParams(vmem_limit_bytes=mebibytes * 1024 * 1024)


def local(
    positions,
    species,
    neighbours,
    embed_one_w,
    embed_one_b,
    embed_two_w,
    embed_two_b,
    embed_three_w,
    embed_three_b,
    fit_one_w,
    fit_one_b,
    fit_two_w,
    fit_two_b,
    fit_three_w,
    fit_three_b,
    fit_out_w,
):
    axes = ("wide", "narrow")
    wide_count = lax.axis_size("wide")
    narrow_count = lax.axis_size("narrow")
    pieces = wide_count * narrow_count
    atoms = positions.shape[4]
    listed = neighbours.shape[4]
    fine = GRID_Y // 2 // pieces
    width_three = embed_three_w.shape[1]
    entries, hidden = fit_one_w.shape
    kinds = species.reshape(1, atoms)

    packed = pl.pallas_call(
        pack_kernel,
        out_shape=shaped((pieces, 4, atoms)),
        in_specs=vmem(2),
        out_specs=vmem(1)[0],
        name="pack",
    )(positions.reshape(3, 1, atoms), kinds)
    table = lax.all_to_all(packed, axes, 0, 0, tiled=True)
    table = table.reshape(wide_count, narrow_count, 4, atoms)

    tall = 4 * ROW_PAD
    bf16 = jnp.bfloat16
    wave_rows = -(-2 * fine // 8) * 8
    angle = np.arange(GRID_Y) * (2.0 * math.pi / GRID_Y)
    constants = np.concatenate(
        [
            np.stack([np.cos(angle), np.sin(angle)]),
            mode_factors(GRID_Y, np.arange(GRID_Y)),
            mode_factors(GRID_X, folded_order(GRID_X)),
            mode_factors(GRID_Z, folded_order(GRID_Z)),
        ]
    )
    constants[2] *= coulomb / (math.pi * GRID_X * GRID_Y * GRID_Z)
    arguments = (
        neighbours.reshape(atoms, listed),
        embed_one_w,
        embed_one_b,
        embed_two_w,
        embed_two_b[None],
        embed_three_w,
        embed_three_b[None],
        fit_one_w.T,
        fit_one_b[None],
        fit_two_w,
        fit_two_b[None],
        fit_three_w,
        fit_three_b[None],
        jnp.asarray(constants, jnp.float32),
    )
    held = [arguments[k] for k in (0, 1, 2, 3, 4, 5, 6, 8, 10, 12, 13, 9, 11, 7)]
    prepared = pl.pallas_call(
        prepare_kernel,
        out_shape=(
            shaped((listed, atoms), jnp.int32),
            shaped((256, 16)),
            shaped((2 * ROW_PAD, 3 * ROW_PAD), bf16),
            shaped((tall, 6 * ROW_PAD), bf16),
            shaped((hidden, entries), bf16),
            shaped((hidden, entries), bf16),
        )
        + (shaped((hidden, hidden), bf16),) * 4
        + (shaped((wave_rows, GRID_Y)), shaped((fine + 1, GRID_Z, GRID_X))),
        in_specs=hbm(len(arguments)),
        out_specs=tuple(vmem(12)),
        scratch_shapes=[
            pltpu.VMEM((16, 256), jnp.float32),
            pltpu.VMEM((256, 256), jnp.float32),
            pltpu.SemaphoreType.DMA((len(held),)),
        ]
        + [pltpu.VMEM(array.shape, array.dtype) for array in held],
        compiler_params=limits(62),
        cost_estimate=pl.CostEstimate(
            flops=1000000, bytes_accessed=8 * entries * hidden, transcendentals=0
        ),
        name="prepare",
    )(*arguments)
    phase, green = prepared[10:]
    fitted = (table, *prepared[:10], fit_out_w.T)
    dipole, shifts = pl.pallas_call(
        centroid_kernel,
        out_shape=(shaped((3, 1, atoms)), shaped((pieces, 4, atoms))),
        in_specs=hbm(12),
        out_specs=tuple(vmem(2)),
        scratch_shapes=[
            pltpu.VMEM((4, tall, atoms), jnp.float32),
            pltpu.VMEM((width_three * AXIS_COLUMNS, atoms), jnp.float32),
            pltpu.SemaphoreType.DMA((len(fitted),)),
        ]
        + [pltpu.VMEM(array.shape, array.dtype) for array in fitted],
        compiler_params=limits(62),
        name="centroids",
    )(*fitted)
    shifts = lax.all_to_all(shifts, axes, 0, 0, tiled=True)
    shifts = shifts.reshape(wide_count, narrow_count, 4, atoms)

    cells_x = GRID_X // wide_count
    copies = 128 // cells_x
    length = wide_count * 2 * atoms
    out_width = 8 * atoms + 128
    partial = pl.pallas_call(
        mesh_kernel,
        out_shape=shaped((wide_count, narrow_count, 1, out_width)),
        in_specs=vmem(8),
        out_specs=vmem(1)[0],
        scratch_shapes=[
            pltpu.VMEM((copies, fine, HALO_Z + GRID_Z, 2 * GRID_X), jnp.float32),
            pltpu.VMEM((fine, GRID_Z, 2 * GRID_X), jnp.float32),
            pltpu.VMEM((wide_count, 2 * fine, HALO_BITS + GRID_Z, 256), bf16),
        ]
        + [pltpu.VMEM((narrow_count, 256, length), bf16), pltpu.VMEM((2, 256, length), bf16)]
        + [pltpu.VMEM((narrow_count, GRID_Z // narrow_count + HALO_Z, length), jnp.float32)]
        + [pltpu.VMEM((narrow_count, wave_rows, length), jnp.float32)] * 2,
        compiler_params=limits(48),
        name="mesh",
    )(
        table,
        shifts,
        phase,
        green,
        *[jnp.asarray(half) for half in halves(fold_table(GRID_X))],
        *[jnp.asarray(half) for half in halves(fold_table(GRID_X).T)],
    )
    arrived = lax.all_to_all(partial.reshape(pieces, 1, out_width), axes, 0, 0, tiled=True)
    atom_field, centroid_field, energy = pl.pallas_call(
        finish_kernel,
        out_shape=(shaped((4, 1, atoms)), shaped((4, 1, atoms)), shaped((1, 128))),
        in_specs=vmem(2),
        out_specs=tuple(vmem(3)),
        name="finish",
    )(arrived, kinds)
    atom_field = atom_field.reshape(4, 1, 1, 1, atoms)
    centroid_field = centroid_field.reshape(4, 1, 1, 1, atoms)
    return (dipole.reshape(3, 1, 1, 1, atoms), atom_field, centroid_field, energy[0, 0])


def solution(mesh):
    column = P(None, "wide", "narrow", None, None)
    in_specs = (column, P("wide", "narrow", None, None), P("wide", "narrow", None, None, None))
    in_specs = in_specs + (P(),) * 13
    out_specs = (column, column, column, P())
    return jax.shard_map(local, mesh=mesh, in_specs=in_specs, out_specs=out_specs, check_vma=False)
```

```python
import math

import jax
import jax.numpy as jnp
import numpy as np
from jax import lax
from jax.experimental import pallas as pl
from jax.experimental.pallas import tpu as pltpu
from jax.sharding import PartitionSpec as P

GRID_X = 256
GRID_Y = 256
GRID_Z = 256
AXIS_COLUMNS = 16

radius_scale = 24.0
wannier_reach = 0.5
ewald_beta = 0.9
coulomb = 0.25

ROW_PAD = 32
SLOT_CHUNK = 16
HALO_X = 16
HALO_Z = 8
HALO_BITS = 16

NN = (((1,), (0,)), ((), ()))
NT = (((1,), (1,)), ((), ()))


def split(value):
    high = value.astype(jnp.bfloat16)
    low = (value - high.astype(jnp.float32)).astype(jnp.bfloat16)
    return high, low


def multiply(left, right, dims=NN):
    def one(a, b):
        return lax.dot_general(a, b, dims, preferred_element_type=jnp.float32)

    return one(left[0], right[0]) + (one(left[1], right[0]) + one(left[0], right[1]))


def spline_pair(offset):
    centred = offset - 2.0
    away = jnp.abs(centred)
    outer = jnp.maximum(2.0 - away, 0.0)
    inner = jnp.maximum(1.0 - away, 0.0)
    outer_square = outer * outer
    inner_square = inner * inner
    value = (outer_square * outer - 4.0 * (inner_square * inner)) * (1.0 / 6.0)
    slope = jnp.where(centred < 0.0, 0.5, -0.5) * (outer_square - 4.0 * inner_square)
    return value, slope


def lookup(row_table, spot):
    found = None
    for part in range(row_table.shape[1] // 128):
        inside = spot // 128 == part
        here = jnp.take_along_axis(
            jnp.broadcast_to(row_table[:, part * 128 : (part + 1) * 128], spot.shape),
            lax.rem(spot, 128),
            axis=1,
            mode="promise_in_bounds",
        )
        found = here if found is None else jnp.where(inside, here, found)
    return found


def pack_kernel(positions, species, out_ref):
    kinds = species[...]
    rows = [positions[component] for component in range(3)]
    rows[0] = jnp.where(kinds > 0, -rows[0], rows[0])
    rows.append(kinds.astype(jnp.float32))
    rows = jnp.concatenate(rows, axis=0)
    for target in range(out_ref.shape[0]):
        out_ref[target] = rows


def prepare_kernel(
    neighbours,
    embed_one_w,
    embed_one_b,
    embed_two_w,
    embed_two_b,
    embed_three_w,
    embed_three_b,
    fit_one_w,
    fit_one_b,
    fit_two_w,
    fit_two_b,
    fit_three_w,
    fit_three_b,
    constants,
    codes_ref,
    columns_ref,
    second_ref,
    third_ref,
    one_high_ref,
    one_low_ref,
    two_high_ref,
    two_low_ref,
    three_high_ref,
    three_low_ref,
    phase_ref,
    green_ref,
    rows,
    square,
    arrivals,
    *held,
):
    sources = (
        neighbours,
        embed_one_w,
        embed_one_b,
        embed_two_w,
        embed_two_b,
        embed_three_w,
        embed_three_b,
        fit_one_b,
        fit_two_b,
        fit_three_b,
        constants,
        fit_two_w,
        fit_three_w,
        fit_one_w,
    )
    copies = [
        pltpu.make_async_copy(source, target, arrivals.at[k])
        for k, (source, target) in enumerate(zip(sources, held))
    ]
    for copy in copies:
        copy.start()
    (
        neighbours,
        embed_one_w,
        embed_one_b,
        embed_two_w,
        embed_two_b,
        embed_three_w,
        embed_three_b,
        fit_one_b,
        fit_two_b,
        fit_three_b,
        constants,
        fit_two_w,
        fit_three_w,
        fit_one_w,
    ) = held
    for copy in copies[:11]:
        copy.wait()
    pieces = lax.axis_size("wide") * lax.axis_size("narrow")
    piece = lax.axis_index("wide") * lax.axis_size("narrow") + lax.axis_index("narrow")
    width_one = embed_one_w.shape[1]
    hidden = fit_two_w.shape[0]
    codes_ref[...] = jnp.transpose(neighbours[...].astype(jnp.float32)).astype(jnp.int32)
    rows[...] = jnp.zeros_like(rows)
    for kind in range(2):
        rows[kind : kind + 1, 0:width_one] = embed_one_w[kind : kind + 1, :]
        rows[2 + kind : 3 + kind, 0:width_one] = embed_one_b[kind : kind + 1, :]
        rows[2 + kind : 3 + kind, width_one : width_one + 1] = jnp.full((1, 1), 40.0, jnp.float32)
    for row, source in ((4, fit_one_b), (5, fit_two_b), (6, fit_three_b)):
        rows[row : row + 1, 0:hidden] = source[...]
    columns_ref[...] = jnp.transpose(rows[...])

    square[...] = jnp.zeros_like(square)
    for k in range(2):
        square[0:width_one, k * ROW_PAD : k * ROW_PAD + width_one] = embed_two_w[
            :, k * width_one : (k + 1) * width_one
        ]
        square[
            width_one : width_one + 1, k * ROW_PAD : k * ROW_PAD + width_one
        ] = embed_two_b[:, k * width_one : (k + 1) * width_one]
    high, low = split(jnp.transpose(square[0:128, 0:128])[0 : 2 * ROW_PAD, 0:ROW_PAD])
    second_ref[...] = jnp.concatenate([high, high, low], axis=1)
    square[0:128, 0:128] = jnp.zeros((128, 128), jnp.float32)
    for g in range(2):
        for k in range(4):
            square[
                g * ROW_PAD : g * ROW_PAD + width_one, k * ROW_PAD : k * ROW_PAD + width_one
            ] = embed_three_w[
                g * width_one : (g + 1) * width_one, k * width_one : (k + 1) * width_one
            ]
    for k in range(4):
        square[
            width_one : width_one + 1, k * ROW_PAD : k * ROW_PAD + width_one
        ] = embed_three_b[:, k * width_one : (k + 1) * width_one]
    high, low = split(jnp.transpose(square[0:128, 0:128])[:, 0 : 2 * ROW_PAD])
    third_ref[...] = jnp.concatenate([high, high, low], axis=1)
    for copy in copies[11:13]:
        copy.wait()
    for source, high_ref, low_ref in (
        (fit_two_w, two_high_ref, two_low_ref),
        (fit_three_w, three_high_ref, three_low_ref),
    ):
        square[0:hidden, 0:hidden] = source[...]
        high_ref[...], low_ref[...] = split(jnp.transpose(square[...])[0:hidden, 0:hidden])

    fine = GRID_Y // 2 // pieces
    shape = (phase_ref.shape[0], 128)
    row = lax.broadcasted_iota(jnp.int32, shape, 0)
    mode = piece * fine + row // 2
    for part in range(GRID_Y // 128):
        cell = lax.broadcasted_iota(jnp.int32, shape, 1) + part * 128
        spot = lax.rem(mode * cell, GRID_Y)
        cosine = lookup(constants[0:1, :], spot)
        sine = lookup(constants[1:2, :], spot)
        alternate = (1 - 2 * lax.rem(cell, 2)).astype(jnp.float32)
        odd = jnp.where(mode == 0, alternate, -sine)
        value = jnp.where(lax.rem(row, 2) == 0, cosine, odd)
        phase_ref[:, part * 128 : (part + 1) * 128] = jnp.where(row < 2 * fine, value, 0.0)

    column = jnp.transpose(constants[...])
    lane = lax.broadcasted_iota(jnp.int32, (1, GRID_Y), 1)
    for j in range(fine + 1):
        here = lane == (GRID_Y // 2 if j == fine else piece * fine + j)
        factor = jnp.sum(jnp.where(here, constants[2:3, :], 0.0), axis=1, keepdims=True)
        part = jnp.sum(jnp.where(here, constants[3:4, :], 0.0), axis=1, keepdims=True)
        wave = (part + constants[5:6, :]) + column[:, 7:8]
        top = (factor * constants[4:5, :]) * column[:, 6:7]
        green_ref[j] = jnp.where(wave == 0.0, 0.0, top / jnp.where(wave == 0.0, 1.0, wave))

    copies[13].wait()
    one_high_ref[...], one_low_ref[...] = split(fit_one_w[...])


def centroid_kernel(
    table,
    codes,
    columns,
    second,
    third,
    one_high,
    one_low,
    two_high,
    two_low,
    three_high,
    three_low,
    fit_out_w,
    dipole_ref,
    shift_ref,
    matrix,
    descriptor,
    arrivals,
    *held,
):
    sources = (table, codes, columns, second, third)
    sources += (one_high, one_low, two_high, two_low, three_high, three_low, fit_out_w)
    copies = [
        pltpu.make_async_copy(source, target, arrivals.at[k])
        for k, (source, target) in enumerate(zip(sources, held))
    ]
    for copy in copies:
        copy.start()
    table, codes, columns, second, third = held[:5]
    one_high, one_low, two_high, two_low, three_high, three_low, fit_out_w = held[5:]
    for copy in copies[:5]:
        copy.wait()
    wide_count, narrow_count, _, atoms = table.shape
    listed = codes.shape[0]
    width_three = fit_out_w.shape[0]
    width_one = width_three // 4
    hidden_width = two_high.shape[0]
    cells = (GRID_X // wide_count, GRID_Y, GRID_Z // narrow_count)
    at_wide = lax.axis_index("wide")
    at_narrow = lax.axis_index("narrow")
    own = jnp.abs(table[at_wide, at_narrow])
    nearby = []
    for step in range(9):
        wide_at = lax.rem(at_wide + (step // 3 - 1) + wide_count, wide_count)
        narrow_at = lax.rem(at_narrow + (step % 3 - 1) + narrow_count, narrow_count)
        nearby.append(table[wide_at, narrow_at])

    second_all = second[...]
    third_all = third[...]
    weight_oxygen = jnp.broadcast_to(columns[0:ROW_PAD, 0:1], (ROW_PAD, atoms))
    weight_hydrogen = jnp.broadcast_to(columns[0:ROW_PAD, 1:2], (ROW_PAD, atoms))
    bias_oxygen = jnp.broadcast_to(columns[0:ROW_PAD, 2:3], (ROW_PAD, atoms))
    bias_hydrogen = jnp.broadcast_to(columns[0:ROW_PAD, 3:4], (ROW_PAD, atoms))
    matrix[...] = jnp.zeros_like(matrix)

    def chunk(first):
        code = codes[pl.ds(first, SLOT_CHUNK), :]
        offset = code // atoms
        slot = code - offset * atoms
        step_x = jnp.where(offset >= 9, 1, 0) + jnp.where(offset >= 18, 1, 0)
        rest = offset - 9 * step_x
        step_z = jnp.where(rest >= 3, 1, 0) + jnp.where(rest >= 6, 1, 0)
        step_y = rest - 3 * step_z
        brick = step_x * 3 + step_z
        found = []
        for component in range(3):
            picked = jnp.zeros((SLOT_CHUNK, atoms), jnp.float32)
            for step in range(9):
                row = jnp.broadcast_to(
                    nearby[step][component : component + 1], (SLOT_CHUNK, atoms)
                )
                here = jnp.take_along_axis(row, slot, axis=1, mode="promise_in_bounds")
                picked = jnp.where(brick == step, here, picked)
            found.append(picked)
        hydrogen = found[0] < 0.0
        found[0] = jnp.abs(found[0])
        scaled = []
        for component, step in enumerate((step_x, step_y, step_z)):
            extent = float(cells[component])
            relative = (step - 1).astype(jnp.float32) * extent + (
                found[component] - own[component : component + 1]
            ) * extent
            scaled.append(relative * (1.0 / radius_scale))
        smooth = 1.0 / (
            1.0 + (scaled[0] * scaled[0] + scaled[1] * scaled[1] + scaled[2] * scaled[2])
        )
        radial = [smooth] + [smooth * part for part in scaled]
        first_layers = []
        for k in range(SLOT_CHUNK):
            row = smooth[k : k + 1]
            kind = hydrogen[k : k + 1]
            weight = jnp.where(kind, weight_hydrogen, weight_oxygen)
            bias = jnp.where(kind, bias_hydrogen, bias_oxygen)
            first_layers.append(jnp.tanh(weight * row + bias))
        layer_one = jnp.concatenate(first_layers, axis=1)
        high, low = split(layer_one)
        layer_two = lax.dot_general(
            second_all,
            jnp.concatenate([high, low, high], axis=0),
            NN,
            preferred_element_type=jnp.float32,
        )
        layer_two = jnp.tanh(layer_two) + jnp.concatenate(
            [layer_one, layer_one], axis=0
        )
        high, low = split(layer_two)
        layer_three = lax.dot_general(
            third_all,
            jnp.concatenate([high, low, high], axis=0),
            NN,
            preferred_element_type=jnp.float32,
        )
        layer_three = jnp.tanh(layer_three) + jnp.concatenate(
            [layer_two, layer_two], axis=0
        )
        for part in range(4):
            total = matrix[part]
            for k in range(SLOT_CHUNK):
                total = total + layer_three[:, k * atoms : (k + 1) * atoms] * radial[part][k : k + 1]
            matrix[part] = total

    def two_chunks(index, carry):
        first = pl.multiple_of(index * (2 * SLOT_CHUNK), 2 * SLOT_CHUNK)
        chunk(first)
        chunk(pl.multiple_of(first + SLOT_CHUNK, SLOT_CHUNK))
        return carry

    lax.fori_loop(0, listed // (2 * SLOT_CHUNK), two_chunks, 0)

    parts = []
    for part in range(4):
        padded = matrix[part] * (1.0 / listed)
        parts.append(
            jnp.concatenate(
                [padded[k * ROW_PAD : k * ROW_PAD + width_one] for k in range(4)], axis=0
            )
        )
    leading = [part[0:AXIS_COLUMNS] for part in parts]
    for row in range(width_three):
        total = parts[0][row : row + 1] * leading[0]
        for part in range(1, 4):
            total = total + parts[part][row : row + 1] * leading[part]
        descriptor[row * AXIS_COLUMNS : (row + 1) * AXIS_COLUMNS, :] = total
    for copy in copies[5:]:
        copy.wait()

    def layer(high_ref, low_ref, given, column):
        weights = (high_ref[...], low_ref[...])
        return jnp.tanh(multiply(weights, split(given)) + columns[0:hidden_width, column : column + 1])

    hidden = layer(one_high, one_low, descriptor[...], 4)
    hidden = hidden + layer(two_high, two_low, hidden, 5)
    hidden = hidden + layer(three_high, three_low, hidden, 6)
    coeffs = multiply(split(fit_out_w[...]), split(hidden))
    vector = jnp.concatenate(
        [jnp.sum(coeffs * parts[1 + c], axis=0, keepdims=True) for c in range(3)], axis=0
    )
    oxygen = 1.0 - own[3:4]
    for c in range(3):
        dipole_ref[c] = vector[c : c + 1] * oxygen
    moved = wannier_reach * jnp.tanh(vector)
    moved = jnp.concatenate([moved, jnp.zeros((1, atoms), jnp.float32)], axis=0)
    for target in range(shift_ref.shape[0]):
        shift_ref[target] = moved


def mesh_kernel(
    table,
    shifts,
    phase,
    green_ref,
    fold_high,
    fold_low,
    unfold_high,
    unfold_low,
    out_ref,
    grid,
    planes,
    packed,
    weights_even,
    weights_odd,
    slopes,
    weights_z,
    waves,
    wave_slopes,
):
    wide_count, narrow_count, _, atoms = table.shape
    cells_x = GRID_X // wide_count
    cells_z = GRID_Z // narrow_count
    window = cells_z + HALO_Z
    reach = cells_x + HALO_X
    pair = 2 * atoms
    length = wide_count * pair
    copies = grid.shape[0]
    fine = grid.shape[1]
    channels = 2 * fine
    rows = phase.shape[0]
    half_x = GRID_X // 2
    half_z = GRID_Z // 2
    piece = lax.axis_index("wide") * narrow_count + lax.axis_index("narrow")
    lane_zero = lax.broadcasted_iota(jnp.int32, (1, half_x), 1) == 0
    row_zero = lax.broadcasted_iota(jnp.int32, (half_z, 1), 0) == 0

    def fold():
        return (fold_high[...], fold_low[...])

    def unfold():
        return (unfold_high[...], unfold_low[...])

    def sites(at_wide, at_narrow):
        atom = jnp.abs(table[at_wide, at_narrow])
        moved = shifts[at_wide, at_narrow]
        found = []
        for component, extent in enumerate((cells_x, GRID_Y, cells_z)):
            start = atom[component : component + 1] * float(extent)
            found.append(jnp.concatenate([start, start + moved[component : component + 1]], axis=1))
        oxygen = 1.0 - atom[3:4]
        found.append(jnp.concatenate([6.0 * oxygen + atom[3:4], -8.0 * oxygen], axis=1))
        return found

    def line(at_narrow):
        groups = [sites(at_wide, at_narrow) for at_wide in range(wide_count)]
        return [jnp.concatenate([g[k] for g in groups], axis=1) for k in range(4)]

    def splines_z(row):
        counter = lax.broadcasted_iota(jnp.int32, (window, 1), 0).astype(jnp.float32)
        return spline_pair(row - (counter - float(HALO_Z)))

    def fill_x(row, targets):
        counter = lax.broadcasted_iota(jnp.int32, (reach, 1), 0).astype(jnp.float32)
        both = spline_pair(row - (counter - float(HALO_X)))
        rest = jnp.zeros((128 - reach, length), jnp.bfloat16)
        for values, ref in zip(both, targets):
            if ref is not None:
                high, low = split(values)
                ref[0:reach, :] = high
                ref[reach:128, :] = rest
                ref[128 : 128 + reach, :] = low
                ref[128 + reach : 256, :] = rest

    grid[:, :, 0:HALO_Z, :] = jnp.zeros((copies, fine, HALO_Z, 2 * GRID_X), jnp.float32)

    weights = (weights_even, weights_odd)

    def spread(index, odd):
        at_narrow = 2 * index + odd
        row_x, row_y, row_z, charge = line(at_narrow)
        lower = jnp.floor(row_y)
        back = lax.broadcasted_iota(jnp.int32, (8, 1), 0)
        value_y, slope_y = spline_pair((row_y - lower) + back.astype(jnp.float32))
        cell = lax.rem(lower.astype(jnp.int32) - back + GRID_Y, GRID_Y)
        wave_blocks = []
        slope_blocks = []
        for block in range(length // 128):
            lanes = slice(block * 128, (block + 1) * 128)
            wave = jnp.zeros((rows, 128), jnp.float32)
            wave_slope = jnp.zeros((rows, 128), jnp.float32)
            for k in range(4):
                spot = jnp.broadcast_to(cell[k : k + 1, lanes], (rows, 128))
                found = lookup(phase[...], spot)
                wave = wave + value_y[k : k + 1, lanes] * found
                wave_slope = wave_slope + slope_y[k : k + 1, lanes] * found
            wave_blocks.append(wave)
            slope_blocks.append(wave_slope)
        wave = jnp.concatenate(wave_blocks, axis=1)
        waves[at_narrow] = wave
        wave_slopes[at_narrow] = jnp.concatenate(slope_blocks, axis=1)
        fill_x(row_x, (weights[odd].at[index], None))
        value_z, _ = splines_z(row_z)
        weights_z[at_narrow] = value_z
        charged = wave * charge
        first = pl.multiple_of(at_narrow * cells_z, HALO_Z)
        for at_wide in range(wide_count):
            lanes = slice(at_wide * pair, (at_wide + 1) * pair)
            near = value_z[:, lanes]
            left = jnp.concatenate(
                [near * charged[c : c + 1, lanes] for c in range(channels)], axis=0
            )
            high, low = split(left)
            across = weights[odd][index, :, lanes]
            total = lax.dot_general(high, across, NT, preferred_element_type=jnp.float32)
            total = total[:, 0:128] + (
                total[:, 128:256]
                + lax.dot_general(low, across[0:128], NT, preferred_element_type=jnp.float32)
            )
            start = at_wide // copies * 128
            for c in range(channels):
                spot = slice(c % 2 * GRID_X + start, c % 2 * GRID_X + start + 128)
                k = at_wide % copies
                part = total[c * window : (c + 1) * window]
                grid[k, c // 2, pl.ds(first, HALO_Z), spot] += part[:HALO_Z]
                grid[k, c // 2, pl.ds(first + HALO_Z, cells_z), spot] = part[HALO_Z:]

    def in_pairs(step):
        def both(index, carry):
            step(index, 0)
            step(index, 1)
            return carry

        lax.fori_loop(0, narrow_count // 2, both, 0)

    in_pairs(spread)

    def gather(j, carry):
        for lanes in (slice(0, GRID_X), slice(GRID_X, 2 * GRID_X)):
            total = None
            for k in range(copies):
                moved = pltpu.roll(grid[k, j, :, lanes], (k * cells_x - HALO_X) % GRID_X, 1)
                total = moved if total is None else total + moved
            planes[j, :, lanes] = total[HALO_Z:]
            planes[j, GRID_Z - HALO_Z :, lanes] += total[:HALO_Z]
        return carry

    lax.fori_loop(0, fine, gather, 0)
    is_first = piece == 0

    def paired(real, imag, zero, axis):
        half = real.shape[axis] // 2
        first = (slice(None),) * axis + (slice(0, half),)
        second = (slice(None),) * axis + (slice(half, 2 * half),)
        real_c, real_s = real[first], real[second]
        if imag is None:
            none = jnp.zeros_like(real_s)
            real_all = [real_c, jnp.where(zero, real_s, real_c)]
            imag_all = [jnp.where(zero, none, -real_s), jnp.where(zero, none, real_s)]
        else:
            imag_c, imag_s = imag[first], imag[second]
            real_all = [
                real_c + jnp.where(zero, 0.0, imag_s),
                jnp.where(zero, real_s, real_c - imag_s),
            ]
            imag_all = [
                imag_c - jnp.where(zero, 0.0, real_s),
                jnp.where(zero, imag_s, imag_c + real_s),
            ]
        return jnp.concatenate(real_all, axis=axis), jnp.concatenate(imag_all, axis=axis)

    def merged(real, imag, zero, axis):
        half = real.shape[axis] // 2
        first = (slice(None),) * axis + (slice(0, half),)
        second = (slice(None),) * axis + (slice(half, 2 * half),)
        real_a, real_b = real[first], real[second]
        imag_a, imag_b = imag[first], imag[second]
        real = [
            real_a + jnp.where(zero, 0.0, real_b),
            jnp.where(zero, real_b, imag_b - imag_a),
        ]
        imag = [
            imag_a + jnp.where(zero, 0.0, imag_b),
            jnp.where(zero, imag_b, real_a - real_b),
        ]
        return jnp.concatenate(real, axis=axis), jnp.concatenate(imag, axis=axis)

    modes = {}
    parts = []

    def slot(j):
        first_imag = planes[0, :, GRID_X:]
        if j == fine:
            real, imag = jnp.where(is_first, first_imag, 0.0), None
        else:
            real, imag = planes[j, :, 0:GRID_X], planes[j, :, GRID_X:]
            if j == 0:
                imag = jnp.where(is_first, 0.0, imag)
        real = split(real)
        imag = None if imag is None else split(imag)
        yield
        real = multiply(real, fold())
        imag = None if imag is None else multiply(imag, fold())
        yield
        real, imag = paired(real, imag, lane_zero, 1)
        real, imag = split(real), split(imag)
        yield
        real, imag = multiply(unfold(), real), multiply(unfold(), imag)
        yield
        real, imag = paired(real, imag, row_zero, 0)
        green = green_ref[j]
        mode = GRID_Y // 2 if j == fine else piece * fine + j
        share = jnp.where((mode == 0) | (mode == GRID_Y // 2), 0.5, 1.0)
        parts.append(share * jnp.sum(green * (real * real + imag * imag), axis=0, keepdims=True))
        real, imag = green * real, green * imag
        if j == fine:
            modes[j] = (real, imag)
            return
        if j == 0:
            real, imag = real - modes[fine][1], imag + modes[fine][0]
        real, imag = merged(real, imag, row_zero, 0)
        real, imag = split(real), split(imag)
        yield
        real, imag = multiply(fold(), real), multiply(fold(), imag)
        yield
        real, imag = merged(real, imag, lane_zero, 1)
        scale = jnp.where(piece * fine + j == 0, 1.0, 2.0)
        real, imag = split(real * scale), split(imag * scale)
        yield
        real, imag = multiply(real, unfold()), multiply(imag, unfold())
        yield
        for k, part in enumerate((real, imag)):
            for at_wide in range(wide_count):
                moved = pltpu.roll(part, (HALO_X - at_wide * cells_x) % GRID_X, 1)[:, 0:128]
                high = moved.astype(jnp.bfloat16).astype(jnp.float32)
                again = pltpu.roll(high, reach % 128, 1)
                low = pltpu.roll(moved - high, 2 * reach % 128, 1)
                sides = []
                for side in range(2):
                    lane = lax.broadcasted_iota(jnp.int32, (1, 128), 1) + side * 128
                    value = jnp.where(lane < 2 * reach, again, low)
                    if side == 0:
                        value = jnp.where(lane < reach, high, value)
                    sides.append(value.astype(jnp.bfloat16))
                block = jnp.concatenate(sides, axis=1)
                packed[at_wide, 2 * j + k, HALO_BITS:, :] = block
                packed[at_wide, 2 * j + k, 0:HALO_BITS, :] = block[GRID_Z - HALO_BITS :]

    waiting = [slot(j) for j in [fine, *range(fine)]]
    running = []
    while waiting or running:
        if waiting:
            running.append(waiting.pop(0))
        running = [one for one in running if next(one, running) is not running]
    energy = sum(parts[1:], parts[0])
    energy = jnp.broadcast_to(jnp.sum(energy, axis=1, keepdims=True), (1, 128))

    def collect(index, odd):
        at_narrow = 2 * index + odd
        row_x, _, row_z, _ = line(at_narrow)
        fill_x(row_x, (None, slopes.at[odd]))
        value_z = weights_z[at_narrow]
        _, slope_z = splines_z(row_z)
        first = pl.multiple_of(at_narrow * cells_z, HALO_BITS)
        wave = waves[at_narrow]
        wave_slope = wave_slopes[at_narrow]
        for at_wide in range(wide_count):
            lanes = slice(at_wide * pair, (at_wide + 1) * pair)
            tall = cells_z + HALO_BITS
            left = jnp.concatenate(
                [packed[at_wide, c, pl.ds(first, tall), :] for c in range(channels)], axis=0
            )

            def across(right):
                high = right[0:reach]
                rest = jnp.zeros((256 - 3 * reach, pair), jnp.bfloat16)
                right = jnp.concatenate([high, right[128 : 128 + reach], high, rest], axis=0)
                return lax.dot_general(left, right, NN, preferred_element_type=jnp.float32)

            value = across(weights[odd][index, :, lanes])
            slope = across(slopes[odd, :, lanes])
            plain = jnp.zeros((window, pair), jnp.float32)
            along_x = plain
            along_y = plain
            for c in range(channels):
                block = slice((c + 1) * tall - window, (c + 1) * tall)
                plain = plain + value[block] * wave[c : c + 1, lanes]
                along_x = along_x + slope[block] * wave[c : c + 1, lanes]
                along_y = along_y + value[block] * wave_slope[c : c + 1, lanes]
            near = value_z[:, lanes]
            near_slope = slope_z[:, lanes]
            results = [
                jnp.sum(near * plain, axis=0, keepdims=True),
                -jnp.sum(near * along_x, axis=0, keepdims=True),
                -jnp.sum(near * along_y, axis=0, keepdims=True),
                -jnp.sum(near_slope * plain, axis=0, keepdims=True),
            ]
            for k, row in enumerate(results):
                out_ref[at_wide, at_narrow, :, k * pair : (k + 1) * pair] = row
            out_ref[at_wide, at_narrow, :, 4 * pair :] = energy

    in_pairs(collect)


def finish_kernel(arrived, species, atom_ref, centroid_ref, energy_ref):
    atoms = species.shape[1]
    total = arrived[0]
    for k in range(1, arrived.shape[0]):
        total = total + arrived[k]
    oxygen = 1.0 - species[...].astype(jnp.float32)
    for k in range(4):
        atom_ref[k] = total[:, 2 * k * atoms : (2 * k + 1) * atoms]
        centroid_ref[k] = total[:, (2 * k + 1) * atoms : (2 * k + 2) * atoms] * oxygen
    energy_ref[...] = total[:, 8 * atoms :] * (1.0 / (atoms * arrived.shape[0]))


def mode_factors(length, order):
    wrapped = np.where(2 * order >= length, order - length, order)
    square = (wrapped / length) ** 2
    ratio = (4.0 + 2.0 * np.cos(2.0 * math.pi * order / length)) / 6.0
    return np.stack([np.exp(-(math.pi**2) * square / ewald_beta**2) / ratio**2, square])


def folded_order(length):
    half = length // 2
    counter = np.arange(half)
    return np.concatenate([counter, np.where(counter == 0, half, length - counter)])


def fold_table(length):
    half = length // 2
    turns = np.outer(np.arange(length), np.arange(half)) % length * (2.0 * math.pi / length)
    sines = np.sin(turns)
    sines[:, 0] = 1.0 - 2.0 * (np.arange(length) % 2)
    return np.concatenate([np.cos(turns), sines], axis=1)


def halves(table):
    high = table.astype(jnp.bfloat16)
    low = (table - high.astype(np.float64)).astype(jnp.bfloat16)
    return high, low


def vmem(count):
    return [pl.BlockSpec(memory_space=pltpu.VMEM)] * count


def hbm(count):
    return [pl.BlockSpec(memory_space=pltpu.HBM)] * count


def shaped(shape, dtype=jnp.float32):
    return jax.ShapeDtypeStruct(shape, dtype)


def limits(mebibytes):
    return pltpu.CompilerParams(vmem_limit_bytes=mebibytes * 1024 * 1024)


def local(
    positions,
    species,
    neighbours,
    embed_one_w,
    embed_one_b,
    embed_two_w,
    embed_two_b,
    embed_three_w,
    embed_three_b,
    fit_one_w,
    fit_one_b,
    fit_two_w,
    fit_two_b,
    fit_three_w,
    fit_three_b,
    fit_out_w,
):
    axes = ("wide", "narrow")
    wide_count = lax.axis_size("wide")
    narrow_count = lax.axis_size("narrow")
    pieces = wide_count * narrow_count
    atoms = positions.shape[4]
    listed = neighbours.shape[4]
    fine = GRID_Y // 2 // pieces
    width_three = embed_three_w.shape[1]
    entries, hidden = fit_one_w.shape
    kinds = species.reshape(1, atoms)

    packed = pl.pallas_call(
        pack_kernel,
        out_shape=shaped((pieces, 4, atoms)),
        in_specs=vmem(2),
        out_specs=vmem(1)[0],
        name="pack",
    )(positions.reshape(3, 1, atoms), kinds)
    table = lax.all_to_all(packed, axes, 0, 0, tiled=True)
    table = table.reshape(wide_count, narrow_count, 4, atoms)

    tall = 4 * ROW_PAD
    bf16 = jnp.bfloat16
    wave_rows = -(-2 * fine // 8) * 8
    angle = np.arange(GRID_Y) * (2.0 * math.pi / GRID_Y)
    constants = np.concatenate(
        [
            np.stack([np.cos(angle), np.sin(angle)]),
            mode_factors(GRID_Y, np.arange(GRID_Y)),
            mode_factors(GRID_X, folded_order(GRID_X)),
            mode_factors(GRID_Z, folded_order(GRID_Z)),
        ]
    )
    constants[2] *= coulomb / (math.pi * GRID_X * GRID_Y * GRID_Z)
    arguments = (
        neighbours.reshape(atoms, listed),
        embed_one_w,
        embed_one_b,
        embed_two_w,
        embed_two_b[None],
        embed_three_w,
        embed_three_b[None],
        fit_one_w.T,
        fit_one_b[None],
        fit_two_w,
        fit_two_b[None],
        fit_three_w,
        fit_three_b[None],
        jnp.asarray(constants, jnp.float32),
    )
    held = [arguments[k] for k in (0, 1, 2, 3, 4, 5, 6, 8, 10, 12, 13, 9, 11, 7)]
    prepared = pl.pallas_call(
        prepare_kernel,
        out_shape=(
            shaped((listed, atoms), jnp.int32),
            shaped((256, 16)),
            shaped((2 * ROW_PAD, 3 * ROW_PAD), bf16),
            shaped((tall, 6 * ROW_PAD), bf16),
            shaped((hidden, entries), bf16),
            shaped((hidden, entries), bf16),
        )
        + (shaped((hidden, hidden), bf16),) * 4
        + (shaped((wave_rows, GRID_Y)), shaped((fine + 1, GRID_Z, GRID_X))),
        in_specs=hbm(len(arguments)),
        out_specs=tuple(vmem(12)),
        scratch_shapes=[
            pltpu.VMEM((16, 256), jnp.float32),
            pltpu.VMEM((256, 256), jnp.float32),
            pltpu.SemaphoreType.DMA((len(held),)),
        ]
        + [pltpu.VMEM(array.shape, array.dtype) for array in held],
        compiler_params=limits(62),
        cost_estimate=pl.CostEstimate(
            flops=1000000, bytes_accessed=8 * entries * hidden, transcendentals=0
        ),
        name="prepare",
    )(*arguments)
    phase, green = prepared[10:]
    fitted = (table, *prepared[:10], fit_out_w.T)
    dipole, shifts = pl.pallas_call(
        centroid_kernel,
        out_shape=(shaped((3, 1, atoms)), shaped((pieces, 4, atoms))),
        in_specs=hbm(12),
        out_specs=tuple(vmem(2)),
        scratch_shapes=[
            pltpu.VMEM((4, tall, atoms), jnp.float32),
            pltpu.VMEM((width_three * AXIS_COLUMNS, atoms), jnp.float32),
            pltpu.SemaphoreType.DMA((len(fitted),)),
        ]
        + [pltpu.VMEM(array.shape, array.dtype) for array in fitted],
        compiler_params=limits(62),
        name="centroids",
    )(*fitted)
    shifts = lax.all_to_all(shifts, axes, 0, 0, tiled=True)
    shifts = shifts.reshape(wide_count, narrow_count, 4, atoms)

    cells_x = GRID_X // wide_count
    copies = 128 // cells_x
    length = wide_count * 2 * atoms
    out_width = 8 * atoms + 128
    partial = pl.pallas_call(
        mesh_kernel,
        out_shape=shaped((wide_count, narrow_count, 1, out_width)),
        in_specs=vmem(8),
        out_specs=vmem(1)[0],
        scratch_shapes=[
            pltpu.VMEM((copies, fine, HALO_Z + GRID_Z, 2 * GRID_X), jnp.float32),
            pltpu.VMEM((fine, GRID_Z, 2 * GRID_X), jnp.float32),
            pltpu.VMEM((wide_count, 2 * fine, HALO_BITS + GRID_Z, 256), bf16),
        ]
        + [pltpu.VMEM((narrow_count // 2, 256, length), bf16)] * 2
        + [pltpu.VMEM((2, 256, length), bf16)]
        + [pltpu.VMEM((narrow_count, GRID_Z // narrow_count + HALO_Z, length), jnp.float32)]
        + [pltpu.VMEM((narrow_count, wave_rows, length), jnp.float32)] * 2,
        compiler_params=limits(48),
        name="mesh",
    )(
        table,
        shifts,
        phase,
        green,
        *[jnp.asarray(half) for half in halves(fold_table(GRID_X))],
        *[jnp.asarray(half) for half in halves(fold_table(GRID_X).T)],
    )
    arrived = lax.all_to_all(partial.reshape(pieces, 1, out_width), axes, 0, 0, tiled=True)
    atom_field, centroid_field, energy = pl.pallas_call(
        finish_kernel,
        out_shape=(shaped((4, 1, atoms)), shaped((4, 1, atoms)), shaped((1, 128))),
        in_specs=vmem(2),
        out_specs=tuple(vmem(3)),
        name="finish",
    )(arrived, kinds)
    atom_field = atom_field.reshape(4, 1, 1, 1, atoms)
    centroid_field = centroid_field.reshape(4, 1, 1, 1, atoms)
    return (dipole.reshape(3, 1, 1, 1, atoms), atom_field, centroid_field, energy[0, 0])


def solution(mesh):
    column = P(None, "wide", "narrow", None, None)
    in_specs = (column, P("wide", "narrow", None, None), P("wide", "narrow", None, None, None))
    in_specs = in_specs + (P(),) * 13
    out_specs = (column, column, column, P())
    return jax.shard_map(local, mesh=mesh, in_specs=in_specs, out_specs=out_specs, check_vma=False)
```

```python
import math

import jax
import jax.numpy as jnp
import numpy as np
from jax import lax
from jax.experimental import pallas as pl
from jax.experimental.pallas import tpu as pltpu
from jax.sharding import PartitionSpec as P

GRID_X = 256
GRID_Y = 256
GRID_Z = 256
AXIS_COLUMNS = 16

radius_scale = 24.0
wannier_reach = 0.5
ewald_beta = 0.9
coulomb = 0.25

ROW_PAD = 32
SLOT_CHUNK = 16
HALO_X = 16
HALO_Z = 8
HALO_BITS = 16

NN = (((1,), (0,)), ((), ()))
NT = (((1,), (1,)), ((), ()))


def split(value):
    high = value.astype(jnp.bfloat16)
    low = (value - high.astype(jnp.float32)).astype(jnp.bfloat16)
    return high, low


def multiply(left, right, dims=NN):
    def one(a, b):
        return lax.dot_general(a, b, dims, preferred_element_type=jnp.float32)

    return one(left[0], right[0]) + (one(left[1], right[0]) + one(left[0], right[1]))


def skewed(waiting):
    running = []
    while waiting or running:
        if waiting:
            running.append(waiting.pop(0))
        running = [one for one in running if next(one, running) is not running]


def spline_pair(offset):
    centred = offset - 2.0
    away = jnp.abs(centred)
    outer = jnp.maximum(2.0 - away, 0.0)
    inner = jnp.maximum(1.0 - away, 0.0)
    outer_square = outer * outer
    inner_square = inner * inner
    value = (outer_square * outer - 4.0 * (inner_square * inner)) * (1.0 / 6.0)
    slope = jnp.where(centred < 0.0, 0.5, -0.5) * (outer_square - 4.0 * inner_square)
    return value, slope


def lookup(row_table, spot):
    found = None
    for part in range(row_table.shape[1] // 128):
        inside = spot // 128 == part
        here = jnp.take_along_axis(
            jnp.broadcast_to(row_table[:, part * 128 : (part + 1) * 128], spot.shape),
            lax.rem(spot, 128),
            axis=1,
            mode="promise_in_bounds",
        )
        found = here if found is None else jnp.where(inside, here, found)
    return found


def pack_kernel(positions, species, out_ref):
    kinds = species[...]
    rows = [positions[component] for component in range(3)]
    rows[0] = jnp.where(kinds > 0, -rows[0], rows[0])
    rows.append(kinds.astype(jnp.float32))
    rows = jnp.concatenate(rows, axis=0)
    for target in range(out_ref.shape[0]):
        out_ref[target] = rows


def prepare_kernel(
    neighbours,
    embed_one_w,
    embed_one_b,
    embed_two_w,
    embed_two_b,
    embed_three_w,
    embed_three_b,
    fit_one_w,
    fit_one_b,
    fit_two_w,
    fit_two_b,
    fit_three_w,
    fit_three_b,
    constants,
    codes_ref,
    columns_ref,
    second_ref,
    third_ref,
    one_high_ref,
    one_low_ref,
    two_high_ref,
    two_low_ref,
    three_high_ref,
    three_low_ref,
    phase_ref,
    green_ref,
    rows,
    square,
    arrivals,
    *held,
):
    sources = (
        neighbours,
        embed_one_w,
        embed_one_b,
        embed_two_w,
        embed_two_b,
        embed_three_w,
        embed_three_b,
        fit_one_b,
        fit_two_b,
        fit_three_b,
        constants,
        fit_two_w,
        fit_three_w,
        fit_one_w,
    )
    copies = [
        pltpu.make_async_copy(source, target, arrivals.at[k])
        for k, (source, target) in enumerate(zip(sources, held))
    ]
    for copy in copies:
        copy.start()
    (
        neighbours,
        embed_one_w,
        embed_one_b,
        embed_two_w,
        embed_two_b,
        embed_three_w,
        embed_three_b,
        fit_one_b,
        fit_two_b,
        fit_three_b,
        constants,
        fit_two_w,
        fit_three_w,
        fit_one_w,
    ) = held
    for copy in copies[:11]:
        copy.wait()
    pieces = lax.axis_size("wide") * lax.axis_size("narrow")
    piece = lax.axis_index("wide") * lax.axis_size("narrow") + lax.axis_index("narrow")
    width_one = embed_one_w.shape[1]
    hidden = fit_two_w.shape[0]
    codes_ref[...] = jnp.transpose(neighbours[...].astype(jnp.float32)).astype(jnp.int32)
    rows[...] = jnp.zeros_like(rows)
    for kind in range(2):
        rows[kind : kind + 1, 0:width_one] = embed_one_w[kind : kind + 1, :]
        rows[2 + kind : 3 + kind, 0:width_one] = embed_one_b[kind : kind + 1, :]
        rows[2 + kind : 3 + kind, width_one : width_one + 1] = jnp.full((1, 1), 40.0, jnp.float32)
    for row, source in ((4, fit_one_b), (5, fit_two_b), (6, fit_three_b)):
        rows[row : row + 1, 0:hidden] = source[...]
    columns_ref[...] = jnp.transpose(rows[...])

    square[...] = jnp.zeros_like(square)
    for k in range(2):
        square[0:width_one, k * ROW_PAD : k * ROW_PAD + width_one] = embed_two_w[
            :, k * width_one : (k + 1) * width_one
        ]
        square[
            width_one : width_one + 1, k * ROW_PAD : k * ROW_PAD + width_one
        ] = embed_two_b[:, k * width_one : (k + 1) * width_one]
    high, low = split(jnp.transpose(square[0:128, 0:128])[0 : 2 * ROW_PAD, 0:ROW_PAD])
    second_ref[...] = jnp.concatenate([high, high, low], axis=1)
    square[0:128, 0:128] = jnp.zeros((128, 128), jnp.float32)
    for g in range(2):
        for k in range(4):
            square[
                g * ROW_PAD : g * ROW_PAD + width_one, k * ROW_PAD : k * ROW_PAD + width_one
            ] = embed_three_w[
                g * width_one : (g + 1) * width_one, k * width_one : (k + 1) * width_one
            ]
    for k in range(4):
        square[
            width_one : width_one + 1, k * ROW_PAD : k * ROW_PAD + width_one
        ] = embed_three_b[:, k * width_one : (k + 1) * width_one]
    high, low = split(jnp.transpose(square[0:128, 0:128])[:, 0 : 2 * ROW_PAD])
    third_ref[...] = jnp.concatenate([high, high, low], axis=1)
    for copy in copies[11:13]:
        copy.wait()
    for source, high_ref, low_ref in (
        (fit_two_w, two_high_ref, two_low_ref),
        (fit_three_w, three_high_ref, three_low_ref),
    ):
        square[0:hidden, 0:hidden] = source[...]
        high_ref[...], low_ref[...] = split(jnp.transpose(square[...])[0:hidden, 0:hidden])

    fine = GRID_Y // 2 // pieces
    shape = (phase_ref.shape[0], 128)
    row = lax.broadcasted_iota(jnp.int32, shape, 0)
    mode = piece * fine + row // 2
    for part in range(GRID_Y // 128):
        cell = lax.broadcasted_iota(jnp.int32, shape, 1) + part * 128
        spot = lax.rem(mode * cell, GRID_Y)
        cosine = lookup(constants[0:1, :], spot)
        sine = lookup(constants[1:2, :], spot)
        alternate = (1 - 2 * lax.rem(cell, 2)).astype(jnp.float32)
        odd = jnp.where(mode == 0, alternate, -sine)
        value = jnp.where(lax.rem(row, 2) == 0, cosine, odd)
        phase_ref[:, part * 128 : (part + 1) * 128] = jnp.where(row < 2 * fine, value, 0.0)

    column = jnp.transpose(constants[...])
    lane = lax.broadcasted_iota(jnp.int32, (1, GRID_Y), 1)
    for j in range(fine + 1):
        here = lane == (GRID_Y // 2 if j == fine else piece * fine + j)
        factor = jnp.sum(jnp.where(here, constants[2:3, :], 0.0), axis=1, keepdims=True)
        part = jnp.sum(jnp.where(here, constants[3:4, :], 0.0), axis=1, keepdims=True)
        wave = (part + constants[5:6, :]) + column[:, 7:8]
        top = (factor * constants[4:5, :]) * column[:, 6:7]
        green_ref[j] = jnp.where(wave == 0.0, 0.0, top / jnp.where(wave == 0.0, 1.0, wave))

    copies[13].wait()
    one_high_ref[...], one_low_ref[...] = split(fit_one_w[...])


def centroid_kernel(
    table,
    codes,
    columns,
    second,
    third,
    one_high,
    one_low,
    two_high,
    two_low,
    three_high,
    three_low,
    fit_out_w,
    dipole_ref,
    shift_ref,
    matrix,
    descriptor,
    embedded_even,
    embedded_odd,
    arrivals,
    *held,
):
    sources = (table, codes, columns, second, third)
    sources += (one_high, one_low, two_high, two_low, three_high, three_low, fit_out_w)
    copies = [
        pltpu.make_async_copy(source, target, arrivals.at[k])
        for k, (source, target) in enumerate(zip(sources, held))
    ]
    for copy in copies:
        copy.start()
    table, codes, columns, second, third = held[:5]
    one_high, one_low, two_high, two_low, three_high, three_low, fit_out_w = held[5:]
    for copy in copies[:5]:
        copy.wait()
    wide_count, narrow_count, _, atoms = table.shape
    listed = codes.shape[0]
    width_three = fit_out_w.shape[0]
    width_one = width_three // 4
    hidden_width = two_high.shape[0]
    cells = (GRID_X // wide_count, GRID_Y, GRID_Z // narrow_count)
    at_wide = lax.axis_index("wide")
    at_narrow = lax.axis_index("narrow")
    own = jnp.abs(table[at_wide, at_narrow])
    nearby = []
    for step in range(9):
        wide_at = lax.rem(at_wide + (step // 3 - 1) + wide_count, wide_count)
        narrow_at = lax.rem(at_narrow + (step % 3 - 1) + narrow_count, narrow_count)
        nearby.append(table[wide_at, narrow_at])

    second_all = second[...]
    third_all = third[...]
    weight_oxygen = jnp.broadcast_to(columns[0:ROW_PAD, 0:1], (ROW_PAD, atoms))
    weight_hydrogen = jnp.broadcast_to(columns[0:ROW_PAD, 1:2], (ROW_PAD, atoms))
    bias_oxygen = jnp.broadcast_to(columns[0:ROW_PAD, 2:3], (ROW_PAD, atoms))
    bias_hydrogen = jnp.broadcast_to(columns[0:ROW_PAD, 3:4], (ROW_PAD, atoms))
    matrix[...] = jnp.zeros_like(matrix)

    def chunk(first, embedded):
        code = codes[pl.ds(first, SLOT_CHUNK), :]
        offset = code // atoms
        slot = code - offset * atoms
        step_x = jnp.where(offset >= 9, 1, 0) + jnp.where(offset >= 18, 1, 0)
        rest = offset - 9 * step_x
        step_z = jnp.where(rest >= 3, 1, 0) + jnp.where(rest >= 6, 1, 0)
        step_y = rest - 3 * step_z
        brick = step_x * 3 + step_z
        found = []
        for component in range(3):
            picked = jnp.zeros((SLOT_CHUNK, atoms), jnp.float32)
            for step in range(9):
                row = jnp.broadcast_to(
                    nearby[step][component : component + 1], (SLOT_CHUNK, atoms)
                )
                here = jnp.take_along_axis(row, slot, axis=1, mode="promise_in_bounds")
                picked = jnp.where(brick == step, here, picked)
            found.append(picked)
        hydrogen = found[0] < 0.0
        found[0] = jnp.abs(found[0])
        scaled = []
        for component, step in enumerate((step_x, step_y, step_z)):
            extent = float(cells[component])
            relative = (step - 1).astype(jnp.float32) * extent + (
                found[component] - own[component : component + 1]
            ) * extent
            scaled.append(relative * (1.0 / radius_scale))
        smooth = 1.0 / (
            1.0 + (scaled[0] * scaled[0] + scaled[1] * scaled[1] + scaled[2] * scaled[2])
        )
        radial = [smooth] + [smooth * part for part in scaled]
        def slot_pair(k):
            layers = []
            for slot_at in (k, k + 1):
                row = smooth[slot_at : slot_at + 1]
                kind = hydrogen[slot_at : slot_at + 1]
                weight = jnp.where(kind, weight_hydrogen, weight_oxygen)
                bias = jnp.where(kind, bias_hydrogen, bias_oxygen)
                layers.append(jnp.tanh(weight * row + bias))
            layer = jnp.concatenate(layers, axis=1)
            high, low = split(layer)
            yield
            given = lax.dot_general(
                second_all,
                jnp.concatenate([high, low, high], axis=0),
                NN,
                preferred_element_type=jnp.float32,
            )
            yield
            layer = jnp.tanh(given) + jnp.concatenate([layer, layer], axis=0)
            high, low = split(layer)
            yield
            given = lax.dot_general(
                third_all,
                jnp.concatenate([high, low, high], axis=0),
                NN,
                preferred_element_type=jnp.float32,
            )
            yield
            embedded[:, k * atoms : (k + 2) * atoms] = jnp.tanh(given) + jnp.concatenate(
                [layer, layer], axis=0
            )

        skewed([slot_pair(k) for k in range(0, SLOT_CHUNK, 2)])
        for block in range(4):
            lines = slice(block * ROW_PAD, (block + 1) * ROW_PAD)
            totals = [matrix[part, lines, :] for part in range(4)]
            for k in range(SLOT_CHUNK):
                value = embedded[lines, k * atoms : (k + 1) * atoms]
                for part in range(4):
                    totals[part] = totals[part] + value * radial[part][k : k + 1]
            for part in range(4):
                matrix[part, lines, :] = totals[part]

    def two_chunks(index, carry):
        first = pl.multiple_of(index * (2 * SLOT_CHUNK), 2 * SLOT_CHUNK)
        chunk(first, embedded_even)
        chunk(pl.multiple_of(first + SLOT_CHUNK, SLOT_CHUNK), embedded_odd)
        return carry

    lax.fori_loop(0, listed // (2 * SLOT_CHUNK), two_chunks, 0)

    parts = []
    for part in range(4):
        padded = matrix[part] * (1.0 / listed)
        parts.append(
            jnp.concatenate(
                [padded[k * ROW_PAD : k * ROW_PAD + width_one] for k in range(4)], axis=0
            )
        )
    leading = [part[0:AXIS_COLUMNS] for part in parts]
    for row in range(width_three):
        total = parts[0][row : row + 1] * leading[0]
        for part in range(1, 4):
            total = total + parts[part][row : row + 1] * leading[part]
        descriptor[row * AXIS_COLUMNS : (row + 1) * AXIS_COLUMNS, :] = total
    for copy in copies[5:]:
        copy.wait()

    def layer(high_ref, low_ref, given, column):
        weights = (high_ref[...], low_ref[...])
        return jnp.tanh(multiply(weights, split(given)) + columns[0:hidden_width, column : column + 1])

    hidden = layer(one_high, one_low, descriptor[...], 4)
    hidden = hidden + layer(two_high, two_low, hidden, 5)
    hidden = hidden + layer(three_high, three_low, hidden, 6)
    coeffs = multiply(split(fit_out_w[...]), split(hidden))
    vector = jnp.concatenate(
        [jnp.sum(coeffs * parts[1 + c], axis=0, keepdims=True) for c in range(3)], axis=0
    )
    oxygen = 1.0 - own[3:4]
    for c in range(3):
        dipole_ref[c] = vector[c : c + 1] * oxygen
    moved = wannier_reach * jnp.tanh(vector)
    moved = jnp.concatenate([moved, jnp.zeros((1, atoms), jnp.float32)], axis=0)
    for target in range(shift_ref.shape[0]):
        shift_ref[target] = moved


def splines_z(row, window):
    counter = lax.broadcasted_iota(jnp.int32, (window, 1), 0).astype(jnp.float32)
    return spline_pair(row - (counter - float(HALO_Z)))


def splines_x(row, reach, value_ref, slope_ref):
    counter = lax.broadcasted_iota(jnp.int32, (reach, 1), 0).astype(jnp.float32)
    both = spline_pair(row - (counter - float(HALO_X)))
    rest = jnp.zeros((128 - reach, row.shape[1]), jnp.bfloat16)
    for values, ref in zip(both, (value_ref, slope_ref)):
        if ref is not None:
            high, low = split(values)
            ref[0:reach, :] = high
            ref[reach:128, :] = rest
            ref[128 : 128 + reach, :] = low
            ref[128 + reach : 256, :] = rest


def in_pairs(count, step):
    def both(index, carry):
        step(index, 0)
        step(index, 1)
        return carry

    lax.fori_loop(0, count // 2, both, 0)


def site_rows(table, shifts, at_narrow):
    wide_count, narrow_count, _, _ = table.shape
    extents = (GRID_X // wide_count, GRID_Y, GRID_Z // narrow_count)
    rows = [[], [], [], []]
    for at_wide in range(wide_count):
        atom = jnp.abs(table[at_wide, at_narrow])
        for component, extent in enumerate(extents):
            row = atom[component : component + 1] * float(extent)
            if shifts is not None:
                row = row + shifts[at_wide, at_narrow, component : component + 1, :]
            rows[component].append(row)
        hydrogen = atom[3:4]
        oxygen = 1.0 - hydrogen
        rows[3].append(6.0 * oxygen + hydrogen if shifts is None else -8.0 * oxygen)
    return [jnp.concatenate(row, axis=1) for row in rows]


def spread_sites(table, shifts, phase, grid, weights, weights_z, waves, wave_slopes):
    wide_count, narrow_count, _, atoms = table.shape
    cells_x = GRID_X // wide_count
    cells_z = GRID_Z // narrow_count
    window = cells_z + HALO_Z
    copies, fine = grid.shape[:2]
    rows = phase.shape[0]
    grid[:, :, 0:HALO_Z, :] = jnp.zeros((copies, fine, HALO_Z, 2 * GRID_X), jnp.float32)

    def spread(index, odd):
        at_narrow = 2 * index + odd
        row_x, row_y, row_z, charge = site_rows(table, shifts, at_narrow)
        lower = jnp.floor(row_y)
        back = lax.broadcasted_iota(jnp.int32, (8, 1), 0)
        value_y, slope_y = spline_pair((row_y - lower) + back.astype(jnp.float32))
        cell = lax.rem(lower.astype(jnp.int32) - back + GRID_Y, GRID_Y)
        wave_blocks = []
        slope_blocks = []
        for at_wide in range(wide_count):
            lanes = slice(at_wide * atoms, (at_wide + 1) * atoms)
            wave = jnp.zeros((rows, atoms), jnp.float32)
            wave_slope = jnp.zeros((rows, atoms), jnp.float32)
            for k in range(4):
                spot = jnp.broadcast_to(cell[k : k + 1, lanes], (rows, atoms))
                found = lookup(phase[...], spot)
                wave = wave + value_y[k : k + 1, lanes] * found
                wave_slope = wave_slope + slope_y[k : k + 1, lanes] * found
            wave_blocks.append(wave)
            slope_blocks.append(wave_slope)
        wave = jnp.concatenate(wave_blocks, axis=1)
        waves[at_narrow] = wave
        wave_slopes[at_narrow] = jnp.concatenate(slope_blocks, axis=1)
        splines_x(row_x, cells_x + HALO_X, weights[odd].at[index], None)
        value_z, _ = splines_z(row_z, window)
        weights_z[at_narrow] = value_z
        charged = wave * charge
        first = pl.multiple_of(at_narrow * cells_z, HALO_Z)
        for at_wide in range(wide_count):
            lanes = slice(at_wide * atoms, (at_wide + 1) * atoms)
            near = value_z[:, lanes]
            left = jnp.concatenate(
                [near * charged[c : c + 1, lanes] for c in range(2 * fine)], axis=0
            )
            across = weights[odd][index, :, lanes]
            total = lax.dot_general(
                jnp.concatenate(split(left), axis=1),
                jnp.concatenate([across, across], axis=1),
                NT,
                preferred_element_type=jnp.float32,
            )
            total = total[:, 0:128] + total[:, 128:256]
            start = at_wide // copies * 128
            for c in range(2 * fine):
                spot = slice(c % 2 * GRID_X + start, c % 2 * GRID_X + start + 128)
                k = at_wide % copies
                part = total[c * window : (c + 1) * window]
                grid[k, c // 2, pl.ds(first, HALO_Z), spot] += part[:HALO_Z]
                grid[k, c // 2, pl.ds(first + HALO_Z, cells_z), spot] = part[HALO_Z:]

    in_pairs(narrow_count, spread)


def joined(grid, j, lanes, cells_x):
    total = None
    for k in range(grid.shape[0]):
        moved = pltpu.roll(grid[k, j, :, lanes], (k * cells_x - HALO_X) % GRID_X, 1)
        total = moved if total is None else total + moved
    plane = total[HALO_Z:]
    rest = plane[: GRID_Z - HALO_Z]
    return jnp.concatenate([rest, plane[GRID_Z - HALO_Z :] + total[:HALO_Z]], axis=0)


HALVES = (slice(0, GRID_X), slice(GRID_X, 2 * GRID_X))


def start_all(sources, targets, arrivals):
    copies = [
        pltpu.make_async_copy(source, target, arrivals.at[k])
        for k, (source, target) in enumerate(zip(sources, targets))
    ]
    for copy in copies:
        copy.start()
    return copies


def atoms_kernel(table, phase, *refs):
    outs, (grid, leaving, planes_leaving), kept = refs[:6], refs[6:9], refs[9:]
    planes, weights_even, weights_odd, weights_z, waves, wave_slopes = kept
    cells_x = GRID_X // table.shape[0]
    spread_sites(
        table, None, phase, grid, (weights_even, weights_odd), weights_z, waves, wave_slopes
    )
    copies = start_all(kept[1:], outs[1:], leaving)
    for j in range(grid.shape[1]):
        for lanes in HALVES:
            planes[j, :, lanes] = joined(grid, j, lanes, cells_x)
        out = pltpu.make_async_copy(planes.at[j], outs[0].at[j], planes_leaving.at[j])
        out.start()
        copies.append(out)
    for copy in copies:
        copy.wait()


def mesh_kernel(*refs):
    sources, out_ref, refs = refs[:14], refs[14], refs[15:]
    grid, packed, weights_even, weights_odd, weights_z, waves, wave_slopes = refs[:7]
    slopes, arrivals = refs[7:9]
    held = refs[9:]
    arriving = start_all(sources, held, arrivals)
    table, shifts, phase, planes, green_ref = held[:5]
    fold_high, fold_low, unfold_high, unfold_low = held[5:9]
    atom_weights = held[9:11]
    atom_weights_z, atom_waves, atom_wave_slopes = held[11:]
    weights = (weights_even, weights_odd)
    wide_count, narrow_count, _, atoms = table.shape
    cells_x = GRID_X // wide_count
    cells_z = GRID_Z // narrow_count
    window = cells_z + HALO_Z
    copies, fine = grid.shape[:2]
    channels = 2 * fine
    reach = cells_x + HALO_X
    piece = lax.axis_index("wide") * narrow_count + lax.axis_index("narrow")
    lane_zero = lax.broadcasted_iota(jnp.int32, (1, GRID_X // 2), 1) == 0
    row_zero = lax.broadcasted_iota(jnp.int32, (GRID_Z // 2, 1), 0) == 0

    def fold():
        return (fold_high[...], fold_low[...])

    def unfold():
        return (unfold_high[...], unfold_low[...])

    for copy in arriving[:3]:
        copy.wait()
    spread_sites(table, shifts, phase, grid, weights, weights_z, waves, wave_slopes)
    for copy in arriving[3:9]:
        copy.wait()

    for j in range(fine):
        for lanes in HALVES:
            planes[j, :, lanes] += joined(grid, j, lanes, cells_x)

    is_first = piece == 0

    def paired(real, imag, zero, axis):
        half = real.shape[axis] // 2
        first = (slice(None),) * axis + (slice(0, half),)
        second = (slice(None),) * axis + (slice(half, 2 * half),)
        real_c, real_s = real[first], real[second]
        if imag is None:
            none = jnp.zeros_like(real_s)
            real_all = [real_c, jnp.where(zero, real_s, real_c)]
            imag_all = [jnp.where(zero, none, -real_s), jnp.where(zero, none, real_s)]
        else:
            imag_c, imag_s = imag[first], imag[second]
            real_all = [
                real_c + jnp.where(zero, 0.0, imag_s),
                jnp.where(zero, real_s, real_c - imag_s),
            ]
            imag_all = [
                imag_c - jnp.where(zero, 0.0, real_s),
                jnp.where(zero, imag_s, imag_c + real_s),
            ]
        return jnp.concatenate(real_all, axis=axis), jnp.concatenate(imag_all, axis=axis)

    def merged(real, imag, zero, axis):
        half = real.shape[axis] // 2
        first = (slice(None),) * axis + (slice(0, half),)
        second = (slice(None),) * axis + (slice(half, 2 * half),)
        real_a, real_b = real[first], real[second]
        imag_a, imag_b = imag[first], imag[second]
        real = [
            real_a + jnp.where(zero, 0.0, real_b),
            jnp.where(zero, real_b, imag_b - imag_a),
        ]
        imag = [
            imag_a + jnp.where(zero, 0.0, imag_b),
            jnp.where(zero, imag_b, real_a - real_b),
        ]
        return jnp.concatenate(real, axis=axis), jnp.concatenate(imag, axis=axis)

    modes = {}
    parts = []

    def slot(j):
        first_imag = planes[0, :, GRID_X:]
        if j == fine:
            real, imag = jnp.where(is_first, first_imag, 0.0), None
        else:
            real, imag = planes[j, :, 0:GRID_X], planes[j, :, GRID_X:]
            if j == 0:
                imag = jnp.where(is_first, 0.0, imag)
        real = split(real)
        imag = None if imag is None else split(imag)
        yield
        real = multiply(real, fold())
        imag = None if imag is None else multiply(imag, fold())
        yield
        real, imag = paired(real, imag, lane_zero, 1)
        real, imag = split(real), split(imag)
        yield
        real, imag = multiply(unfold(), real), multiply(unfold(), imag)
        yield
        real, imag = paired(real, imag, row_zero, 0)
        green = green_ref[j]
        mode = GRID_Y // 2 if j == fine else piece * fine + j
        share = jnp.where((mode == 0) | (mode == GRID_Y // 2), 0.5, 1.0)
        parts.append(share * jnp.sum(green * (real * real + imag * imag), axis=0, keepdims=True))
        real, imag = green * real, green * imag
        if j == fine:
            modes[j] = (real, imag)
            return
        if j == 0:
            real, imag = real - modes[fine][1], imag + modes[fine][0]
        real, imag = merged(real, imag, row_zero, 0)
        real, imag = split(real), split(imag)
        yield
        real, imag = multiply(fold(), real), multiply(fold(), imag)
        yield
        real, imag = merged(real, imag, lane_zero, 1)
        scale = jnp.where(piece * fine + j == 0, 1.0, 2.0)
        real, imag = split(real * scale), split(imag * scale)
        yield
        real, imag = multiply(real, unfold()), multiply(imag, unfold())
        yield
        for k, part in enumerate((real, imag)):
            for at_wide in range(wide_count):
                moved = pltpu.roll(part, (HALO_X - at_wide * cells_x) % GRID_X, 1)[:, 0:128]
                high = moved.astype(jnp.bfloat16).astype(jnp.float32)
                again = pltpu.roll(high, reach % 128, 1)
                low = pltpu.roll(moved - high, 2 * reach % 128, 1)
                sides = []
                for side in range(2):
                    lane = lax.broadcasted_iota(jnp.int32, (1, 128), 1) + side * 128
                    value = jnp.where(lane < 2 * reach, again, low)
                    if side == 0:
                        value = jnp.where(lane < reach, high, value)
                    sides.append(value.astype(jnp.bfloat16))
                block = jnp.concatenate(sides, axis=1)
                packed[at_wide, 2 * j + k, HALO_BITS:, :] = block
                packed[at_wide, 2 * j + k, 0:HALO_BITS, :] = block[GRID_Z - HALO_BITS :]

    skewed([slot(j) for j in [fine, *range(fine)]])
    energy = sum(parts[1:], parts[0])
    energy = jnp.broadcast_to(jnp.sum(energy, axis=1, keepdims=True), (1, 128))

    for copy in arriving[9:]:
        copy.wait()

    def collect(index, odd):
        at_narrow = 2 * index + odd
        kinds = (
            (None, atom_weights, atom_weights_z, atom_waves, atom_wave_slopes),
            (shifts, weights, weights_z, waves, wave_slopes),
        )
        slopes_z = []
        for kind, given in enumerate(kinds):
            row_x, _, row_z, _ = site_rows(table, given[0], at_narrow)
            splines_x(row_x, cells_x + HALO_X, None, slopes.at[odd, kind])
            slopes_z.append(splines_z(row_z, window)[1])
        first = pl.multiple_of(at_narrow * cells_z, HALO_BITS)
        tall = cells_z + HALO_BITS
        for at_wide in range(wide_count):
            lanes = slice(at_wide * atoms, (at_wide + 1) * atoms)
            left = jnp.concatenate(
                [packed[at_wide, c, pl.ds(first, tall), :] for c in range(channels)], axis=0
            )

            def across(right):
                high = right[0:reach]
                rest = jnp.zeros((256 - 3 * reach, 2 * atoms), jnp.bfloat16)
                right = jnp.concatenate([high, right[128 : 128 + reach], high, rest], axis=0)
                return lax.dot_general(left, right, NN, preferred_element_type=jnp.float32)

            def both(which):
                return jnp.concatenate([given[which][at_narrow, :, lanes] for given in kinds], axis=1)

            value = across(
                jnp.concatenate([given[1][odd][index, :, lanes] for given in kinds], axis=1)
            )
            slope = across(
                jnp.concatenate([slopes[odd, kind, :, lanes] for kind in range(2)], axis=1)
            )
            near = both(2)
            near_slope = jnp.concatenate([row[:, lanes] for row in slopes_z], axis=1)
            wave = both(3)
            wave_slope = both(4)
            plain = jnp.zeros((window, 2 * atoms), jnp.float32)
            along_x = plain
            along_y = plain
            for c in range(channels):
                block = slice((c + 1) * tall - window, (c + 1) * tall)
                plain = plain + value[block] * wave[c : c + 1]
                along_x = along_x + slope[block] * wave[c : c + 1]
                along_y = along_y + value[block] * wave_slope[c : c + 1]
            results = [
                jnp.sum(near * plain, axis=0, keepdims=True),
                -jnp.sum(near * along_x, axis=0, keepdims=True),
                -jnp.sum(near * along_y, axis=0, keepdims=True),
                -jnp.sum(near_slope * plain, axis=0, keepdims=True),
            ]
            for k, row in enumerate(results):
                out_ref[at_wide, at_narrow, :, 2 * k * atoms : 2 * (k + 1) * atoms] = row
            out_ref[at_wide, at_narrow, :, 8 * atoms :] = energy

    in_pairs(narrow_count, collect)


def finish_kernel(arrived, species, atom_ref, centroid_ref, energy_ref):
    atoms = species.shape[1]
    total = arrived[0]
    for k in range(1, arrived.shape[0]):
        total = total + arrived[k]
    oxygen = 1.0 - species[...].astype(jnp.float32)
    for k in range(4):
        atom_ref[k] = total[:, 2 * k * atoms : (2 * k + 1) * atoms]
        centroid_ref[k] = total[:, (2 * k + 1) * atoms : (2 * k + 2) * atoms] * oxygen
    energy_ref[...] = total[:, 8 * atoms :] * (1.0 / (atoms * arrived.shape[0]))


def mode_factors(length, order):
    wrapped = np.where(2 * order >= length, order - length, order)
    square = (wrapped / length) ** 2
    ratio = (4.0 + 2.0 * np.cos(2.0 * math.pi * order / length)) / 6.0
    return np.stack([np.exp(-(math.pi**2) * square / ewald_beta**2) / ratio**2, square])


def folded_order(length):
    half = length // 2
    counter = np.arange(half)
    return np.concatenate([counter, np.where(counter == 0, half, length - counter)])


def fold_table(length):
    half = length // 2
    turns = np.outer(np.arange(length), np.arange(half)) % length * (2.0 * math.pi / length)
    sines = np.sin(turns)
    sines[:, 0] = 1.0 - 2.0 * (np.arange(length) % 2)
    return np.concatenate([np.cos(turns), sines], axis=1)


def halves(table):
    high = table.astype(jnp.bfloat16)
    low = (table - high.astype(np.float64)).astype(jnp.bfloat16)
    return high, low


def vmem(count):
    return [pl.BlockSpec(memory_space=pltpu.VMEM)] * count


def hbm(count):
    return [pl.BlockSpec(memory_space=pltpu.HBM)] * count


def shaped(shape, dtype=jnp.float32):
    return jax.ShapeDtypeStruct(shape, dtype)


def limits(mebibytes):
    return pltpu.CompilerParams(vmem_limit_bytes=mebibytes * 1024 * 1024)


def local(
    positions,
    species,
    neighbours,
    embed_one_w,
    embed_one_b,
    embed_two_w,
    embed_two_b,
    embed_three_w,
    embed_three_b,
    fit_one_w,
    fit_one_b,
    fit_two_w,
    fit_two_b,
    fit_three_w,
    fit_three_b,
    fit_out_w,
):
    axes = ("wide", "narrow")
    wide_count = lax.axis_size("wide")
    narrow_count = lax.axis_size("narrow")
    pieces = wide_count * narrow_count
    atoms = positions.shape[4]
    listed = neighbours.shape[4]
    fine = GRID_Y // 2 // pieces
    width_three = embed_three_w.shape[1]
    entries, hidden = fit_one_w.shape
    kinds = species.reshape(1, atoms)

    packed = pl.pallas_call(
        pack_kernel,
        out_shape=shaped((pieces, 4, atoms)),
        in_specs=vmem(2),
        out_specs=vmem(1)[0],
        name="pack",
    )(positions.reshape(3, 1, atoms), kinds)
    table = lax.all_to_all(packed, axes, 0, 0, tiled=True)
    table = table.reshape(wide_count, narrow_count, 4, atoms)

    tall = 4 * ROW_PAD
    bf16 = jnp.bfloat16
    wave_rows = -(-2 * fine // 8) * 8
    angle = np.arange(GRID_Y) * (2.0 * math.pi / GRID_Y)
    constants = np.concatenate(
        [
            np.stack([np.cos(angle), np.sin(angle)]),
            mode_factors(GRID_Y, np.arange(GRID_Y)),
            mode_factors(GRID_X, folded_order(GRID_X)),
            mode_factors(GRID_Z, folded_order(GRID_Z)),
        ]
    )
    constants[2] *= coulomb / (math.pi * GRID_X * GRID_Y * GRID_Z)
    arguments = (
        neighbours.reshape(atoms, listed),
        embed_one_w,
        embed_one_b,
        embed_two_w,
        embed_two_b[None],
        embed_three_w,
        embed_three_b[None],
        fit_one_w.T,
        fit_one_b[None],
        fit_two_w,
        fit_two_b[None],
        fit_three_w,
        fit_three_b[None],
        jnp.asarray(constants, jnp.float32),
    )
    held = [arguments[k] for k in (0, 1, 2, 3, 4, 5, 6, 8, 10, 12, 13, 9, 11, 7)]
    prepared = pl.pallas_call(
        prepare_kernel,
        out_shape=(
            shaped((listed, atoms), jnp.int32),
            shaped((256, 16)),
            shaped((2 * ROW_PAD, 3 * ROW_PAD), bf16),
            shaped((tall, 6 * ROW_PAD), bf16),
            shaped((hidden, entries), bf16),
            shaped((hidden, entries), bf16),
        )
        + (shaped((hidden, hidden), bf16),) * 4
        + (shaped((wave_rows, GRID_Y)), shaped((fine + 1, GRID_Z, GRID_X))),
        in_specs=hbm(len(arguments)),
        out_specs=tuple(vmem(12)),
        scratch_shapes=[
            pltpu.VMEM((16, 256), jnp.float32),
            pltpu.VMEM((256, 256), jnp.float32),
            pltpu.SemaphoreType.DMA((len(held),)),
        ]
        + [pltpu.VMEM(array.shape, array.dtype) for array in held],
        compiler_params=limits(62),
        cost_estimate=pl.CostEstimate(
            flops=1000000, bytes_accessed=8 * entries * hidden, transcendentals=0
        ),
        name="prepare",
    )(*arguments)
    phase, green = prepared[10:]
    fitted = (table, *prepared[:10], fit_out_w.T)
    dipole, shifts = pl.pallas_call(
        centroid_kernel,
        out_shape=(shaped((3, 1, atoms)), shaped((pieces, 4, atoms))),
        in_specs=hbm(12),
        out_specs=tuple(vmem(2)),
        scratch_shapes=[
            pltpu.VMEM((4, tall, atoms), jnp.float32),
            pltpu.VMEM((width_three * AXIS_COLUMNS, atoms), jnp.float32),
            pltpu.VMEM((tall, SLOT_CHUNK * atoms), jnp.float32),
            pltpu.VMEM((tall, SLOT_CHUNK * atoms), jnp.float32),
            pltpu.SemaphoreType.DMA((len(fitted),)),
        ]
        + [pltpu.VMEM(array.shape, array.dtype) for array in fitted],
        compiler_params=limits(62),
        name="centroids",
    )(*fitted)
    shifts = lax.all_to_all(shifts, axes, 0, 0, tiled=True)
    shifts = shifts.reshape(wide_count, narrow_count, 4, atoms)

    copies = 128 // (GRID_X // wide_count)
    window = GRID_Z // narrow_count + HALO_Z
    length = wide_count * atoms
    grid = pltpu.VMEM((copies, fine, HALO_Z + GRID_Z, 2 * GRID_X), jnp.float32)
    planes = shaped((fine, GRID_Z, 2 * GRID_X))
    kept = (
        shaped((narrow_count // 2, 256, length), bf16),
        shaped((narrow_count // 2, 256, length), bf16),
        shaped((narrow_count, window, length)),
        shaped((narrow_count, wave_rows, length)),
        shaped((narrow_count, wave_rows, length)),
    )
    spread_atoms = pl.pallas_call(
        atoms_kernel,
        out_shape=(planes,) + kept,
        in_specs=vmem(2),
        out_specs=tuple(hbm(6)),
        scratch_shapes=[
            grid,
            pltpu.SemaphoreType.DMA((len(kept),)),
            pltpu.SemaphoreType.DMA((fine,)),
        ]
        + [pltpu.VMEM(array.shape, array.dtype) for array in (planes,) + kept],
        compiler_params=limits(62),
        cost_estimate=pl.CostEstimate(
            flops=2 * 3 * pieces * atoms * 2 * fine * window * 128,
            bytes_accessed=8 * 1024 * 1024,
            transcendentals=0,
        ),
        name="atoms",
    )(table, phase)
    out_width = 8 * atoms + 128
    tables = halves(fold_table(GRID_X)) + halves(fold_table(GRID_X).T)
    tables = [jnp.asarray(half) for half in tables]
    given = (table, shifts, phase, spread_atoms[0], green, *tables, *spread_atoms[1:])
    partial = pl.pallas_call(
        mesh_kernel,
        out_shape=shaped((wide_count, narrow_count, 1, out_width)),
        in_specs=hbm(len(given)),
        out_specs=vmem(1)[0],
        scratch_shapes=[
            grid,
            pltpu.VMEM((wide_count, 2 * fine, HALO_BITS + GRID_Z, 256), bf16),
        ]
        + [pltpu.VMEM(array.shape, array.dtype) for array in kept]
        + [pltpu.VMEM((2, 2, 256, length), bf16), pltpu.SemaphoreType.DMA((len(given),))]
        + [pltpu.VMEM(array.shape, array.dtype) for array in given],
        compiler_params=limits(62),
        name="mesh",
    )(*given)
    arrived = lax.all_to_all(partial.reshape(pieces, 1, out_width), axes, 0, 0, tiled=True)
    atom_field, centroid_field, energy = pl.pallas_call(
        finish_kernel,
        out_shape=(shaped((4, 1, atoms)), shaped((4, 1, atoms)), shaped((1, 128))),
        in_specs=vmem(2),
        out_specs=tuple(vmem(3)),
        name="finish",
    )(arrived, kinds)
    atom_field = atom_field.reshape(4, 1, 1, 1, atoms)
    centroid_field = centroid_field.reshape(4, 1, 1, 1, atoms)
    return (dipole.reshape(3, 1, 1, 1, atoms), atom_field, centroid_field, energy[0, 0])


def solution(mesh):
    column = P(None, "wide", "narrow", None, None)
    in_specs = (column, P("wide", "narrow", None, None), P("wide", "narrow", None, None, None))
    in_specs = in_specs + (P(),) * 13
    out_specs = (column, column, column, P())
    return jax.shard_map(local, mesh=mesh, in_specs=in_specs, out_specs=out_specs, check_vma=False)
```

```python
import math

import jax
import jax.numpy as jnp
import numpy as np
from jax import lax
from jax.experimental import pallas as pl
from jax.experimental.pallas import tpu as pltpu
from jax.sharding import PartitionSpec as P

GRID_X = 256
GRID_Y = 256
GRID_Z = 256
AXIS_COLUMNS = 16

radius_scale = 24.0
wannier_reach = 0.5
ewald_beta = 0.9
coulomb = 0.25

ROW_PAD = 32
SLOT_CHUNK = 16
HALO_X = 16
HALO_Z = 8
HALO_BITS = 16

NN = (((1,), (0,)), ((), ()))
NT = (((1,), (1,)), ((), ()))


def split(value):
    high = value.astype(jnp.bfloat16)
    low = (value - high.astype(jnp.float32)).astype(jnp.bfloat16)
    return high, low


def multiply(left, right, dims=NN):
    def one(a, b):
        return lax.dot_general(a, b, dims, preferred_element_type=jnp.float32)

    return one(left[0], right[0]) + (one(left[1], right[0]) + one(left[0], right[1]))


def by_right(left, right):
    rows = left[0].shape[0]
    both = lax.dot_general(
        jnp.concatenate(left, axis=0), right[0], NN, preferred_element_type=jnp.float32
    )
    rest = lax.dot_general(left[0], right[1], NN, preferred_element_type=jnp.float32)
    return both[:rows] + (both[rows:] + rest)


def by_left(left, right):
    rows = left.shape[0] // 2
    both = lax.dot_general(left, right[0], NN, preferred_element_type=jnp.float32)
    rest = lax.dot_general(left[:rows], right[1], NN, preferred_element_type=jnp.float32)
    return both[:rows] + (both[rows:] + rest)


def spline_pair(offset):
    centred = offset - 2.0
    away = jnp.abs(centred)
    outer = jnp.maximum(2.0 - away, 0.0)
    inner = jnp.maximum(1.0 - away, 0.0)
    outer_square = outer * outer
    inner_square = inner * inner
    value = (outer_square * outer - 4.0 * (inner_square * inner)) * (1.0 / 6.0)
    slope = jnp.where(centred < 0.0, 0.5, -0.5) * (outer_square - 4.0 * inner_square)
    return value, slope


def lookup(row_table, spot):
    found = None
    for part in range(row_table.shape[1] // 128):
        inside = spot // 128 == part
        here = jnp.take_along_axis(
            jnp.broadcast_to(row_table[:, part * 128 : (part + 1) * 128], spot.shape),
            lax.rem(spot, 128),
            axis=1,
            mode="promise_in_bounds",
        )
        found = here if found is None else jnp.where(inside, here, found)
    return found


def pack_kernel(positions, species, out_ref):
    kinds = species[...]
    rows = [positions[component] for component in range(3)]
    rows[0] = jnp.where(kinds > 0, -rows[0], rows[0])
    rows.append(kinds.astype(jnp.float32))
    rows = jnp.concatenate(rows, axis=0)
    for target in range(out_ref.shape[0]):
        out_ref[target] = rows


def prepare_kernel(
    neighbours,
    embed_one_w,
    embed_one_b,
    embed_two_w,
    embed_two_b,
    embed_three_w,
    embed_three_b,
    fit_one_w,
    fit_one_b,
    fit_two_w,
    fit_two_b,
    fit_three_w,
    fit_three_b,
    constants,
    codes_ref,
    columns_ref,
    second_ref,
    third_ref,
    one_high_ref,
    one_low_ref,
    two_high_ref,
    two_low_ref,
    three_high_ref,
    three_low_ref,
    phase_ref,
    green_ref,
    rows,
    square,
    arrivals,
    *held,
):
    sources = (
        neighbours,
        embed_one_w,
        embed_one_b,
        embed_two_w,
        embed_two_b,
        embed_three_w,
        embed_three_b,
        fit_one_b,
        fit_two_b,
        fit_three_b,
        constants,
        fit_two_w,
        fit_three_w,
        fit_one_w,
    )
    copies = [
        pltpu.make_async_copy(source, target, arrivals.at[k])
        for k, (source, target) in enumerate(zip(sources, held))
    ]
    for copy in copies:
        copy.start()
    (
        neighbours,
        embed_one_w,
        embed_one_b,
        embed_two_w,
        embed_two_b,
        embed_three_w,
        embed_three_b,
        fit_one_b,
        fit_two_b,
        fit_three_b,
        constants,
        fit_two_w,
        fit_three_w,
        fit_one_w,
    ) = held
    for copy in copies[:11]:
        copy.wait()
    pieces = lax.axis_size("wide") * lax.axis_size("narrow")
    piece = lax.axis_index("wide") * lax.axis_size("narrow") + lax.axis_index("narrow")
    width_one = embed_one_w.shape[1]
    hidden = fit_two_w.shape[0]
    codes_ref[...] = jnp.transpose(neighbours[...].astype(jnp.float32)).astype(jnp.int32)
    rows[...] = jnp.zeros_like(rows)
    for kind in range(2):
        rows[kind : kind + 1, 0:width_one] = embed_one_w[kind : kind + 1, :]
        rows[2 + kind : 3 + kind, 0:width_one] = embed_one_b[kind : kind + 1, :]
        rows[2 + kind : 3 + kind, width_one : width_one + 1] = jnp.full((1, 1), 40.0, jnp.float32)
    for row, source in ((4, fit_one_b), (5, fit_two_b), (6, fit_three_b)):
        rows[row : row + 1, 0:hidden] = source[...]
    columns_ref[...] = jnp.transpose(rows[...])

    square[...] = jnp.zeros_like(square)
    for k in range(2):
        square[0:width_one, k * ROW_PAD : k * ROW_PAD + width_one] = embed_two_w[
            :, k * width_one : (k + 1) * width_one
        ]
        square[
            width_one : width_one + 1, k * ROW_PAD : k * ROW_PAD + width_one
        ] = embed_two_b[:, k * width_one : (k + 1) * width_one]
    high, low = split(jnp.transpose(square[0:128, 0:128])[0 : 2 * ROW_PAD, 0:ROW_PAD])
    second_ref[...] = jnp.concatenate([high, high, low], axis=1)
    square[0:128, 0:128] = jnp.zeros((128, 128), jnp.float32)
    for g in range(2):
        for k in range(4):
            square[
                g * ROW_PAD : g * ROW_PAD + width_one, k * ROW_PAD : k * ROW_PAD + width_one
            ] = embed_three_w[
                g * width_one : (g + 1) * width_one, k * width_one : (k + 1) * width_one
            ]
    for k in range(4):
        square[
            width_one : width_one + 1, k * ROW_PAD : k * ROW_PAD + width_one
        ] = embed_three_b[:, k * width_one : (k + 1) * width_one]
    high, low = split(jnp.transpose(square[0:128, 0:128])[:, 0 : 2 * ROW_PAD])
    third_ref[...] = jnp.concatenate([high, high, low], axis=1)
    for copy in copies[11:13]:
        copy.wait()
    for source, high_ref, low_ref in (
        (fit_two_w, two_high_ref, two_low_ref),
        (fit_three_w, three_high_ref, three_low_ref),
    ):
        square[0:hidden, 0:hidden] = source[...]
        high_ref[...], low_ref[...] = split(jnp.transpose(square[...])[0:hidden, 0:hidden])

    fine = GRID_Y // 2 // pieces
    shape = (phase_ref.shape[0], 128)
    row = lax.broadcasted_iota(jnp.int32, shape, 0)
    mode = piece * fine + row // 2
    for part in range(GRID_Y // 128):
        cell = lax.broadcasted_iota(jnp.int32, shape, 1) + part * 128
        spot = lax.rem(mode * cell, GRID_Y)
        cosine = lookup(constants[0:1, :], spot)
        sine = lookup(constants[1:2, :], spot)
        alternate = (1 - 2 * lax.rem(cell, 2)).astype(jnp.float32)
        odd = jnp.where(mode == 0, alternate, -sine)
        value = jnp.where(lax.rem(row, 2) == 0, cosine, odd)
        phase_ref[:, part * 128 : (part + 1) * 128] = jnp.where(row < 2 * fine, value, 0.0)

    column = jnp.transpose(constants[...])
    lane = lax.broadcasted_iota(jnp.int32, (1, GRID_Y), 1)
    for j in range(fine + 1):
        here = lane == (GRID_Y // 2 if j == fine else piece * fine + j)
        factor = jnp.sum(jnp.where(here, constants[2:3, :], 0.0), axis=1, keepdims=True)
        part = jnp.sum(jnp.where(here, constants[3:4, :], 0.0), axis=1, keepdims=True)
        wave = (part + constants[5:6, :]) + column[:, 7:8]
        top = (factor * constants[4:5, :]) * column[:, 6:7]
        green_ref[j] = jnp.where(wave == 0.0, 0.0, top / jnp.where(wave == 0.0, 1.0, wave))

    copies[13].wait()
    one_high_ref[...], one_low_ref[...] = split(fit_one_w[...])


def centroid_kernel(
    table,
    codes,
    columns,
    second,
    third,
    one_high,
    one_low,
    two_high,
    two_low,
    three_high,
    three_low,
    fit_out_w,
    dipole_ref,
    shift_ref,
    matrix,
    descriptor,
    arrivals,
    *held,
):
    sources = (table, codes, columns, second, third)
    sources += (one_high, one_low, two_high, two_low, three_high, three_low, fit_out_w)
    copies = [
        pltpu.make_async_copy(source, target, arrivals.at[k])
        for k, (source, target) in enumerate(zip(sources, held))
    ]
    for copy in copies:
        copy.start()
    table, codes, columns, second, third = held[:5]
    one_high, one_low, two_high, two_low, three_high, three_low, fit_out_w = held[5:]
    for copy in copies[:5]:
        copy.wait()
    wide_count, narrow_count, _, atoms = table.shape
    listed = codes.shape[0]
    width_three = fit_out_w.shape[0]
    width_one = width_three // 4
    hidden_width = two_high.shape[0]
    cells = (GRID_X // wide_count, GRID_Y, GRID_Z // narrow_count)
    at_wide = lax.axis_index("wide")
    at_narrow = lax.axis_index("narrow")
    own = jnp.abs(table[at_wide, at_narrow])
    nearby = []
    for step in range(9):
        wide_at = lax.rem(at_wide + (step // 3 - 1) + wide_count, wide_count)
        narrow_at = lax.rem(at_narrow + (step % 3 - 1) + narrow_count, narrow_count)
        nearby.append(table[wide_at, narrow_at])

    second_all = second[...]
    third_all = third[...]
    weight_oxygen = jnp.broadcast_to(columns[0:ROW_PAD, 0:1], (ROW_PAD, atoms))
    weight_hydrogen = jnp.broadcast_to(columns[0:ROW_PAD, 1:2], (ROW_PAD, atoms))
    bias_oxygen = jnp.broadcast_to(columns[0:ROW_PAD, 2:3], (ROW_PAD, atoms))
    bias_hydrogen = jnp.broadcast_to(columns[0:ROW_PAD, 3:4], (ROW_PAD, atoms))
    matrix[...] = jnp.zeros_like(matrix)

    def chunk(first):
        code = codes[pl.ds(first, SLOT_CHUNK), :]
        offset = code // atoms
        slot = code - offset * atoms
        step_x = jnp.where(offset >= 9, 1, 0) + jnp.where(offset >= 18, 1, 0)
        rest = offset - 9 * step_x
        step_z = jnp.where(rest >= 3, 1, 0) + jnp.where(rest >= 6, 1, 0)
        step_y = rest - 3 * step_z
        brick = step_x * 3 + step_z
        found = []
        for component in range(3):
            picked = jnp.zeros((SLOT_CHUNK, atoms), jnp.float32)
            for step in range(9):
                row = jnp.broadcast_to(
                    nearby[step][component : component + 1], (SLOT_CHUNK, atoms)
                )
                here = jnp.take_along_axis(row, slot, axis=1, mode="promise_in_bounds")
                picked = jnp.where(brick == step, here, picked)
            found.append(picked)
        hydrogen = found[0] < 0.0
        found[0] = jnp.abs(found[0])
        scaled = []
        for component, step in enumerate((step_x, step_y, step_z)):
            extent = float(cells[component])
            relative = (step - 1).astype(jnp.float32) * extent + (
                found[component] - own[component : component + 1]
            ) * extent
            scaled.append(relative * (1.0 / radius_scale))
        smooth = 1.0 / (
            1.0 + (scaled[0] * scaled[0] + scaled[1] * scaled[1] + scaled[2] * scaled[2])
        )
        radial = [smooth] + [smooth * part for part in scaled]
        first_layers = []
        for k in range(SLOT_CHUNK):
            row = smooth[k : k + 1]
            kind = hydrogen[k : k + 1]
            weight = jnp.where(kind, weight_hydrogen, weight_oxygen)
            bias = jnp.where(kind, bias_hydrogen, bias_oxygen)
            first_layers.append(jnp.tanh(weight * row + bias))
        layer_one = jnp.concatenate(first_layers, axis=1)
        high, low = split(layer_one)
        layer_two = lax.dot_general(
            second_all,
            jnp.concatenate([high, low, high], axis=0),
            NN,
            preferred_element_type=jnp.float32,
        )
        layer_two = jnp.tanh(layer_two) + jnp.concatenate(
            [layer_one, layer_one], axis=0
        )
        high, low = split(layer_two)
        layer_three = lax.dot_general(
            third_all,
            jnp.concatenate([high, low, high], axis=0),
            NN,
            preferred_element_type=jnp.float32,
        )
        layer_three = jnp.tanh(layer_three) + jnp.concatenate(
            [layer_two, layer_two], axis=0
        )
        for part in range(4):
            total = matrix[part]
            for k in range(SLOT_CHUNK):
                total = total + layer_three[:, k * atoms : (k + 1) * atoms] * radial[part][k : k + 1]
            matrix[part] = total

    def two_chunks(index, carry):
        first = pl.multiple_of(index * (2 * SLOT_CHUNK), 2 * SLOT_CHUNK)
        chunk(first)
        chunk(pl.multiple_of(first + SLOT_CHUNK, SLOT_CHUNK))
        return carry

    lax.fori_loop(0, listed // (2 * SLOT_CHUNK), two_chunks, 0)

    parts = []
    for part in range(4):
        padded = matrix[part] * (1.0 / listed)
        parts.append(
            jnp.concatenate(
                [padded[k * ROW_PAD : k * ROW_PAD + width_one] for k in range(4)], axis=0
            )
        )
    leading = [part[0:AXIS_COLUMNS] for part in parts]
    for row in range(width_three):
        total = parts[0][row : row + 1] * leading[0]
        for part in range(1, 4):
            total = total + parts[part][row : row + 1] * leading[part]
        descriptor[row * AXIS_COLUMNS : (row + 1) * AXIS_COLUMNS, :] = total
    for copy in copies[5:]:
        copy.wait()

    def layer(high_ref, low_ref, given, column):
        weights = (high_ref[...], low_ref[...])
        return jnp.tanh(multiply(weights, split(given)) + columns[0:hidden_width, column : column + 1])

    hidden = layer(one_high, one_low, descriptor[...], 4)
    hidden = hidden + layer(two_high, two_low, hidden, 5)
    hidden = hidden + layer(three_high, three_low, hidden, 6)
    coeffs = multiply(split(fit_out_w[...]), split(hidden))
    vector = jnp.concatenate(
        [jnp.sum(coeffs * parts[1 + c], axis=0, keepdims=True) for c in range(3)], axis=0
    )
    oxygen = 1.0 - own[3:4]
    for c in range(3):
        dipole_ref[c] = vector[c : c + 1] * oxygen
    moved = wannier_reach * jnp.tanh(vector)
    moved = jnp.concatenate([moved, jnp.zeros((1, atoms), jnp.float32)], axis=0)
    for target in range(shift_ref.shape[0]):
        shift_ref[target] = moved


def mesh_kernel(
    table,
    shifts,
    phase,
    green_ref,
    fold_stack,
    unfold_stack,
    out_ref,
    grid,
    planes,
    packed,
    weights_even,
    weights_odd,
    slopes_even,
    slopes_odd,
    weights_z,
    slopes_z,
    waves,
    wave_slopes,
):
    wide_count, narrow_count, _, atoms = table.shape
    cells_x = GRID_X // wide_count
    cells_z = GRID_Z // narrow_count
    window = cells_z + HALO_Z
    reach = cells_x + HALO_X
    pair = 2 * atoms
    length = wide_count * pair
    copies = grid.shape[0]
    fine = grid.shape[1]
    channels = 2 * fine
    rows = phase.shape[0]
    half_x = GRID_X // 2
    half_z = GRID_Z // 2
    piece = lax.axis_index("wide") * narrow_count + lax.axis_index("narrow")
    lane_zero = lax.broadcasted_iota(jnp.int32, (1, half_x), 1) == 0
    row_zero = lax.broadcasted_iota(jnp.int32, (half_z, 1), 0) == 0

    def fold():
        return (fold_stack[0:GRID_X, :], fold_stack[GRID_X:, :])

    def unfold():
        return (unfold_stack[0:GRID_X, :], unfold_stack[GRID_X:, :])

    def sites(at_wide, at_narrow):
        atom = jnp.abs(table[at_wide, at_narrow])
        moved = shifts[at_wide, at_narrow]
        found = []
        for component, extent in enumerate((cells_x, GRID_Y, cells_z)):
            start = atom[component : component + 1] * float(extent)
            found.append(jnp.concatenate([start, start + moved[component : component + 1]], axis=1))
        oxygen = 1.0 - atom[3:4]
        found.append(jnp.concatenate([6.0 * oxygen + atom[3:4], -8.0 * oxygen], axis=1))
        return found

    def line(at_narrow):
        groups = [sites(at_wide, at_narrow) for at_wide in range(wide_count)]
        return [jnp.concatenate([g[k] for g in groups], axis=1) for k in range(4)]

    def splines_z(row):
        counter = lax.broadcasted_iota(jnp.int32, (window, 1), 0).astype(jnp.float32)
        return spline_pair(row - (counter - float(HALO_Z)))

    def fill_x(row, targets):
        counter = lax.broadcasted_iota(jnp.int32, (reach, 1), 0).astype(jnp.float32)
        both = spline_pair(row - (counter - float(HALO_X)))
        rest = jnp.zeros((128 - reach, length), jnp.bfloat16)
        for values, ref in zip(both, targets):
            high, low = split(values)
            ref[0:reach, :] = high
            ref[reach:128, :] = rest
            ref[128 : 128 + reach, :] = low
            ref[128 + reach : 256, :] = rest

    grid[:, :, 0:HALO_Z, :] = jnp.zeros((copies, fine, HALO_Z, 2 * GRID_X), jnp.float32)

    weights = (weights_even, weights_odd)
    slopes = (slopes_even, slopes_odd)

    def spread(index, odd):
        at_narrow = 2 * index + odd
        row_x, row_y, row_z, charge = line(at_narrow)
        lower = jnp.floor(row_y)
        back = lax.broadcasted_iota(jnp.int32, (8, 1), 0)
        value_y, slope_y = spline_pair((row_y - lower) + back.astype(jnp.float32))
        cell = lax.rem(lower.astype(jnp.int32) - back + GRID_Y, GRID_Y)
        wave_blocks = []
        slope_blocks = []
        for block in range(length // 128):
            lanes = slice(block * 128, (block + 1) * 128)
            wave = jnp.zeros((rows, 128), jnp.float32)
            wave_slope = jnp.zeros((rows, 128), jnp.float32)
            for k in range(4):
                spot = jnp.broadcast_to(cell[k : k + 1, lanes], (rows, 128))
                found = lookup(phase[...], spot)
                wave = wave + value_y[k : k + 1, lanes] * found
                wave_slope = wave_slope + slope_y[k : k + 1, lanes] * found
            wave_blocks.append(wave)
            slope_blocks.append(wave_slope)
        wave = jnp.concatenate(wave_blocks, axis=1)
        waves[at_narrow] = wave
        wave_slopes[at_narrow] = jnp.concatenate(slope_blocks, axis=1)
        fill_x(row_x, (weights[odd].at[index], slopes[odd].at[index]))
        value_z, slope_z = splines_z(row_z)
        weights_z[at_narrow] = value_z
        slopes_z[at_narrow] = slope_z
        charged = wave * charge
        first = pl.multiple_of(at_narrow * cells_z, HALO_Z)
        for at_wide in range(wide_count):
            lanes = slice(at_wide * pair, (at_wide + 1) * pair)
            near = value_z[:, lanes]
            left = jnp.concatenate(
                [near * charged[c : c + 1, lanes] for c in range(channels)], axis=0
            )
            total = lax.dot_general(
                jnp.concatenate(split(left), axis=0),
                weights[odd][index, :, lanes],
                NT,
                preferred_element_type=jnp.float32,
            )
            tall = channels * window
            total = total[:tall, 0:128] + (total[:tall, 128:256] + total[tall:, 0:128])
            start = at_wide // copies * 128
            for c in range(channels):
                spot = slice(c % 2 * GRID_X + start, c % 2 * GRID_X + start + 128)
                k = at_wide % copies
                part = total[c * window : (c + 1) * window]
                grid[k, c // 2, pl.ds(first, HALO_Z), spot] += part[:HALO_Z]
                grid[k, c // 2, pl.ds(first + HALO_Z, cells_z), spot] = part[HALO_Z:]

    def in_pairs(step):
        def both(index, carry):
            step(index, 0)
            step(index, 1)
            return carry

        lax.fori_loop(0, narrow_count // 2, both, 0)

    in_pairs(spread)

    def gather(j, carry):
        for lanes in (slice(0, GRID_X), slice(GRID_X, 2 * GRID_X)):
            total = None
            for k in range(copies):
                moved = pltpu.roll(grid[k, j, :, lanes], (k * cells_x - HALO_X) % GRID_X, 1)
                total = moved if total is None else total + moved
            planes[j, :, lanes] = total[HALO_Z:]
            planes[j, GRID_Z - HALO_Z :, lanes] += total[:HALO_Z]
        return carry

    lax.fori_loop(0, fine, gather, 0)
    is_first = piece == 0

    def paired(real, imag, zero, axis):
        half = real.shape[axis] // 2
        first = (slice(None),) * axis + (slice(0, half),)
        second = (slice(None),) * axis + (slice(half, 2 * half),)
        real_c, real_s = real[first], real[second]
        if imag is None:
            none = jnp.zeros_like(real_s)
            real_all = [real_c, jnp.where(zero, real_s, real_c)]
            imag_all = [jnp.where(zero, none, -real_s), jnp.where(zero, none, real_s)]
        else:
            imag_c, imag_s = imag[first], imag[second]
            real_all = [
                real_c + jnp.where(zero, 0.0, imag_s),
                jnp.where(zero, real_s, real_c - imag_s),
            ]
            imag_all = [
                imag_c - jnp.where(zero, 0.0, real_s),
                jnp.where(zero, imag_s, imag_c + real_s),
            ]
        return jnp.concatenate(real_all, axis=axis), jnp.concatenate(imag_all, axis=axis)

    def merged(real, imag, zero, axis):
        half = real.shape[axis] // 2
        first = (slice(None),) * axis + (slice(0, half),)
        second = (slice(None),) * axis + (slice(half, 2 * half),)
        real_a, real_b = real[first], real[second]
        imag_a, imag_b = imag[first], imag[second]
        real = [
            real_a + jnp.where(zero, 0.0, real_b),
            jnp.where(zero, real_b, imag_b - imag_a),
        ]
        imag = [
            imag_a + jnp.where(zero, 0.0, imag_b),
            jnp.where(zero, imag_b, real_a - real_b),
        ]
        return jnp.concatenate(real, axis=axis), jnp.concatenate(imag, axis=axis)

    modes = {}
    parts = []

    def slot(j):
        first_imag = planes[0, :, GRID_X:]
        if j == fine:
            real, imag = jnp.where(is_first, first_imag, 0.0), None
        else:
            real, imag = planes[j, :, 0:GRID_X], planes[j, :, GRID_X:]
            if j == 0:
                imag = jnp.where(is_first, 0.0, imag)
        real = split(real)
        imag = None if imag is None else split(imag)
        yield
        real = by_right(real, fold())
        imag = None if imag is None else by_right(imag, fold())
        yield
        real, imag = paired(real, imag, lane_zero, 1)
        real, imag = split(real), split(imag)
        yield
        real, imag = by_left(unfold_stack[...], real), by_left(unfold_stack[...], imag)
        yield
        real, imag = paired(real, imag, row_zero, 0)
        green = green_ref[j]
        mode = GRID_Y // 2 if j == fine else piece * fine + j
        share = jnp.where((mode == 0) | (mode == GRID_Y // 2), 0.5, 1.0)
        parts.append(share * jnp.sum(green * (real * real + imag * imag), axis=0, keepdims=True))
        real, imag = green * real, green * imag
        if j == fine:
            modes[j] = (real, imag)
            return
        if j == 0:
            real, imag = real - modes[fine][1], imag + modes[fine][0]
        real, imag = merged(real, imag, row_zero, 0)
        real, imag = split(real), split(imag)
        yield
        real, imag = by_left(fold_stack[...], real), by_left(fold_stack[...], imag)
        yield
        real, imag = merged(real, imag, lane_zero, 1)
        scale = jnp.where(piece * fine + j == 0, 1.0, 2.0)
        real, imag = split(real * scale), split(imag * scale)
        yield
        real, imag = by_right(real, unfold()), by_right(imag, unfold())
        yield
        for k, part in enumerate((real, imag)):
            for at_wide in range(wide_count):
                moved = pltpu.roll(part, (HALO_X - at_wide * cells_x) % GRID_X, 1)[:, 0:128]
                high = moved.astype(jnp.bfloat16).astype(jnp.float32)
                again = pltpu.roll(high, reach % 128, 1)
                low = pltpu.roll(moved - high, 2 * reach % 128, 1)
                sides = []
                for side in range(2):
                    lane = lax.broadcasted_iota(jnp.int32, (1, 128), 1) + side * 128
                    value = jnp.where(lane < 2 * reach, again, low)
                    if side == 0:
                        value = jnp.where(lane < reach, high, value)
                    sides.append(value.astype(jnp.bfloat16))
                block = jnp.concatenate(sides, axis=1)
                packed[at_wide, 2 * j + k, HALO_BITS:, :] = block
                packed[at_wide, 2 * j + k, 0:HALO_BITS, :] = block[GRID_Z - HALO_BITS :]

    waiting = [slot(j) for j in [fine, *range(fine)]]
    running = []
    while waiting or running:
        if waiting:
            running.append(waiting.pop(0))
        running = [one for one in running if next(one, running) is not running]
    energy = sum(parts[1:], parts[0])
    energy = jnp.broadcast_to(jnp.sum(energy, axis=1, keepdims=True), (1, 128))

    def collect(index, odd):
        at_narrow = 2 * index + odd
        value_z = weights_z[at_narrow]
        slope_z = slopes_z[at_narrow]
        first = pl.multiple_of(at_narrow * cells_z, HALO_BITS)
        wave = waves[at_narrow]
        wave_slope = wave_slopes[at_narrow]
        for at_wide in range(wide_count):
            lanes = slice(at_wide * pair, (at_wide + 1) * pair)
            tall = cells_z + HALO_BITS
            left = jnp.concatenate(
                [packed[at_wide, c, pl.ds(first, tall), :] for c in range(channels)], axis=0
            )

            def across(right):
                high = right[0:reach]
                rest = jnp.zeros((256 - 3 * reach, pair), jnp.bfloat16)
                right = jnp.concatenate([high, right[128 : 128 + reach], high, rest], axis=0)
                return lax.dot_general(left, right, NN, preferred_element_type=jnp.float32)

            value = across(weights[odd][index, :, lanes])
            slope = across(slopes[odd][index, :, lanes])
            plain = jnp.zeros((window, pair), jnp.float32)
            along_x = plain
            along_y = plain
            for c in range(channels):
                block = slice((c + 1) * tall - window, (c + 1) * tall)
                plain = plain + value[block] * wave[c : c + 1, lanes]
                along_x = along_x + slope[block] * wave[c : c + 1, lanes]
                along_y = along_y + value[block] * wave_slope[c : c + 1, lanes]
            near = value_z[:, lanes]
            near_slope = slope_z[:, lanes]
            results = [
                jnp.sum(near * plain, axis=0, keepdims=True),
                -jnp.sum(near * along_x, axis=0, keepdims=True),
                -jnp.sum(near * along_y, axis=0, keepdims=True),
                -jnp.sum(near_slope * plain, axis=0, keepdims=True),
            ]
            for k, row in enumerate(results):
                out_ref[at_wide, at_narrow, :, k * pair : (k + 1) * pair] = row
            out_ref[at_wide, at_narrow, :, 4 * pair :] = energy

    in_pairs(collect)


def finish_kernel(arrived, species, atom_ref, centroid_ref, energy_ref):
    atoms = species.shape[1]
    total = arrived[0]
    for k in range(1, arrived.shape[0]):
        total = total + arrived[k]
    oxygen = 1.0 - species[...].astype(jnp.float32)
    for k in range(4):
        atom_ref[k] = total[:, 2 * k * atoms : (2 * k + 1) * atoms]
        centroid_ref[k] = total[:, (2 * k + 1) * atoms : (2 * k + 2) * atoms] * oxygen
    energy_ref[...] = total[:, 8 * atoms :] * (1.0 / (atoms * arrived.shape[0]))


def mode_factors(length, order):
    wrapped = np.where(2 * order >= length, order - length, order)
    square = (wrapped / length) ** 2
    ratio = (4.0 + 2.0 * np.cos(2.0 * math.pi * order / length)) / 6.0
    return np.stack([np.exp(-(math.pi**2) * square / ewald_beta**2) / ratio**2, square])


def folded_order(length):
    half = length // 2
    counter = np.arange(half)
    return np.concatenate([counter, np.where(counter == 0, half, length - counter)])


def fold_table(length):
    half = length // 2
    turns = np.outer(np.arange(length), np.arange(half)) % length * (2.0 * math.pi / length)
    sines = np.sin(turns)
    sines[:, 0] = 1.0 - 2.0 * (np.arange(length) % 2)
    return np.concatenate([np.cos(turns), sines], axis=1)


def halves(table):
    high = table.astype(jnp.bfloat16)
    low = (table - high.astype(np.float64)).astype(jnp.bfloat16)
    return high, low


def vmem(count):
    return [pl.BlockSpec(memory_space=pltpu.VMEM)] * count


def hbm(count):
    return [pl.BlockSpec(memory_space=pltpu.HBM)] * count


def shaped(shape, dtype=jnp.float32):
    return jax.ShapeDtypeStruct(shape, dtype)


def limits(mebibytes):
    return pltpu.CompilerParams(vmem_limit_bytes=mebibytes * 1024 * 1024)


def local(
    positions,
    species,
    neighbours,
    embed_one_w,
    embed_one_b,
    embed_two_w,
    embed_two_b,
    embed_three_w,
    embed_three_b,
    fit_one_w,
    fit_one_b,
    fit_two_w,
    fit_two_b,
    fit_three_w,
    fit_three_b,
    fit_out_w,
):
    axes = ("wide", "narrow")
    wide_count = lax.axis_size("wide")
    narrow_count = lax.axis_size("narrow")
    pieces = wide_count * narrow_count
    atoms = positions.shape[4]
    listed = neighbours.shape[4]
    fine = GRID_Y // 2 // pieces
    width_three = embed_three_w.shape[1]
    entries, hidden = fit_one_w.shape
    kinds = species.reshape(1, atoms)

    packed = pl.pallas_call(
        pack_kernel,
        out_shape=shaped((pieces, 4, atoms)),
        in_specs=vmem(2),
        out_specs=vmem(1)[0],
        name="pack",
    )(positions.reshape(3, 1, atoms), kinds)
    table = lax.all_to_all(packed, axes, 0, 0, tiled=True)
    table = table.reshape(wide_count, narrow_count, 4, atoms)

    tall = 4 * ROW_PAD
    bf16 = jnp.bfloat16
    wave_rows = -(-2 * fine // 8) * 8
    angle = np.arange(GRID_Y) * (2.0 * math.pi / GRID_Y)
    constants = np.concatenate(
        [
            np.stack([np.cos(angle), np.sin(angle)]),
            mode_factors(GRID_Y, np.arange(GRID_Y)),
            mode_factors(GRID_X, folded_order(GRID_X)),
            mode_factors(GRID_Z, folded_order(GRID_Z)),
        ]
    )
    constants[2] *= coulomb / (math.pi * GRID_X * GRID_Y * GRID_Z)
    arguments = (
        neighbours.reshape(atoms, listed),
        embed_one_w,
        embed_one_b,
        embed_two_w,
        embed_two_b[None],
        embed_three_w,
        embed_three_b[None],
        fit_one_w.T,
        fit_one_b[None],
        fit_two_w,
        fit_two_b[None],
        fit_three_w,
        fit_three_b[None],
        jnp.asarray(constants, jnp.float32),
    )
    held = [arguments[k] for k in (0, 1, 2, 3, 4, 5, 6, 8, 10, 12, 13, 9, 11, 7)]
    prepared = pl.pallas_call(
        prepare_kernel,
        out_shape=(
            shaped((listed, atoms), jnp.int32),
            shaped((256, 16)),
            shaped((2 * ROW_PAD, 3 * ROW_PAD), bf16),
            shaped((tall, 6 * ROW_PAD), bf16),
            shaped((hidden, entries), bf16),
            shaped((hidden, entries), bf16),
        )
        + (shaped((hidden, hidden), bf16),) * 4
        + (shaped((wave_rows, GRID_Y)), shaped((fine + 1, GRID_Z, GRID_X))),
        in_specs=hbm(len(arguments)),
        out_specs=tuple(vmem(12)),
        scratch_shapes=[
            pltpu.VMEM((16, 256), jnp.float32),
            pltpu.VMEM((256, 256), jnp.float32),
            pltpu.SemaphoreType.DMA((len(held),)),
        ]
        + [pltpu.VMEM(array.shape, array.dtype) for array in held],
        compiler_params=limits(62),
        cost_estimate=pl.CostEstimate(
            flops=1000000, bytes_accessed=8 * entries * hidden, transcendentals=0
        ),
        name="prepare",
    )(*arguments)
    phase, green = prepared[10:]
    fitted = (table, *prepared[:10], fit_out_w.T)
    dipole, shifts = pl.pallas_call(
        centroid_kernel,
        out_shape=(shaped((3, 1, atoms)), shaped((pieces, 4, atoms))),
        in_specs=hbm(12),
        out_specs=tuple(vmem(2)),
        scratch_shapes=[
            pltpu.VMEM((4, tall, atoms), jnp.float32),
            pltpu.VMEM((width_three * AXIS_COLUMNS, atoms), jnp.float32),
            pltpu.SemaphoreType.DMA((len(fitted),)),
        ]
        + [pltpu.VMEM(array.shape, array.dtype) for array in fitted],
        compiler_params=limits(62),
        name="centroids",
    )(*fitted)
    shifts = lax.all_to_all(shifts, axes, 0, 0, tiled=True)
    shifts = shifts.reshape(wide_count, narrow_count, 4, atoms)

    cells_x = GRID_X // wide_count
    copies = 128 // cells_x
    length = wide_count * 2 * atoms
    out_width = 8 * atoms + 128
    partial = pl.pallas_call(
        mesh_kernel,
        out_shape=shaped((wide_count, narrow_count, 1, out_width)),
        in_specs=vmem(6),
        out_specs=vmem(1)[0],
        scratch_shapes=[
            pltpu.VMEM((copies, fine, HALO_Z + GRID_Z, 2 * GRID_X), jnp.float32),
            pltpu.VMEM((fine, GRID_Z, 2 * GRID_X), jnp.float32),
            pltpu.VMEM((wide_count, 2 * fine, HALO_BITS + GRID_Z, 256), bf16),
        ]
        + [pltpu.VMEM((narrow_count // 2, 256, length), bf16)] * 4
        + [pltpu.VMEM((narrow_count, GRID_Z // narrow_count + HALO_Z, length), jnp.float32)] * 2
        + [pltpu.VMEM((narrow_count, wave_rows, length), jnp.float32)] * 2,
        compiler_params=limits(48),
        name="mesh",
    )(
        table,
        shifts,
        phase,
        green,
        jnp.asarray(np.concatenate(halves(fold_table(GRID_X)))),
        jnp.asarray(np.concatenate(halves(fold_table(GRID_X).T))),
    )
    arrived = lax.all_to_all(partial.reshape(pieces, 1, out_width), axes, 0, 0, tiled=True)
    atom_field, centroid_field, energy = pl.pallas_call(
        finish_kernel,
        out_shape=(shaped((4, 1, atoms)), shaped((4, 1, atoms)), shaped((1, 128))),
        in_specs=vmem(2),
        out_specs=tuple(vmem(3)),
        name="finish",
    )(arrived, kinds)
    atom_field = atom_field.reshape(4, 1, 1, 1, atoms)
    centroid_field = centroid_field.reshape(4, 1, 1, 1, atoms)
    return (dipole.reshape(3, 1, 1, 1, atoms), atom_field, centroid_field, energy[0, 0])


def solution(mesh):
    column = P(None, "wide", "narrow", None, None)
    in_specs = (column, P("wide", "narrow", None, None), P("wide", "narrow", None, None, None))
    in_specs = in_specs + (P(),) * 13
    out_specs = (column, column, column, P())
    return jax.shard_map(local, mesh=mesh, in_specs=in_specs, out_specs=out_specs, check_vma=False)
```

```python
import math

import jax
import jax.numpy as jnp
import numpy as np
from jax import lax
from jax.experimental import pallas as pl
from jax.experimental.pallas import tpu as pltpu
from jax.sharding import PartitionSpec as P

GRID_X = 256
GRID_Y = 256
GRID_Z = 256
AXIS_COLUMNS = 16

radius_scale = 24.0
wannier_reach = 0.5
ewald_beta = 0.9
coulomb = 0.25

ROW_PAD = 32
SLOT_CHUNK = 16
HALO_X = 16
HALO_Z = 8
HALO_BITS = 16

NN = (((1,), (0,)), ((), ()))
NT = (((1,), (1,)), ((), ()))


def split(value):
    high = value.astype(jnp.bfloat16)
    low = (value - high.astype(jnp.float32)).astype(jnp.bfloat16)
    return high, low


def multiply(left, right, dims=NN):
    def one(a, b):
        return lax.dot_general(a, b, dims, preferred_element_type=jnp.float32)

    return one(left[0], right[0]) + (one(left[1], right[0]) + one(left[0], right[1]))


def by_right(lefts, right):
    rows = lefts[0][0].shape[0]
    width = right.shape[1] // 2
    stacked = jnp.concatenate([half for left in lefts for half in left], axis=0)
    both = lax.dot_general(stacked, right, NN, preferred_element_type=jnp.float32)
    results = []
    for k in range(len(lefts)):
        high = both[2 * k * rows : (2 * k + 1) * rows]
        low = both[(2 * k + 1) * rows : (2 * k + 2) * rows]
        results.append(high[:, :width] + (high[:, width:] + low[:, :width]))
    return results


def by_left(left, rights):
    rows = left.shape[0] // 2
    width = rights[0][0].shape[1]
    highs, lows = (jnp.concatenate(half, axis=1) for half in zip(*rights))
    both = lax.dot_general(left, highs, NN, preferred_element_type=jnp.float32)
    rest = lax.dot_general(left[:rows], lows, NN, preferred_element_type=jnp.float32)
    total = both[:rows] + (both[rows:] + rest)
    return total[:, :width], total[:, width:]


def spline_pair(offset):
    centred = offset - 2.0
    away = jnp.abs(centred)
    outer = jnp.maximum(2.0 - away, 0.0)
    inner = jnp.maximum(1.0 - away, 0.0)
    outer_square = outer * outer
    inner_square = inner * inner
    value = (outer_square * outer - 4.0 * (inner_square * inner)) * (1.0 / 6.0)
    slope = jnp.where(centred < 0.0, 0.5, -0.5) * (outer_square - 4.0 * inner_square)
    return value, slope


def lookup(row_table, spot):
    found = None
    for part in range(row_table.shape[1] // 128):
        inside = spot // 128 == part
        here = jnp.take_along_axis(
            jnp.broadcast_to(row_table[:, part * 128 : (part + 1) * 128], spot.shape),
            lax.rem(spot, 128),
            axis=1,
            mode="promise_in_bounds",
        )
        found = here if found is None else jnp.where(inside, here, found)
    return found


def pack_kernel(positions, species, out_ref):
    kinds = species[...]
    rows = [positions[component] for component in range(3)]
    rows[0] = jnp.where(kinds > 0, -rows[0], rows[0])
    rows.append(kinds.astype(jnp.float32))
    rows = jnp.concatenate(rows, axis=0)
    for target in range(out_ref.shape[0]):
        out_ref[target] = rows


def prepare_kernel(
    neighbours,
    embed_one_w,
    embed_one_b,
    embed_two_w,
    embed_two_b,
    embed_three_w,
    embed_three_b,
    fit_one_w,
    fit_one_b,
    fit_two_w,
    fit_two_b,
    fit_three_w,
    fit_three_b,
    constants,
    codes_ref,
    columns_ref,
    second_ref,
    third_ref,
    one_high_ref,
    one_low_ref,
    two_high_ref,
    two_low_ref,
    three_high_ref,
    three_low_ref,
    phase_ref,
    green_ref,
    rows,
    square,
    arrivals,
    *held,
):
    sources = (
        neighbours,
        embed_one_w,
        embed_one_b,
        embed_two_w,
        embed_two_b,
        embed_three_w,
        embed_three_b,
        fit_one_b,
        fit_two_b,
        fit_three_b,
        constants,
        fit_two_w,
        fit_three_w,
        fit_one_w,
    )
    copies = [
        pltpu.make_async_copy(source, target, arrivals.at[k])
        for k, (source, target) in enumerate(zip(sources, held))
    ]
    for copy in copies:
        copy.start()
    (
        neighbours,
        embed_one_w,
        embed_one_b,
        embed_two_w,
        embed_two_b,
        embed_three_w,
        embed_three_b,
        fit_one_b,
        fit_two_b,
        fit_three_b,
        constants,
        fit_two_w,
        fit_three_w,
        fit_one_w,
    ) = held
    for copy in copies[:11]:
        copy.wait()
    pieces = lax.axis_size("wide") * lax.axis_size("narrow")
    piece = lax.axis_index("wide") * lax.axis_size("narrow") + lax.axis_index("narrow")
    width_one = embed_one_w.shape[1]
    hidden = fit_two_w.shape[0]
    codes_ref[...] = jnp.transpose(neighbours[...].astype(jnp.float32)).astype(jnp.int32)
    rows[...] = jnp.zeros_like(rows)
    for kind in range(2):
        rows[kind : kind + 1, 0:width_one] = embed_one_w[kind : kind + 1, :]
        rows[2 + kind : 3 + kind, 0:width_one] = embed_one_b[kind : kind + 1, :]
        rows[2 + kind : 3 + kind, width_one : width_one + 1] = jnp.full((1, 1), 40.0, jnp.float32)
    for row, source in ((4, fit_one_b), (5, fit_two_b), (6, fit_three_b)):
        rows[row : row + 1, 0:hidden] = source[...]
    columns_ref[...] = jnp.transpose(rows[...])

    square[...] = jnp.zeros_like(square)
    for k in range(2):
        square[0:width_one, k * ROW_PAD : k * ROW_PAD + width_one] = embed_two_w[
            :, k * width_one : (k + 1) * width_one
        ]
        square[
            width_one : width_one + 1, k * ROW_PAD : k * ROW_PAD + width_one
        ] = embed_two_b[:, k * width_one : (k + 1) * width_one]
    high, low = split(jnp.transpose(square[0:128, 0:128])[0 : 2 * ROW_PAD, 0:ROW_PAD])
    second_ref[...] = jnp.concatenate([high, high, low], axis=1)
    square[0:128, 0:128] = jnp.zeros((128, 128), jnp.float32)
    for g in range(2):
        for k in range(4):
            square[
                g * ROW_PAD : g * ROW_PAD + width_one, k * ROW_PAD : k * ROW_PAD + width_one
            ] = embed_three_w[
                g * width_one : (g + 1) * width_one, k * width_one : (k + 1) * width_one
            ]
    for k in range(4):
        square[
            width_one : width_one + 1, k * ROW_PAD : k * ROW_PAD + width_one
        ] = embed_three_b[:, k * width_one : (k + 1) * width_one]
    high, low = split(jnp.transpose(square[0:128, 0:128])[:, 0 : 2 * ROW_PAD])
    third_ref[...] = jnp.concatenate([high, high, low], axis=1)
    for copy in copies[11:13]:
        copy.wait()
    for source, high_ref, low_ref in (
        (fit_two_w, two_high_ref, two_low_ref),
        (fit_three_w, three_high_ref, three_low_ref),
    ):
        square[0:hidden, 0:hidden] = source[...]
        high_ref[...], low_ref[...] = split(jnp.transpose(square[...])[0:hidden, 0:hidden])

    fine = GRID_Y // 2 // pieces
    shape = (phase_ref.shape[0], 128)
    row = lax.broadcasted_iota(jnp.int32, shape, 0)
    mode = piece * fine + row // 2
    for part in range(GRID_Y // 128):
        cell = lax.broadcasted_iota(jnp.int32, shape, 1) + part * 128
        spot = lax.rem(mode * cell, GRID_Y)
        cosine = lookup(constants[0:1, :], spot)
        sine = lookup(constants[1:2, :], spot)
        alternate = (1 - 2 * lax.rem(cell, 2)).astype(jnp.float32)
        odd = jnp.where(mode == 0, alternate, -sine)
        value = jnp.where(lax.rem(row, 2) == 0, cosine, odd)
        phase_ref[:, part * 128 : (part + 1) * 128] = jnp.where(row < 2 * fine, value, 0.0)

    column = jnp.transpose(constants[...])
    lane = lax.broadcasted_iota(jnp.int32, (1, GRID_Y), 1)
    for j in range(fine + 1):
        here = lane == (GRID_Y // 2 if j == fine else piece * fine + j)
        factor = jnp.sum(jnp.where(here, constants[2:3, :], 0.0), axis=1, keepdims=True)
        part = jnp.sum(jnp.where(here, constants[3:4, :], 0.0), axis=1, keepdims=True)
        wave = (part + constants[5:6, :]) + column[:, 7:8]
        top = (factor * constants[4:5, :]) * column[:, 6:7]
        green_ref[j] = jnp.where(wave == 0.0, 0.0, top / jnp.where(wave == 0.0, 1.0, wave))

    copies[13].wait()
    one_high_ref[...], one_low_ref[...] = split(fit_one_w[...])


def centroid_kernel(
    table,
    codes,
    columns,
    second,
    third,
    one_high,
    one_low,
    two_high,
    two_low,
    three_high,
    three_low,
    fit_out_w,
    dipole_ref,
    shift_ref,
    matrix,
    descriptor,
    arrivals,
    *held,
):
    sources = (table, codes, columns, second, third)
    sources += (one_high, one_low, two_high, two_low, three_high, three_low, fit_out_w)
    copies = [
        pltpu.make_async_copy(source, target, arrivals.at[k])
        for k, (source, target) in enumerate(zip(sources, held))
    ]
    for copy in copies:
        copy.start()
    table, codes, columns, second, third = held[:5]
    one_high, one_low, two_high, two_low, three_high, three_low, fit_out_w = held[5:]
    for copy in copies[:5]:
        copy.wait()
    wide_count, narrow_count, _, atoms = table.shape
    listed = codes.shape[0]
    width_three = fit_out_w.shape[0]
    width_one = width_three // 4
    hidden_width = two_high.shape[0]
    cells = (GRID_X // wide_count, GRID_Y, GRID_Z // narrow_count)
    at_wide = lax.axis_index("wide")
    at_narrow = lax.axis_index("narrow")
    own = jnp.abs(table[at_wide, at_narrow])
    nearby = []
    for step in range(9):
        wide_at = lax.rem(at_wide + (step // 3 - 1) + wide_count, wide_count)
        narrow_at = lax.rem(at_narrow + (step % 3 - 1) + narrow_count, narrow_count)
        nearby.append(table[wide_at, narrow_at])

    second_all = second[...]
    third_all = third[...]
    weight_oxygen = jnp.broadcast_to(columns[0:ROW_PAD, 0:1], (ROW_PAD, atoms))
    weight_hydrogen = jnp.broadcast_to(columns[0:ROW_PAD, 1:2], (ROW_PAD, atoms))
    bias_oxygen = jnp.broadcast_to(columns[0:ROW_PAD, 2:3], (ROW_PAD, atoms))
    bias_hydrogen = jnp.broadcast_to(columns[0:ROW_PAD, 3:4], (ROW_PAD, atoms))
    matrix[...] = jnp.zeros_like(matrix)

    def chunk(first):
        code = codes[pl.ds(first, SLOT_CHUNK), :]
        offset = code // atoms
        slot = code - offset * atoms
        step_x = jnp.where(offset >= 9, 1, 0) + jnp.where(offset >= 18, 1, 0)
        rest = offset - 9 * step_x
        step_z = jnp.where(rest >= 3, 1, 0) + jnp.where(rest >= 6, 1, 0)
        step_y = rest - 3 * step_z
        brick = step_x * 3 + step_z
        found = []
        for component in range(3):
            picked = jnp.zeros((SLOT_CHUNK, atoms), jnp.float32)
            for step in range(9):
                row = jnp.broadcast_to(
                    nearby[step][component : component + 1], (SLOT_CHUNK, atoms)
                )
                here = jnp.take_along_axis(row, slot, axis=1, mode="promise_in_bounds")
                picked = jnp.where(brick == step, here, picked)
            found.append(picked)
        hydrogen = found[0] < 0.0
        found[0] = jnp.abs(found[0])
        scaled = []
        for component, step in enumerate((step_x, step_y, step_z)):
            extent = float(cells[component])
            relative = (step - 1).astype(jnp.float32) * extent + (
                found[component] - own[component : component + 1]
            ) * extent
            scaled.append(relative * (1.0 / radius_scale))
        smooth = 1.0 / (
            1.0 + (scaled[0] * scaled[0] + scaled[1] * scaled[1] + scaled[2] * scaled[2])
        )
        radial = [smooth] + [smooth * part for part in scaled]
        first_layers = []
        for k in range(SLOT_CHUNK):
            row = smooth[k : k + 1]
            kind = hydrogen[k : k + 1]
            weight = jnp.where(kind, weight_hydrogen, weight_oxygen)
            bias = jnp.where(kind, bias_hydrogen, bias_oxygen)
            first_layers.append(jnp.tanh(weight * row + bias))
        layer_one = jnp.concatenate(first_layers, axis=1)
        high, low = split(layer_one)
        layer_two = lax.dot_general(
            second_all,
            jnp.concatenate([high, low, high], axis=0),
            NN,
            preferred_element_type=jnp.float32,
        )
        layer_two = jnp.tanh(layer_two) + jnp.concatenate(
            [layer_one, layer_one], axis=0
        )
        high, low = split(layer_two)
        layer_three = lax.dot_general(
            third_all,
            jnp.concatenate([high, low, high], axis=0),
            NN,
            preferred_element_type=jnp.float32,
        )
        layer_three = jnp.tanh(layer_three) + jnp.concatenate(
            [layer_two, layer_two], axis=0
        )
        for part in range(4):
            total = matrix[part]
            for k in range(SLOT_CHUNK):
                total = total + layer_three[:, k * atoms : (k + 1) * atoms] * radial[part][k : k + 1]
            matrix[part] = total

    def two_chunks(index, carry):
        first = pl.multiple_of(index * (2 * SLOT_CHUNK), 2 * SLOT_CHUNK)
        chunk(first)
        chunk(pl.multiple_of(first + SLOT_CHUNK, SLOT_CHUNK))
        return carry

    lax.fori_loop(0, listed // (2 * SLOT_CHUNK), two_chunks, 0)

    parts = []
    for part in range(4):
        padded = matrix[part] * (1.0 / listed)
        parts.append(
            jnp.concatenate(
                [padded[k * ROW_PAD : k * ROW_PAD + width_one] for k in range(4)], axis=0
            )
        )
    leading = [part[0:AXIS_COLUMNS] for part in parts]
    for row in range(width_three):
        total = parts[0][row : row + 1] * leading[0]
        for part in range(1, 4):
            total = total + parts[part][row : row + 1] * leading[part]
        descriptor[row * AXIS_COLUMNS : (row + 1) * AXIS_COLUMNS, :] = total
    for copy in copies[5:]:
        copy.wait()

    def layer(high_ref, low_ref, given, column):
        weights = (high_ref[...], low_ref[...])
        return jnp.tanh(multiply(weights, split(given)) + columns[0:hidden_width, column : column + 1])

    hidden = layer(one_high, one_low, descriptor[...], 4)
    hidden = hidden + layer(two_high, two_low, hidden, 5)
    hidden = hidden + layer(three_high, three_low, hidden, 6)
    coeffs = multiply(split(fit_out_w[...]), split(hidden))
    vector = jnp.concatenate(
        [jnp.sum(coeffs * parts[1 + c], axis=0, keepdims=True) for c in range(3)], axis=0
    )
    oxygen = 1.0 - own[3:4]
    for c in range(3):
        dipole_ref[c] = vector[c : c + 1] * oxygen
    moved = wannier_reach * jnp.tanh(vector)
    moved = jnp.concatenate([moved, jnp.zeros((1, atoms), jnp.float32)], axis=0)
    for target in range(shift_ref.shape[0]):
        shift_ref[target] = moved


def mesh_kernel(
    table,
    shifts,
    phase,
    green_ref,
    fold_stack,
    unfold_stack,
    fold_wide,
    unfold_wide,
    out_ref,
    grid,
    planes,
    packed,
    weights_even,
    weights_odd,
    slopes_even,
    slopes_odd,
    weights_z,
    slopes_z,
    waves,
    wave_slopes,
):
    wide_count, narrow_count, _, atoms = table.shape
    cells_x = GRID_X // wide_count
    cells_z = GRID_Z // narrow_count
    window = cells_z + HALO_Z
    reach = cells_x + HALO_X
    pair = 2 * atoms
    length = wide_count * pair
    copies = grid.shape[0]
    fine = grid.shape[1]
    channels = 2 * fine
    rows = phase.shape[0]
    half_x = GRID_X // 2
    half_z = GRID_Z // 2
    piece = lax.axis_index("wide") * narrow_count + lax.axis_index("narrow")
    lane_zero = lax.broadcasted_iota(jnp.int32, (1, half_x), 1) == 0
    row_zero = lax.broadcasted_iota(jnp.int32, (half_z, 1), 0) == 0

    def sites(at_wide, at_narrow):
        atom = jnp.abs(table[at_wide, at_narrow])
        moved = shifts[at_wide, at_narrow]
        found = []
        for component, extent in enumerate((cells_x, GRID_Y, cells_z)):
            start = atom[component : component + 1] * float(extent)
            found.append(jnp.concatenate([start, start + moved[component : component + 1]], axis=1))
        oxygen = 1.0 - atom[3:4]
        found.append(jnp.concatenate([6.0 * oxygen + atom[3:4], -8.0 * oxygen], axis=1))
        return found

    def line(at_narrow):
        groups = [sites(at_wide, at_narrow) for at_wide in range(wide_count)]
        return [jnp.concatenate([g[k] for g in groups], axis=1) for k in range(4)]

    def splines_z(row):
        counter = lax.broadcasted_iota(jnp.int32, (window, 1), 0).astype(jnp.float32)
        return spline_pair(row - (counter - float(HALO_Z)))

    def fill_x(row, targets):
        counter = lax.broadcasted_iota(jnp.int32, (reach, 1), 0).astype(jnp.float32)
        both = spline_pair(row - (counter - float(HALO_X)))
        rest = jnp.zeros((128 - reach, length), jnp.bfloat16)
        for values, ref in zip(both, targets):
            high, low = split(values)
            ref[0:reach, :] = high
            ref[reach:128, :] = rest
            ref[128 : 128 + reach, :] = low
            ref[128 + reach : 256, :] = rest

    grid[:, :, 0:HALO_Z, :] = jnp.zeros((copies, fine, HALO_Z, 2 * GRID_X), jnp.float32)

    weights = (weights_even, weights_odd)
    slopes = (slopes_even, slopes_odd)

    def spread(index, odd):
        at_narrow = 2 * index + odd
        row_x, row_y, row_z, charge = line(at_narrow)
        lower = jnp.floor(row_y)
        back = lax.broadcasted_iota(jnp.int32, (8, 1), 0)
        value_y, slope_y = spline_pair((row_y - lower) + back.astype(jnp.float32))
        cell = lax.rem(lower.astype(jnp.int32) - back + GRID_Y, GRID_Y)
        wave_blocks = []
        slope_blocks = []
        for block in range(length // 128):
            lanes = slice(block * 128, (block + 1) * 128)
            wave = jnp.zeros((rows, 128), jnp.float32)
            wave_slope = jnp.zeros((rows, 128), jnp.float32)
            for k in range(4):
                spot = jnp.broadcast_to(cell[k : k + 1, lanes], (rows, 128))
                found = lookup(phase[...], spot)
                wave = wave + value_y[k : k + 1, lanes] * found
                wave_slope = wave_slope + slope_y[k : k + 1, lanes] * found
            wave_blocks.append(wave)
            slope_blocks.append(wave_slope)
        wave = jnp.concatenate(wave_blocks, axis=1)
        waves[at_narrow] = wave
        wave_slopes[at_narrow] = jnp.concatenate(slope_blocks, axis=1)
        fill_x(row_x, (weights[odd].at[index], slopes[odd].at[index]))
        value_z, slope_z = splines_z(row_z)
        weights_z[at_narrow] = value_z
        slopes_z[at_narrow] = slope_z
        charged = wave * charge
        first = pl.multiple_of(at_narrow * cells_z, HALO_Z)
        for at_wide in range(wide_count):
            lanes = slice(at_wide * pair, (at_wide + 1) * pair)
            near = value_z[:, lanes]
            left = jnp.concatenate(
                [near * charged[c : c + 1, lanes] for c in range(channels)], axis=0
            )
            total = lax.dot_general(
                jnp.concatenate(split(left), axis=0),
                weights[odd][index, :, lanes],
                NT,
                preferred_element_type=jnp.float32,
            )
            tall = channels * window
            total = total[:tall, 0:128] + (total[:tall, 128:256] + total[tall:, 0:128])
            start = at_wide // copies * 128
            for c in range(channels):
                spot = slice(c % 2 * GRID_X + start, c % 2 * GRID_X + start + 128)
                k = at_wide % copies
                part = total[c * window : (c + 1) * window]
                grid[k, c // 2, pl.ds(first, HALO_Z), spot] += part[:HALO_Z]
                grid[k, c // 2, pl.ds(first + HALO_Z, cells_z), spot] = part[HALO_Z:]

    def in_pairs(step):
        def both(index, carry):
            step(index, 0)
            step(index, 1)
            return carry

        lax.fori_loop(0, narrow_count // 2, both, 0)

    in_pairs(spread)

    def gather(j, carry):
        for lanes in (slice(0, GRID_X), slice(GRID_X, 2 * GRID_X)):
            total = None
            for k in range(copies):
                moved = pltpu.roll(grid[k, j, :, lanes], (k * cells_x - HALO_X) % GRID_X, 1)
                total = moved if total is None else total + moved
            planes[j, :, lanes] = total[HALO_Z:]
            planes[j, GRID_Z - HALO_Z :, lanes] += total[:HALO_Z]
        return carry

    lax.fori_loop(0, fine, gather, 0)
    is_first = piece == 0

    def paired(real, imag, zero, axis):
        half = real.shape[axis] // 2
        first = (slice(None),) * axis + (slice(0, half),)
        second = (slice(None),) * axis + (slice(half, 2 * half),)
        real_c, real_s = real[first], real[second]
        if imag is None:
            none = jnp.zeros_like(real_s)
            real_all = [real_c, jnp.where(zero, real_s, real_c)]
            imag_all = [jnp.where(zero, none, -real_s), jnp.where(zero, none, real_s)]
        else:
            imag_c, imag_s = imag[first], imag[second]
            real_all = [
                real_c + jnp.where(zero, 0.0, imag_s),
                jnp.where(zero, real_s, real_c - imag_s),
            ]
            imag_all = [
                imag_c - jnp.where(zero, 0.0, real_s),
                jnp.where(zero, imag_s, imag_c + real_s),
            ]
        return jnp.concatenate(real_all, axis=axis), jnp.concatenate(imag_all, axis=axis)

    def merged(real, imag, zero, axis):
        half = real.shape[axis] // 2
        first = (slice(None),) * axis + (slice(0, half),)
        second = (slice(None),) * axis + (slice(half, 2 * half),)
        real_a, real_b = real[first], real[second]
        imag_a, imag_b = imag[first], imag[second]
        real = [
            real_a + jnp.where(zero, 0.0, real_b),
            jnp.where(zero, real_b, imag_b - imag_a),
        ]
        imag = [
            imag_a + jnp.where(zero, 0.0, imag_b),
            jnp.where(zero, imag_b, real_a - real_b),
        ]
        return jnp.concatenate(real, axis=axis), jnp.concatenate(imag, axis=axis)

    modes = {}
    parts = []

    def slot(j):
        first_imag = planes[0, :, GRID_X:]
        if j == fine:
            real, imag = jnp.where(is_first, first_imag, 0.0), None
        else:
            real, imag = planes[j, :, 0:GRID_X], planes[j, :, GRID_X:]
            if j == 0:
                imag = jnp.where(is_first, 0.0, imag)
        real = split(real)
        imag = None if imag is None else split(imag)
        yield
        if imag is None:
            (real,) = by_right([real], fold_wide[...])
        else:
            real, imag = by_right([real, imag], fold_wide[...])
        yield
        real, imag = paired(real, imag, lane_zero, 1)
        real, imag = split(real), split(imag)
        yield
        real, imag = by_left(unfold_stack[...], [real, imag])
        yield
        real, imag = paired(real, imag, row_zero, 0)
        green = green_ref[j]
        mode = GRID_Y // 2 if j == fine else piece * fine + j
        share = jnp.where((mode == 0) | (mode == GRID_Y // 2), 0.5, 1.0)
        parts.append(share * jnp.sum(green * (real * real + imag * imag), axis=0, keepdims=True))
        real, imag = green * real, green * imag
        if j == fine:
            modes[j] = (real, imag)
            return
        if j == 0:
            real, imag = real - modes[fine][1], imag + modes[fine][0]
        real, imag = merged(real, imag, row_zero, 0)
        real, imag = split(real), split(imag)
        yield
        real, imag = by_left(fold_stack[...], [real, imag])
        yield
        real, imag = merged(real, imag, lane_zero, 1)
        scale = jnp.where(piece * fine + j == 0, 1.0, 2.0)
        real, imag = split(real * scale), split(imag * scale)
        yield
        real, imag = by_right([real, imag], unfold_wide[...])
        yield
        for k, part in enumerate((real, imag)):
            for at_wide in range(wide_count):
                moved = pltpu.roll(part, (HALO_X - at_wide * cells_x) % GRID_X, 1)[:, 0:128]
                high = moved.astype(jnp.bfloat16).astype(jnp.float32)
                again = pltpu.roll(high, reach % 128, 1)
                low = pltpu.roll(moved - high, 2 * reach % 128, 1)
                sides = []
                for side in range(2):
                    lane = lax.broadcasted_iota(jnp.int32, (1, 128), 1) + side * 128
                    value = jnp.where(lane < 2 * reach, again, low)
                    if side == 0:
                        value = jnp.where(lane < reach, high, value)
                    sides.append(value.astype(jnp.bfloat16))
                block = jnp.concatenate(sides, axis=1)
                packed[at_wide, 2 * j + k, HALO_BITS:, :] = block
                packed[at_wide, 2 * j + k, 0:HALO_BITS, :] = block[GRID_Z - HALO_BITS :]

    waiting = [slot(j) for j in [fine, *range(fine)]]
    running = []
    while waiting or running:
        if waiting:
            running.append(waiting.pop(0))
        running = [one for one in running if next(one, running) is not running]
    energy = sum(parts[1:], parts[0])
    energy = jnp.broadcast_to(jnp.sum(energy, axis=1, keepdims=True), (1, 128))

    def collect(index, odd):
        at_narrow = 2 * index + odd
        value_z = weights_z[at_narrow]
        slope_z = slopes_z[at_narrow]
        first = pl.multiple_of(at_narrow * cells_z, HALO_BITS)
        wave = waves[at_narrow]
        wave_slope = wave_slopes[at_narrow]
        for at_wide in range(wide_count):
            lanes = slice(at_wide * pair, (at_wide + 1) * pair)
            tall = cells_z + HALO_BITS
            left = jnp.concatenate(
                [packed[at_wide, c, pl.ds(first, tall), :] for c in range(channels)], axis=0
            )

            right = jnp.concatenate(
                [weights[odd][index, :, lanes], slopes[odd][index, :, lanes]], axis=1
            )
            high = right[0:reach]
            rest = jnp.zeros((256 - 3 * reach, 2 * pair), jnp.bfloat16)
            right = jnp.concatenate([high, right[128 : 128 + reach], high, rest], axis=0)
            both = lax.dot_general(left, right, NN, preferred_element_type=jnp.float32)
            value = both[:, 0:pair]
            slope = both[:, pair:]
            plain = jnp.zeros((window, pair), jnp.float32)
            along_x = plain
            along_y = plain
            for c in range(channels):
                block = slice((c + 1) * tall - window, (c + 1) * tall)
                plain = plain + value[block] * wave[c : c + 1, lanes]
                along_x = along_x + slope[block] * wave[c : c + 1, lanes]
                along_y = along_y + value[block] * wave_slope[c : c + 1, lanes]
            near = value_z[:, lanes]
            near_slope = slope_z[:, lanes]
            results = [
                jnp.sum(near * plain, axis=0, keepdims=True),
                -jnp.sum(near * along_x, axis=0, keepdims=True),
                -jnp.sum(near * along_y, axis=0, keepdims=True),
                -jnp.sum(near_slope * plain, axis=0, keepdims=True),
            ]
            for k, row in enumerate(results):
                out_ref[at_wide, at_narrow, :, k * pair : (k + 1) * pair] = row
            out_ref[at_wide, at_narrow, :, 4 * pair :] = energy

    in_pairs(collect)


def finish_kernel(arrived, species, atom_ref, centroid_ref, energy_ref):
    atoms = species.shape[1]
    total = arrived[0]
    for k in range(1, arrived.shape[0]):
        total = total + arrived[k]
    oxygen = 1.0 - species[...].astype(jnp.float32)
    for k in range(4):
        atom_ref[k] = total[:, 2 * k * atoms : (2 * k + 1) * atoms]
        centroid_ref[k] = total[:, (2 * k + 1) * atoms : (2 * k + 2) * atoms] * oxygen
    energy_ref[...] = total[:, 8 * atoms :] * (1.0 / (atoms * arrived.shape[0]))


def mode_factors(length, order):
    wrapped = np.where(2 * order >= length, order - length, order)
    square = (wrapped / length) ** 2
    ratio = (4.0 + 2.0 * np.cos(2.0 * math.pi * order / length)) / 6.0
    return np.stack([np.exp(-(math.pi**2) * square / ewald_beta**2) / ratio**2, square])


def folded_order(length):
    half = length // 2
    counter = np.arange(half)
    return np.concatenate([counter, np.where(counter == 0, half, length - counter)])


def fold_table(length):
    half = length // 2
    turns = np.outer(np.arange(length), np.arange(half)) % length * (2.0 * math.pi / length)
    sines = np.sin(turns)
    sines[:, 0] = 1.0 - 2.0 * (np.arange(length) % 2)
    return np.concatenate([np.cos(turns), sines], axis=1)


def halves(table):
    high = table.astype(jnp.bfloat16)
    low = (table - high.astype(np.float64)).astype(jnp.bfloat16)
    return high, low


def vmem(count):
    return [pl.BlockSpec(memory_space=pltpu.VMEM)] * count


def hbm(count):
    return [pl.BlockSpec(memory_space=pltpu.HBM)] * count


def shaped(shape, dtype=jnp.float32):
    return jax.ShapeDtypeStruct(shape, dtype)


def limits(mebibytes):
    return pltpu.CompilerParams(vmem_limit_bytes=mebibytes * 1024 * 1024)


def local(
    positions,
    species,
    neighbours,
    embed_one_w,
    embed_one_b,
    embed_two_w,
    embed_two_b,
    embed_three_w,
    embed_three_b,
    fit_one_w,
    fit_one_b,
    fit_two_w,
    fit_two_b,
    fit_three_w,
    fit_three_b,
    fit_out_w,
):
    axes = ("wide", "narrow")
    wide_count = lax.axis_size("wide")
    narrow_count = lax.axis_size("narrow")
    pieces = wide_count * narrow_count
    atoms = positions.shape[4]
    listed = neighbours.shape[4]
    fine = GRID_Y // 2 // pieces
    width_three = embed_three_w.shape[1]
    entries, hidden = fit_one_w.shape
    kinds = species.reshape(1, atoms)

    packed = pl.pallas_call(
        pack_kernel,
        out_shape=shaped((pieces, 4, atoms)),
        in_specs=vmem(2),
        out_specs=vmem(1)[0],
        name="pack",
    )(positions.reshape(3, 1, atoms), kinds)
    table = lax.all_to_all(packed, axes, 0, 0, tiled=True)
    table = table.reshape(wide_count, narrow_count, 4, atoms)

    tall = 4 * ROW_PAD
    bf16 = jnp.bfloat16
    wave_rows = -(-2 * fine // 8) * 8
    angle = np.arange(GRID_Y) * (2.0 * math.pi / GRID_Y)
    constants = np.concatenate(
        [
            np.stack([np.cos(angle), np.sin(angle)]),
            mode_factors(GRID_Y, np.arange(GRID_Y)),
            mode_factors(GRID_X, folded_order(GRID_X)),
            mode_factors(GRID_Z, folded_order(GRID_Z)),
        ]
    )
    constants[2] *= coulomb / (math.pi * GRID_X * GRID_Y * GRID_Z)
    arguments = (
        neighbours.reshape(atoms, listed),
        embed_one_w,
        embed_one_b,
        embed_two_w,
        embed_two_b[None],
        embed_three_w,
        embed_three_b[None],
        fit_one_w.T,
        fit_one_b[None],
        fit_two_w,
        fit_two_b[None],
        fit_three_w,
        fit_three_b[None],
        jnp.asarray(constants, jnp.float32),
    )
    held = [arguments[k] for k in (0, 1, 2, 3, 4, 5, 6, 8, 10, 12, 13, 9, 11, 7)]
    prepared = pl.pallas_call(
        prepare_kernel,
        out_shape=(
            shaped((listed, atoms), jnp.int32),
            shaped((256, 16)),
            shaped((2 * ROW_PAD, 3 * ROW_PAD), bf16),
            shaped((tall, 6 * ROW_PAD), bf16),
            shaped((hidden, entries), bf16),
            shaped((hidden, entries), bf16),
        )
        + (shaped((hidden, hidden), bf16),) * 4
        + (shaped((wave_rows, GRID_Y)), shaped((fine + 1, GRID_Z, GRID_X))),
        in_specs=hbm(len(arguments)),
        out_specs=tuple(vmem(12)),
        scratch_shapes=[
            pltpu.VMEM((16, 256), jnp.float32),
            pltpu.VMEM((256, 256), jnp.float32),
            pltpu.SemaphoreType.DMA((len(held),)),
        ]
        + [pltpu.VMEM(array.shape, array.dtype) for array in held],
        compiler_params=limits(62),
        cost_estimate=pl.CostEstimate(
            flops=1000000, bytes_accessed=8 * entries * hidden, transcendentals=0
        ),
        name="prepare",
    )(*arguments)
    phase, green = prepared[10:]
    fitted = (table, *prepared[:10], fit_out_w.T)
    dipole, shifts = pl.pallas_call(
        centroid_kernel,
        out_shape=(shaped((3, 1, atoms)), shaped((pieces, 4, atoms))),
        in_specs=hbm(12),
        out_specs=tuple(vmem(2)),
        scratch_shapes=[
            pltpu.VMEM((4, tall, atoms), jnp.float32),
            pltpu.VMEM((width_three * AXIS_COLUMNS, atoms), jnp.float32),
            pltpu.SemaphoreType.DMA((len(fitted),)),
        ]
        + [pltpu.VMEM(array.shape, array.dtype) for array in fitted],
        compiler_params=limits(62),
        name="centroids",
    )(*fitted)
    shifts = lax.all_to_all(shifts, axes, 0, 0, tiled=True)
    shifts = shifts.reshape(wide_count, narrow_count, 4, atoms)

    cells_x = GRID_X // wide_count
    copies = 128 // cells_x
    length = wide_count * 2 * atoms
    out_width = 8 * atoms + 128
    partial = pl.pallas_call(
        mesh_kernel,
        out_shape=shaped((wide_count, narrow_count, 1, out_width)),
        in_specs=vmem(8),
        out_specs=vmem(1)[0],
        scratch_shapes=[
            pltpu.VMEM((copies, fine, HALO_Z + GRID_Z, 2 * GRID_X), jnp.float32),
            pltpu.VMEM((fine, GRID_Z, 2 * GRID_X), jnp.float32),
            pltpu.VMEM((wide_count, 2 * fine, HALO_BITS + GRID_Z, 256), bf16),
        ]
        + [pltpu.VMEM((narrow_count // 2, 256, length), bf16)] * 4
        + [pltpu.VMEM((narrow_count, GRID_Z // narrow_count + HALO_Z, length), jnp.float32)] * 2
        + [pltpu.VMEM((narrow_count, wave_rows, length), jnp.float32)] * 2,
        compiler_params=limits(48),
        name="mesh",
    )(
        table,
        shifts,
        phase,
        green,
        *[
            jnp.asarray(np.concatenate(halves(table_of), axis=axis))
            for axis in range(2)
            for table_of in (fold_table(GRID_X), fold_table(GRID_X).T)
        ],
    )
    arrived = lax.all_to_all(partial.reshape(pieces, 1, out_width), axes, 0, 0, tiled=True)
    atom_field, centroid_field, energy = pl.pallas_call(
        finish_kernel,
        out_shape=(shaped((4, 1, atoms)), shaped((4, 1, atoms)), shaped((1, 128))),
        in_specs=vmem(2),
        out_specs=tuple(vmem(3)),
        name="finish",
    )(arrived, kinds)
    atom_field = atom_field.reshape(4, 1, 1, 1, atoms)
    centroid_field = centroid_field.reshape(4, 1, 1, 1, atoms)
    return (dipole.reshape(3, 1, 1, 1, atoms), atom_field, centroid_field, energy[0, 0])


def solution(mesh):
    column = P(None, "wide", "narrow", None, None)
    in_specs = (column, P("wide", "narrow", None, None), P("wide", "narrow", None, None, None))
    in_specs = in_specs + (P(),) * 13
    out_specs = (column, column, column, P())
    return jax.shard_map(local, mesh=mesh, in_specs=in_specs, out_specs=out_specs, check_vma=False)
```

```python
import math

import jax
import jax.numpy as jnp
import numpy as np
from jax import lax
from jax.experimental import pallas as pl
from jax.experimental.pallas import tpu as pltpu
from jax.sharding import PartitionSpec as P

GRID_X = 256
GRID_Y = 256
GRID_Z = 256
AXIS_COLUMNS = 16

radius_scale = 24.0
wannier_reach = 0.5
ewald_beta = 0.9
coulomb = 0.25

ROW_PAD = 32
SLOT_CHUNK = 16
HALO_X = 16
HALO_Z = 8
HALO_BITS = 16

NN = (((1,), (0,)), ((), ()))
NT = (((1,), (1,)), ((), ()))


def split(value):
    high = value.astype(jnp.bfloat16)
    low = (value - high.astype(jnp.float32)).astype(jnp.bfloat16)
    return high, low


def multiply(left, right, dims=NN):
    def one(a, b):
        return lax.dot_general(a, b, dims, preferred_element_type=jnp.float32)

    return one(left[0], right[0]) + (one(left[1], right[0]) + one(left[0], right[1]))


def by_right(left, right):
    rows = left[0].shape[0]
    both = lax.dot_general(
        jnp.concatenate(left, axis=0), right[0], NN, preferred_element_type=jnp.float32
    )
    rest = lax.dot_general(left[0], right[1], NN, preferred_element_type=jnp.float32)
    return both[:rows] + (both[rows:] + rest)


def by_left(left, right):
    rows = left.shape[0] // 2
    both = lax.dot_general(left, right[0], NN, preferred_element_type=jnp.float32)
    rest = lax.dot_general(left[:rows], right[1], NN, preferred_element_type=jnp.float32)
    return both[:rows] + (both[rows:] + rest)


def spline_pair(offset):
    centred = offset - 2.0
    away = jnp.abs(centred)
    outer = jnp.maximum(2.0 - away, 0.0)
    inner = jnp.maximum(1.0 - away, 0.0)
    outer_square = outer * outer
    inner_square = inner * inner
    value = (outer_square * outer - 4.0 * (inner_square * inner)) * (1.0 / 6.0)
    slope = jnp.where(centred < 0.0, 0.5, -0.5) * (outer_square - 4.0 * inner_square)
    return value, slope


def wrapped(value, length):
    if length & (length - 1) == 0:
        return jnp.bitwise_and(value, length - 1)
    return lax.rem(value, length)


def lookup(row_table, spot):
    found = None
    lane = jnp.bitwise_and(spot, 127)
    block = lax.shift_right_logical(spot, 7)
    for part in range(row_table.shape[1] // 128):
        inside = block == part
        here = jnp.take_along_axis(
            jnp.broadcast_to(row_table[:, part * 128 : (part + 1) * 128], spot.shape),
            lane,
            axis=1,
            mode="promise_in_bounds",
        )
        found = here if found is None else jnp.where(inside, here, found)
    return found


def pack_kernel(positions, species, out_ref):
    kinds = species[...]
    rows = [positions[component] for component in range(3)]
    rows[0] = jnp.where(kinds > 0, -rows[0], rows[0])
    rows.append(kinds.astype(jnp.float32))
    rows = jnp.concatenate(rows, axis=0)
    for target in range(out_ref.shape[0]):
        out_ref[target] = rows


def prepare_kernel(
    neighbours,
    embed_one_w,
    embed_one_b,
    embed_two_w,
    embed_two_b,
    embed_three_w,
    embed_three_b,
    fit_one_w,
    fit_one_b,
    fit_two_w,
    fit_two_b,
    fit_three_w,
    fit_three_b,
    constants,
    codes_ref,
    columns_ref,
    second_ref,
    third_ref,
    one_high_ref,
    one_low_ref,
    two_high_ref,
    two_low_ref,
    three_high_ref,
    three_low_ref,
    phase_ref,
    green_ref,
    rows,
    square,
    arrivals,
    *held,
):
    sources = (
        neighbours,
        embed_one_w,
        embed_one_b,
        embed_two_w,
        embed_two_b,
        embed_three_w,
        embed_three_b,
        fit_one_b,
        fit_two_b,
        fit_three_b,
        constants,
        fit_two_w,
        fit_three_w,
        fit_one_w,
    )
    copies = [
        pltpu.make_async_copy(source, target, arrivals.at[k])
        for k, (source, target) in enumerate(zip(sources, held))
    ]
    for copy in copies:
        copy.start()
    (
        neighbours,
        embed_one_w,
        embed_one_b,
        embed_two_w,
        embed_two_b,
        embed_three_w,
        embed_three_b,
        fit_one_b,
        fit_two_b,
        fit_three_b,
        constants,
        fit_two_w,
        fit_three_w,
        fit_one_w,
    ) = held
    for copy in copies[:11]:
        copy.wait()
    pieces = lax.axis_size("wide") * lax.axis_size("narrow")
    piece = lax.axis_index("wide") * lax.axis_size("narrow") + lax.axis_index("narrow")
    width_one = embed_one_w.shape[1]
    hidden = fit_two_w.shape[0]
    codes_ref[...] = jnp.transpose(neighbours[...].astype(jnp.float32)).astype(jnp.int32)
    rows[...] = jnp.zeros_like(rows)
    for kind in range(2):
        rows[kind : kind + 1, 0:width_one] = embed_one_w[kind : kind + 1, :]
        rows[2 + kind : 3 + kind, 0:width_one] = embed_one_b[kind : kind + 1, :]
        rows[2 + kind : 3 + kind, width_one : width_one + 1] = jnp.full((1, 1), 40.0, jnp.float32)
    for row, source in ((4, fit_one_b), (5, fit_two_b), (6, fit_three_b)):
        rows[row : row + 1, 0:hidden] = source[...]
    columns_ref[...] = jnp.transpose(rows[...])

    row = lax.broadcasted_iota(jnp.int32, square.shape, 0)
    lane = lax.broadcasted_iota(jnp.int32, square.shape, 1)
    for width, weight, bias, target in (
        (width_one, embed_two_w, embed_two_b, second_ref),
        (2 * width_one, embed_three_w, embed_three_b, third_ref),
    ):
        tall, deep = target.shape[0] // 2, target.shape[1] // 3
        again = (lane - tall == row) | (lane - tall == row + width)
        again = (again & (row < width)) | ((lane - tall == 2 * width) & (row == width))
        square[...] = jnp.where(again, 1.0, 0.0)
        square[0:width, 0 : 2 * width] = weight[...]
        square[width : width + 1, 0 : 2 * width] = bias[...]
        high, low = split(jnp.transpose(square[...])[0 : 2 * tall, 0:deep])
        target[...] = jnp.concatenate([high, high, low], axis=1)
    square[...] = jnp.zeros_like(square)
    for copy in copies[11:13]:
        copy.wait()
    for source, high_ref, low_ref in (
        (fit_two_w, two_high_ref, two_low_ref),
        (fit_three_w, three_high_ref, three_low_ref),
    ):
        square[0:hidden, 0:hidden] = source[...]
        high_ref[...], low_ref[...] = split(jnp.transpose(square[...])[0:hidden, 0:hidden])

    fine = GRID_Y // 2 // pieces
    shape = (phase_ref.shape[0], 128)
    row = lax.broadcasted_iota(jnp.int32, shape, 0)
    mode = piece * fine + row // 2
    for part in range(GRID_Y // 128):
        cell = lax.broadcasted_iota(jnp.int32, shape, 1) + part * 128
        spot = wrapped(mode * cell, GRID_Y)
        cosine = lookup(constants[0:1, :], spot)
        sine = lookup(constants[1:2, :], spot)
        alternate = (1 - 2 * lax.rem(cell, 2)).astype(jnp.float32)
        odd = jnp.where(mode == 0, alternate, -sine)
        value = jnp.where(lax.rem(row, 2) == 0, cosine, odd)
        phase_ref[:, part * 128 : (part + 1) * 128] = jnp.where(row < 2 * fine, value, 0.0)

    column = jnp.transpose(constants[...])
    lane = lax.broadcasted_iota(jnp.int32, (1, GRID_Y), 1)
    for j in range(fine + 1):
        here = lane == (GRID_Y // 2 if j == fine else piece * fine + j)
        factor = jnp.sum(jnp.where(here, constants[2:3, :], 0.0), axis=1, keepdims=True)
        part = jnp.sum(jnp.where(here, constants[3:4, :], 0.0), axis=1, keepdims=True)
        wave = (part + constants[5:6, :]) + column[:, 7:8]
        top = (factor * constants[4:5, :]) * column[:, 6:7]
        green_ref[j] = jnp.where(wave == 0.0, 0.0, top / jnp.where(wave == 0.0, 1.0, wave))

    copies[13].wait()
    one_high_ref[...], one_low_ref[...] = split(fit_one_w[...])


def centroid_kernel(
    table,
    codes,
    columns,
    second,
    third,
    one_high,
    one_low,
    two_high,
    two_low,
    three_high,
    three_low,
    fit_out_w,
    dipole_ref,
    shift_ref,
    matrix,
    descriptor,
    arrivals,
    *held,
):
    sources = (table, codes, columns, second, third)
    sources += (one_high, one_low, two_high, two_low, three_high, three_low, fit_out_w)
    copies = [
        pltpu.make_async_copy(source, target, arrivals.at[k])
        for k, (source, target) in enumerate(zip(sources, held))
    ]
    for copy in copies:
        copy.start()
    table, codes, columns, second, third = held[:5]
    one_high, one_low, two_high, two_low, three_high, three_low, fit_out_w = held[5:]
    for copy in copies[:5]:
        copy.wait()
    wide_count, narrow_count, _, atoms = table.shape
    listed = codes.shape[0]
    width_three = fit_out_w.shape[0]
    width_one = width_three // 4
    hidden_width = two_high.shape[0]
    cells = (GRID_X // wide_count, GRID_Y, GRID_Z // narrow_count)
    at_wide = lax.axis_index("wide")
    at_narrow = lax.axis_index("narrow")
    own = jnp.abs(table[at_wide, at_narrow])
    nearby = []
    for step in range(9):
        wide_at = lax.rem(at_wide + (step // 3 - 1) + wide_count, wide_count)
        narrow_at = lax.rem(at_narrow + (step % 3 - 1) + narrow_count, narrow_count)
        nearby.append(table[wide_at, narrow_at])

    second_all = second[...]
    third_all = third[...]
    weight_oxygen = jnp.broadcast_to(columns[0:ROW_PAD, 0:1], (ROW_PAD, atoms))
    weight_hydrogen = jnp.broadcast_to(columns[0:ROW_PAD, 1:2], (ROW_PAD, atoms))
    bias_oxygen = jnp.broadcast_to(columns[0:ROW_PAD, 2:3], (ROW_PAD, atoms))
    bias_hydrogen = jnp.broadcast_to(columns[0:ROW_PAD, 3:4], (ROW_PAD, atoms))
    matrix[...] = jnp.zeros_like(matrix)

    def chunk(first):
        code = codes[pl.ds(first, SLOT_CHUNK), :]
        slot = wrapped(code, atoms)
        if atoms & (atoms - 1) == 0:
            offset = lax.shift_right_logical(code, atoms.bit_length() - 1)
        else:
            offset = code // atoms
        step_x = jnp.where(offset >= 9, 1, 0) + jnp.where(offset >= 18, 1, 0)
        rest = offset - 9 * step_x
        step_z = jnp.where(rest >= 3, 1, 0) + jnp.where(rest >= 6, 1, 0)
        step_y = rest - 3 * step_z
        brick = step_x * 3 + step_z
        found = []
        for component in range(3):
            picked = jnp.zeros((SLOT_CHUNK, atoms), jnp.float32)
            for step in range(9):
                row = jnp.broadcast_to(
                    nearby[step][component : component + 1], (SLOT_CHUNK, atoms)
                )
                here = jnp.take_along_axis(row, slot, axis=1, mode="promise_in_bounds")
                picked = jnp.where(brick == step, here, picked)
            found.append(picked)
        hydrogen = found[0] < 0.0
        found[0] = jnp.abs(found[0])
        scaled = []
        for component, step in enumerate((step_x, step_y, step_z)):
            extent = float(cells[component])
            relative = (step - 1).astype(jnp.float32) * extent + (
                found[component] - own[component : component + 1]
            ) * extent
            scaled.append(relative * (1.0 / radius_scale))
        smooth = 1.0 / (
            1.0 + (scaled[0] * scaled[0] + scaled[1] * scaled[1] + scaled[2] * scaled[2])
        )
        radial = [smooth] + [smooth * part for part in scaled]
        first_layers = []
        for k in range(SLOT_CHUNK):
            row = smooth[k : k + 1]
            kind = hydrogen[k : k + 1]
            weight = jnp.where(kind, weight_hydrogen, weight_oxygen)
            bias = jnp.where(kind, bias_hydrogen, bias_oxygen)
            first_layers.append(jnp.tanh(weight * row + bias))
        layer_one = jnp.concatenate(first_layers, axis=1)
        high, low = split(layer_one)
        both = lax.dot_general(
            second_all,
            jnp.concatenate([high, low, high], axis=0),
            NN,
            preferred_element_type=jnp.float32,
        )
        tall = both.shape[0] // 2
        layer_two = jnp.tanh(both[:tall]) + both[tall:]
        deep = third_all.shape[1] // 3
        rest = jnp.zeros((deep - tall, layer_two.shape[1]), jnp.float32)
        high, low = split(jnp.concatenate([layer_two, rest], axis=0))
        both = lax.dot_general(
            third_all,
            jnp.concatenate([high, low, high], axis=0),
            NN,
            preferred_element_type=jnp.float32,
        )
        tall = both.shape[0] // 2
        layer_three = jnp.tanh(both[:tall]) + both[tall:]
        for part in range(4):
            total = matrix[part]
            for k in range(SLOT_CHUNK):
                total = total + layer_three[:, k * atoms : (k + 1) * atoms] * radial[part][k : k + 1]
            matrix[part] = total

    def two_chunks(index, carry):
        first = pl.multiple_of(index * (2 * SLOT_CHUNK), 2 * SLOT_CHUNK)
        chunk(first)
        chunk(pl.multiple_of(first + SLOT_CHUNK, SLOT_CHUNK))
        return carry

    lax.fori_loop(0, listed // (2 * SLOT_CHUNK), two_chunks, 0)

    parts = []
    for part in range(4):
        parts.append(matrix[part, 0:width_three, :] * (1.0 / listed))
    leading = [part[0:AXIS_COLUMNS] for part in parts]
    for row in range(width_three):
        total = parts[0][row : row + 1] * leading[0]
        for part in range(1, 4):
            total = total + parts[part][row : row + 1] * leading[part]
        descriptor[row * AXIS_COLUMNS : (row + 1) * AXIS_COLUMNS, :] = total
    for copy in copies[5:]:
        copy.wait()

    def layer(high_ref, low_ref, given, column):
        weights = (high_ref[...], low_ref[...])
        return jnp.tanh(multiply(weights, split(given)) + columns[0:hidden_width, column : column + 1])

    hidden = layer(one_high, one_low, descriptor[...], 4)
    hidden = hidden + layer(two_high, two_low, hidden, 5)
    hidden = hidden + layer(three_high, three_low, hidden, 6)
    coeffs = multiply(split(fit_out_w[...]), split(hidden))
    vector = jnp.concatenate(
        [jnp.sum(coeffs * parts[1 + c], axis=0, keepdims=True) for c in range(3)], axis=0
    )
    oxygen = 1.0 - own[3:4]
    for c in range(3):
        dipole_ref[c] = vector[c : c + 1] * oxygen
    moved = wannier_reach * jnp.tanh(vector)
    moved = jnp.concatenate([moved, jnp.zeros((1, atoms), jnp.float32)], axis=0)
    for target in range(shift_ref.shape[0]):
        shift_ref[target] = moved


def mesh_kernel(
    table,
    shifts,
    phase,
    green_ref,
    fold_stack,
    unfold_stack,
    out_ref,
    grid,
    planes,
    packed,
    weights_even,
    weights_odd,
    slopes_even,
    slopes_odd,
    weights_z,
    slopes_z,
    waves,
    wave_slopes,
):
    wide_count, narrow_count, _, atoms = table.shape
    cells_x = GRID_X // wide_count
    cells_z = GRID_Z // narrow_count
    window = cells_z + HALO_Z
    reach = cells_x + HALO_X
    pair = 2 * atoms
    length = wide_count * pair
    copies = grid.shape[0]
    fine = grid.shape[1]
    channels = 2 * fine
    rows = phase.shape[0]
    half_x = GRID_X // 2
    half_z = GRID_Z // 2
    piece = lax.axis_index("wide") * narrow_count + lax.axis_index("narrow")
    lane_zero = lax.broadcasted_iota(jnp.int32, (1, half_x), 1) == 0
    row_zero = lax.broadcasted_iota(jnp.int32, (half_z, 1), 0) == 0

    def fold():
        return (fold_stack[0:GRID_X, :], fold_stack[GRID_X:, :])

    def unfold():
        return (unfold_stack[0:GRID_X, :], unfold_stack[GRID_X:, :])

    def sites(at_wide, at_narrow):
        atom = jnp.abs(table[at_wide, at_narrow])
        moved = shifts[at_wide, at_narrow]
        found = []
        for component, extent in enumerate((cells_x, GRID_Y, cells_z)):
            start = atom[component : component + 1] * float(extent)
            found.append(jnp.concatenate([start, start + moved[component : component + 1]], axis=1))
        oxygen = 1.0 - atom[3:4]
        found.append(jnp.concatenate([6.0 * oxygen + atom[3:4], -8.0 * oxygen], axis=1))
        return found

    def line(at_narrow):
        groups = [sites(at_wide, at_narrow) for at_wide in range(wide_count)]
        return [jnp.concatenate([g[k] for g in groups], axis=1) for k in range(4)]

    def splines_z(row):
        counter = lax.broadcasted_iota(jnp.int32, (window, 1), 0).astype(jnp.float32)
        return spline_pair(row - (counter - float(HALO_Z)))

    def fill_x(row, targets):
        counter = lax.broadcasted_iota(jnp.int32, (reach, 1), 0).astype(jnp.float32)
        both = spline_pair(row - (counter - float(HALO_X)))
        rest = jnp.zeros((128 - reach, length), jnp.bfloat16)
        for values, ref in zip(both, targets):
            high, low = split(values)
            ref[0:reach, :] = high
            ref[reach:128, :] = rest
            ref[128 : 128 + reach, :] = low
            ref[128 + reach : 256, :] = rest

    grid[:, :, 0:HALO_Z, :] = jnp.zeros((copies, fine, HALO_Z, 2 * GRID_X), jnp.float32)

    weights = (weights_even, weights_odd)
    slopes = (slopes_even, slopes_odd)

    def spread(index, odd):
        at_narrow = 2 * index + odd
        row_x, row_y, row_z, charge = line(at_narrow)
        lower = jnp.floor(row_y)
        back = lax.broadcasted_iota(jnp.int32, (8, 1), 0)
        value_y, slope_y = spline_pair((row_y - lower) + back.astype(jnp.float32))
        cell = wrapped(lower.astype(jnp.int32) - back + GRID_Y, GRID_Y)
        wave_blocks = []
        slope_blocks = []
        for block in range(length // 128):
            lanes = slice(block * 128, (block + 1) * 128)
            wave = jnp.zeros((rows, 128), jnp.float32)
            wave_slope = jnp.zeros((rows, 128), jnp.float32)
            for k in range(4):
                spot = jnp.broadcast_to(cell[k : k + 1, lanes], (rows, 128))
                found = lookup(phase[...], spot)
                wave = wave + value_y[k : k + 1, lanes] * found
                wave_slope = wave_slope + slope_y[k : k + 1, lanes] * found
            wave_blocks.append(wave)
            slope_blocks.append(wave_slope)
        wave = jnp.concatenate(wave_blocks, axis=1)
        waves[at_narrow] = wave
        wave_slopes[at_narrow] = jnp.concatenate(slope_blocks, axis=1)
        fill_x(row_x, (weights[odd].at[index], slopes[odd].at[index]))
        value_z, slope_z = splines_z(row_z)
        weights_z[at_narrow] = value_z
        slopes_z[at_narrow] = slope_z
        charged = wave * charge
        first = pl.multiple_of(at_narrow * cells_z, HALO_Z)
        for at_wide in range(wide_count):
            lanes = slice(at_wide * pair, (at_wide + 1) * pair)
            near = value_z[:, lanes]
            left = jnp.concatenate(
                [near * charged[c : c + 1, lanes] for c in range(channels)], axis=0
            )
            total = lax.dot_general(
                jnp.concatenate(split(left), axis=0),
                weights[odd][index, :, lanes],
                NT,
                preferred_element_type=jnp.float32,
            )
            tall = channels * window
            total = total[:tall, 0:128] + (total[:tall, 128:256] + total[tall:, 0:128])
            start = at_wide // copies * 128
            for c in range(channels):
                spot = slice(c % 2 * GRID_X + start, c % 2 * GRID_X + start + 128)
                k = at_wide % copies
                part = total[c * window : (c + 1) * window]
                grid[k, c // 2, pl.ds(first, HALO_Z), spot] += part[:HALO_Z]
                grid[k, c // 2, pl.ds(first + HALO_Z, cells_z), spot] = part[HALO_Z:]

    def in_pairs(step):
        def both(index, carry):
            step(index, 0)
            step(index, 1)
            return carry

        lax.fori_loop(0, narrow_count // 2, both, 0)

    in_pairs(spread)

    def gather(j, carry):
        for lanes in (slice(0, GRID_X), slice(GRID_X, 2 * GRID_X)):
            total = None
            for k in range(copies):
                moved = pltpu.roll(grid[k, j, :, lanes], (k * cells_x - HALO_X) % GRID_X, 1)
                total = moved if total is None else total + moved
            planes[j, :, lanes] = total[HALO_Z:]
            planes[j, GRID_Z - HALO_Z :, lanes] += total[:HALO_Z]
        return carry

    lax.fori_loop(0, fine, gather, 0)
    is_first = piece == 0

    def paired(real, imag, zero, axis):
        half = real.shape[axis] // 2
        first = (slice(None),) * axis + (slice(0, half),)
        second = (slice(None),) * axis + (slice(half, 2 * half),)
        real_c, real_s = real[first], real[second]
        if imag is None:
            none = jnp.zeros_like(real_s)
            real_all = [real_c, jnp.where(zero, real_s, real_c)]
            imag_all = [jnp.where(zero, none, -real_s), jnp.where(zero, none, real_s)]
        else:
            imag_c, imag_s = imag[first], imag[second]
            real_all = [
                real_c + jnp.where(zero, 0.0, imag_s),
                jnp.where(zero, real_s, real_c - imag_s),
            ]
            imag_all = [
                imag_c - jnp.where(zero, 0.0, real_s),
                jnp.where(zero, imag_s, imag_c + real_s),
            ]
        return jnp.concatenate(real_all, axis=axis), jnp.concatenate(imag_all, axis=axis)

    def merged(real, imag, zero, axis):
        half = real.shape[axis] // 2
        first = (slice(None),) * axis + (slice(0, half),)
        second = (slice(None),) * axis + (slice(half, 2 * half),)
        real_a, real_b = real[first], real[second]
        imag_a, imag_b = imag[first], imag[second]
        real = [
            real_a + jnp.where(zero, 0.0, real_b),
            jnp.where(zero, real_b, imag_b - imag_a),
        ]
        imag = [
            imag_a + jnp.where(zero, 0.0, imag_b),
            jnp.where(zero, imag_b, real_a - real_b),
        ]
        return jnp.concatenate(real, axis=axis), jnp.concatenate(imag, axis=axis)

    modes = {}
    parts = []

    def slot(j):
        first_imag = planes[0, :, GRID_X:]
        if j == fine:
            real, imag = jnp.where(is_first, first_imag, 0.0), None
        else:
            real, imag = planes[j, :, 0:GRID_X], planes[j, :, GRID_X:]
            if j == 0:
                imag = jnp.where(is_first, 0.0, imag)
        real = split(real)
        imag = None if imag is None else split(imag)
        yield
        real = by_right(real, fold())
        imag = None if imag is None else by_right(imag, fold())
        yield
        real, imag = paired(real, imag, lane_zero, 1)
        real, imag = split(real), split(imag)
        yield
        real, imag = by_left(unfold_stack[...], real), by_left(unfold_stack[...], imag)
        yield
        real, imag = paired(real, imag, row_zero, 0)
        green = green_ref[j]
        mode = GRID_Y // 2 if j == fine else piece * fine + j
        share = jnp.where((mode == 0) | (mode == GRID_Y // 2), 0.5, 1.0)
        parts.append(share * jnp.sum(green * (real * real + imag * imag), axis=0, keepdims=True))
        real, imag = green * real, green * imag
        if j == fine:
            modes[j] = (real, imag)
            return
        if j == 0:
            real, imag = real - modes[fine][1], imag + modes[fine][0]
        real, imag = merged(real, imag, row_zero, 0)
        real, imag = split(real), split(imag)
        yield
        real, imag = by_left(fold_stack[...], real), by_left(fold_stack[...], imag)
        yield
        real, imag = merged(real, imag, lane_zero, 1)
        scale = jnp.where(piece * fine + j == 0, 1.0, 2.0)
        real, imag = split(real * scale), split(imag * scale)
        yield
        real, imag = by_right(real, unfold()), by_right(imag, unfold())
        yield
        for k, part in enumerate((real, imag)):
            turned = [
                pltpu.roll(part, (HALO_X - at_wide * cells_x) % GRID_X, 1)
                for at_wide in range(copies)
            ]
            for at_wide in range(wide_count):
                start = at_wide // copies * 128
                moved = turned[at_wide % copies][:, start : start + 128]
                high = moved.astype(jnp.bfloat16).astype(jnp.float32)
                again = pltpu.roll(high, reach % 128, 1)
                low = pltpu.roll(moved - high, 2 * reach % 128, 1)
                sides = []
                for side in range(2):
                    lane = lax.broadcasted_iota(jnp.int32, (1, 128), 1) + side * 128
                    value = jnp.where(lane < 2 * reach, again, low)
                    if side == 0:
                        value = jnp.where(lane < reach, high, value)
                    sides.append(value.astype(jnp.bfloat16))
                block = jnp.concatenate(sides, axis=1)
                packed[at_wide, 2 * j + k, HALO_BITS:, :] = block
                packed[at_wide, 2 * j + k, 0:HALO_BITS, :] = block[GRID_Z - HALO_BITS :]

    waiting = [slot(j) for j in [fine, *range(fine)]]
    running = []
    while waiting or running:
        if waiting:
            running.append(waiting.pop(0))
        running = [one for one in running if next(one, running) is not running]
    energy = sum(parts[1:], parts[0])
    energy = jnp.broadcast_to(jnp.sum(energy, axis=1, keepdims=True), (1, 128))

    def collect(index, odd):
        at_narrow = 2 * index + odd
        value_z = weights_z[at_narrow]
        slope_z = slopes_z[at_narrow]
        first = pl.multiple_of(at_narrow * cells_z, HALO_BITS)
        wave = waves[at_narrow]
        wave_slope = wave_slopes[at_narrow]
        for at_wide in range(wide_count):
            lanes = slice(at_wide * pair, (at_wide + 1) * pair)
            tall = cells_z + HALO_BITS
            left = jnp.concatenate(
                [packed[at_wide, c, pl.ds(first, tall), :] for c in range(channels)], axis=0
            )

            def across(right):
                high = right[0:reach]
                rest = jnp.zeros((256 - 3 * reach, pair), jnp.bfloat16)
                right = jnp.concatenate([high, right[128 : 128 + reach], high, rest], axis=0)
                return lax.dot_general(left, right, NN, preferred_element_type=jnp.float32)

            value = across(weights[odd][index, :, lanes])
            slope = across(slopes[odd][index, :, lanes])
            plain = jnp.zeros((window, pair), jnp.float32)
            along_x = plain
            along_y = plain
            for c in range(channels):
                block = slice((c + 1) * tall - window, (c + 1) * tall)
                plain = plain + value[block] * wave[c : c + 1, lanes]
                along_x = along_x + slope[block] * wave[c : c + 1, lanes]
                along_y = along_y + value[block] * wave_slope[c : c + 1, lanes]
            near = value_z[:, lanes]
            near_slope = slope_z[:, lanes]
            results = [
                jnp.sum(near * plain, axis=0, keepdims=True),
                -jnp.sum(near * along_x, axis=0, keepdims=True),
                -jnp.sum(near * along_y, axis=0, keepdims=True),
                -jnp.sum(near_slope * plain, axis=0, keepdims=True),
            ]
            for k, row in enumerate(results):
                out_ref[at_wide, at_narrow, :, k * pair : (k + 1) * pair] = row
            out_ref[at_wide, at_narrow, :, 4 * pair :] = energy

    in_pairs(collect)


def finish_kernel(arrived, species, atom_ref, centroid_ref, energy_ref):
    atoms = species.shape[1]
    total = arrived[0]
    for k in range(1, arrived.shape[0]):
        total = total + arrived[k]
    oxygen = 1.0 - species[...].astype(jnp.float32)
    for k in range(4):
        atom_ref[k] = total[:, 2 * k * atoms : (2 * k + 1) * atoms]
        centroid_ref[k] = total[:, (2 * k + 1) * atoms : (2 * k + 2) * atoms] * oxygen
    energy_ref[...] = total[:, 8 * atoms :] * (1.0 / (atoms * arrived.shape[0]))


def mode_factors(length, order):
    wrapped = np.where(2 * order >= length, order - length, order)
    square = (wrapped / length) ** 2
    ratio = (4.0 + 2.0 * np.cos(2.0 * math.pi * order / length)) / 6.0
    return np.stack([np.exp(-(math.pi**2) * square / ewald_beta**2) / ratio**2, square])


def folded_order(length):
    half = length // 2
    counter = np.arange(half)
    return np.concatenate([counter, np.where(counter == 0, half, length - counter)])


def fold_table(length):
    half = length // 2
    turns = np.outer(np.arange(length), np.arange(half)) % length * (2.0 * math.pi / length)
    sines = np.sin(turns)
    sines[:, 0] = 1.0 - 2.0 * (np.arange(length) % 2)
    return np.concatenate([np.cos(turns), sines], axis=1)


def halves(table):
    high = table.astype(jnp.bfloat16)
    low = (table - high.astype(np.float64)).astype(jnp.bfloat16)
    return high, low


def vmem(count):
    return [pl.BlockSpec(memory_space=pltpu.VMEM)] * count


def hbm(count):
    return [pl.BlockSpec(memory_space=pltpu.HBM)] * count


def shaped(shape, dtype=jnp.float32):
    return jax.ShapeDtypeStruct(shape, dtype)


def limits(mebibytes):
    return pltpu.CompilerParams(vmem_limit_bytes=mebibytes * 1024 * 1024)


def local(
    positions,
    species,
    neighbours,
    embed_one_w,
    embed_one_b,
    embed_two_w,
    embed_two_b,
    embed_three_w,
    embed_three_b,
    fit_one_w,
    fit_one_b,
    fit_two_w,
    fit_two_b,
    fit_three_w,
    fit_three_b,
    fit_out_w,
):
    axes = ("wide", "narrow")
    wide_count = lax.axis_size("wide")
    narrow_count = lax.axis_size("narrow")
    pieces = wide_count * narrow_count
    atoms = positions.shape[4]
    listed = neighbours.shape[4]
    fine = GRID_Y // 2 // pieces
    width_three = embed_three_w.shape[1]
    entries, hidden = fit_one_w.shape
    kinds = species.reshape(1, atoms)

    packed = pl.pallas_call(
        pack_kernel,
        out_shape=shaped((pieces, 4, atoms)),
        in_specs=vmem(2),
        out_specs=vmem(1)[0],
        name="pack",
    )(positions.reshape(3, 1, atoms), kinds)
    table = lax.all_to_all(packed, axes, 0, 0, tiled=True)
    table = table.reshape(wide_count, narrow_count, 4, atoms)

    tall_two = -(-(width_three // 2 + 1) // 8) * 8
    tall_three = -(-width_three // 8) * 8
    bf16 = jnp.bfloat16
    wave_rows = -(-2 * fine // 8) * 8
    angle = np.arange(GRID_Y) * (2.0 * math.pi / GRID_Y)
    constants = np.concatenate(
        [
            np.stack([np.cos(angle), np.sin(angle)]),
            mode_factors(GRID_Y, np.arange(GRID_Y)),
            mode_factors(GRID_X, folded_order(GRID_X)),
            mode_factors(GRID_Z, folded_order(GRID_Z)),
        ]
    )
    constants[2] *= coulomb / (math.pi * GRID_X * GRID_Y * GRID_Z)
    arguments = (
        neighbours.reshape(atoms, listed),
        embed_one_w,
        embed_one_b,
        embed_two_w,
        embed_two_b[None],
        embed_three_w,
        embed_three_b[None],
        fit_one_w.T,
        fit_one_b[None],
        fit_two_w,
        fit_two_b[None],
        fit_three_w,
        fit_three_b[None],
        jnp.asarray(constants, jnp.float32),
    )
    held = [arguments[k] for k in (0, 1, 2, 3, 4, 5, 6, 8, 10, 12, 13, 9, 11, 7)]
    prepared = pl.pallas_call(
        prepare_kernel,
        out_shape=(
            shaped((listed, atoms), jnp.int32),
            shaped((256, 16)),
            shaped((2 * tall_two, 3 * ROW_PAD), bf16),
            shaped((2 * tall_three, 6 * ROW_PAD), bf16),
            shaped((hidden, entries), bf16),
            shaped((hidden, entries), bf16),
        )
        + (shaped((hidden, hidden), bf16),) * 4
        + (shaped((wave_rows, GRID_Y)), shaped((fine + 1, GRID_Z, GRID_X))),
        in_specs=hbm(len(arguments)),
        out_specs=tuple(vmem(12)),
        scratch_shapes=[
            pltpu.VMEM((16, 256), jnp.float32),
            pltpu.VMEM((256, 256), jnp.float32),
            pltpu.SemaphoreType.DMA((len(held),)),
        ]
        + [pltpu.VMEM(array.shape, array.dtype) for array in held],
        compiler_params=limits(62),
        cost_estimate=pl.CostEstimate(
            flops=1000000, bytes_accessed=8 * entries * hidden, transcendentals=0
        ),
        name="prepare",
    )(*arguments)
    phase, green = prepared[10:]
    fitted = (table, *prepared[:10], fit_out_w.T)
    dipole, shifts = pl.pallas_call(
        centroid_kernel,
        out_shape=(shaped((3, 1, atoms)), shaped((pieces, 4, atoms))),
        in_specs=hbm(12),
        out_specs=tuple(vmem(2)),
        scratch_shapes=[
            pltpu.VMEM((4, tall_three, atoms), jnp.float32),
            pltpu.VMEM((width_three * AXIS_COLUMNS, atoms), jnp.float32),
            pltpu.SemaphoreType.DMA((len(fitted),)),
        ]
        + [pltpu.VMEM(array.shape, array.dtype) for array in fitted],
        compiler_params=limits(62),
        name="centroids",
    )(*fitted)
    shifts = lax.all_to_all(shifts, axes, 0, 0, tiled=True)
    shifts = shifts.reshape(wide_count, narrow_count, 4, atoms)

    cells_x = GRID_X // wide_count
    copies = 128 // cells_x
    length = wide_count * 2 * atoms
    out_width = 8 * atoms + 128
    partial = pl.pallas_call(
        mesh_kernel,
        out_shape=shaped((wide_count, narrow_count, 1, out_width)),
        in_specs=vmem(6),
        out_specs=vmem(1)[0],
        scratch_shapes=[
            pltpu.VMEM((copies, fine, HALO_Z + GRID_Z, 2 * GRID_X), jnp.float32),
            pltpu.VMEM((fine, GRID_Z, 2 * GRID_X), jnp.float32),
            pltpu.VMEM((wide_count, 2 * fine, HALO_BITS + GRID_Z, 256), bf16),
        ]
        + [pltpu.VMEM((narrow_count // 2, 256, length), bf16)] * 4
        + [pltpu.VMEM((narrow_count, GRID_Z // narrow_count + HALO_Z, length), jnp.float32)] * 2
        + [pltpu.VMEM((narrow_count, wave_rows, length), jnp.float32)] * 2,
        compiler_params=limits(48),
        name="mesh",
    )(
        table,
        shifts,
        phase,
        green,
        jnp.asarray(np.concatenate(halves(fold_table(GRID_X)))),
        jnp.asarray(np.concatenate(halves(fold_table(GRID_X).T))),
    )
    arrived = lax.all_to_all(partial.reshape(pieces, 1, out_width), axes, 0, 0, tiled=True)
    atom_field, centroid_field, energy = pl.pallas_call(
        finish_kernel,
        out_shape=(shaped((4, 1, atoms)), shaped((4, 1, atoms)), shaped((1, 128))),
        in_specs=vmem(2),
        out_specs=tuple(vmem(3)),
        name="finish",
    )(arrived, kinds)
    atom_field = atom_field.reshape(4, 1, 1, 1, atoms)
    centroid_field = centroid_field.reshape(4, 1, 1, 1, atoms)
    return (dipole.reshape(3, 1, 1, 1, atoms), atom_field, centroid_field, energy[0, 0])


def solution(mesh):
    column = P(None, "wide", "narrow", None, None)
    in_specs = (column, P("wide", "narrow", None, None), P("wide", "narrow", None, None, None))
    in_specs = in_specs + (P(),) * 13
    out_specs = (column, column, column, P())
    return jax.shard_map(local, mesh=mesh, in_specs=in_specs, out_specs=out_specs, check_vma=False)
```

```python
import math

import jax
import jax.numpy as jnp
import numpy as np
from jax import lax
from jax.experimental import pallas as pl
from jax.experimental.pallas import tpu as pltpu
from jax.sharding import PartitionSpec as P

GRID_X = 256
GRID_Y = 256
GRID_Z = 256
AXIS_COLUMNS = 16

radius_scale = 24.0
wannier_reach = 0.5
ewald_beta = 0.9
coulomb = 0.25

ROW_PAD = 32
LOOP_BODY = 4
SLOT_CHUNK = 16
HALO_X = 16
HALO_Z = 8
HALO_BITS = 16

NN = (((1,), (0,)), ((), ()))
NT = (((1,), (1,)), ((), ()))


def split(value):
    high = value.astype(jnp.bfloat16)
    low = (value - high.astype(jnp.float32)).astype(jnp.bfloat16)
    return high, low


def multiply(left, right, dims=NN):
    def one(a, b):
        return lax.dot_general(a, b, dims, preferred_element_type=jnp.float32)

    return one(left[0], right[0]) + (one(left[1], right[0]) + one(left[0], right[1]))


def by_right(left, right):
    rows = left[0].shape[0]
    both = lax.dot_general(
        jnp.concatenate(left, axis=0), right[0], NN, preferred_element_type=jnp.float32
    )
    rest = lax.dot_general(left[0], right[1], NN, preferred_element_type=jnp.float32)
    return both[:rows] + (both[rows:] + rest)


def by_left(left, right):
    rows = left.shape[0] // 2
    both = lax.dot_general(left, right[0], NN, preferred_element_type=jnp.float32)
    rest = lax.dot_general(left[:rows], right[1], NN, preferred_element_type=jnp.float32)
    return both[:rows] + (both[rows:] + rest)


def spline_pair(offset):
    centred = offset - 2.0
    away = jnp.abs(centred)
    outer = jnp.maximum(2.0 - away, 0.0)
    inner = jnp.maximum(1.0 - away, 0.0)
    outer_square = outer * outer
    inner_square = inner * inner
    value = (outer_square * outer - 4.0 * (inner_square * inner)) * (1.0 / 6.0)
    slope = jnp.where(centred < 0.0, 0.5, -0.5) * (outer_square - 4.0 * inner_square)
    return value, slope


def wrapped(value, length):
    if length & (length - 1) == 0:
        return jnp.bitwise_and(value, length - 1)
    return lax.rem(value, length)


def lookup(row_table, spot):
    found = None
    lane = jnp.bitwise_and(spot, 127)
    block = lax.shift_right_logical(spot, 7)
    for part in range(row_table.shape[1] // 128):
        inside = block == part
        here = jnp.take_along_axis(
            jnp.broadcast_to(row_table[:, part * 128 : (part + 1) * 128], spot.shape),
            lane,
            axis=1,
            mode="promise_in_bounds",
        )
        found = here if found is None else jnp.where(inside, here, found)
    return found


def pack_kernel(positions, species, out_ref):
    kinds = species[...]
    rows = [positions[component] for component in range(3)]
    rows[0] = jnp.where(kinds > 0, -rows[0], rows[0])
    rows.append(kinds.astype(jnp.float32))
    rows = jnp.concatenate(rows, axis=0)
    for target in range(out_ref.shape[0]):
        out_ref[target] = rows


def prepare_kernel(
    neighbours,
    embed_one_w,
    embed_one_b,
    embed_two_w,
    embed_two_b,
    embed_three_w,
    embed_three_b,
    fit_one_w,
    fit_one_b,
    fit_two_w,
    fit_two_b,
    fit_three_w,
    fit_three_b,
    constants,
    codes_ref,
    columns_ref,
    second_ref,
    third_ref,
    one_high_ref,
    one_low_ref,
    two_high_ref,
    two_low_ref,
    three_high_ref,
    three_low_ref,
    phase_ref,
    green_ref,
    rows,
    square,
    arrivals,
    *held,
):
    sources = (
        neighbours,
        embed_one_w,
        embed_one_b,
        embed_two_w,
        embed_two_b,
        embed_three_w,
        embed_three_b,
        fit_one_b,
        fit_two_b,
        fit_three_b,
        constants,
        fit_two_w,
        fit_three_w,
        fit_one_w,
    )
    copies = [
        pltpu.make_async_copy(source, target, arrivals.at[k])
        for k, (source, target) in enumerate(zip(sources, held))
    ]
    for copy in copies:
        copy.start()
    (
        neighbours,
        embed_one_w,
        embed_one_b,
        embed_two_w,
        embed_two_b,
        embed_three_w,
        embed_three_b,
        fit_one_b,
        fit_two_b,
        fit_three_b,
        constants,
        fit_two_w,
        fit_three_w,
        fit_one_w,
    ) = held
    for copy in copies[:11]:
        copy.wait()
    pieces = lax.axis_size("wide") * lax.axis_size("narrow")
    piece = lax.axis_index("wide") * lax.axis_size("narrow") + lax.axis_index("narrow")
    width_one = embed_one_w.shape[1]
    hidden = fit_two_w.shape[0]
    codes_ref[...] = jnp.transpose(neighbours[...].astype(jnp.float32)).astype(jnp.int32)
    rows[...] = jnp.zeros_like(rows)
    for kind in range(2):
        rows[kind : kind + 1, 0:width_one] = embed_one_w[kind : kind + 1, :]
        rows[2 + kind : 3 + kind, 0:width_one] = embed_one_b[kind : kind + 1, :]
        rows[2 + kind : 3 + kind, width_one : width_one + 1] = jnp.full((1, 1), 40.0, jnp.float32)
    for row, source in ((4, fit_one_b), (5, fit_two_b), (6, fit_three_b)):
        rows[row : row + 1, 0:hidden] = source[...]
    columns_ref[...] = jnp.transpose(rows[...])

    row = lax.broadcasted_iota(jnp.int32, square.shape, 0)
    lane = lax.broadcasted_iota(jnp.int32, square.shape, 1)
    for width, weight, bias, target in (
        (width_one, embed_two_w, embed_two_b, second_ref),
        (2 * width_one, embed_three_w, embed_three_b, third_ref),
    ):
        tall, deep = target.shape[0] // 2, target.shape[1] // 3
        again = (lane - tall == row) | (lane - tall == row + width)
        again = (again & (row < width)) | ((lane - tall == 2 * width) & (row == width))
        square[...] = jnp.where(again, 1.0, 0.0)
        square[0:width, 0 : 2 * width] = weight[...]
        square[width : width + 1, 0 : 2 * width] = bias[...]
        high, low = split(jnp.transpose(square[...])[0 : 2 * tall, 0:deep])
        target[...] = jnp.concatenate([high, high, low], axis=1)
    square[...] = jnp.zeros_like(square)
    for copy in copies[11:13]:
        copy.wait()
    for source, high_ref, low_ref in (
        (fit_two_w, two_high_ref, two_low_ref),
        (fit_three_w, three_high_ref, three_low_ref),
    ):
        square[0:hidden, 0:hidden] = source[...]
        high_ref[...], low_ref[...] = split(jnp.transpose(square[...])[0:hidden, 0:hidden])

    fine = GRID_Y // 2 // pieces
    shape = (phase_ref.shape[0], 128)
    row = lax.broadcasted_iota(jnp.int32, shape, 0)
    mode = piece * fine + row // 2
    for part in range(GRID_Y // 128):
        cell = lax.broadcasted_iota(jnp.int32, shape, 1) + part * 128
        spot = wrapped(mode * cell, GRID_Y)
        cosine = lookup(constants[0:1, :], spot)
        sine = lookup(constants[1:2, :], spot)
        alternate = (1 - 2 * lax.rem(cell, 2)).astype(jnp.float32)
        odd = jnp.where(mode == 0, alternate, -sine)
        value = jnp.where(lax.rem(row, 2) == 0, cosine, odd)
        phase_ref[:, part * 128 : (part + 1) * 128] = jnp.where(row < 2 * fine, value, 0.0)

    column = jnp.transpose(constants[...])
    lane = lax.broadcasted_iota(jnp.int32, (1, GRID_Y), 1)
    for j in range(fine + 1):
        here = lane == (GRID_Y // 2 if j == fine else piece * fine + j)
        factor = jnp.sum(jnp.where(here, constants[2:3, :], 0.0), axis=1, keepdims=True)
        part = jnp.sum(jnp.where(here, constants[3:4, :], 0.0), axis=1, keepdims=True)
        wave = (part + constants[5:6, :]) + column[:, 7:8]
        top = (factor * constants[4:5, :]) * column[:, 6:7]
        green_ref[j] = jnp.where(wave == 0.0, 0.0, top / jnp.where(wave == 0.0, 1.0, wave))

    copies[13].wait()
    one_high_ref[...], one_low_ref[...] = split(fit_one_w[...])


def centroid_kernel(
    table,
    codes,
    columns,
    second,
    third,
    one_high,
    one_low,
    two_high,
    two_low,
    three_high,
    three_low,
    fit_out_w,
    dipole_ref,
    shift_ref,
    table_ref,
    matrix,
    descriptor,
    arrivals,
    *held,
):
    sources = (table, codes, columns, second, third)
    sources += (one_high, one_low, two_high, two_low, three_high, three_low, fit_out_w)
    copies = [
        pltpu.make_async_copy(source, target, arrivals.at[k])
        for k, (source, target) in enumerate(zip(sources, held))
    ]
    for copy in copies:
        copy.start()
    table, codes, columns, second, third = held[:5]
    one_high, one_low, two_high, two_low, three_high, three_low, fit_out_w = held[5:]
    for copy in copies[:5]:
        copy.wait()
    handing_on = pltpu.make_async_copy(table, table_ref, arrivals.at[len(copies)])
    handing_on.start()
    wide_count, narrow_count, _, atoms = table.shape
    listed = codes.shape[0]
    width_three = fit_out_w.shape[0]
    width_one = width_three // 4
    hidden_width = two_high.shape[0]
    cells = (GRID_X // wide_count, GRID_Y, GRID_Z // narrow_count)
    at_wide = lax.axis_index("wide")
    at_narrow = lax.axis_index("narrow")
    own = jnp.abs(table[at_wide, at_narrow])
    nearby = []
    for step in range(9):
        wide_at = lax.rem(at_wide + (step // 3 - 1) + wide_count, wide_count)
        narrow_at = lax.rem(at_narrow + (step % 3 - 1) + narrow_count, narrow_count)
        nearby.append(table[wide_at, narrow_at])

    second_all = second[...]
    third_all = third[...]
    weight_oxygen = jnp.broadcast_to(columns[0:ROW_PAD, 0:1], (ROW_PAD, atoms))
    weight_hydrogen = jnp.broadcast_to(columns[0:ROW_PAD, 1:2], (ROW_PAD, atoms))
    bias_oxygen = jnp.broadcast_to(columns[0:ROW_PAD, 2:3], (ROW_PAD, atoms))
    bias_hydrogen = jnp.broadcast_to(columns[0:ROW_PAD, 3:4], (ROW_PAD, atoms))
    matrix[...] = jnp.zeros_like(matrix)

    def chunk(first):
        code = codes[pl.ds(first, SLOT_CHUNK), :]
        slot = wrapped(code, atoms)
        if atoms & (atoms - 1) == 0:
            offset = lax.shift_right_logical(code, atoms.bit_length() - 1)
        else:
            offset = code // atoms
        step_x = jnp.where(offset >= 9, 1, 0) + jnp.where(offset >= 18, 1, 0)
        rest = offset - 9 * step_x
        step_z = jnp.where(rest >= 3, 1, 0) + jnp.where(rest >= 6, 1, 0)
        step_y = rest - 3 * step_z
        brick = step_x * 3 + step_z
        found = []
        for component in range(3):
            picked = jnp.zeros((SLOT_CHUNK, atoms), jnp.float32)
            for step in range(9):
                row = jnp.broadcast_to(
                    nearby[step][component : component + 1], (SLOT_CHUNK, atoms)
                )
                here = jnp.take_along_axis(row, slot, axis=1, mode="promise_in_bounds")
                picked = jnp.where(brick == step, here, picked)
            found.append(picked)
        hydrogen = found[0] < 0.0
        found[0] = jnp.abs(found[0])
        scaled = []
        for component, step in enumerate((step_x, step_y, step_z)):
            extent = float(cells[component])
            relative = (step - 1).astype(jnp.float32) * extent + (
                found[component] - own[component : component + 1]
            ) * extent
            scaled.append(relative * (1.0 / radius_scale))
        smooth = 1.0 / (
            1.0 + (scaled[0] * scaled[0] + scaled[1] * scaled[1] + scaled[2] * scaled[2])
        )
        radial = [smooth] + [smooth * part for part in scaled]
        first_layers = []
        for k in range(SLOT_CHUNK):
            row = smooth[k : k + 1]
            kind = hydrogen[k : k + 1]
            weight = jnp.where(kind, weight_hydrogen, weight_oxygen)
            bias = jnp.where(kind, bias_hydrogen, bias_oxygen)
            first_layers.append(jnp.tanh(weight * row + bias))
        layer_one = jnp.concatenate(first_layers, axis=1)
        high, low = split(layer_one)
        both = lax.dot_general(
            second_all,
            jnp.concatenate([high, low, high], axis=0),
            NN,
            preferred_element_type=jnp.float32,
        )
        tall = both.shape[0] // 2
        layer_two = jnp.tanh(both[:tall]) + both[tall:]
        deep = third_all.shape[1] // 3
        rest = jnp.zeros((deep - tall, layer_two.shape[1]), jnp.float32)
        high, low = split(jnp.concatenate([layer_two, rest], axis=0))
        both = lax.dot_general(
            third_all,
            jnp.concatenate([high, low, high], axis=0),
            NN,
            preferred_element_type=jnp.float32,
        )
        tall = both.shape[0] // 2
        layer_three = jnp.tanh(both[:tall]) + both[tall:]
        for part in range(4):
            total = matrix[part]
            for k in range(SLOT_CHUNK):
                total = total + layer_three[:, k * atoms : (k + 1) * atoms] * radial[part][k : k + 1]
            matrix[part] = total

    def chunks(index, carry):
        for step in range(LOOP_BODY):
            chunk(pl.multiple_of((index * LOOP_BODY + step) * SLOT_CHUNK, SLOT_CHUNK))
        return carry

    lax.fori_loop(0, listed // (LOOP_BODY * SLOT_CHUNK), chunks, 0)

    parts = []
    for part in range(4):
        parts.append(matrix[part, 0:width_three, :] * (1.0 / listed))
    leading = [part[0:AXIS_COLUMNS] for part in parts]
    for row in range(width_three):
        total = parts[0][row : row + 1] * leading[0]
        for part in range(1, 4):
            total = total + parts[part][row : row + 1] * leading[part]
        descriptor[row * AXIS_COLUMNS : (row + 1) * AXIS_COLUMNS, :] = total
    for copy in copies[5:]:
        copy.wait()

    def layer(high_ref, low_ref, given, column):
        weights = (high_ref[...], low_ref[...])
        return jnp.tanh(multiply(weights, split(given)) + columns[0:hidden_width, column : column + 1])

    hidden = layer(one_high, one_low, descriptor[...], 4)
    hidden = hidden + layer(two_high, two_low, hidden, 5)
    hidden = hidden + layer(three_high, three_low, hidden, 6)
    coeffs = multiply(split(fit_out_w[...]), split(hidden))
    vector = jnp.concatenate(
        [jnp.sum(coeffs * parts[1 + c], axis=0, keepdims=True) for c in range(3)], axis=0
    )
    oxygen = 1.0 - own[3:4]
    for c in range(3):
        dipole_ref[c] = vector[c : c + 1] * oxygen
    moved = wannier_reach * jnp.tanh(vector)
    moved = jnp.concatenate([moved, jnp.zeros((1, atoms), jnp.float32)], axis=0)
    for target in range(shift_ref.shape[0]):
        shift_ref[target] = moved
    handing_on.wait()


def mesh_kernel(
    table,
    shifts,
    phase,
    green_ref,
    fold_stack,
    unfold_stack,
    out_ref,
    grid,
    planes,
    packed,
    weights_z,
    slopes_z,
    waves,
    wave_slopes,
    *across_refs,
):
    wide_count, narrow_count, _, atoms = table.shape
    cells_x = GRID_X // wide_count
    cells_z = GRID_Z // narrow_count
    window = cells_z + HALO_Z
    reach = cells_x + HALO_X
    pair = 2 * atoms
    length = wide_count * pair
    copies = grid.shape[0]
    fine = grid.shape[1]
    channels = 2 * fine
    rows = phase.shape[0]
    half_x = GRID_X // 2
    half_z = GRID_Z // 2
    piece = lax.axis_index("wide") * narrow_count + lax.axis_index("narrow")
    lane_zero = lax.broadcasted_iota(jnp.int32, (1, half_x), 1) == 0
    row_zero = lax.broadcasted_iota(jnp.int32, (half_z, 1), 0) == 0

    def fold():
        return (fold_stack[0:GRID_X, :], fold_stack[GRID_X:, :])

    def unfold():
        return (unfold_stack[0:GRID_X, :], unfold_stack[GRID_X:, :])

    def sites(at_wide, at_narrow):
        atom = jnp.abs(table[at_wide, at_narrow])
        moved = shifts[at_wide, at_narrow]
        found = []
        for component, extent in enumerate((cells_x, GRID_Y, cells_z)):
            start = atom[component : component + 1] * float(extent)
            found.append(jnp.concatenate([start, start + moved[component : component + 1]], axis=1))
        oxygen = 1.0 - atom[3:4]
        found.append(jnp.concatenate([6.0 * oxygen + atom[3:4], -8.0 * oxygen], axis=1))
        return found

    def line(at_narrow):
        groups = [sites(at_wide, at_narrow) for at_wide in range(wide_count)]
        return [jnp.concatenate([g[k] for g in groups], axis=1) for k in range(4)]

    def splines_z(row):
        counter = lax.broadcasted_iota(jnp.int32, (window, 1), 0).astype(jnp.float32)
        return spline_pair(row - (counter - float(HALO_Z)))

    def fill_x(row, targets):
        counter = lax.broadcasted_iota(jnp.int32, (reach, 1), 0).astype(jnp.float32)
        both = spline_pair(row - (counter - float(HALO_X)))
        rest = jnp.zeros((128 - reach, length), jnp.bfloat16)
        for values, ref in zip(both, targets):
            high, low = split(values)
            ref[0:reach, :] = high
            ref[reach:128, :] = rest
            ref[128 : 128 + reach, :] = low
            ref[128 + reach : 256, :] = rest

    grid[:, :, 0:HALO_Z, :] = jnp.zeros((copies, fine, HALO_Z, 2 * GRID_X), jnp.float32)

    weights = across_refs[:LOOP_BODY]
    slopes = across_refs[LOOP_BODY:]

    def spread(index, odd):
        at_narrow = LOOP_BODY * index + odd
        row_x, row_y, row_z, charge = line(at_narrow)
        lower = jnp.floor(row_y)
        back = lax.broadcasted_iota(jnp.int32, (8, 1), 0)
        value_y, slope_y = spline_pair((row_y - lower) + back.astype(jnp.float32))
        cell = wrapped(lower.astype(jnp.int32) - back + GRID_Y, GRID_Y)
        wave_blocks = []
        slope_blocks = []
        for block in range(length // 128):
            lanes = slice(block * 128, (block + 1) * 128)
            wave = jnp.zeros((rows, 128), jnp.float32)
            wave_slope = jnp.zeros((rows, 128), jnp.float32)
            for k in range(4):
                spot = jnp.broadcast_to(cell[k : k + 1, lanes], (rows, 128))
                found = lookup(phase[...], spot)
                wave = wave + value_y[k : k + 1, lanes] * found
                wave_slope = wave_slope + slope_y[k : k + 1, lanes] * found
            wave_blocks.append(wave)
            slope_blocks.append(wave_slope)
        wave = jnp.concatenate(wave_blocks, axis=1)
        waves[at_narrow] = wave
        wave_slopes[at_narrow] = jnp.concatenate(slope_blocks, axis=1)
        fill_x(row_x, (weights[odd].at[index], slopes[odd].at[index]))
        value_z, slope_z = splines_z(row_z)
        weights_z[at_narrow] = value_z
        slopes_z[at_narrow] = slope_z
        charged = wave * charge
        first = pl.multiple_of(at_narrow * cells_z, HALO_Z)
        for at_wide in range(wide_count):
            lanes = slice(at_wide * pair, (at_wide + 1) * pair)
            near = value_z[:, lanes]
            left = jnp.concatenate(
                [near * charged[c : c + 1, lanes] for c in range(channels)], axis=0
            )
            high, low = split(left)
            across = weights[odd][index, :, lanes]
            total = lax.dot_general(high, across, NT, preferred_element_type=jnp.float32)
            rest = lax.dot_general(low, across[0:128], NT, preferred_element_type=jnp.float32)
            total = total[:, 0:128] + (total[:, 128:256] + rest)
            start = at_wide // copies * 128
            for c in range(channels):
                spot = slice(c % 2 * GRID_X + start, c % 2 * GRID_X + start + 128)
                k = at_wide % copies
                part = total[c * window : (c + 1) * window]
                grid[k, c // 2, pl.ds(first, HALO_Z), spot] += part[:HALO_Z]
                grid[k, c // 2, pl.ds(first + HALO_Z, cells_z), spot] = part[HALO_Z:]

    def in_groups(step):
        def body(index, carry):
            for odd in range(LOOP_BODY):
                step(index, odd)
            return carry

        lax.fori_loop(0, narrow_count // LOOP_BODY, body, 0)

    in_groups(spread)

    def gather(j, carry):
        for lanes in (slice(0, GRID_X), slice(GRID_X, 2 * GRID_X)):
            total = None
            for k in range(copies):
                moved = pltpu.roll(grid[k, j, :, lanes], (k * cells_x - HALO_X) % GRID_X, 1)
                total = moved if total is None else total + moved
            planes[j, :, lanes] = total[HALO_Z:]
            planes[j, GRID_Z - HALO_Z :, lanes] += total[:HALO_Z]
        return carry

    lax.fori_loop(0, fine, gather, 0)
    is_first = piece == 0

    def paired(real, imag, zero, axis):
        half = real.shape[axis] // 2
        first = (slice(None),) * axis + (slice(0, half),)
        second = (slice(None),) * axis + (slice(half, 2 * half),)
        real_c, real_s = real[first], real[second]
        if imag is None:
            none = jnp.zeros_like(real_s)
            real_all = [real_c, jnp.where(zero, real_s, real_c)]
            imag_all = [jnp.where(zero, none, -real_s), jnp.where(zero, none, real_s)]
        else:
            imag_c, imag_s = imag[first], imag[second]
            real_all = [
                real_c + jnp.where(zero, 0.0, imag_s),
                jnp.where(zero, real_s, real_c - imag_s),
            ]
            imag_all = [
                imag_c - jnp.where(zero, 0.0, real_s),
                jnp.where(zero, imag_s, imag_c + real_s),
            ]
        return jnp.concatenate(real_all, axis=axis), jnp.concatenate(imag_all, axis=axis)

    def merged(real, imag, zero, axis):
        half = real.shape[axis] // 2
        first = (slice(None),) * axis + (slice(0, half),)
        second = (slice(None),) * axis + (slice(half, 2 * half),)
        real_a, real_b = real[first], real[second]
        imag_a, imag_b = imag[first], imag[second]
        real = [
            real_a + jnp.where(zero, 0.0, real_b),
            jnp.where(zero, real_b, imag_b - imag_a),
        ]
        imag = [
            imag_a + jnp.where(zero, 0.0, imag_b),
            jnp.where(zero, imag_b, real_a - real_b),
        ]
        return jnp.concatenate(real, axis=axis), jnp.concatenate(imag, axis=axis)

    modes = {}
    parts = []

    def slot(j):
        first_imag = planes[0, :, GRID_X:]
        if j == fine:
            real, imag = jnp.where(is_first, first_imag, 0.0), None
        else:
            real, imag = planes[j, :, 0:GRID_X], planes[j, :, GRID_X:]
            if j == 0:
                imag = jnp.where(is_first, 0.0, imag)
        real = split(real)
        imag = None if imag is None else split(imag)
        yield
        real = by_right(real, fold())
        imag = None if imag is None else by_right(imag, fold())
        yield
        real, imag = paired(real, imag, lane_zero, 1)
        real, imag = split(real), split(imag)
        yield
        real, imag = by_left(unfold_stack[...], real), by_left(unfold_stack[...], imag)
        yield
        real, imag = paired(real, imag, row_zero, 0)
        green = green_ref[j]
        mode = GRID_Y // 2 if j == fine else piece * fine + j
        share = jnp.where((mode == 0) | (mode == GRID_Y // 2), 0.5, 1.0)
        parts.append(share * jnp.sum(green * (real * real + imag * imag), axis=0, keepdims=True))
        real, imag = green * real, green * imag
        if j == fine:
            modes[j] = (real, imag)
            return
        if j == 0:
            real, imag = real - modes[fine][1], imag + modes[fine][0]
        real, imag = merged(real, imag, row_zero, 0)
        real, imag = split(real), split(imag)
        yield
        real, imag = by_left(fold_stack[...], real), by_left(fold_stack[...], imag)
        yield
        real, imag = merged(real, imag, lane_zero, 1)
        scale = jnp.where(piece * fine + j == 0, 1.0, 2.0)
        real, imag = split(real * scale), split(imag * scale)
        yield
        real, imag = by_right(real, unfold()), by_right(imag, unfold())
        yield
        for k, part in enumerate((real, imag)):
            turned = [
                pltpu.roll(part, (HALO_X - at_wide * cells_x) % GRID_X, 1)
                for at_wide in range(copies)
            ]
            for at_wide in range(wide_count):
                start = at_wide // copies * 128
                moved = turned[at_wide % copies][:, start : start + 128]
                high = moved.astype(jnp.bfloat16).astype(jnp.float32)
                again = pltpu.roll(high, reach % 128, 1)
                low = pltpu.roll(moved - high, 2 * reach % 128, 1)
                sides = []
                for side in range(2):
                    lane = lax.broadcasted_iota(jnp.int32, (1, 128), 1) + side * 128
                    value = jnp.where(lane < 2 * reach, again, low)
                    if side == 0:
                        value = jnp.where(lane < reach, high, value)
                    sides.append(value.astype(jnp.bfloat16))
                block = jnp.concatenate(sides, axis=1)
                packed[at_wide, 2 * j + k, HALO_BITS:, :] = block
                packed[at_wide, 2 * j + k, 0:HALO_BITS, :] = block[GRID_Z - HALO_BITS :]

    waiting = [slot(j) for j in [fine, *range(fine)]]
    running = []
    while waiting or running:
        if waiting:
            running.append(waiting.pop(0))
        running = [one for one in running if next(one, running) is not running]
    energy = sum(parts[1:], parts[0])
    energy = jnp.broadcast_to(jnp.sum(energy, axis=1, keepdims=True), (1, 128))

    def collect(index, odd):
        at_narrow = LOOP_BODY * index + odd
        value_z = weights_z[at_narrow]
        slope_z = slopes_z[at_narrow]
        first = pl.multiple_of(at_narrow * cells_z, HALO_BITS)
        wave = waves[at_narrow]
        wave_slope = wave_slopes[at_narrow]
        for at_wide in range(wide_count):
            lanes = slice(at_wide * pair, (at_wide + 1) * pair)
            tall = cells_z + HALO_BITS
            left = jnp.concatenate(
                [packed[at_wide, c, pl.ds(first, tall), :] for c in range(channels)], axis=0
            )

            def across(right):
                high = right[0:reach]
                rest = jnp.zeros((256 - 3 * reach, pair), jnp.bfloat16)
                right = jnp.concatenate([high, right[128 : 128 + reach], high, rest], axis=0)
                return lax.dot_general(left, right, NN, preferred_element_type=jnp.float32)

            value = across(weights[odd][index, :, lanes])
            slope = across(slopes[odd][index, :, lanes])
            plain = jnp.zeros((window, pair), jnp.float32)
            along_x = plain
            along_y = plain
            for c in range(channels):
                block = slice((c + 1) * tall - window, (c + 1) * tall)
                plain = plain + value[block] * wave[c : c + 1, lanes]
                along_x = along_x + slope[block] * wave[c : c + 1, lanes]
                along_y = along_y + value[block] * wave_slope[c : c + 1, lanes]
            near = value_z[:, lanes]
            near_slope = slope_z[:, lanes]
            results = [
                jnp.sum(near * plain, axis=0, keepdims=True),
                -jnp.sum(near * along_x, axis=0, keepdims=True),
                -jnp.sum(near * along_y, axis=0, keepdims=True),
                -jnp.sum(near_slope * plain, axis=0, keepdims=True),
            ]
            for k, row in enumerate(results):
                out_ref[at_wide, at_narrow, :, k * pair : (k + 1) * pair] = row
            out_ref[at_wide, at_narrow, :, 4 * pair :] = energy

    in_groups(collect)


def finish_kernel(arrived, species, atom_ref, centroid_ref, energy_ref):
    atoms = species.shape[1]
    total = arrived[0]
    for k in range(1, arrived.shape[0]):
        total = total + arrived[k]
    oxygen = 1.0 - species[...].astype(jnp.float32)
    for k in range(4):
        atom_ref[k] = total[:, 2 * k * atoms : (2 * k + 1) * atoms]
        centroid_ref[k] = total[:, (2 * k + 1) * atoms : (2 * k + 2) * atoms] * oxygen
    energy_ref[...] = total[:, 8 * atoms :] * (1.0 / (atoms * arrived.shape[0]))


def mode_factors(length, order):
    wrapped = np.where(2 * order >= length, order - length, order)
    square = (wrapped / length) ** 2
    ratio = (4.0 + 2.0 * np.cos(2.0 * math.pi * order / length)) / 6.0
    return np.stack([np.exp(-(math.pi**2) * square / ewald_beta**2) / ratio**2, square])


def folded_order(length):
    half = length // 2
    counter = np.arange(half)
    return np.concatenate([counter, np.where(counter == 0, half, length - counter)])


def fold_table(length):
    half = length // 2
    turns = np.outer(np.arange(length), np.arange(half)) % length * (2.0 * math.pi / length)
    sines = np.sin(turns)
    sines[:, 0] = 1.0 - 2.0 * (np.arange(length) % 2)
    return np.concatenate([np.cos(turns), sines], axis=1)


def halves(table):
    high = table.astype(jnp.bfloat16)
    low = (table - high.astype(np.float64)).astype(jnp.bfloat16)
    return high, low


def vmem(count):
    return [pl.BlockSpec(memory_space=pltpu.VMEM)] * count


def hbm(count):
    return [pl.BlockSpec(memory_space=pltpu.HBM)] * count


def shaped(shape, dtype=jnp.float32):
    return jax.ShapeDtypeStruct(shape, dtype)


def limits(mebibytes):
    return pltpu.CompilerParams(vmem_limit_bytes=mebibytes * 1024 * 1024)


def local(
    positions,
    species,
    neighbours,
    embed_one_w,
    embed_one_b,
    embed_two_w,
    embed_two_b,
    embed_three_w,
    embed_three_b,
    fit_one_w,
    fit_one_b,
    fit_two_w,
    fit_two_b,
    fit_three_w,
    fit_three_b,
    fit_out_w,
):
    axes = ("wide", "narrow")
    wide_count = lax.axis_size("wide")
    narrow_count = lax.axis_size("narrow")
    pieces = wide_count * narrow_count
    atoms = positions.shape[4]
    listed = neighbours.shape[4]
    fine = GRID_Y // 2 // pieces
    width_three = embed_three_w.shape[1]
    entries, hidden = fit_one_w.shape
    kinds = species.reshape(1, atoms)

    packed = pl.pallas_call(
        pack_kernel,
        out_shape=shaped((pieces, 4, atoms)),
        in_specs=vmem(2),
        out_specs=vmem(1)[0],
        name="pack",
    )(positions.reshape(3, 1, atoms), kinds)
    table = lax.all_to_all(packed, axes, 0, 0, tiled=True)
    table = table.reshape(wide_count, narrow_count, 4, atoms)

    tall_two = -(-(width_three // 2 + 1) // 8) * 8
    tall_three = -(-width_three // 8) * 8
    bf16 = jnp.bfloat16
    wave_rows = -(-2 * fine // 8) * 8
    angle = np.arange(GRID_Y) * (2.0 * math.pi / GRID_Y)
    constants = np.concatenate(
        [
            np.stack([np.cos(angle), np.sin(angle)]),
            mode_factors(GRID_Y, np.arange(GRID_Y)),
            mode_factors(GRID_X, folded_order(GRID_X)),
            mode_factors(GRID_Z, folded_order(GRID_Z)),
        ]
    )
    constants[2] *= coulomb / (math.pi * GRID_X * GRID_Y * GRID_Z)
    arguments = (
        neighbours.reshape(atoms, listed),
        embed_one_w,
        embed_one_b,
        embed_two_w,
        embed_two_b[None],
        embed_three_w,
        embed_three_b[None],
        fit_one_w.T,
        fit_one_b[None],
        fit_two_w,
        fit_two_b[None],
        fit_three_w,
        fit_three_b[None],
        jnp.asarray(constants, jnp.float32),
    )
    held = [arguments[k] for k in (0, 1, 2, 3, 4, 5, 6, 8, 10, 12, 13, 9, 11, 7)]
    prepared = pl.pallas_call(
        prepare_kernel,
        out_shape=(
            shaped((listed, atoms), jnp.int32),
            shaped((256, 16)),
            shaped((2 * tall_two, 3 * ROW_PAD), bf16),
            shaped((2 * tall_three, 6 * ROW_PAD), bf16),
            shaped((hidden, entries), bf16),
            shaped((hidden, entries), bf16),
        )
        + (shaped((hidden, hidden), bf16),) * 4
        + (shaped((wave_rows, GRID_Y)), shaped((fine + 1, GRID_Z, GRID_X))),
        in_specs=hbm(len(arguments)),
        out_specs=tuple(vmem(12)),
        scratch_shapes=[
            pltpu.VMEM((16, 256), jnp.float32),
            pltpu.VMEM((256, 256), jnp.float32),
            pltpu.SemaphoreType.DMA((len(held),)),
        ]
        + [pltpu.VMEM(array.shape, array.dtype) for array in held],
        compiler_params=limits(62),
        cost_estimate=pl.CostEstimate(
            flops=1000000, bytes_accessed=8 * entries * hidden, transcendentals=0
        ),
        name="prepare",
    )(*arguments)
    phase, green = prepared[10:]
    fitted = (table, *prepared[:10], fit_out_w.T)
    dipole, shifts, table = pl.pallas_call(
        centroid_kernel,
        out_shape=(shaped((3, 1, atoms)), shaped((pieces, 4, atoms)), shaped(table.shape)),
        in_specs=hbm(12),
        out_specs=tuple(vmem(2) + hbm(1)),
        scratch_shapes=[
            pltpu.VMEM((4, tall_three, atoms), jnp.float32),
            pltpu.VMEM((width_three * AXIS_COLUMNS, atoms), jnp.float32),
            pltpu.SemaphoreType.DMA((len(fitted) + 1,)),
        ]
        + [pltpu.VMEM(array.shape, array.dtype) for array in fitted],
        compiler_params=limits(62),
        name="centroids",
    )(*fitted)
    shifts = lax.all_to_all(shifts, axes, 0, 0, tiled=True)
    shifts = shifts.reshape(wide_count, narrow_count, 4, atoms)

    cells_x = GRID_X // wide_count
    copies = 128 // cells_x
    length = wide_count * 2 * atoms
    out_width = 8 * atoms + 128
    partial = pl.pallas_call(
        mesh_kernel,
        out_shape=shaped((wide_count, narrow_count, 1, out_width)),
        in_specs=vmem(6),
        out_specs=vmem(1)[0],
        scratch_shapes=[
            pltpu.VMEM((copies, fine, HALO_Z + GRID_Z, 2 * GRID_X), jnp.float32),
            pltpu.VMEM((fine, GRID_Z, 2 * GRID_X), jnp.float32),
            pltpu.VMEM((wide_count, 2 * fine, HALO_BITS + GRID_Z, 256), bf16),
        ]
        + [pltpu.VMEM((narrow_count, GRID_Z // narrow_count + HALO_Z, length), jnp.float32)] * 2
        + [pltpu.VMEM((narrow_count, wave_rows, length), jnp.float32)] * 2
        + [pltpu.VMEM((narrow_count // LOOP_BODY, 256, length), bf16)] * (2 * LOOP_BODY),
        compiler_params=limits(48),
        name="mesh",
    )(
        table,
        shifts,
        phase,
        green,
        jnp.asarray(np.concatenate(halves(fold_table(GRID_X)))),
        jnp.asarray(np.concatenate(halves(fold_table(GRID_X).T))),
    )
    arrived = lax.all_to_all(partial.reshape(pieces, 1, out_width), axes, 0, 0, tiled=True)
    atom_field, centroid_field, energy = pl.pallas_call(
        finish_kernel,
        out_shape=(shaped((4, 1, atoms)), shaped((4, 1, atoms)), shaped((1, 128))),
        in_specs=vmem(2),
        out_specs=tuple(vmem(3)),
        name="finish",
    )(arrived, kinds)
    atom_field = atom_field.reshape(4, 1, 1, 1, atoms)
    centroid_field = centroid_field.reshape(4, 1, 1, 1, atoms)
    return (dipole.reshape(3, 1, 1, 1, atoms), atom_field, centroid_field, energy[0, 0])


def solution(mesh):
    column = P(None, "wide", "narrow", None, None)
    in_specs = (column, P("wide", "narrow", None, None), P("wide", "narrow", None, None, None))
    in_specs = in_specs + (P(),) * 13
    out_specs = (column, column, column, P())
    return jax.shard_map(local, mesh=mesh, in_specs=in_specs, out_specs=out_specs, check_vma=False)
```

```python
import math

import jax
import jax.numpy as jnp
import numpy as np
from jax import lax
from jax.experimental import pallas as pl
from jax.experimental.pallas import tpu as pltpu
from jax.sharding import PartitionSpec as P

GRID_X = 256
GRID_Y = 256
GRID_Z = 256
AXIS_COLUMNS = 16

radius_scale = 24.0
wannier_reach = 0.5
ewald_beta = 0.9
coulomb = 0.25

ROW_PAD = 32
LOOP_BODY = 8
SLOT_CHUNK = 16
HALO_X = 16
HALO_Z = 8
HALO_BITS = 16

NN = (((1,), (0,)), ((), ()))
NT = (((1,), (1,)), ((), ()))


def split(value):
    high = value.astype(jnp.bfloat16)
    low = (value - high.astype(jnp.float32)).astype(jnp.bfloat16)
    return high, low


def multiply(left, right, dims=NN):
    def one(a, b):
        return lax.dot_general(a, b, dims, preferred_element_type=jnp.float32)

    return one(left[0], right[0]) + (one(left[1], right[0]) + one(left[0], right[1]))


def by_right(left, right):
    rows = left[0].shape[0]
    both = lax.dot_general(
        jnp.concatenate(left, axis=0), right[0], NN, preferred_element_type=jnp.float32
    )
    rest = lax.dot_general(left[0], right[1], NN, preferred_element_type=jnp.float32)
    return both[:rows] + (both[rows:] + rest)


def by_left(left, right):
    rows = left.shape[0] // 2
    both = lax.dot_general(left, right[0], NN, preferred_element_type=jnp.float32)
    rest = lax.dot_general(left[:rows], right[1], NN, preferred_element_type=jnp.float32)
    return both[:rows] + (both[rows:] + rest)


def spline_pair(offset):
    centred = offset - 2.0
    away = jnp.abs(centred)
    outer = jnp.maximum(2.0 - away, 0.0)
    inner = jnp.maximum(1.0 - away, 0.0)
    outer_square = outer * outer
    inner_square = inner * inner
    value = (outer_square * outer - 4.0 * (inner_square * inner)) * (1.0 / 6.0)
    slope = jnp.where(centred < 0.0, 0.5, -0.5) * (outer_square - 4.0 * inner_square)
    return value, slope


def wrapped(value, length):
    if length & (length - 1) == 0:
        return jnp.bitwise_and(value, length - 1)
    return lax.rem(value, length)


def lookup(row_table, spot):
    found = None
    lane = jnp.bitwise_and(spot, 127)
    block = lax.shift_right_logical(spot, 7)
    for part in range(row_table.shape[1] // 128):
        inside = block == part
        here = jnp.take_along_axis(
            jnp.broadcast_to(row_table[:, part * 128 : (part + 1) * 128], spot.shape),
            lane,
            axis=1,
            mode="promise_in_bounds",
        )
        found = here if found is None else jnp.where(inside, here, found)
    return found


def pack_kernel(positions, species, out_ref):
    kinds = species[...]
    rows = [positions[component] for component in range(3)]
    rows[0] = jnp.where(kinds > 0, -rows[0], rows[0])
    rows.append(kinds.astype(jnp.float32))
    rows = jnp.concatenate(rows, axis=0)
    for target in range(out_ref.shape[0]):
        out_ref[target] = rows


def prepare_kernel(
    neighbours,
    embed_one_w,
    embed_one_b,
    embed_two_w,
    embed_two_b,
    embed_three_w,
    embed_three_b,
    fit_one_w,
    fit_one_b,
    fit_two_w,
    fit_two_b,
    fit_three_w,
    fit_three_b,
    constants,
    codes_ref,
    columns_ref,
    second_ref,
    third_ref,
    one_high_ref,
    one_low_ref,
    two_high_ref,
    two_low_ref,
    three_high_ref,
    three_low_ref,
    phase_ref,
    green_ref,
    rows,
    square,
    arrivals,
    *held,
):
    sources = (
        neighbours,
        embed_one_w,
        embed_one_b,
        embed_two_w,
        embed_two_b,
        embed_three_w,
        embed_three_b,
        fit_one_b,
        fit_two_b,
        fit_three_b,
        constants,
        fit_two_w,
        fit_three_w,
        fit_one_w,
    )
    copies = [
        pltpu.make_async_copy(source, target, arrivals.at[k])
        for k, (source, target) in enumerate(zip(sources, held))
    ]
    for copy in copies:
        copy.start()
    (
        neighbours,
        embed_one_w,
        embed_one_b,
        embed_two_w,
        embed_two_b,
        embed_three_w,
        embed_three_b,
        fit_one_b,
        fit_two_b,
        fit_three_b,
        constants,
        fit_two_w,
        fit_three_w,
        fit_one_w,
    ) = held
    for copy in copies[:11]:
        copy.wait()
    pieces = lax.axis_size("wide") * lax.axis_size("narrow")
    piece = lax.axis_index("wide") * lax.axis_size("narrow") + lax.axis_index("narrow")
    width_one = embed_one_w.shape[1]
    hidden = fit_two_w.shape[0]
    codes_ref[...] = jnp.transpose(neighbours[...].astype(jnp.float32)).astype(jnp.int32)
    rows[...] = jnp.zeros_like(rows)
    for kind in range(2):
        rows[kind : kind + 1, 0:width_one] = embed_one_w[kind : kind + 1, :]
        rows[2 + kind : 3 + kind, 0:width_one] = embed_one_b[kind : kind + 1, :]
        rows[2 + kind : 3 + kind, width_one : width_one + 1] = jnp.full((1, 1), 40.0, jnp.float32)
    for row, source in ((4, fit_one_b), (5, fit_two_b), (6, fit_three_b)):
        rows[row : row + 1, 0:hidden] = source[...]
    columns_ref[...] = jnp.transpose(rows[...])

    row = lax.broadcasted_iota(jnp.int32, square.shape, 0)
    lane = lax.broadcasted_iota(jnp.int32, square.shape, 1)
    for width, weight, bias, target in (
        (width_one, embed_two_w, embed_two_b, second_ref),
        (2 * width_one, embed_three_w, embed_three_b, third_ref),
    ):
        tall, deep = target.shape[0] // 2, target.shape[1] // 3
        again = (lane - tall == row) | (lane - tall == row + width)
        again = (again & (row < width)) | ((lane - tall == 2 * width) & (row == width))
        square[...] = jnp.where(again, 1.0, 0.0)
        square[0:width, 0 : 2 * width] = weight[...]
        square[width : width + 1, 0 : 2 * width] = bias[...]
        high, low = split(jnp.transpose(square[...])[0 : 2 * tall, 0:deep])
        target[...] = jnp.concatenate([high, high, low], axis=1)
    square[...] = jnp.zeros_like(square)
    for copy in copies[11:13]:
        copy.wait()
    for source, high_ref, low_ref in (
        (fit_two_w, two_high_ref, two_low_ref),
        (fit_three_w, three_high_ref, three_low_ref),
    ):
        square[0:hidden, 0:hidden] = source[...]
        high_ref[...], low_ref[...] = split(jnp.transpose(square[...])[0:hidden, 0:hidden])

    fine = GRID_Y // 2 // pieces
    shape = (phase_ref.shape[0], 128)
    row = lax.broadcasted_iota(jnp.int32, shape, 0)
    mode = piece * fine + row // 2
    for part in range(GRID_Y // 128):
        cell = lax.broadcasted_iota(jnp.int32, shape, 1) + part * 128
        spot = wrapped(mode * cell, GRID_Y)
        cosine = lookup(constants[0:1, :], spot)
        sine = lookup(constants[1:2, :], spot)
        alternate = (1 - 2 * lax.rem(cell, 2)).astype(jnp.float32)
        odd = jnp.where(mode == 0, alternate, -sine)
        value = jnp.where(lax.rem(row, 2) == 0, cosine, odd)
        phase_ref[:, part * 128 : (part + 1) * 128] = jnp.where(row < 2 * fine, value, 0.0)

    column = jnp.transpose(constants[...])
    lane = lax.broadcasted_iota(jnp.int32, (1, GRID_Y), 1)
    for j in range(fine + 1):
        here = lane == (GRID_Y // 2 if j == fine else piece * fine + j)
        factor = jnp.sum(jnp.where(here, constants[2:3, :], 0.0), axis=1, keepdims=True)
        part = jnp.sum(jnp.where(here, constants[3:4, :], 0.0), axis=1, keepdims=True)
        wave = (part + constants[5:6, :]) + column[:, 7:8]
        top = (factor * constants[4:5, :]) * column[:, 6:7]
        green_ref[j] = jnp.where(wave == 0.0, 0.0, top / jnp.where(wave == 0.0, 1.0, wave))

    copies[13].wait()
    one_high_ref[...], one_low_ref[...] = split(fit_one_w[...])


def centroid_kernel(
    table,
    codes,
    columns,
    second,
    third,
    one_high,
    one_low,
    two_high,
    two_low,
    three_high,
    three_low,
    fit_out_w,
    dipole_ref,
    shift_ref,
    table_ref,
    matrix,
    descriptor,
    arrivals,
    *held,
):
    sources = (table, codes, columns, second, third)
    sources += (one_high, one_low, two_high, two_low, three_high, three_low, fit_out_w)
    copies = [
        pltpu.make_async_copy(source, target, arrivals.at[k])
        for k, (source, target) in enumerate(zip(sources, held))
    ]
    for copy in copies:
        copy.start()
    table, codes, columns, second, third = held[:5]
    one_high, one_low, two_high, two_low, three_high, three_low, fit_out_w = held[5:]
    for copy in copies[:5]:
        copy.wait()
    handing_on = pltpu.make_async_copy(table, table_ref, arrivals.at[len(copies)])
    handing_on.start()
    wide_count, narrow_count, _, atoms = table.shape
    listed = codes.shape[0]
    width_three = fit_out_w.shape[0]
    width_one = width_three // 4
    hidden_width = two_high.shape[0]
    cells = (GRID_X // wide_count, GRID_Y, GRID_Z // narrow_count)
    at_wide = lax.axis_index("wide")
    at_narrow = lax.axis_index("narrow")
    own = jnp.abs(table[at_wide, at_narrow])
    nearby = []
    for step in range(9):
        wide_at = lax.rem(at_wide + (step // 3 - 1) + wide_count, wide_count)
        narrow_at = lax.rem(at_narrow + (step % 3 - 1) + narrow_count, narrow_count)
        nearby.append(table[wide_at, narrow_at])

    second_all = second[...]
    third_all = third[...]
    weight_oxygen = jnp.broadcast_to(columns[0:ROW_PAD, 0:1], (ROW_PAD, atoms))
    weight_hydrogen = jnp.broadcast_to(columns[0:ROW_PAD, 1:2], (ROW_PAD, atoms))
    bias_oxygen = jnp.broadcast_to(columns[0:ROW_PAD, 2:3], (ROW_PAD, atoms))
    bias_hydrogen = jnp.broadcast_to(columns[0:ROW_PAD, 3:4], (ROW_PAD, atoms))
    matrix[...] = jnp.zeros_like(matrix)

    def chunk(first):
        code = codes[pl.ds(first, SLOT_CHUNK), :]
        slot = wrapped(code, atoms)
        if atoms & (atoms - 1) == 0:
            offset = lax.shift_right_logical(code, atoms.bit_length() - 1)
        else:
            offset = code // atoms
        step_x = jnp.where(offset >= 9, 1, 0) + jnp.where(offset >= 18, 1, 0)
        rest = offset - 9 * step_x
        step_z = jnp.where(rest >= 3, 1, 0) + jnp.where(rest >= 6, 1, 0)
        step_y = rest - 3 * step_z
        brick = step_x * 3 + step_z
        found = []
        for component in range(3):
            picked = jnp.zeros((SLOT_CHUNK, atoms), jnp.float32)
            for step in range(9):
                row = jnp.broadcast_to(
                    nearby[step][component : component + 1], (SLOT_CHUNK, atoms)
                )
                here = jnp.take_along_axis(row, slot, axis=1, mode="promise_in_bounds")
                picked = jnp.where(brick == step, here, picked)
            found.append(picked)
        hydrogen = found[0] < 0.0
        found[0] = jnp.abs(found[0])
        scaled = []
        for component, step in enumerate((step_x, step_y, step_z)):
            extent = float(cells[component])
            relative = (step - 1).astype(jnp.float32) * extent + (
                found[component] - own[component : component + 1]
            ) * extent
            scaled.append(relative * (1.0 / radius_scale))
        smooth = 1.0 / (
            1.0 + (scaled[0] * scaled[0] + scaled[1] * scaled[1] + scaled[2] * scaled[2])
        )
        radial = [smooth] + [smooth * part for part in scaled]
        first_layers = []
        for k in range(SLOT_CHUNK):
            row = smooth[k : k + 1]
            kind = hydrogen[k : k + 1]
            weight = jnp.where(kind, weight_hydrogen, weight_oxygen)
            bias = jnp.where(kind, bias_hydrogen, bias_oxygen)
            first_layers.append(jnp.tanh(weight * row + bias))
        layer_one = jnp.concatenate(first_layers, axis=1)
        high, low = split(layer_one)
        both = lax.dot_general(
            second_all,
            jnp.concatenate([high, low, high], axis=0),
            NN,
            preferred_element_type=jnp.float32,
        )
        tall = both.shape[0] // 2
        layer_two = jnp.tanh(both[:tall]) + both[tall:]
        deep = third_all.shape[1] // 3
        rest = jnp.zeros((deep - tall, layer_two.shape[1]), jnp.float32)
        high, low = split(jnp.concatenate([layer_two, rest], axis=0))
        both = lax.dot_general(
            third_all,
            jnp.concatenate([high, low, high], axis=0),
            NN,
            preferred_element_type=jnp.float32,
        )
        tall = both.shape[0] // 2
        layer_three = jnp.tanh(both[:tall]) + both[tall:]
        for part in range(4):
            total = matrix[part]
            for k in range(SLOT_CHUNK):
                total = total + layer_three[:, k * atoms : (k + 1) * atoms] * radial[part][k : k + 1]
            matrix[part] = total

    def chunks(index, carry):
        for step in range(LOOP_BODY):
            chunk(pl.multiple_of((index * LOOP_BODY + step) * SLOT_CHUNK, SLOT_CHUNK))
        return carry

    lax.fori_loop(0, listed // (LOOP_BODY * SLOT_CHUNK), chunks, 0)

    parts = []
    for part in range(4):
        parts.append(matrix[part, 0:width_three, :] * (1.0 / listed))
    leading = [part[0:AXIS_COLUMNS] for part in parts]
    for row in range(width_three):
        total = parts[0][row : row + 1] * leading[0]
        for part in range(1, 4):
            total = total + parts[part][row : row + 1] * leading[part]
        descriptor[row * AXIS_COLUMNS : (row + 1) * AXIS_COLUMNS, :] = total
    for copy in copies[5:]:
        copy.wait()

    def layer(high_ref, low_ref, given, column):
        weights = (high_ref[...], low_ref[...])
        return jnp.tanh(multiply(weights, split(given)) + columns[0:hidden_width, column : column + 1])

    hidden = layer(one_high, one_low, descriptor[...], 4)
    hidden = hidden + layer(two_high, two_low, hidden, 5)
    hidden = hidden + layer(three_high, three_low, hidden, 6)
    coeffs = multiply(split(fit_out_w[...]), split(hidden))
    vector = jnp.concatenate(
        [jnp.sum(coeffs * parts[1 + c], axis=0, keepdims=True) for c in range(3)], axis=0
    )
    oxygen = 1.0 - own[3:4]
    for c in range(3):
        dipole_ref[c] = vector[c : c + 1] * oxygen
    moved = wannier_reach * jnp.tanh(vector)
    moved = jnp.concatenate([moved, jnp.zeros((1, atoms), jnp.float32)], axis=0)
    for target in range(shift_ref.shape[0]):
        shift_ref[target] = moved
    handing_on.wait()


def mesh_kernel(
    cells,
    shifts,
    phase,
    green_ref,
    fold_stack,
    unfold_stack,
    out_ref,
    grid,
    planes,
    packed,
    weights_z,
    slopes_z,
    waves,
    wave_slopes,
    *across_refs,
):
    wide_count, narrow_count, _, atoms = cells.shape
    cells_x = GRID_X // wide_count
    cells_z = GRID_Z // narrow_count
    window = cells_z + HALO_Z
    reach = cells_x + HALO_X
    pair = 2 * atoms
    length = wide_count * pair
    copies = grid.shape[0]
    fine = grid.shape[1]
    channels = 2 * fine
    rows = phase.shape[0]
    half_x = GRID_X // 2
    half_z = GRID_Z // 2
    piece = lax.axis_index("wide") * narrow_count + lax.axis_index("narrow")
    lane_zero = lax.broadcasted_iota(jnp.int32, (1, half_x), 1) == 0
    row_zero = lax.broadcasted_iota(jnp.int32, (half_z, 1), 0) == 0

    def fold():
        return (fold_stack[0:GRID_X, :], fold_stack[GRID_X:, :])

    def unfold():
        return (unfold_stack[0:GRID_X, :], unfold_stack[GRID_X:, :])

    def sites(at_wide, at_narrow):
        atom = cells[at_wide, at_narrow]
        moved = shifts[at_wide, at_narrow]
        found = []
        for component in range(3):
            start = atom[component : component + 1]
            found.append(jnp.concatenate([start, start + moved[component : component + 1]], axis=1))
        oxygen = 1.0 - atom[3:4]
        found.append(jnp.concatenate([6.0 * oxygen + atom[3:4], -8.0 * oxygen], axis=1))
        return found

    def line(at_narrow):
        groups = [sites(at_wide, at_narrow) for at_wide in range(wide_count)]
        return [jnp.concatenate([g[k] for g in groups], axis=1) for k in range(4)]

    def splines_z(row):
        counter = lax.broadcasted_iota(jnp.int32, (window, 1), 0).astype(jnp.float32)
        return spline_pair(row - (counter - float(HALO_Z)))

    def fill_x(row, targets):
        counter = lax.broadcasted_iota(jnp.int32, (reach, 1), 0).astype(jnp.float32)
        both = spline_pair(row - (counter - float(HALO_X)))
        rest = jnp.zeros((128 - reach, length), jnp.bfloat16)
        for values, ref in zip(both, targets):
            high, low = split(values)
            ref[0:reach, :] = high
            ref[reach:128, :] = rest
            ref[128 : 128 + reach, :] = low
            ref[128 + reach : 256, :] = rest

    grid[:, :, 0:HALO_Z, :] = jnp.zeros((copies, fine, HALO_Z, 2 * GRID_X), jnp.float32)

    weights = across_refs[:LOOP_BODY]
    slopes = across_refs[LOOP_BODY:]

    def spread(index, odd):
        at_narrow = LOOP_BODY * index + odd
        row_x, row_y, row_z, charge = line(at_narrow)
        lower = jnp.floor(row_y)
        back = lax.broadcasted_iota(jnp.int32, (8, 1), 0)
        value_y, slope_y = spline_pair((row_y - lower) + back.astype(jnp.float32))
        cell = wrapped(lower.astype(jnp.int32) - back + GRID_Y, GRID_Y)
        wave_blocks = []
        slope_blocks = []
        for block in range(length // 128):
            lanes = slice(block * 128, (block + 1) * 128)
            wave = jnp.zeros((rows, 128), jnp.float32)
            wave_slope = jnp.zeros((rows, 128), jnp.float32)
            for k in range(4):
                spot = jnp.broadcast_to(cell[k : k + 1, lanes], (rows, 128))
                found = lookup(phase[...], spot)
                wave = wave + value_y[k : k + 1, lanes] * found
                wave_slope = wave_slope + slope_y[k : k + 1, lanes] * found
            wave_blocks.append(wave)
            slope_blocks.append(wave_slope)
        wave = jnp.concatenate(wave_blocks, axis=1)
        waves[at_narrow] = wave
        wave_slopes[at_narrow] = jnp.concatenate(slope_blocks, axis=1)
        fill_x(row_x, (weights[odd].at[index], slopes[odd].at[index]))
        value_z, slope_z = splines_z(row_z)
        weights_z[at_narrow] = value_z
        slopes_z[at_narrow] = slope_z
        charged = wave * charge
        first = pl.multiple_of(at_narrow * cells_z, HALO_Z)
        for at_wide in range(wide_count):
            lanes = slice(at_wide * pair, (at_wide + 1) * pair)
            near = value_z[:, lanes]
            left = jnp.concatenate(
                [near * charged[c : c + 1, lanes] for c in range(channels)], axis=0
            )
            high, low = split(left)
            across = weights[odd][index, :, lanes]
            total = lax.dot_general(high, across, NT, preferred_element_type=jnp.float32)
            rest = lax.dot_general(low, across[0:128], NT, preferred_element_type=jnp.float32)
            total = total[:, 0:128] + (total[:, 128:256] + rest)
            start = at_wide // copies * 128
            for c in range(channels):
                spot = slice(c % 2 * GRID_X + start, c % 2 * GRID_X + start + 128)
                k = at_wide % copies
                part = total[c * window : (c + 1) * window]
                grid[k, c // 2, pl.ds(first, HALO_Z), spot] += part[:HALO_Z]
                grid[k, c // 2, pl.ds(first + HALO_Z, cells_z), spot] = part[HALO_Z:]

    def in_groups(step):
        def body(index, carry):
            for odd in range(LOOP_BODY):
                step(index, odd)
            return carry

        lax.fori_loop(0, narrow_count // LOOP_BODY, body, 0)

    in_groups(spread)

    def gather(j, carry):
        for lanes in (slice(0, GRID_X), slice(GRID_X, 2 * GRID_X)):
            total = None
            for k in range(copies):
                moved = pltpu.roll(grid[k, j, :, lanes], (k * cells_x - HALO_X) % GRID_X, 1)
                total = moved if total is None else total + moved
            planes[j, :, lanes] = total[HALO_Z:]
            planes[j, GRID_Z - HALO_Z :, lanes] += total[:HALO_Z]
        return carry

    lax.fori_loop(0, fine, gather, 0)
    is_first = piece == 0

    def paired(real, imag, zero, axis):
        half = real.shape[axis] // 2
        first = (slice(None),) * axis + (slice(0, half),)
        second = (slice(None),) * axis + (slice(half, 2 * half),)
        real_c, real_s = real[first], real[second]
        if imag is None:
            none = jnp.zeros_like(real_s)
            real_all = [real_c, jnp.where(zero, real_s, real_c)]
            imag_all = [jnp.where(zero, none, -real_s), jnp.where(zero, none, real_s)]
        else:
            imag_c, imag_s = imag[first], imag[second]
            real_all = [
                real_c + jnp.where(zero, 0.0, imag_s),
                jnp.where(zero, real_s, real_c - imag_s),
            ]
            imag_all = [
                imag_c - jnp.where(zero, 0.0, real_s),
                jnp.where(zero, imag_s, imag_c + real_s),
            ]
        return jnp.concatenate(real_all, axis=axis), jnp.concatenate(imag_all, axis=axis)

    def merged(real, imag, zero, axis):
        half = real.shape[axis] // 2
        first = (slice(None),) * axis + (slice(0, half),)
        second = (slice(None),) * axis + (slice(half, 2 * half),)
        real_a, real_b = real[first], real[second]
        imag_a, imag_b = imag[first], imag[second]
        real = [
            real_a + jnp.where(zero, 0.0, real_b),
            jnp.where(zero, real_b, imag_b - imag_a),
        ]
        imag = [
            imag_a + jnp.where(zero, 0.0, imag_b),
            jnp.where(zero, imag_b, real_a - real_b),
        ]
        return jnp.concatenate(real, axis=axis), jnp.concatenate(imag, axis=axis)

    modes = {}
    parts = []

    def slot(j):
        first_imag = planes[0, :, GRID_X:]
        if j == fine:
            real, imag = jnp.where(is_first, first_imag, 0.0), None
        else:
            real, imag = planes[j, :, 0:GRID_X], planes[j, :, GRID_X:]
            if j == 0:
                imag = jnp.where(is_first, 0.0, imag)
        real = split(real)
        imag = None if imag is None else split(imag)
        yield
        real = by_right(real, fold())
        imag = None if imag is None else by_right(imag, fold())
        yield
        real, imag = paired(real, imag, lane_zero, 1)
        real, imag = split(real), split(imag)
        yield
        real, imag = by_left(unfold_stack[...], real), by_left(unfold_stack[...], imag)
        yield
        real, imag = paired(real, imag, row_zero, 0)
        green = green_ref[j]
        mode = GRID_Y // 2 if j == fine else piece * fine + j
        share = jnp.where((mode == 0) | (mode == GRID_Y // 2), 0.5, 1.0)
        parts.append(share * jnp.sum(green * (real * real + imag * imag), axis=0, keepdims=True))
        real, imag = green * real, green * imag
        if j == fine:
            modes[j] = (real, imag)
            return
        if j == 0:
            real, imag = real - modes[fine][1], imag + modes[fine][0]
        real, imag = merged(real, imag, row_zero, 0)
        real, imag = split(real), split(imag)
        yield
        real, imag = by_left(fold_stack[...], real), by_left(fold_stack[...], imag)
        yield
        real, imag = merged(real, imag, lane_zero, 1)
        scale = jnp.where(piece * fine + j == 0, 1.0, 2.0)
        real, imag = split(real * scale), split(imag * scale)
        yield
        real, imag = by_right(real, unfold()), by_right(imag, unfold())
        yield
        for k, part in enumerate((real, imag)):
            turned = [
                pltpu.roll(part, (HALO_X - at_wide * cells_x) % GRID_X, 1)
                for at_wide in range(copies)
            ]
            for at_wide in range(wide_count):
                start = at_wide // copies * 128
                moved = turned[at_wide % copies][:, start : start + 128]
                high = moved.astype(jnp.bfloat16).astype(jnp.float32)
                again = pltpu.roll(high, reach % 128, 1)
                low = pltpu.roll(moved - high, 2 * reach % 128, 1)
                sides = []
                for side in range(2):
                    lane = lax.broadcasted_iota(jnp.int32, (1, 128), 1) + side * 128
                    value = jnp.where(lane < 2 * reach, again, low)
                    if side == 0:
                        value = jnp.where(lane < reach, high, value)
                    sides.append(value.astype(jnp.bfloat16))
                block = jnp.concatenate(sides, axis=1)
                packed[at_wide, 2 * j + k, HALO_BITS:, :] = block
                packed[at_wide, 2 * j + k, 0:HALO_BITS, :] = block[GRID_Z - HALO_BITS :]

    waiting = [slot(j) for j in [fine, *range(fine)]]
    running = []
    while waiting or running:
        if waiting:
            running.append(waiting.pop(0))
        running = [one for one in running if next(one, running) is not running]
    energy = sum(parts[1:], parts[0])
    energy = jnp.broadcast_to(jnp.sum(energy, axis=1, keepdims=True), (1, 128))

    def collect(index, odd):
        at_narrow = LOOP_BODY * index + odd
        value_z = weights_z[at_narrow]
        slope_z = slopes_z[at_narrow]
        first = pl.multiple_of(at_narrow * cells_z, HALO_BITS)
        wave = waves[at_narrow]
        wave_slope = wave_slopes[at_narrow]
        for at_wide in range(wide_count):
            lanes = slice(at_wide * pair, (at_wide + 1) * pair)
            tall = cells_z + HALO_BITS
            left = jnp.concatenate(
                [packed[at_wide, c, pl.ds(first, tall), :] for c in range(channels)], axis=0
            )

            def across(right):
                high = right[0:reach]
                rest = jnp.zeros((256 - 3 * reach, pair), jnp.bfloat16)
                right = jnp.concatenate([high, right[128 : 128 + reach], high, rest], axis=0)
                return lax.dot_general(left, right, NN, preferred_element_type=jnp.float32)

            value = across(weights[odd][index, :, lanes])
            slope = across(slopes[odd][index, :, lanes])
            plain = jnp.zeros((window, pair), jnp.float32)
            along_x = plain
            along_y = plain
            for c in range(channels):
                block = slice((c + 1) * tall - window, (c + 1) * tall)
                plain = plain + value[block] * wave[c : c + 1, lanes]
                along_x = along_x + slope[block] * wave[c : c + 1, lanes]
                along_y = along_y + value[block] * wave_slope[c : c + 1, lanes]
            near = value_z[:, lanes]
            near_slope = slope_z[:, lanes]
            results = [
                jnp.sum(near * plain, axis=0, keepdims=True),
                -jnp.sum(near * along_x, axis=0, keepdims=True),
                -jnp.sum(near * along_y, axis=0, keepdims=True),
                -jnp.sum(near_slope * plain, axis=0, keepdims=True),
            ]
            for k, row in enumerate(results):
                out_ref[at_wide, at_narrow, :, k * pair : (k + 1) * pair] = row
            out_ref[at_wide, at_narrow, :, 4 * pair :] = energy

    in_groups(collect)


def finish_kernel(arrived, species, atom_ref, centroid_ref, energy_ref):
    atoms = species.shape[1]
    total = arrived[0]
    for k in range(1, arrived.shape[0]):
        total = total + arrived[k]
    oxygen = 1.0 - species[...].astype(jnp.float32)
    for k in range(4):
        atom_ref[k] = total[:, 2 * k * atoms : (2 * k + 1) * atoms]
        centroid_ref[k] = total[:, (2 * k + 1) * atoms : (2 * k + 2) * atoms] * oxygen
    energy_ref[...] = total[:, 8 * atoms :] * (1.0 / (atoms * arrived.shape[0]))


def mode_factors(length, order):
    wrapped = np.where(2 * order >= length, order - length, order)
    square = (wrapped / length) ** 2
    ratio = (4.0 + 2.0 * np.cos(2.0 * math.pi * order / length)) / 6.0
    return np.stack([np.exp(-(math.pi**2) * square / ewald_beta**2) / ratio**2, square])


def folded_order(length):
    half = length // 2
    counter = np.arange(half)
    return np.concatenate([counter, np.where(counter == 0, half, length - counter)])


def fold_table(length):
    half = length // 2
    turns = np.outer(np.arange(length), np.arange(half)) % length * (2.0 * math.pi / length)
    sines = np.sin(turns)
    sines[:, 0] = 1.0 - 2.0 * (np.arange(length) % 2)
    return np.concatenate([np.cos(turns), sines], axis=1)


def halves(table):
    high = table.astype(jnp.bfloat16)
    low = (table - high.astype(np.float64)).astype(jnp.bfloat16)
    return high, low


def vmem(count):
    return [pl.BlockSpec(memory_space=pltpu.VMEM)] * count


def hbm(count):
    return [pl.BlockSpec(memory_space=pltpu.HBM)] * count


def shaped(shape, dtype=jnp.float32):
    return jax.ShapeDtypeStruct(shape, dtype)


def limits(mebibytes):
    return pltpu.CompilerParams(vmem_limit_bytes=mebibytes * 1024 * 1024)


def local(
    positions,
    species,
    neighbours,
    embed_one_w,
    embed_one_b,
    embed_two_w,
    embed_two_b,
    embed_three_w,
    embed_three_b,
    fit_one_w,
    fit_one_b,
    fit_two_w,
    fit_two_b,
    fit_three_w,
    fit_three_b,
    fit_out_w,
):
    axes = ("wide", "narrow")
    wide_count = lax.axis_size("wide")
    narrow_count = lax.axis_size("narrow")
    pieces = wide_count * narrow_count
    atoms = positions.shape[4]
    listed = neighbours.shape[4]
    fine = GRID_Y // 2 // pieces
    width_three = embed_three_w.shape[1]
    entries, hidden = fit_one_w.shape
    kinds = species.reshape(1, atoms)

    packed = pl.pallas_call(
        pack_kernel,
        out_shape=shaped((pieces, 4, atoms)),
        in_specs=vmem(2),
        out_specs=vmem(1)[0],
        name="pack",
    )(positions.reshape(3, 1, atoms), kinds)
    table = lax.all_to_all(packed, axes, 0, 0, tiled=True)
    table = table.reshape(wide_count, narrow_count, 4, atoms)

    tall_two = -(-(width_three // 2 + 1) // 8) * 8
    tall_three = -(-width_three // 8) * 8
    bf16 = jnp.bfloat16
    wave_rows = -(-2 * fine // 8) * 8
    angle = np.arange(GRID_Y) * (2.0 * math.pi / GRID_Y)
    constants = np.concatenate(
        [
            np.stack([np.cos(angle), np.sin(angle)]),
            mode_factors(GRID_Y, np.arange(GRID_Y)),
            mode_factors(GRID_X, folded_order(GRID_X)),
            mode_factors(GRID_Z, folded_order(GRID_Z)),
        ]
    )
    constants[2] *= coulomb / (math.pi * GRID_X * GRID_Y * GRID_Z)
    arguments = (
        neighbours.reshape(atoms, listed),
        embed_one_w,
        embed_one_b,
        embed_two_w,
        embed_two_b[None],
        embed_three_w,
        embed_three_b[None],
        fit_one_w.T,
        fit_one_b[None],
        fit_two_w,
        fit_two_b[None],
        fit_three_w,
        fit_three_b[None],
        jnp.asarray(constants, jnp.float32),
    )
    held = [arguments[k] for k in (0, 1, 2, 3, 4, 5, 6, 8, 10, 12, 13, 9, 11, 7)]
    prepared = pl.pallas_call(
        prepare_kernel,
        out_shape=(
            shaped((listed, atoms), jnp.int32),
            shaped((256, 16)),
            shaped((2 * tall_two, 3 * ROW_PAD), bf16),
            shaped((2 * tall_three, 6 * ROW_PAD), bf16),
            shaped((hidden, entries), bf16),
            shaped((hidden, entries), bf16),
        )
        + (shaped((hidden, hidden), bf16),) * 4
        + (shaped((wave_rows, GRID_Y)), shaped((fine + 1, GRID_Z, GRID_X))),
        in_specs=hbm(len(arguments)),
        out_specs=tuple(vmem(12)),
        scratch_shapes=[
            pltpu.VMEM((16, 256), jnp.float32),
            pltpu.VMEM((256, 256), jnp.float32),
            pltpu.SemaphoreType.DMA((len(held),)),
        ]
        + [pltpu.VMEM(array.shape, array.dtype) for array in held],
        compiler_params=limits(62),
        cost_estimate=pl.CostEstimate(
            flops=1000000, bytes_accessed=8 * entries * hidden, transcendentals=0
        ),
        name="prepare",
    )(*arguments)
    phase, green = prepared[10:]
    fitted = (table, *prepared[:10], fit_out_w.T)
    dipole, shifts, table = pl.pallas_call(
        centroid_kernel,
        out_shape=(shaped((3, 1, atoms)), shaped((pieces, 4, atoms)), shaped(table.shape)),
        in_specs=hbm(12),
        out_specs=tuple(vmem(2) + hbm(1)),
        scratch_shapes=[
            pltpu.VMEM((4, tall_three, atoms), jnp.float32),
            pltpu.VMEM((width_three * AXIS_COLUMNS, atoms), jnp.float32),
            pltpu.SemaphoreType.DMA((len(fitted) + 1,)),
        ]
        + [pltpu.VMEM(array.shape, array.dtype) for array in fitted],
        compiler_params=limits(62),
        name="centroids",
    )(*fitted)
    shifts = lax.all_to_all(shifts, axes, 0, 0, tiled=True)
    shifts = shifts.reshape(wide_count, narrow_count, 4, atoms)

    cells_x = GRID_X // wide_count
    copies = 128 // cells_x
    component = lax.broadcasted_iota(jnp.int32, table.shape, 2)
    extents = (cells_x, GRID_Y, GRID_Z // narrow_count)
    cells = jnp.abs(table)
    for k, extent in enumerate(extents):
        cells = jnp.where(component == k, cells * float(extent), cells)
    length = wide_count * 2 * atoms
    out_width = 8 * atoms + 128
    partial = pl.pallas_call(
        mesh_kernel,
        out_shape=shaped((wide_count, narrow_count, 1, out_width)),
        in_specs=vmem(6),
        out_specs=vmem(1)[0],
        scratch_shapes=[
            pltpu.VMEM((copies, fine, HALO_Z + GRID_Z, 2 * GRID_X), jnp.float32),
            pltpu.VMEM((fine, GRID_Z, 2 * GRID_X), jnp.float32),
            pltpu.VMEM((wide_count, 2 * fine, HALO_BITS + GRID_Z, 256), bf16),
        ]
        + [pltpu.VMEM((narrow_count, GRID_Z // narrow_count + HALO_Z, length), jnp.float32)] * 2
        + [pltpu.VMEM((narrow_count, wave_rows, length), jnp.float32)] * 2
        + [pltpu.VMEM((narrow_count // LOOP_BODY, 256, length), bf16)] * (2 * LOOP_BODY),
        compiler_params=limits(48),
        name="mesh",
    )(
        cells,
        shifts,
        phase,
        green,
        jnp.asarray(np.concatenate(halves(fold_table(GRID_X)))),
        jnp.asarray(np.concatenate(halves(fold_table(GRID_X).T))),
    )
    arrived = lax.all_to_all(partial.reshape(pieces, 1, out_width), axes, 0, 0, tiled=True)
    atom_field, centroid_field, energy = pl.pallas_call(
        finish_kernel,
        out_shape=(shaped((4, 1, atoms)), shaped((4, 1, atoms)), shaped((1, 128))),
        in_specs=vmem(2),
        out_specs=tuple(vmem(3)),
        name="finish",
    )(arrived, kinds)
    atom_field = atom_field.reshape(4, 1, 1, 1, atoms)
    centroid_field = centroid_field.reshape(4, 1, 1, 1, atoms)
    return (dipole.reshape(3, 1, 1, 1, atoms), atom_field, centroid_field, energy[0, 0])


def solution(mesh):
    column = P(None, "wide", "narrow", None, None)
    in_specs = (column, P("wide", "narrow", None, None), P("wide", "narrow", None, None, None))
    in_specs = in_specs + (P(),) * 13
    out_specs = (column, column, column, P())
    return jax.shard_map(local, mesh=mesh, in_specs=in_specs, out_specs=out_specs, check_vma=False)
```

```python
import math

import jax
import jax.numpy as jnp
import numpy as np
from jax import lax
from jax.experimental import pallas as pl
from jax.experimental.pallas import tpu as pltpu
from jax.sharding import PartitionSpec as P

GRID_X = 256
GRID_Y = 256
GRID_Z = 256
AXIS_COLUMNS = 16

radius_scale = 24.0
wannier_reach = 0.5
ewald_beta = 0.9
coulomb = 0.25

ROW_PAD = 32
LOOP_BODY = 4
CHUNK_BODY = 8
SLOT_CHUNK = 16
HALO_X = 16
HALO_Z = 8
HALO_BITS = 16

NN = (((1,), (0,)), ((), ()))
NT = (((1,), (1,)), ((), ()))


def split(value):
    high = value.astype(jnp.bfloat16)
    low = (value - high.astype(jnp.float32)).astype(jnp.bfloat16)
    return high, low


def multiply(left, right, dims=NN):
    def one(a, b):
        return lax.dot_general(a, b, dims, preferred_element_type=jnp.float32)

    return one(left[0], right[0]) + (one(left[1], right[0]) + one(left[0], right[1]))


def by_right(left, right):
    rows = left[0].shape[0]
    both = lax.dot_general(
        jnp.concatenate(left, axis=0), right[0], NN, preferred_element_type=jnp.float32
    )
    rest = lax.dot_general(left[0], right[1], NN, preferred_element_type=jnp.float32)
    return both[:rows] + (both[rows:] + rest)


def by_left(left, right):
    rows = left.shape[0] // 2
    both = lax.dot_general(left, right[0], NN, preferred_element_type=jnp.float32)
    rest = lax.dot_general(left[:rows], right[1], NN, preferred_element_type=jnp.float32)
    return both[:rows] + (both[rows:] + rest)


def spline_pair(offset):
    centred = offset - 2.0
    away = jnp.abs(centred)
    outer = jnp.maximum(2.0 - away, 0.0)
    inner = jnp.maximum(1.0 - away, 0.0)
    outer_square = outer * outer
    inner_square = inner * inner
    value = (outer_square * outer - 4.0 * (inner_square * inner)) * (1.0 / 6.0)
    slope = jnp.where(centred < 0.0, 0.5, -0.5) * (outer_square - 4.0 * inner_square)
    return value, slope


def wrapped(value, length):
    if length & (length - 1) == 0:
        return jnp.bitwise_and(value, length - 1)
    return lax.rem(value, length)


def lookup(row_table, spot):
    found = None
    lane = jnp.bitwise_and(spot, 127)
    block = lax.shift_right_logical(spot, 7)
    for part in range(row_table.shape[1] // 128):
        inside = block == part
        here = jnp.take_along_axis(
            jnp.broadcast_to(row_table[:, part * 128 : (part + 1) * 128], spot.shape),
            lane,
            axis=1,
            mode="promise_in_bounds",
        )
        found = here if found is None else jnp.where(inside, here, found)
    return found


def pack_kernel(positions, species, out_ref):
    kinds = species[...]
    rows = [positions[component] for component in range(3)]
    rows[0] = jnp.where(kinds > 0, -rows[0], rows[0])
    rows.append(kinds.astype(jnp.float32))
    rows = jnp.concatenate(rows, axis=0)
    for target in range(out_ref.shape[0]):
        out_ref[target] = rows


def prepare_kernel(
    neighbours,
    embed_one_w,
    embed_one_b,
    embed_two_w,
    embed_two_b,
    embed_three_w,
    embed_three_b,
    fit_one_w,
    fit_one_b,
    fit_two_w,
    fit_two_b,
    fit_three_w,
    fit_three_b,
    constants,
    codes_ref,
    columns_ref,
    second_ref,
    third_ref,
    one_high_ref,
    one_low_ref,
    two_high_ref,
    two_low_ref,
    three_high_ref,
    three_low_ref,
    phase_ref,
    green_ref,
    rows,
    square,
    arrivals,
    *held,
):
    sources = (
        neighbours,
        embed_one_w,
        embed_one_b,
        embed_two_w,
        embed_two_b,
        embed_three_w,
        embed_three_b,
        fit_one_b,
        fit_two_b,
        fit_three_b,
        constants,
        fit_two_w,
        fit_three_w,
        fit_one_w,
    )
    copies = [
        pltpu.make_async_copy(source, target, arrivals.at[k])
        for k, (source, target) in enumerate(zip(sources, held))
    ]
    for copy in copies:
        copy.start()
    (
        neighbours,
        embed_one_w,
        embed_one_b,
        embed_two_w,
        embed_two_b,
        embed_three_w,
        embed_three_b,
        fit_one_b,
        fit_two_b,
        fit_three_b,
        constants,
        fit_two_w,
        fit_three_w,
        fit_one_w,
    ) = held
    for copy in copies[:11]:
        copy.wait()
    pieces = lax.axis_size("wide") * lax.axis_size("narrow")
    piece = lax.axis_index("wide") * lax.axis_size("narrow") + lax.axis_index("narrow")
    width_one = embed_one_w.shape[1]
    hidden = fit_two_w.shape[0]
    codes_ref[...] = jnp.transpose(neighbours[...].astype(jnp.float32)).astype(jnp.int32)
    rows[...] = jnp.zeros_like(rows)
    for kind in range(2):
        rows[kind : kind + 1, 0:width_one] = embed_one_w[kind : kind + 1, :]
        rows[2 + kind : 3 + kind, 0:width_one] = embed_one_b[kind : kind + 1, :]
        rows[2 + kind : 3 + kind, width_one : width_one + 1] = jnp.full((1, 1), 40.0, jnp.float32)
    for row, source in ((4, fit_one_b), (5, fit_two_b), (6, fit_three_b)):
        rows[row : row + 1, 0:hidden] = source[...]
    columns_ref[...] = jnp.transpose(rows[...])

    row = lax.broadcasted_iota(jnp.int32, square.shape, 0)
    lane = lax.broadcasted_iota(jnp.int32, square.shape, 1)
    for width, weight, bias, target in (
        (width_one, embed_two_w, embed_two_b, second_ref),
        (2 * width_one, embed_three_w, embed_three_b, third_ref),
    ):
        tall, deep = target.shape[0] // 2, target.shape[1] // 3
        again = (lane - tall == row) | (lane - tall == row + width)
        again = (again & (row < width)) | ((lane - tall == 2 * width) & (row == width))
        square[...] = jnp.where(again, 1.0, 0.0)
        square[0:width, 0 : 2 * width] = weight[...]
        square[width : width + 1, 0 : 2 * width] = bias[...]
        high, low = split(jnp.transpose(square[...])[0 : 2 * tall, 0:deep])
        target[...] = jnp.concatenate([high, high, low], axis=1)
    square[...] = jnp.zeros_like(square)
    for copy in copies[11:13]:
        copy.wait()
    for source, high_ref, low_ref in (
        (fit_two_w, two_high_ref, two_low_ref),
        (fit_three_w, three_high_ref, three_low_ref),
    ):
        square[0:hidden, 0:hidden] = source[...]
        high_ref[...], low_ref[...] = split(jnp.transpose(square[...])[0:hidden, 0:hidden])

    fine = GRID_Y // 2 // pieces
    shape = (phase_ref.shape[0], 128)
    row = lax.broadcasted_iota(jnp.int32, shape, 0)
    mode = piece * fine + row // 2
    for part in range(GRID_Y // 128):
        cell = lax.broadcasted_iota(jnp.int32, shape, 1) + part * 128
        spot = wrapped(mode * cell, GRID_Y)
        cosine = lookup(constants[0:1, :], spot)
        sine = lookup(constants[1:2, :], spot)
        alternate = (1 - 2 * lax.rem(cell, 2)).astype(jnp.float32)
        odd = jnp.where(mode == 0, alternate, -sine)
        value = jnp.where(lax.rem(row, 2) == 0, cosine, odd)
        phase_ref[:, part * 128 : (part + 1) * 128] = jnp.where(row < 2 * fine, value, 0.0)

    column = jnp.transpose(constants[...])
    lane = lax.broadcasted_iota(jnp.int32, (1, GRID_Y), 1)
    for j in range(fine + 1):
        here = lane == (GRID_Y // 2 if j == fine else piece * fine + j)
        factor = jnp.sum(jnp.where(here, constants[2:3, :], 0.0), axis=1, keepdims=True)
        part = jnp.sum(jnp.where(here, constants[3:4, :], 0.0), axis=1, keepdims=True)
        wave = (part + constants[5:6, :]) + column[:, 7:8]
        top = (factor * constants[4:5, :]) * column[:, 6:7]
        green_ref[j] = jnp.where(wave == 0.0, 0.0, top / jnp.where(wave == 0.0, 1.0, wave))

    copies[13].wait()
    one_high_ref[...], one_low_ref[...] = split(fit_one_w[...])


def centroid_kernel(
    table,
    codes,
    columns,
    second,
    third,
    one_high,
    one_low,
    two_high,
    two_low,
    three_high,
    three_low,
    fit_out_w,
    dipole_ref,
    shift_ref,
    table_ref,
    matrix,
    descriptor,
    arrivals,
    *held,
):
    sources = (table, codes, columns, second, third)
    sources += (one_high, one_low, two_high, two_low, three_high, three_low, fit_out_w)
    copies = [
        pltpu.make_async_copy(source, target, arrivals.at[k])
        for k, (source, target) in enumerate(zip(sources, held))
    ]
    for copy in copies:
        copy.start()
    table, codes, columns, second, third = held[:5]
    one_high, one_low, two_high, two_low, three_high, three_low, fit_out_w = held[5:]
    for copy in copies[:5]:
        copy.wait()
    handing_on = pltpu.make_async_copy(table, table_ref, arrivals.at[len(copies)])
    handing_on.start()
    wide_count, narrow_count, _, atoms = table.shape
    listed = codes.shape[0]
    width_three = fit_out_w.shape[0]
    width_one = width_three // 4
    hidden_width = two_high.shape[0]
    cells = (GRID_X // wide_count, GRID_Y, GRID_Z // narrow_count)
    at_wide = lax.axis_index("wide")
    at_narrow = lax.axis_index("narrow")
    own = jnp.abs(table[at_wide, at_narrow])
    nearby = []
    for step in range(9):
        wide_at = lax.rem(at_wide + (step // 3 - 1) + wide_count, wide_count)
        narrow_at = lax.rem(at_narrow + (step % 3 - 1) + narrow_count, narrow_count)
        nearby.append(table[wide_at, narrow_at])

    second_all = second[...]
    third_all = third[...]
    weight_oxygen = jnp.broadcast_to(columns[0:ROW_PAD, 0:1], (ROW_PAD, atoms))
    weight_hydrogen = jnp.broadcast_to(columns[0:ROW_PAD, 1:2], (ROW_PAD, atoms))
    bias_oxygen = jnp.broadcast_to(columns[0:ROW_PAD, 2:3], (ROW_PAD, atoms))
    bias_hydrogen = jnp.broadcast_to(columns[0:ROW_PAD, 3:4], (ROW_PAD, atoms))
    matrix[...] = jnp.zeros_like(matrix)

    def chunk(first):
        code = codes[pl.ds(first, SLOT_CHUNK), :]
        slot = wrapped(code, atoms)
        if atoms & (atoms - 1) == 0:
            offset = lax.shift_right_logical(code, atoms.bit_length() - 1)
        else:
            offset = code // atoms
        step_x = jnp.where(offset >= 9, 1, 0) + jnp.where(offset >= 18, 1, 0)
        rest = offset - 9 * step_x
        step_z = jnp.where(rest >= 3, 1, 0) + jnp.where(rest >= 6, 1, 0)
        step_y = rest - 3 * step_z
        brick = step_x * 3 + step_z
        found = []
        for component in range(3):
            picked = jnp.zeros((SLOT_CHUNK, atoms), jnp.float32)
            for step in range(9):
                row = jnp.broadcast_to(
                    nearby[step][component : component + 1], (SLOT_CHUNK, atoms)
                )
                here = jnp.take_along_axis(row, slot, axis=1, mode="promise_in_bounds")
                picked = jnp.where(brick == step, here, picked)
            found.append(picked)
        hydrogen = found[0] < 0.0
        found[0] = jnp.abs(found[0])
        scaled = []
        for component, step in enumerate((step_x, step_y, step_z)):
            extent = float(cells[component])
            relative = (step - 1).astype(jnp.float32) * extent + (
                found[component] - own[component : component + 1]
            ) * extent
            scaled.append(relative * (1.0 / radius_scale))
        smooth = 1.0 / (
            1.0 + (scaled[0] * scaled[0] + scaled[1] * scaled[1] + scaled[2] * scaled[2])
        )
        radial = [smooth] + [smooth * part for part in scaled]
        first_layers = []
        for k in range(SLOT_CHUNK):
            row = smooth[k : k + 1]
            kind = hydrogen[k : k + 1]
            weight = jnp.where(kind, weight_hydrogen, weight_oxygen)
            bias = jnp.where(kind, bias_hydrogen, bias_oxygen)
            first_layers.append(jnp.tanh(weight * row + bias))
        layer_one = jnp.concatenate(first_layers, axis=1)
        high, low = split(layer_one)
        both = lax.dot_general(
            second_all,
            jnp.concatenate([high, low, high], axis=0),
            NN,
            preferred_element_type=jnp.float32,
        )
        tall = both.shape[0] // 2
        layer_two = jnp.tanh(both[:tall]) + both[tall:]
        deep = third_all.shape[1] // 3
        rest = jnp.zeros((deep - tall, layer_two.shape[1]), jnp.float32)
        high, low = split(jnp.concatenate([layer_two, rest], axis=0))
        both = lax.dot_general(
            third_all,
            jnp.concatenate([high, low, high], axis=0),
            NN,
            preferred_element_type=jnp.float32,
        )
        tall = both.shape[0] // 2
        layer_three = jnp.tanh(both[:tall]) + both[tall:]
        for part in range(4):
            total = matrix[part]
            for k in range(SLOT_CHUNK):
                total = total + layer_three[:, k * atoms : (k + 1) * atoms] * radial[part][k : k + 1]
            matrix[part] = total

    def chunks(index, carry):
        for step in range(CHUNK_BODY):
            chunk(pl.multiple_of((index * CHUNK_BODY + step) * SLOT_CHUNK, SLOT_CHUNK))
        return carry

    lax.fori_loop(0, listed // (CHUNK_BODY * SLOT_CHUNK), chunks, 0)

    parts = []
    for part in range(4):
        parts.append(matrix[part, 0:width_three, :] * (1.0 / listed))
    leading = [part[0:AXIS_COLUMNS] for part in parts]
    for row in range(width_three):
        total = parts[0][row : row + 1] * leading[0]
        for part in range(1, 4):
            total = total + parts[part][row : row + 1] * leading[part]
        descriptor[row * AXIS_COLUMNS : (row + 1) * AXIS_COLUMNS, :] = total
    for copy in copies[5:]:
        copy.wait()

    def layer(high_ref, low_ref, given, column):
        weights = (high_ref[...], low_ref[...])
        return jnp.tanh(multiply(weights, split(given)) + columns[0:hidden_width, column : column + 1])

    hidden = layer(one_high, one_low, descriptor[...], 4)
    hidden = hidden + layer(two_high, two_low, hidden, 5)
    hidden = hidden + layer(three_high, three_low, hidden, 6)
    coeffs = multiply(split(fit_out_w[...]), split(hidden))
    vector = jnp.concatenate(
        [jnp.sum(coeffs * parts[1 + c], axis=0, keepdims=True) for c in range(3)], axis=0
    )
    oxygen = 1.0 - own[3:4]
    for c in range(3):
        dipole_ref[c] = vector[c : c + 1] * oxygen
    moved = wannier_reach * jnp.tanh(vector)
    moved = jnp.concatenate([moved, jnp.zeros((1, atoms), jnp.float32)], axis=0)
    for target in range(shift_ref.shape[0]):
        shift_ref[target] = moved
    handing_on.wait()


def mesh_kernel(
    cells,
    shifts,
    phase,
    green_ref,
    fold_stack,
    unfold_stack,
    out_ref,
    grid,
    planes,
    packed,
    weights_z,
    slopes_z,
    waves,
    wave_slopes,
    *across_refs,
):
    wide_count, narrow_count, _, atoms = cells.shape
    cells_x = GRID_X // wide_count
    cells_z = GRID_Z // narrow_count
    window = cells_z + HALO_Z
    reach = cells_x + HALO_X
    pair = 2 * atoms
    length = wide_count * pair
    copies = grid.shape[0]
    fine = grid.shape[1]
    channels = 2 * fine
    rows = phase.shape[0]
    half_x = GRID_X // 2
    half_z = GRID_Z // 2
    piece = lax.axis_index("wide") * narrow_count + lax.axis_index("narrow")
    lane_zero = lax.broadcasted_iota(jnp.int32, (1, half_x), 1) == 0
    row_zero = lax.broadcasted_iota(jnp.int32, (half_z, 1), 0) == 0

    def fold():
        return (fold_stack[0:GRID_X, :], fold_stack[GRID_X:, :])

    def unfold():
        return (unfold_stack[0:GRID_X, :], unfold_stack[GRID_X:, :])

    def sites(at_wide, at_narrow):
        atom = cells[at_wide, at_narrow]
        moved = shifts[at_wide, at_narrow]
        found = []
        for component in range(3):
            start = atom[component : component + 1]
            found.append(jnp.concatenate([start, start + moved[component : component + 1]], axis=1))
        oxygen = 1.0 - atom[3:4]
        found.append(jnp.concatenate([6.0 * oxygen + atom[3:4], -8.0 * oxygen], axis=1))
        return found

    def line(at_narrow):
        groups = [sites(at_wide, at_narrow) for at_wide in range(wide_count)]
        return [jnp.concatenate([g[k] for g in groups], axis=1) for k in range(4)]

    def splines_z(row):
        counter = lax.broadcasted_iota(jnp.int32, (window, 1), 0).astype(jnp.float32)
        return spline_pair(row - (counter - float(HALO_Z)))

    def fill_x(row, targets):
        counter = lax.broadcasted_iota(jnp.int32, (reach, 1), 0).astype(jnp.float32)
        both = spline_pair(row - (counter - float(HALO_X)))
        rest = jnp.zeros((128 - reach, length), jnp.bfloat16)
        for values, ref in zip(both, targets):
            high, low = split(values)
            ref[0:reach, :] = high
            ref[reach:128, :] = rest
            ref[128 : 128 + reach, :] = low
            ref[128 + reach : 256, :] = rest

    grid[:, :, 0:HALO_Z, :] = jnp.zeros((copies, fine, HALO_Z, 2 * GRID_X), jnp.float32)

    weights = across_refs[:LOOP_BODY]
    slopes = across_refs[LOOP_BODY:]

    def spread(index, odd):
        at_narrow = LOOP_BODY * index + odd
        row_x, row_y, row_z, charge = line(at_narrow)
        lower = jnp.floor(row_y)
        back = lax.broadcasted_iota(jnp.int32, (8, 1), 0)
        value_y, slope_y = spline_pair((row_y - lower) + back.astype(jnp.float32))
        cell = wrapped(lower.astype(jnp.int32) - back + GRID_Y, GRID_Y)
        wave_blocks = []
        slope_blocks = []
        for block in range(length // 128):
            lanes = slice(block * 128, (block + 1) * 128)
            wave = jnp.zeros((rows, 128), jnp.float32)
            wave_slope = jnp.zeros((rows, 128), jnp.float32)
            for k in range(4):
                spot = jnp.broadcast_to(cell[k : k + 1, lanes], (rows, 128))
                found = lookup(phase[...], spot)
                wave = wave + value_y[k : k + 1, lanes] * found
                wave_slope = wave_slope + slope_y[k : k + 1, lanes] * found
            wave_blocks.append(wave)
            slope_blocks.append(wave_slope)
        wave = jnp.concatenate(wave_blocks, axis=1)
        waves[at_narrow] = wave
        wave_slopes[at_narrow] = jnp.concatenate(slope_blocks, axis=1)
        fill_x(row_x, (weights[odd].at[index], slopes[odd].at[index]))
        value_z, slope_z = splines_z(row_z)
        weights_z[at_narrow] = value_z
        slopes_z[at_narrow] = slope_z
        charged = wave * charge
        first = pl.multiple_of(at_narrow * cells_z, HALO_Z)
        for at_wide in range(wide_count):
            lanes = slice(at_wide * pair, (at_wide + 1) * pair)
            near = value_z[:, lanes]
            left = jnp.concatenate(
                [near * charged[c : c + 1, lanes] for c in range(channels)], axis=0
            )
            high, low = split(left)
            across = weights[odd][index, :, lanes]
            total = lax.dot_general(high, across, NT, preferred_element_type=jnp.float32)
            rest = lax.dot_general(low, across[0:128], NT, preferred_element_type=jnp.float32)
            total = total[:, 0:128] + (total[:, 128:256] + rest)
            start = at_wide // copies * 128
            for c in range(channels):
                spot = slice(c % 2 * GRID_X + start, c % 2 * GRID_X + start + 128)
                k = at_wide % copies
                part = total[c * window : (c + 1) * window]
                grid[k, c // 2, pl.ds(first, HALO_Z), spot] += part[:HALO_Z]
                grid[k, c // 2, pl.ds(first + HALO_Z, cells_z), spot] = part[HALO_Z:]

    def in_groups(step):
        def body(index, carry):
            for odd in range(LOOP_BODY):
                step(index, odd)
            return carry

        lax.fori_loop(0, narrow_count // LOOP_BODY, body, 0)

    in_groups(spread)

    def gather(j, carry):
        for lanes in (slice(0, GRID_X), slice(GRID_X, 2 * GRID_X)):
            total = None
            for k in range(copies):
                moved = pltpu.roll(grid[k, j, :, lanes], (k * cells_x - HALO_X) % GRID_X, 1)
                total = moved if total is None else total + moved
            planes[j, :, lanes] = total[HALO_Z:]
            planes[j, GRID_Z - HALO_Z :, lanes] += total[:HALO_Z]
        return carry

    lax.fori_loop(0, fine, gather, 0)
    is_first = piece == 0

    def paired(real, imag, zero, axis):
        half = real.shape[axis] // 2
        first = (slice(None),) * axis + (slice(0, half),)
        second = (slice(None),) * axis + (slice(half, 2 * half),)
        real_c, real_s = real[first], real[second]
        if imag is None:
            none = jnp.zeros_like(real_s)
            real_all = [real_c, jnp.where(zero, real_s, real_c)]
            imag_all = [jnp.where(zero, none, -real_s), jnp.where(zero, none, real_s)]
        else:
            imag_c, imag_s = imag[first], imag[second]
            real_all = [
                real_c + jnp.where(zero, 0.0, imag_s),
                jnp.where(zero, real_s, real_c - imag_s),
            ]
            imag_all = [
                imag_c - jnp.where(zero, 0.0, real_s),
                jnp.where(zero, imag_s, imag_c + real_s),
            ]
        return jnp.concatenate(real_all, axis=axis), jnp.concatenate(imag_all, axis=axis)

    def merged(real, imag, zero, axis):
        half = real.shape[axis] // 2
        first = (slice(None),) * axis + (slice(0, half),)
        second = (slice(None),) * axis + (slice(half, 2 * half),)
        real_a, real_b = real[first], real[second]
        imag_a, imag_b = imag[first], imag[second]
        real = [
            real_a + jnp.where(zero, 0.0, real_b),
            jnp.where(zero, real_b, imag_b - imag_a),
        ]
        imag = [
            imag_a + jnp.where(zero, 0.0, imag_b),
            jnp.where(zero, imag_b, real_a - real_b),
        ]
        return jnp.concatenate(real, axis=axis), jnp.concatenate(imag, axis=axis)

    modes = {}
    parts = []

    def slot(j):
        first_imag = planes[0, :, GRID_X:]
        if j == fine:
            real, imag = jnp.where(is_first, first_imag, 0.0), None
        else:
            real, imag = planes[j, :, 0:GRID_X], planes[j, :, GRID_X:]
            if j == 0:
                imag = jnp.where(is_first, 0.0, imag)
        real = split(real)
        imag = None if imag is None else split(imag)
        yield
        real = by_right(real, fold())
        imag = None if imag is None else by_right(imag, fold())
        yield
        real, imag = paired(real, imag, lane_zero, 1)
        real, imag = split(real), split(imag)
        yield
        real, imag = by_left(unfold_stack[...], real), by_left(unfold_stack[...], imag)
        yield
        real, imag = paired(real, imag, row_zero, 0)
        green = green_ref[j]
        mode = GRID_Y // 2 if j == fine else piece * fine + j
        share = jnp.where((mode == 0) | (mode == GRID_Y // 2), 0.5, 1.0)
        parts.append(share * jnp.sum(green * (real * real + imag * imag), axis=0, keepdims=True))
        real, imag = green * real, green * imag
        if j == fine:
            modes[j] = (real, imag)
            return
        if j == 0:
            real, imag = real - modes[fine][1], imag + modes[fine][0]
        real, imag = merged(real, imag, row_zero, 0)
        real, imag = split(real), split(imag)
        yield
        real, imag = by_left(fold_stack[...], real), by_left(fold_stack[...], imag)
        yield
        real, imag = merged(real, imag, lane_zero, 1)
        scale = jnp.where(piece * fine + j == 0, 1.0, 2.0)
        real, imag = split(real * scale), split(imag * scale)
        yield
        real, imag = by_right(real, unfold()), by_right(imag, unfold())
        yield
        for k, part in enumerate((real, imag)):
            turned = [
                pltpu.roll(part, (HALO_X - at_wide * cells_x) % GRID_X, 1)
                for at_wide in range(copies)
            ]
            for at_wide in range(wide_count):
                start = at_wide // copies * 128
                moved = turned[at_wide % copies][:, start : start + 128]
                high = moved.astype(jnp.bfloat16).astype(jnp.float32)
                again = pltpu.roll(high, reach % 128, 1)
                low = pltpu.roll(moved - high, 2 * reach % 128, 1)
                sides = []
                for side in range(2):
                    lane = lax.broadcasted_iota(jnp.int32, (1, 128), 1) + side * 128
                    value = jnp.where(lane < 2 * reach, again, low)
                    if side == 0:
                        value = jnp.where(lane < reach, high, value)
                    sides.append(value.astype(jnp.bfloat16))
                block = jnp.concatenate(sides, axis=1)
                packed[at_wide, 2 * j + k, HALO_BITS:, :] = block
                packed[at_wide, 2 * j + k, 0:HALO_BITS, :] = block[GRID_Z - HALO_BITS :]

    waiting = [slot(j) for j in [fine, *range(fine)]]
    running = []
    while waiting or running:
        if waiting:
            running.append(waiting.pop(0))
        running = [one for one in running if next(one, running) is not running]
    energy = sum(parts[1:], parts[0])
    energy = jnp.broadcast_to(jnp.sum(energy, axis=1, keepdims=True), (1, 128))

    def collect(index, odd):
        at_narrow = LOOP_BODY * index + odd
        value_z = weights_z[at_narrow]
        slope_z = slopes_z[at_narrow]
        first = pl.multiple_of(at_narrow * cells_z, HALO_BITS)
        wave = waves[at_narrow]
        wave_slope = wave_slopes[at_narrow]
        for at_wide in range(wide_count):
            lanes = slice(at_wide * pair, (at_wide + 1) * pair)
            tall = cells_z + HALO_BITS
            left = jnp.concatenate(
                [packed[at_wide, c, pl.ds(first, tall), :] for c in range(channels)], axis=0
            )

            def across(right):
                high = right[0:reach]
                rest = jnp.zeros((256 - 3 * reach, pair), jnp.bfloat16)
                right = jnp.concatenate([high, right[128 : 128 + reach], high, rest], axis=0)
                return lax.dot_general(left, right, NN, preferred_element_type=jnp.float32)

            value = across(weights[odd][index, :, lanes])
            slope = across(slopes[odd][index, :, lanes])
            plain = jnp.zeros((window, pair), jnp.float32)
            along_x = plain
            along_y = plain
            for c in range(channels):
                block = slice((c + 1) * tall - window, (c + 1) * tall)
                plain = plain + value[block] * wave[c : c + 1, lanes]
                along_x = along_x + slope[block] * wave[c : c + 1, lanes]
                along_y = along_y + value[block] * wave_slope[c : c + 1, lanes]
            near = value_z[:, lanes]
            near_slope = slope_z[:, lanes]
            results = [
                jnp.sum(near * plain, axis=0, keepdims=True),
                -jnp.sum(near * along_x, axis=0, keepdims=True),
                -jnp.sum(near * along_y, axis=0, keepdims=True),
                -jnp.sum(near_slope * plain, axis=0, keepdims=True),
            ]
            for k, row in enumerate(results):
                out_ref[at_wide, at_narrow, :, k * pair : (k + 1) * pair] = row
            out_ref[at_wide, at_narrow, :, 4 * pair :] = energy

    in_groups(collect)


def finish_kernel(arrived, species, atom_ref, centroid_ref, energy_ref):
    atoms = species.shape[1]
    total = arrived[0]
    for k in range(1, arrived.shape[0]):
        total = total + arrived[k]
    oxygen = 1.0 - species[...].astype(jnp.float32)
    for k in range(4):
        atom_ref[k] = total[:, 2 * k * atoms : (2 * k + 1) * atoms]
        centroid_ref[k] = total[:, (2 * k + 1) * atoms : (2 * k + 2) * atoms] * oxygen
    energy_ref[...] = total[:, 8 * atoms :] * (1.0 / (atoms * arrived.shape[0]))


def mode_factors(length, order):
    wrapped = np.where(2 * order >= length, order - length, order)
    square = (wrapped / length) ** 2
    ratio = (4.0 + 2.0 * np.cos(2.0 * math.pi * order / length)) / 6.0
    return np.stack([np.exp(-(math.pi**2) * square / ewald_beta**2) / ratio**2, square])


def folded_order(length):
    half = length // 2
    counter = np.arange(half)
    return np.concatenate([counter, np.where(counter == 0, half, length - counter)])


def fold_table(length):
    half = length // 2
    turns = np.outer(np.arange(length), np.arange(half)) % length * (2.0 * math.pi / length)
    sines = np.sin(turns)
    sines[:, 0] = 1.0 - 2.0 * (np.arange(length) % 2)
    return np.concatenate([np.cos(turns), sines], axis=1)


def halves(table):
    high = table.astype(jnp.bfloat16)
    low = (table - high.astype(np.float64)).astype(jnp.bfloat16)
    return high, low


def vmem(count):
    return [pl.BlockSpec(memory_space=pltpu.VMEM)] * count


def hbm(count):
    return [pl.BlockSpec(memory_space=pltpu.HBM)] * count


def shaped(shape, dtype=jnp.float32):
    return jax.ShapeDtypeStruct(shape, dtype)


def limits(mebibytes):
    return pltpu.CompilerParams(vmem_limit_bytes=mebibytes * 1024 * 1024)


def local(
    positions,
    species,
    neighbours,
    embed_one_w,
    embed_one_b,
    embed_two_w,
    embed_two_b,
    embed_three_w,
    embed_three_b,
    fit_one_w,
    fit_one_b,
    fit_two_w,
    fit_two_b,
    fit_three_w,
    fit_three_b,
    fit_out_w,
):
    axes = ("wide", "narrow")
    wide_count = lax.axis_size("wide")
    narrow_count = lax.axis_size("narrow")
    pieces = wide_count * narrow_count
    atoms = positions.shape[4]
    listed = neighbours.shape[4]
    fine = GRID_Y // 2 // pieces
    width_three = embed_three_w.shape[1]
    entries, hidden = fit_one_w.shape
    kinds = species.reshape(1, atoms)

    packed = pl.pallas_call(
        pack_kernel,
        out_shape=shaped((pieces, 4, atoms)),
        in_specs=vmem(2),
        out_specs=vmem(1)[0],
        name="pack",
    )(positions.reshape(3, 1, atoms), kinds)
    table = lax.all_to_all(packed, axes, 0, 0, tiled=True)
    table = table.reshape(wide_count, narrow_count, 4, atoms)

    tall_two = -(-(width_three // 2 + 1) // 8) * 8
    tall_three = -(-width_three // 8) * 8
    bf16 = jnp.bfloat16
    wave_rows = -(-2 * fine // 8) * 8
    angle = np.arange(GRID_Y) * (2.0 * math.pi / GRID_Y)
    constants = np.concatenate(
        [
            np.stack([np.cos(angle), np.sin(angle)]),
            mode_factors(GRID_Y, np.arange(GRID_Y)),
            mode_factors(GRID_X, folded_order(GRID_X)),
            mode_factors(GRID_Z, folded_order(GRID_Z)),
        ]
    )
    constants[2] *= coulomb / (math.pi * GRID_X * GRID_Y * GRID_Z)
    arguments = (
        neighbours.reshape(atoms, listed),
        embed_one_w,
        embed_one_b,
        embed_two_w,
        embed_two_b[None],
        embed_three_w,
        embed_three_b[None],
        fit_one_w.T,
        fit_one_b[None],
        fit_two_w,
        fit_two_b[None],
        fit_three_w,
        fit_three_b[None],
        jnp.asarray(constants, jnp.float32),
    )
    held = [arguments[k] for k in (0, 1, 2, 3, 4, 5, 6, 8, 10, 12, 13, 9, 11, 7)]
    prepared = pl.pallas_call(
        prepare_kernel,
        out_shape=(
            shaped((listed, atoms), jnp.int32),
            shaped((256, 16)),
            shaped((2 * tall_two, 3 * ROW_PAD), bf16),
            shaped((2 * tall_three, 6 * ROW_PAD), bf16),
            shaped((hidden, entries), bf16),
            shaped((hidden, entries), bf16),
        )
        + (shaped((hidden, hidden), bf16),) * 4
        + (shaped((wave_rows, GRID_Y)), shaped((fine + 1, GRID_Z, GRID_X))),
        in_specs=hbm(len(arguments)),
        out_specs=tuple(vmem(12)),
        scratch_shapes=[
            pltpu.VMEM((16, 256), jnp.float32),
            pltpu.VMEM((256, 256), jnp.float32),
            pltpu.SemaphoreType.DMA((len(held),)),
        ]
        + [pltpu.VMEM(array.shape, array.dtype) for array in held],
        compiler_params=limits(62),
        cost_estimate=pl.CostEstimate(
            flops=1000000, bytes_accessed=8 * entries * hidden, transcendentals=0
        ),
        name="prepare",
    )(*arguments)
    phase, green = prepared[10:]
    fitted = (table, *prepared[:10], fit_out_w.T)
    dipole, shifts, table = pl.pallas_call(
        centroid_kernel,
        out_shape=(shaped((3, 1, atoms)), shaped((pieces, 4, atoms)), shaped(table.shape)),
        in_specs=hbm(12),
        out_specs=tuple(vmem(2) + hbm(1)),
        scratch_shapes=[
            pltpu.VMEM((4, tall_three, atoms), jnp.float32),
            pltpu.VMEM((width_three * AXIS_COLUMNS, atoms), jnp.float32),
            pltpu.SemaphoreType.DMA((len(fitted) + 1,)),
        ]
        + [pltpu.VMEM(array.shape, array.dtype) for array in fitted],
        compiler_params=limits(62),
        name="centroids",
    )(*fitted)
    shifts = lax.all_to_all(shifts, axes, 0, 0, tiled=True)
    shifts = shifts.reshape(wide_count, narrow_count, 4, atoms)

    cells_x = GRID_X // wide_count
    copies = 128 // cells_x
    component = lax.broadcasted_iota(jnp.int32, table.shape, 2)
    extents = (cells_x, GRID_Y, GRID_Z // narrow_count)
    cells = jnp.abs(table)
    for k, extent in enumerate(extents):
        cells = jnp.where(component == k, cells * float(extent), cells)
    length = wide_count * 2 * atoms
    out_width = 8 * atoms + 128
    partial = pl.pallas_call(
        mesh_kernel,
        out_shape=shaped((wide_count, narrow_count, 1, out_width)),
        in_specs=vmem(6),
        out_specs=vmem(1)[0],
        scratch_shapes=[
            pltpu.VMEM((copies, fine, HALO_Z + GRID_Z, 2 * GRID_X), jnp.float32),
            pltpu.VMEM((fine, GRID_Z, 2 * GRID_X), jnp.float32),
            pltpu.VMEM((wide_count, 2 * fine, HALO_BITS + GRID_Z, 256), bf16),
        ]
        + [pltpu.VMEM((narrow_count, GRID_Z // narrow_count + HALO_Z, length), jnp.float32)] * 2
        + [pltpu.VMEM((narrow_count, wave_rows, length), jnp.float32)] * 2
        + [pltpu.VMEM((narrow_count // LOOP_BODY, 256, length), bf16)] * (2 * LOOP_BODY),
        compiler_params=limits(48),
        name="mesh",
    )(
        cells,
        shifts,
        phase,
        green,
        jnp.asarray(np.concatenate(halves(fold_table(GRID_X)))),
        jnp.asarray(np.concatenate(halves(fold_table(GRID_X).T))),
    )
    arrived = lax.all_to_all(partial.reshape(pieces, 1, out_width), axes, 0, 0, tiled=True)
    atom_field, centroid_field, energy = pl.pallas_call(
        finish_kernel,
        out_shape=(shaped((4, 1, atoms)), shaped((4, 1, atoms)), shaped((1, 128))),
        in_specs=vmem(2),
        out_specs=tuple(vmem(3)),
        name="finish",
    )(arrived, kinds)
    atom_field = atom_field.reshape(4, 1, 1, 1, atoms)
    centroid_field = centroid_field.reshape(4, 1, 1, 1, atoms)
    return (dipole.reshape(3, 1, 1, 1, atoms), atom_field, centroid_field, energy[0, 0])


def solution(mesh):
    column = P(None, "wide", "narrow", None, None)
    in_specs = (column, P("wide", "narrow", None, None), P("wide", "narrow", None, None, None))
    in_specs = in_specs + (P(),) * 13
    out_specs = (column, column, column, P())
    return jax.shard_map(local, mesh=mesh, in_specs=in_specs, out_specs=out_specs, check_vma=False)
```

```python
import math

import jax
import jax.numpy as jnp
import numpy as np
from jax import lax
from jax.experimental import pallas as pl
from jax.experimental.pallas import tpu as pltpu
from jax.sharding import PartitionSpec as P

GRID_X = 256
GRID_Y = 256
GRID_Z = 256
AXIS_COLUMNS = 16

radius_scale = 24.0
wannier_reach = 0.5
ewald_beta = 0.9
coulomb = 0.25

ROW_PAD = 32
LOOP_BODY = 4
CHUNK_BODY = 4
SLOT_CHUNK = 32
HALO_X = 16
HALO_Z = 8
HALO_BITS = 16

NN = (((1,), (0,)), ((), ()))
NT = (((1,), (1,)), ((), ()))


def split(value):
    high = value.astype(jnp.bfloat16)
    low = (value - high.astype(jnp.float32)).astype(jnp.bfloat16)
    return high, low


def multiply(left, right, dims=NN):
    def one(a, b):
        return lax.dot_general(a, b, dims, preferred_element_type=jnp.float32)

    return one(left[0], right[0]) + (one(left[1], right[0]) + one(left[0], right[1]))


def by_right(left, right):
    rows = left[0].shape[0]
    both = lax.dot_general(
        jnp.concatenate(left, axis=0), right[0], NN, preferred_element_type=jnp.float32
    )
    rest = lax.dot_general(left[0], right[1], NN, preferred_element_type=jnp.float32)
    return both[:rows] + (both[rows:] + rest)


def by_left(left, right):
    rows = left.shape[0] // 2
    both = lax.dot_general(left, right[0], NN, preferred_element_type=jnp.float32)
    rest = lax.dot_general(left[:rows], right[1], NN, preferred_element_type=jnp.float32)
    return both[:rows] + (both[rows:] + rest)


def spline_pair(offset):
    centred = offset - 2.0
    away = jnp.abs(centred)
    outer = jnp.maximum(2.0 - away, 0.0)
    inner = jnp.maximum(1.0 - away, 0.0)
    outer_square = outer * outer
    inner_square = inner * inner
    value = (outer_square * outer - 4.0 * (inner_square * inner)) * (1.0 / 6.0)
    slope = jnp.where(centred < 0.0, 0.5, -0.5) * (outer_square - 4.0 * inner_square)
    return value, slope


def wrapped(value, length):
    if length & (length - 1) == 0:
        return jnp.bitwise_and(value, length - 1)
    return lax.rem(value, length)


def lookup(row_table, spot):
    found = None
    lane = jnp.bitwise_and(spot, 127)
    block = lax.shift_right_logical(spot, 7)
    for part in range(row_table.shape[1] // 128):
        inside = block == part
        here = jnp.take_along_axis(
            jnp.broadcast_to(row_table[:, part * 128 : (part + 1) * 128], spot.shape),
            lane,
            axis=1,
            mode="promise_in_bounds",
        )
        found = here if found is None else jnp.where(inside, here, found)
    return found


def pack_kernel(positions, species, out_ref):
    kinds = species[...]
    rows = [positions[component] for component in range(3)]
    rows[0] = jnp.where(kinds > 0, -rows[0], rows[0])
    rows.append(kinds.astype(jnp.float32))
    rows = jnp.concatenate(rows, axis=0)
    for target in range(out_ref.shape[0]):
        out_ref[target] = rows


def prepare_kernel(
    neighbours,
    embed_one_w,
    embed_one_b,
    embed_two_w,
    embed_two_b,
    embed_three_w,
    embed_three_b,
    fit_one_w,
    fit_one_b,
    fit_two_w,
    fit_two_b,
    fit_three_w,
    fit_three_b,
    constants,
    codes_ref,
    columns_ref,
    second_ref,
    third_ref,
    one_high_ref,
    one_low_ref,
    two_high_ref,
    two_low_ref,
    three_high_ref,
    three_low_ref,
    phase_ref,
    green_ref,
    rows,
    square,
    arrivals,
    *held,
):
    sources = (
        neighbours,
        embed_one_w,
        embed_one_b,
        embed_two_w,
        embed_two_b,
        embed_three_w,
        embed_three_b,
        fit_one_b,
        fit_two_b,
        fit_three_b,
        constants,
        fit_two_w,
        fit_three_w,
        fit_one_w,
    )
    copies = [
        pltpu.make_async_copy(source, target, arrivals.at[k])
        for k, (source, target) in enumerate(zip(sources, held))
    ]
    for copy in copies:
        copy.start()
    (
        neighbours,
        embed_one_w,
        embed_one_b,
        embed_two_w,
        embed_two_b,
        embed_three_w,
        embed_three_b,
        fit_one_b,
        fit_two_b,
        fit_three_b,
        constants,
        fit_two_w,
        fit_three_w,
        fit_one_w,
    ) = held
    for copy in copies[:11]:
        copy.wait()
    pieces = lax.axis_size("wide") * lax.axis_size("narrow")
    piece = lax.axis_index("wide") * lax.axis_size("narrow") + lax.axis_index("narrow")
    width_one = embed_one_w.shape[1]
    hidden = fit_two_w.shape[0]
    codes_ref[...] = jnp.transpose(neighbours[...].astype(jnp.float32)).astype(jnp.int32)
    rows[...] = jnp.zeros_like(rows)
    for kind in range(2):
        rows[kind : kind + 1, 0:width_one] = embed_one_w[kind : kind + 1, :]
        rows[2 + kind : 3 + kind, 0:width_one] = embed_one_b[kind : kind + 1, :]
        rows[2 + kind : 3 + kind, width_one : width_one + 1] = jnp.full((1, 1), 40.0, jnp.float32)
    for row, source in ((4, fit_one_b), (5, fit_two_b), (6, fit_three_b)):
        rows[row : row + 1, 0:hidden] = source[...]
    columns_ref[...] = jnp.transpose(rows[...])

    row = lax.broadcasted_iota(jnp.int32, square.shape, 0)
    lane = lax.broadcasted_iota(jnp.int32, square.shape, 1)
    for width, weight, bias, target in (
        (width_one, embed_two_w, embed_two_b, second_ref),
        (2 * width_one, embed_three_w, embed_three_b, third_ref),
    ):
        tall, deep = target.shape[0] // 2, target.shape[1] // 3
        again = (lane - tall == row) | (lane - tall == row + width)
        again = (again & (row < width)) | ((lane - tall == 2 * width) & (row == width))
        square[...] = jnp.where(again, 1.0, 0.0)
        square[0:width, 0 : 2 * width] = weight[...]
        square[width : width + 1, 0 : 2 * width] = bias[...]
        high, low = split(jnp.transpose(square[...])[0 : 2 * tall, 0:deep])
        target[...] = jnp.concatenate([high, high, low], axis=1)
    square[...] = jnp.zeros_like(square)
    for copy in copies[11:13]:
        copy.wait()
    for source, high_ref, low_ref in (
        (fit_two_w, two_high_ref, two_low_ref),
        (fit_three_w, three_high_ref, three_low_ref),
    ):
        square[0:hidden, 0:hidden] = source[...]
        high_ref[...], low_ref[...] = split(jnp.transpose(square[...])[0:hidden, 0:hidden])

    fine = GRID_Y // 2 // pieces
    shape = (phase_ref.shape[0], 128)
    row = lax.broadcasted_iota(jnp.int32, shape, 0)
    mode = piece * fine + row // 2
    for part in range(GRID_Y // 128):
        cell = lax.broadcasted_iota(jnp.int32, shape, 1) + part * 128
        spot = wrapped(mode * cell, GRID_Y)
        cosine = lookup(constants[0:1, :], spot)
        sine = lookup(constants[1:2, :], spot)
        alternate = (1 - 2 * lax.rem(cell, 2)).astype(jnp.float32)
        odd = jnp.where(mode == 0, alternate, -sine)
        value = jnp.where(lax.rem(row, 2) == 0, cosine, odd)
        phase_ref[:, part * 128 : (part + 1) * 128] = jnp.where(row < 2 * fine, value, 0.0)

    column = jnp.transpose(constants[...])
    lane = lax.broadcasted_iota(jnp.int32, (1, GRID_Y), 1)
    for j in range(fine + 1):
        here = lane == (GRID_Y // 2 if j == fine else piece * fine + j)
        factor = jnp.sum(jnp.where(here, constants[2:3, :], 0.0), axis=1, keepdims=True)
        part = jnp.sum(jnp.where(here, constants[3:4, :], 0.0), axis=1, keepdims=True)
        wave = (part + constants[5:6, :]) + column[:, 7:8]
        top = (factor * constants[4:5, :]) * column[:, 6:7]
        green_ref[j] = jnp.where(wave == 0.0, 0.0, top / jnp.where(wave == 0.0, 1.0, wave))

    copies[13].wait()
    one_high_ref[...], one_low_ref[...] = split(fit_one_w[...])


def centroid_kernel(
    table,
    codes,
    columns,
    second,
    third,
    one_high,
    one_low,
    two_high,
    two_low,
    three_high,
    three_low,
    fit_out_w,
    dipole_ref,
    shift_ref,
    table_ref,
    matrix,
    descriptor,
    arrivals,
    *held,
):
    sources = (table, codes, columns, second, third)
    sources += (one_high, one_low, two_high, two_low, three_high, three_low, fit_out_w)
    copies = [
        pltpu.make_async_copy(source, target, arrivals.at[k])
        for k, (source, target) in enumerate(zip(sources, held))
    ]
    for copy in copies:
        copy.start()
    table, codes, columns, second, third = held[:5]
    one_high, one_low, two_high, two_low, three_high, three_low, fit_out_w = held[5:]
    for copy in copies[:5]:
        copy.wait()
    handing_on = pltpu.make_async_copy(table, table_ref, arrivals.at[len(copies)])
    handing_on.start()
    wide_count, narrow_count, _, atoms = table.shape
    listed = codes.shape[0]
    width_three = fit_out_w.shape[0]
    width_one = width_three // 4
    hidden_width = two_high.shape[0]
    cells = (GRID_X // wide_count, GRID_Y, GRID_Z // narrow_count)
    at_wide = lax.axis_index("wide")
    at_narrow = lax.axis_index("narrow")
    own = jnp.abs(table[at_wide, at_narrow])
    nearby = []
    for step in range(9):
        wide_at = lax.rem(at_wide + (step // 3 - 1) + wide_count, wide_count)
        narrow_at = lax.rem(at_narrow + (step % 3 - 1) + narrow_count, narrow_count)
        nearby.append(table[wide_at, narrow_at])

    second_all = second[...]
    third_all = third[...]
    weight_oxygen = jnp.broadcast_to(columns[0:ROW_PAD, 0:1], (ROW_PAD, atoms))
    weight_hydrogen = jnp.broadcast_to(columns[0:ROW_PAD, 1:2], (ROW_PAD, atoms))
    bias_oxygen = jnp.broadcast_to(columns[0:ROW_PAD, 2:3], (ROW_PAD, atoms))
    bias_hydrogen = jnp.broadcast_to(columns[0:ROW_PAD, 3:4], (ROW_PAD, atoms))
    matrix[...] = jnp.zeros_like(matrix)

    def chunk(first):
        code = codes[pl.ds(first, SLOT_CHUNK), :]
        slot = wrapped(code, atoms)
        if atoms & (atoms - 1) == 0:
            offset = lax.shift_right_logical(code, atoms.bit_length() - 1)
        else:
            offset = code // atoms
        step_x = jnp.where(offset >= 9, 1, 0) + jnp.where(offset >= 18, 1, 0)
        rest = offset - 9 * step_x
        step_z = jnp.where(rest >= 3, 1, 0) + jnp.where(rest >= 6, 1, 0)
        step_y = rest - 3 * step_z
        brick = step_x * 3 + step_z
        found = []
        for component in range(3):
            picked = jnp.zeros((SLOT_CHUNK, atoms), jnp.float32)
            for step in range(9):
                row = jnp.broadcast_to(
                    nearby[step][component : component + 1], (SLOT_CHUNK, atoms)
                )
                here = jnp.take_along_axis(row, slot, axis=1, mode="promise_in_bounds")
                picked = jnp.where(brick == step, here, picked)
            found.append(picked)
        hydrogen = found[0] < 0.0
        found[0] = jnp.abs(found[0])
        scaled = []
        for component, step in enumerate((step_x, step_y, step_z)):
            extent = float(cells[component])
            relative = (step - 1).astype(jnp.float32) * extent + (
                found[component] - own[component : component + 1]
            ) * extent
            scaled.append(relative * (1.0 / radius_scale))
        smooth = 1.0 / (
            1.0 + (scaled[0] * scaled[0] + scaled[1] * scaled[1] + scaled[2] * scaled[2])
        )
        radial = [smooth] + [smooth * part for part in scaled]
        first_layers = []
        for k in range(SLOT_CHUNK):
            row = smooth[k : k + 1]
            kind = hydrogen[k : k + 1]
            weight = jnp.where(kind, weight_hydrogen, weight_oxygen)
            bias = jnp.where(kind, bias_hydrogen, bias_oxygen)
            first_layers.append(jnp.tanh(weight * row + bias))
        layer_one = jnp.concatenate(first_layers, axis=1)
        high, low = split(layer_one)
        both = lax.dot_general(
            second_all,
            jnp.concatenate([high, low, high], axis=0),
            NN,
            preferred_element_type=jnp.float32,
        )
        tall = both.shape[0] // 2
        layer_two = jnp.tanh(both[:tall]) + both[tall:]
        deep = third_all.shape[1] // 3
        rest = jnp.zeros((deep - tall, layer_two.shape[1]), jnp.float32)
        high, low = split(jnp.concatenate([layer_two, rest], axis=0))
        both = lax.dot_general(
            third_all,
            jnp.concatenate([high, low, high], axis=0),
            NN,
            preferred_element_type=jnp.float32,
        )
        tall = both.shape[0] // 2
        layer_three = jnp.tanh(both[:tall]) + both[tall:]
        for part in range(4):
            total = matrix[part]
            for k in range(SLOT_CHUNK):
                total = total + layer_three[:, k * atoms : (k + 1) * atoms] * radial[part][k : k + 1]
            matrix[part] = total

    def chunks(index, carry):
        for step in range(CHUNK_BODY):
            chunk(pl.multiple_of((index * CHUNK_BODY + step) * SLOT_CHUNK, SLOT_CHUNK))
        return carry

    lax.fori_loop(0, listed // (CHUNK_BODY * SLOT_CHUNK), chunks, 0)

    parts = []
    for part in range(4):
        parts.append(matrix[part, 0:width_three, :] * (1.0 / listed))
    leading = [part[0:AXIS_COLUMNS] for part in parts]
    for row in range(width_three):
        total = parts[0][row : row + 1] * leading[0]
        for part in range(1, 4):
            total = total + parts[part][row : row + 1] * leading[part]
        descriptor[row * AXIS_COLUMNS : (row + 1) * AXIS_COLUMNS, :] = total
    for copy in copies[5:]:
        copy.wait()

    def layer(high_ref, low_ref, given, column):
        weights = (high_ref[...], low_ref[...])
        return jnp.tanh(multiply(weights, split(given)) + columns[0:hidden_width, column : column + 1])

    hidden = layer(one_high, one_low, descriptor[...], 4)
    hidden = hidden + layer(two_high, two_low, hidden, 5)
    hidden = hidden + layer(three_high, three_low, hidden, 6)
    coeffs = multiply(split(fit_out_w[...]), split(hidden))
    vector = jnp.concatenate(
        [jnp.sum(coeffs * parts[1 + c], axis=0, keepdims=True) for c in range(3)], axis=0
    )
    oxygen = 1.0 - own[3:4]
    for c in range(3):
        dipole_ref[c] = vector[c : c + 1] * oxygen
    moved = wannier_reach * jnp.tanh(vector)
    moved = jnp.concatenate([moved, jnp.zeros((1, atoms), jnp.float32)], axis=0)
    for target in range(shift_ref.shape[0]):
        shift_ref[target] = moved
    handing_on.wait()


def mesh_kernel(
    cells,
    shifts,
    phase,
    green_ref,
    fold_stack,
    unfold_stack,
    out_ref,
    grid,
    planes,
    packed,
    weights_z,
    slopes_z,
    waves,
    wave_slopes,
    *across_refs,
):
    wide_count, narrow_count, _, atoms = cells.shape
    cells_x = GRID_X // wide_count
    cells_z = GRID_Z // narrow_count
    window = cells_z + HALO_Z
    reach = cells_x + HALO_X
    pair = 2 * atoms
    length = wide_count * pair
    copies = grid.shape[0]
    fine = grid.shape[1]
    channels = 2 * fine
    rows = phase.shape[0]
    half_x = GRID_X // 2
    half_z = GRID_Z // 2
    piece = lax.axis_index("wide") * narrow_count + lax.axis_index("narrow")
    lane_zero = lax.broadcasted_iota(jnp.int32, (1, half_x), 1) == 0
    row_zero = lax.broadcasted_iota(jnp.int32, (half_z, 1), 0) == 0

    def fold():
        return (fold_stack[0:GRID_X, :], fold_stack[GRID_X:, :])

    def unfold():
        return (unfold_stack[0:GRID_X, :], unfold_stack[GRID_X:, :])

    def sites(at_wide, at_narrow):
        atom = cells[at_wide, at_narrow]
        moved = shifts[at_wide, at_narrow]
        found = []
        for component in range(3):
            start = atom[component : component + 1]
            found.append(jnp.concatenate([start, start + moved[component : component + 1]], axis=1))
        oxygen = 1.0 - atom[3:4]
        found.append(jnp.concatenate([6.0 * oxygen + atom[3:4], -8.0 * oxygen], axis=1))
        return found

    def line(at_narrow):
        groups = [sites(at_wide, at_narrow) for at_wide in range(wide_count)]
        return [jnp.concatenate([g[k] for g in groups], axis=1) for k in range(4)]

    def splines_z(row):
        counter = lax.broadcasted_iota(jnp.int32, (window, 1), 0).astype(jnp.float32)
        return spline_pair(row - (counter - float(HALO_Z)))

    def fill_x(row, targets):
        counter = lax.broadcasted_iota(jnp.int32, (reach, 1), 0).astype(jnp.float32)
        both = spline_pair(row - (counter - float(HALO_X)))
        rest = jnp.zeros((128 - reach, length), jnp.bfloat16)
        for values, ref in zip(both, targets):
            high, low = split(values)
            ref[0:reach, :] = high
            ref[reach:128, :] = rest
            ref[128 : 128 + reach, :] = low
            ref[128 + reach : 256, :] = rest

    grid[:, :, 0:HALO_Z, :] = jnp.zeros((copies, fine, HALO_Z, 2 * GRID_X), jnp.float32)

    weights = across_refs[:LOOP_BODY]
    slopes = across_refs[LOOP_BODY:]

    def spread(index, odd):
        at_narrow = LOOP_BODY * index + odd
        row_x, row_y, row_z, charge = line(at_narrow)
        lower = jnp.floor(row_y)
        back = lax.broadcasted_iota(jnp.int32, (8, 1), 0)
        value_y, slope_y = spline_pair((row_y - lower) + back.astype(jnp.float32))
        cell = wrapped(lower.astype(jnp.int32) - back + GRID_Y, GRID_Y)
        wave_blocks = []
        slope_blocks = []
        for block in range(length // 128):
            lanes = slice(block * 128, (block + 1) * 128)
            wave = jnp.zeros((rows, 128), jnp.float32)
            wave_slope = jnp.zeros((rows, 128), jnp.float32)
            for k in range(4):
                spot = jnp.broadcast_to(cell[k : k + 1, lanes], (rows, 128))
                found = lookup(phase[...], spot)
                wave = wave + value_y[k : k + 1, lanes] * found
                wave_slope = wave_slope + slope_y[k : k + 1, lanes] * found
            wave_blocks.append(wave)
            slope_blocks.append(wave_slope)
        wave = jnp.concatenate(wave_blocks, axis=1)
        waves[at_narrow] = wave
        wave_slopes[at_narrow] = jnp.concatenate(slope_blocks, axis=1)
        fill_x(row_x, (weights[odd].at[index], slopes[odd].at[index]))
        value_z, slope_z = splines_z(row_z)
        weights_z[at_narrow] = value_z
        slopes_z[at_narrow] = slope_z
        charged = wave * charge
        first = pl.multiple_of(at_narrow * cells_z, HALO_Z)
        for at_wide in range(wide_count):
            lanes = slice(at_wide * pair, (at_wide + 1) * pair)
            near = value_z[:, lanes]
            left = jnp.concatenate(
                [near * charged[c : c + 1, lanes] for c in range(channels)], axis=0
            )
            high, low = split(left)
            across = weights[odd][index, :, lanes]
            total = lax.dot_general(high, across, NT, preferred_element_type=jnp.float32)
            rest = lax.dot_general(low, across[0:128], NT, preferred_element_type=jnp.float32)
            total = total[:, 0:128] + (total[:, 128:256] + rest)
            start = at_wide // copies * 128
            for c in range(channels):
                spot = slice(c % 2 * GRID_X + start, c % 2 * GRID_X + start + 128)
                k = at_wide % copies
                part = total[c * window : (c + 1) * window]
                grid[k, c // 2, pl.ds(first, HALO_Z), spot] += part[:HALO_Z]
                grid[k, c // 2, pl.ds(first + HALO_Z, cells_z), spot] = part[HALO_Z:]

    def in_groups(step):
        def body(index, carry):
            for odd in range(LOOP_BODY):
                step(index, odd)
            return carry

        lax.fori_loop(0, narrow_count // LOOP_BODY, body, 0)

    in_groups(spread)

    def gather(j, carry):
        for lanes in (slice(0, GRID_X), slice(GRID_X, 2 * GRID_X)):
            total = None
            for k in range(copies):
                moved = pltpu.roll(grid[k, j, :, lanes], (k * cells_x - HALO_X) % GRID_X, 1)
                total = moved if total is None else total + moved
            planes[j, :, lanes] = total[HALO_Z:]
            planes[j, GRID_Z - HALO_Z :, lanes] += total[:HALO_Z]
        return carry

    lax.fori_loop(0, fine, gather, 0)
    is_first = piece == 0

    def paired(real, imag, zero, axis):
        half = real.shape[axis] // 2
        first = (slice(None),) * axis + (slice(0, half),)
        second = (slice(None),) * axis + (slice(half, 2 * half),)
        real_c, real_s = real[first], real[second]
        if imag is None:
            none = jnp.zeros_like(real_s)
            real_all = [real_c, jnp.where(zero, real_s, real_c)]
            imag_all = [jnp.where(zero, none, -real_s), jnp.where(zero, none, real_s)]
        else:
            imag_c, imag_s = imag[first], imag[second]
            real_all = [
                real_c + jnp.where(zero, 0.0, imag_s),
                jnp.where(zero, real_s, real_c - imag_s),
            ]
            imag_all = [
                imag_c - jnp.where(zero, 0.0, real_s),
                jnp.where(zero, imag_s, imag_c + real_s),
            ]
        return jnp.concatenate(real_all, axis=axis), jnp.concatenate(imag_all, axis=axis)

    def merged(real, imag, zero, axis):
        half = real.shape[axis] // 2
        first = (slice(None),) * axis + (slice(0, half),)
        second = (slice(None),) * axis + (slice(half, 2 * half),)
        real_a, real_b = real[first], real[second]
        imag_a, imag_b = imag[first], imag[second]
        real = [
            real_a + jnp.where(zero, 0.0, real_b),
            jnp.where(zero, real_b, imag_b - imag_a),
        ]
        imag = [
            imag_a + jnp.where(zero, 0.0, imag_b),
            jnp.where(zero, imag_b, real_a - real_b),
        ]
        return jnp.concatenate(real, axis=axis), jnp.concatenate(imag, axis=axis)

    modes = {}
    parts = []

    def slot(j):
        first_imag = planes[0, :, GRID_X:]
        if j == fine:
            real, imag = jnp.where(is_first, first_imag, 0.0), None
        else:
            real, imag = planes[j, :, 0:GRID_X], planes[j, :, GRID_X:]
            if j == 0:
                imag = jnp.where(is_first, 0.0, imag)
        real = split(real)
        imag = None if imag is None else split(imag)
        yield
        real = by_right(real, fold())
        imag = None if imag is None else by_right(imag, fold())
        yield
        real, imag = paired(real, imag, lane_zero, 1)
        real, imag = split(real), split(imag)
        yield
        real, imag = by_left(unfold_stack[...], real), by_left(unfold_stack[...], imag)
        yield
        real, imag = paired(real, imag, row_zero, 0)
        green = green_ref[j]
        mode = GRID_Y // 2 if j == fine else piece * fine + j
        share = jnp.where((mode == 0) | (mode == GRID_Y // 2), 0.5, 1.0)
        parts.append(share * jnp.sum(green * (real * real + imag * imag), axis=0, keepdims=True))
        real, imag = green * real, green * imag
        if j == fine:
            modes[j] = (real, imag)
            return
        if j == 0:
            real, imag = real - modes[fine][1], imag + modes[fine][0]
        real, imag = merged(real, imag, row_zero, 0)
        real, imag = split(real), split(imag)
        yield
        real, imag = by_left(fold_stack[...], real), by_left(fold_stack[...], imag)
        yield
        real, imag = merged(real, imag, lane_zero, 1)
        scale = jnp.where(piece * fine + j == 0, 1.0, 2.0)
        real, imag = split(real * scale), split(imag * scale)
        yield
        real, imag = by_right(real, unfold()), by_right(imag, unfold())
        yield
        for k, part in enumerate((real, imag)):
            turned = [
                pltpu.roll(part, (HALO_X - at_wide * cells_x) % GRID_X, 1)
                for at_wide in range(copies)
            ]
            for at_wide in range(wide_count):
                start = at_wide // copies * 128
                moved = turned[at_wide % copies][:, start : start + 128]
                high = moved.astype(jnp.bfloat16).astype(jnp.float32)
                again = pltpu.roll(high, reach % 128, 1)
                low = pltpu.roll(moved - high, 2 * reach % 128, 1)
                sides = []
                for side in range(2):
                    lane = lax.broadcasted_iota(jnp.int32, (1, 128), 1) + side * 128
                    value = jnp.where(lane < 2 * reach, again, low)
                    if side == 0:
                        value = jnp.where(lane < reach, high, value)
                    sides.append(value.astype(jnp.bfloat16))
                block = jnp.concatenate(sides, axis=1)
                packed[at_wide, 2 * j + k, HALO_BITS:, :] = block
                packed[at_wide, 2 * j + k, 0:HALO_BITS, :] = block[GRID_Z - HALO_BITS :]

    waiting = [slot(j) for j in [fine, *range(fine)]]
    running = []
    while waiting or running:
        if waiting:
            running.append(waiting.pop(0))
        running = [one for one in running if next(one, running) is not running]
    energy = sum(parts[1:], parts[0])
    energy = jnp.broadcast_to(jnp.sum(energy, axis=1, keepdims=True), (1, 128))

    def collect(index, odd):
        at_narrow = LOOP_BODY * index + odd
        value_z = weights_z[at_narrow]
        slope_z = slopes_z[at_narrow]
        first = pl.multiple_of(at_narrow * cells_z, HALO_BITS)
        wave = waves[at_narrow]
        wave_slope = wave_slopes[at_narrow]
        for at_wide in range(wide_count):
            lanes = slice(at_wide * pair, (at_wide + 1) * pair)
            tall = cells_z + HALO_BITS
            left = jnp.concatenate(
                [packed[at_wide, c, pl.ds(first, tall), :] for c in range(channels)], axis=0
            )

            def across(right):
                high = right[0:reach]
                rest = jnp.zeros((256 - 3 * reach, pair), jnp.bfloat16)
                right = jnp.concatenate([high, right[128 : 128 + reach], high, rest], axis=0)
                return lax.dot_general(left, right, NN, preferred_element_type=jnp.float32)

            value = across(weights[odd][index, :, lanes])
            slope = across(slopes[odd][index, :, lanes])
            plain = jnp.zeros((window, pair), jnp.float32)
            along_x = plain
            along_y = plain
            for c in range(channels):
                block = slice((c + 1) * tall - window, (c + 1) * tall)
                plain = plain + value[block] * wave[c : c + 1, lanes]
                along_x = along_x + slope[block] * wave[c : c + 1, lanes]
                along_y = along_y + value[block] * wave_slope[c : c + 1, lanes]
            near = value_z[:, lanes]
            near_slope = slope_z[:, lanes]
            results = [
                jnp.sum(near * plain, axis=0, keepdims=True),
                -jnp.sum(near * along_x, axis=0, keepdims=True),
                -jnp.sum(near * along_y, axis=0, keepdims=True),
                -jnp.sum(near_slope * plain, axis=0, keepdims=True),
            ]
            for k, row in enumerate(results):
                out_ref[at_wide, at_narrow, :, k * pair : (k + 1) * pair] = row
            out_ref[at_wide, at_narrow, :, 4 * pair :] = energy

    in_groups(collect)


def finish_kernel(arrived, species, atom_ref, centroid_ref, energy_ref):
    atoms = species.shape[1]
    total = arrived[0]
    for k in range(1, arrived.shape[0]):
        total = total + arrived[k]
    oxygen = 1.0 - species[...].astype(jnp.float32)
    for k in range(4):
        atom_ref[k] = total[:, 2 * k * atoms : (2 * k + 1) * atoms]
        centroid_ref[k] = total[:, (2 * k + 1) * atoms : (2 * k + 2) * atoms] * oxygen
    energy_ref[...] = total[:, 8 * atoms :] * (1.0 / (atoms * arrived.shape[0]))


def mode_factors(length, order):
    wrapped = np.where(2 * order >= length, order - length, order)
    square = (wrapped / length) ** 2
    ratio = (4.0 + 2.0 * np.cos(2.0 * math.pi * order / length)) / 6.0
    return np.stack([np.exp(-(math.pi**2) * square / ewald_beta**2) / ratio**2, square])


def folded_order(length):
    half = length // 2
    counter = np.arange(half)
    return np.concatenate([counter, np.where(counter == 0, half, length - counter)])


def fold_table(length):
    half = length // 2
    turns = np.outer(np.arange(length), np.arange(half)) % length * (2.0 * math.pi / length)
    sines = np.sin(turns)
    sines[:, 0] = 1.0 - 2.0 * (np.arange(length) % 2)
    return np.concatenate([np.cos(turns), sines], axis=1)


def halves(table):
    high = table.astype(jnp.bfloat16)
    low = (table - high.astype(np.float64)).astype(jnp.bfloat16)
    return high, low


def vmem(count):
    return [pl.BlockSpec(memory_space=pltpu.VMEM)] * count


def hbm(count):
    return [pl.BlockSpec(memory_space=pltpu.HBM)] * count


def shaped(shape, dtype=jnp.float32):
    return jax.ShapeDtypeStruct(shape, dtype)


def limits(mebibytes):
    return pltpu.CompilerParams(vmem_limit_bytes=mebibytes * 1024 * 1024)


def local(
    positions,
    species,
    neighbours,
    embed_one_w,
    embed_one_b,
    embed_two_w,
    embed_two_b,
    embed_three_w,
    embed_three_b,
    fit_one_w,
    fit_one_b,
    fit_two_w,
    fit_two_b,
    fit_three_w,
    fit_three_b,
    fit_out_w,
):
    axes = ("wide", "narrow")
    wide_count = lax.axis_size("wide")
    narrow_count = lax.axis_size("narrow")
    pieces = wide_count * narrow_count
    atoms = positions.shape[4]
    listed = neighbours.shape[4]
    fine = GRID_Y // 2 // pieces
    width_three = embed_three_w.shape[1]
    entries, hidden = fit_one_w.shape
    kinds = species.reshape(1, atoms)

    packed = pl.pallas_call(
        pack_kernel,
        out_shape=shaped((pieces, 4, atoms)),
        in_specs=vmem(2),
        out_specs=vmem(1)[0],
        name="pack",
    )(positions.reshape(3, 1, atoms), kinds)
    table = lax.all_to_all(packed, axes, 0, 0, tiled=True)
    table = table.reshape(wide_count, narrow_count, 4, atoms)

    tall_two = -(-(width_three // 2 + 1) // 8) * 8
    tall_three = -(-width_three // 8) * 8
    bf16 = jnp.bfloat16
    wave_rows = -(-2 * fine // 8) * 8
    angle = np.arange(GRID_Y) * (2.0 * math.pi / GRID_Y)
    constants = np.concatenate(
        [
            np.stack([np.cos(angle), np.sin(angle)]),
            mode_factors(GRID_Y, np.arange(GRID_Y)),
            mode_factors(GRID_X, folded_order(GRID_X)),
            mode_factors(GRID_Z, folded_order(GRID_Z)),
        ]
    )
    constants[2] *= coulomb / (math.pi * GRID_X * GRID_Y * GRID_Z)
    arguments = (
        neighbours.reshape(atoms, listed),
        embed_one_w,
        embed_one_b,
        embed_two_w,
        embed_two_b[None],
        embed_three_w,
        embed_three_b[None],
        fit_one_w.T,
        fit_one_b[None],
        fit_two_w,
        fit_two_b[None],
        fit_three_w,
        fit_three_b[None],
        jnp.asarray(constants, jnp.float32),
    )
    held = [arguments[k] for k in (0, 1, 2, 3, 4, 5, 6, 8, 10, 12, 13, 9, 11, 7)]
    prepared = pl.pallas_call(
        prepare_kernel,
        out_shape=(
            shaped((listed, atoms), jnp.int32),
            shaped((256, 16)),
            shaped((2 * tall_two, 3 * ROW_PAD), bf16),
            shaped((2 * tall_three, 6 * ROW_PAD), bf16),
            shaped((hidden, entries), bf16),
            shaped((hidden, entries), bf16),
        )
        + (shaped((hidden, hidden), bf16),) * 4
        + (shaped((wave_rows, GRID_Y)), shaped((fine + 1, GRID_Z, GRID_X))),
        in_specs=hbm(len(arguments)),
        out_specs=tuple(vmem(12)),
        scratch_shapes=[
            pltpu.VMEM((16, 256), jnp.float32),
            pltpu.VMEM((256, 256), jnp.float32),
            pltpu.SemaphoreType.DMA((len(held),)),
        ]
        + [pltpu.VMEM(array.shape, array.dtype) for array in held],
        compiler_params=limits(62),
        cost_estimate=pl.CostEstimate(
            flops=1000000, bytes_accessed=8 * entries * hidden, transcendentals=0
        ),
        name="prepare",
    )(*arguments)
    phase, green = prepared[10:]
    fitted = (table, *prepared[:10], fit_out_w.T)
    dipole, shifts, table = pl.pallas_call(
        centroid_kernel,
        out_shape=(shaped((3, 1, atoms)), shaped((pieces, 4, atoms)), shaped(table.shape)),
        in_specs=hbm(12),
        out_specs=tuple(vmem(2) + hbm(1)),
        scratch_shapes=[
            pltpu.VMEM((4, tall_three, atoms), jnp.float32),
            pltpu.VMEM((width_three * AXIS_COLUMNS, atoms), jnp.float32),
            pltpu.SemaphoreType.DMA((len(fitted) + 1,)),
        ]
        + [pltpu.VMEM(array.shape, array.dtype) for array in fitted],
        compiler_params=limits(62),
        name="centroids",
    )(*fitted)
    shifts = lax.all_to_all(shifts, axes, 0, 0, tiled=True)
    shifts = shifts.reshape(wide_count, narrow_count, 4, atoms)

    cells_x = GRID_X // wide_count
    copies = 128 // cells_x
    component = lax.broadcasted_iota(jnp.int32, table.shape, 2)
    extents = (cells_x, GRID_Y, GRID_Z // narrow_count)
    cells = jnp.abs(table)
    for k, extent in enumerate(extents):
        cells = jnp.where(component == k, cells * float(extent), cells)
    length = wide_count * 2 * atoms
    out_width = 8 * atoms + 128
    partial = pl.pallas_call(
        mesh_kernel,
        out_shape=shaped((wide_count, narrow_count, 1, out_width)),
        in_specs=vmem(6),
        out_specs=vmem(1)[0],
        scratch_shapes=[
            pltpu.VMEM((copies, fine, HALO_Z + GRID_Z, 2 * GRID_X), jnp.float32),
            pltpu.VMEM((fine, GRID_Z, 2 * GRID_X), jnp.float32),
            pltpu.VMEM((wide_count, 2 * fine, HALO_BITS + GRID_Z, 256), bf16),
        ]
        + [pltpu.VMEM((narrow_count, GRID_Z // narrow_count + HALO_Z, length), jnp.float32)] * 2
        + [pltpu.VMEM((narrow_count, wave_rows, length), jnp.float32)] * 2
        + [pltpu.VMEM((narrow_count // LOOP_BODY, 256, length), bf16)] * (2 * LOOP_BODY),
        compiler_params=limits(48),
        name="mesh",
    )(
        cells,
        shifts,
        phase,
        green,
        jnp.asarray(np.concatenate(halves(fold_table(GRID_X)))),
        jnp.asarray(np.concatenate(halves(fold_table(GRID_X).T))),
    )
    arrived = lax.all_to_all(partial.reshape(pieces, 1, out_width), axes, 0, 0, tiled=True)
    atom_field, centroid_field, energy = pl.pallas_call(
        finish_kernel,
        out_shape=(shaped((4, 1, atoms)), shaped((4, 1, atoms)), shaped((1, 128))),
        in_specs=vmem(2),
        out_specs=tuple(vmem(3)),
        name="finish",
    )(arrived, kinds)
    atom_field = atom_field.reshape(4, 1, 1, 1, atoms)
    centroid_field = centroid_field.reshape(4, 1, 1, 1, atoms)
    return (dipole.reshape(3, 1, 1, 1, atoms), atom_field, centroid_field, energy[0, 0])


def solution(mesh):
    column = P(None, "wide", "narrow", None, None)
    in_specs = (column, P("wide", "narrow", None, None), P("wide", "narrow", None, None, None))
    in_specs = in_specs + (P(),) * 13
    out_specs = (column, column, column, P())
    return jax.shard_map(local, mesh=mesh, in_specs=in_specs, out_specs=out_specs, check_vma=False)
```
